32 devices in a mesh: dp: 4 (over y, core), heads: 8 (over z, x).
Axes of the slice: x: 2, y: 2, z: 4, core: 2. Of those that a mesh axis runs over, the one named last changes fastest.
Arguments:
- block_in: bfloat16 [8192, 2048], P(('dp', 'heads')), may hold values from -6 to 6
- seq_counts: int32 [4, 2], P('dp'), may hold values from 0 to 4, as said below
- norm1_gain: float32 [2048], replicated, may hold values from 0.5 to 1.5
- w_qkvg: bfloat16 [2048, 4, 2048], P(None, None, 'heads'), may hold values from -0.125 to 0.125
- conv_weight: float32 [3, 4, 2048], P(None, None, 'heads'), may hold values from -3 to 3
- w_gates: bfloat16 [2048, 2, 16], P(None, None, 'heads'), may hold values from -0.125 to 0.125
- gate_params: float32 [2, 16], P(None, 'heads'), may hold values from -9 to 1, as said below
- out_gain: float32 [128], replicated, may hold values from 0.5 to 1.5
- w_out: bfloat16 [2048, 2048], P('heads'), may hold values from -0.25 to 0.25
- norm2_gain: float32 [2048], replicated, may hold values from 0.5 to 1.5
- w_gate_up: bfloat16 [2048, 2, 5632], P(None, None, 'heads'), may hold values from -0.125 to 0.125
- w_down: bfloat16 [5632, 2048], P('heads'), may hold values from -0.078125 to 0.078125
- cotangent: bfloat16 [8192, 2048], P(('dp', 'heads')), may hold values from -6 to 6
Outputs:
- layer_out: bfloat16 [8192, 2048], P(('dp', 'heads'))
- grad_in: float32 [8192, 2048], P(('dp', 'heads'))
- grad_norm1_gain: float32 [2048], replicated
- grad_w_qkvg: float32 [2048, 4, 2048], P(None, None, 'heads')
- grad_conv_weight: float32 [3, 4, 2048], P(None, None, 'heads')
- grad_w_gates: float32 [2048, 2, 16], P(None, None, 'heads')
- grad_gate_params: float32 [2, 16], P(None, 'heads')
- grad_out_gain: float32 [128], replicated
- grad_w_out: float32 [2048, 2048], P('heads')
- grad_norm2_gain: float32 [2048], replicated
- grad_w_gate_up: float32 [2048, 2, 5632], P(None, None, 'heads')
- grad_w_down: float32 [5632, 2048], P('heads')
The draws below stay inside these ranges and needn't reach their ends.
Inputs may be any that keep to these rules, and one draw needn't show every extreme that they name: `seq_counts`: column 0 counts sequences of 512 tokens, column 1 sequence of 2048 tokens. A replica holds either one long sequence and no short one, or 1 to 4 short ones and no long one. In every draw some replica holds a long sequence and some other replica holds 4 short ones. `gate_params`: row 0 is a log decay rate, row 1 a bias.
All inputs are finite; a program needn't handle non-finite values.
Results may differ from the reference program's by a relative error of at most 0.017.
Values may be sent and summed in bfloat16 or wider, within the bound.
A program may use at most 256 MiB of HBM per device.

```python
import jax
import jax.numpy as jnp
from jax import lax

D = 2048
H = 16
HD = 128
FF = 5632
CONV = 4
BLOCK_LEN = 64
SHORTS = 4
SEQ_SHORT = 512
TOK_REP = 2048
TOKENS = 8192
N_DP = 4


def draw_seq_counts(key, part):
    key = jax.random.fold_in(key, 3)
    keys = jax.random.split(key, 4)
    replica = jnp.arange(N_DP, dtype=jnp.int32)
    long_one = jax.random.randint(keys[0], (), 0, N_DP)
    full_one = (long_one + 1 + jax.random.randint(keys[1], (), 0, N_DP - 1)) % N_DP
    longer = jax.random.randint(keys[2], (N_DP,), 0, 3) == 0
    shorts = jax.random.randint(keys[3], (N_DP,), 1, SHORTS + 1)
    longer = jnp.where(replica == long_one, True, jnp.where(replica == full_one, False, longer))
    shorts = jnp.where(replica == full_one, SHORTS, shorts)
    return jnp.stack([jnp.where(longer, 0, shorts), longer.astype(jnp.int32)], 1).astype(jnp.int32)


def draw_gate_params(key, part):
    key = jax.random.fold_in(key, 7)
    first_key, second_key = jax.random.split(key)
    rates = jax.random.uniform(first_key, (H,), jnp.float32, -9.0, -2.5)
    biases = jax.random.uniform(second_key, (H,), jnp.float32, -1.0, 1.0)
    return jnp.stack([rates, biases])


def block_scale(own_key, shape, cuts, smallest, top_value):
    level, own = 1.0, jax.random.fold_in(own_key, 6)
    for dim, shards_of in cuts:
        steps = jnp.exp(jax.random.uniform(jax.random.fold_in(own, dim), (shards_of,), jnp.float32, smallest / len(cuts), top_value / len(cuts)))
        level = level * jnp.repeat(steps, shape[dim] // shards_of).reshape([-1 if axis == dim else 1 for axis in range(len(shape))])
    return level


def centred(rng, extent, scale, most, pieces=(), held_as=jnp.bfloat16):
    drawn = jax.random.normal(rng, extent, jnp.float32) * scale
    if len(pieces) > 0:
        drawn = block_scale(rng, extent, pieces, -0.22, 0.18) * drawn
    return jnp.clip(drawn, min=-most, max=most).astype(held_as)


def setup_inputs(seed: int = 0) -> dict:
    seeds = jax.random.split(jax.random.key(seed), 14)
    block_in = centred(seeds[0], (TOKENS, D), 1.0, 6.0, ((0, 32),))
    seq_counts = draw_seq_counts(jax.random.fold_in(seeds[13], 71), 0)
    norm1_gain = jnp.clip(1.0 + 0.1 * jax.random.normal(seeds[2], (D,), jnp.float32), 0.5, 1.5)
    w_qkvg = centred(seeds[3], (D, 4, H * HD), D ** -0.5, 0.125, ((2, 8),))
    conv_weight = centred(seeds[4], (3, CONV, H * HD), 0.5, 3.0, ((2, 8),), jnp.float32)
    w_gates = centred(seeds[5], (D, 2, H), D ** -0.5, 0.125, ((2, 8),))
    gate_params = draw_gate_params(jax.random.fold_in(seeds[13], 71), 0)
    out_gain = jnp.clip(1.0 + 0.1 * jax.random.normal(seeds[7], (HD,), jnp.float32), 0.5, 1.5)
    w_out = centred(seeds[8], (H * HD, D), (H * HD // 4) ** -0.5, 0.25, ((0, 8),))
    norm2_gain = jnp.clip(1.0 + 0.1 * jax.random.normal(seeds[9], (D,), jnp.float32), 0.5, 1.5)
    w_gate_up = centred(seeds[10], (D, 2, FF), D ** -0.5, 0.125, ((2, 8),))
    w_down = centred(seeds[11], (FF, D), FF ** -0.5, 0.078125, ((0, 8),))
    cotangent = centred(seeds[12], (TOKENS, D), 1.0, 6.0, ((0, 32),))
    return dict(block_in=block_in, seq_counts=seq_counts, norm1_gain=norm1_gain, w_qkvg=w_qkvg, conv_weight=conv_weight, w_gates=w_gates, gate_params=gate_params, out_gain=out_gain, w_out=w_out, norm2_gain=norm2_gain, w_gate_up=w_gate_up, w_down=w_down, cotangent=cotangent)


@jax.custom_vjp
def low(v):
    return lax.optimization_barrier(v.astype(jnp.bfloat16)).astype(jnp.float32)

@jax.custom_vjp
def low_back(v):
    return v

def low_keep(v):
    return (low(v), None)

def low_pass(kept, grad):
    return (grad,)

def back_keep(v):
    return (v, None)

def back_low(kept, grad):
    return (low(grad),)
low.defvjp(low_keep, low_pass)
low_back.defvjp(back_keep, back_low)
epsilon = 1e-06
highest = lax.Precision.HIGHEST

def rms_rows(values, gain):
    return values * lax.rsqrt(lax.optimization_barrier(jnp.mean(values * values, axis=-1, keepdims=True)) + epsilon) * gain

def layout(counts_row, row_count):
    row_index = jnp.arange(row_count, dtype=jnp.int32)
    longer = counts_row[1] > 0
    position = jnp.where(longer, row_index, row_index % SEQ_SHORT).astype(jnp.int32)
    live_rows = jnp.where(longer, True, row_index < counts_row[0] * SEQ_SHORT).astype(jnp.float32)
    return (position, live_rows)

def block_step(state_in, inputs):
    query, key_vec, value, log_decay, beta_gate, keep_flag = inputs
    state_in = state_in * keep_flag
    block_rows = query.shape[0]
    cumulative = jnp.cumsum(log_decay, axis=0)
    row_index = jnp.arange(block_rows)[:, None]
    col_index = jnp.arange(block_rows)[None, :]
    lower_mask = row_index > col_index
    lower_incl = row_index >= col_index
    log_ratio = cumulative.T[:, :, None] - cumulative.T[:, None, :]
    strict = jnp.where(lower_mask, jnp.exp(jnp.where(lower_mask, log_ratio, 0.0)), 0.0)
    inclusive = jnp.where(lower_incl, jnp.exp(jnp.where(lower_incl, log_ratio, 0.0)), 0.0)
    decay_in = jnp.exp(cumulative).T[:, :, None]
    beta_rows = beta_gate.T[:, :, None]
    key_gram = jnp.einsum('ihd,jhd->hij', key_vec, key_vec, precision=highest)
    link_matrix = beta_rows * key_gram * strict
    right_side = beta_rows * (jnp.transpose(value, (1, 0, 2)) - decay_in * jnp.einsum('ihk,hvk->hiv', key_vec, state_in, precision=highest))
    power_term = -link_matrix
    delta_rows = right_side
    for doubling in range(block_rows.bit_length() - 1):
        delta_rows = delta_rows + jnp.einsum('hij,hjv->hiv', power_term, delta_rows, precision=highest)
        power_term = jnp.einsum('hij,hjk->hik', power_term, power_term, precision=highest)
    query_gram = jnp.einsum('ihd,jhd->hij', query, key_vec, precision=highest) * inclusive
    carried = decay_in * jnp.einsum('ihk,hvk->hiv', query, state_in, precision=highest)
    block_out = carried + jnp.einsum('hij,hjv->hiv', query_gram, delta_rows, precision=highest)
    tail_decay = jnp.exp(cumulative[-1][None, :] - cumulative)
    new_state = jnp.exp(cumulative[-1])[:, None, None] * state_in + jnp.einsum('hjv,jhk->hvk', delta_rows * tail_decay.T[:, :, None], key_vec, precision=highest)
    return (new_state, jnp.transpose(block_out, (1, 0, 2)))

def mixer(pre_main, pre_gates, conv_weight, gate_params, out_gain, position):
    row_count = pre_main.shape[0]
    channels = pre_main.shape[1] // 4
    heads_here = pre_gates.shape[1] // 2
    head_size = channels // heads_here
    triple = pre_main[:, :3 * channels].reshape(row_count, 3, channels)
    convolved = jnp.zeros_like(triple)
    for lag_step in range(conv_weight.shape[1]):
        shifted = jnp.pad(triple, ((lag_step, 0), (0, 0), (0, 0)))[:row_count]
        valid_rows = (position >= lag_step).astype(jnp.float32)[:, None, None]
        convolved = convolved + shifted * valid_rows * conv_weight[:, lag_step, :][None]
    convolved = jax.nn.silu(convolved)
    query = convolved[:, 0].reshape(row_count, heads_here, head_size)
    key_vec = convolved[:, 1].reshape(row_count, heads_here, head_size)
    value = convolved[:, 2].reshape(row_count, heads_here, head_size)
    query = query * lax.rsqrt(lax.optimization_barrier(jnp.sum(query * query, axis=-1, keepdims=True)) + epsilon) * head_size ** (-0.5)
    key_vec = key_vec * lax.rsqrt(lax.optimization_barrier(jnp.sum(key_vec * key_vec, axis=-1, keepdims=True)) + epsilon)
    log_decay = -jnp.exp(gate_params[0])[None] * jax.nn.softplus(pre_gates[:, :heads_here] + gate_params[1][None])
    beta_gate = jax.nn.sigmoid(pre_gates[:, heads_here:])
    keep_flags = (position[::BLOCK_LEN] > 0).astype(jnp.float32)
    blocks = row_count // BLOCK_LEN

    def to_blocks(array):
        return array.reshape((blocks, BLOCK_LEN) + array.shape[1:])
    start_state = jnp.zeros((heads_here, head_size, head_size), jnp.float32)
    final, block_outs = lax.scan(jax.checkpoint(block_step), start_state, (to_blocks(query), to_blocks(key_vec), to_blocks(value), to_blocks(log_decay), to_blocks(beta_gate), keep_flags))
    raw_out = block_outs.reshape(row_count, heads_here, head_size)
    normed = rms_rows(raw_out, out_gain)
    gate_out = jax.nn.silu(pre_main[:, 3 * channels:]).reshape(row_count, heads_here, head_size)
    return (normed * gate_out).reshape(row_count, channels)

def forward(block_in, seq_counts, norm1_gain, w_qkvg, conv_weight, w_gates, gate_params, out_gain, w_out, norm2_gain, w_gate_up, w_down):
    main_weight = w_qkvg.reshape(D, -1)
    gates_weight = w_gates.reshape(D, -1)
    feed_weight = w_gate_up.reshape(D, -1)

    def replica_layer(carried, pair):
        replica_x, counts_row = pair
        position, live_rows = layout(counts_row, TOK_REP)
        normed1 = low(rms_rows(replica_x, norm1_gain))
        pre_main = low_back(jnp.dot(normed1, main_weight, precision=highest, preferred_element_type=jnp.float32))
        pre_gates = low_back(jnp.dot(normed1, gates_weight, precision=highest, preferred_element_type=jnp.float32))
        mixed_out = low(mixer(pre_main, pre_gates, conv_weight, gate_params, out_gain, position))
        branch = low_back(jnp.dot(mixed_out, w_out, precision=highest, preferred_element_type=jnp.float32))
        middle = replica_x + live_rows[:, None] * branch
        normed2 = low(rms_rows(middle, norm2_gain))
        gate_up = low_back(jnp.dot(normed2, feed_weight, precision=highest, preferred_element_type=jnp.float32))
        hidden = low(jax.nn.silu(gate_up[:, :FF]) * gate_up[:, FF:])
        feed = low_back(jnp.dot(hidden, w_down, precision=highest, preferred_element_type=jnp.float32))
        return (carried, middle + live_rows[:, None] * feed)
    unused, outputs = lax.scan(replica_layer, jnp.zeros((), jnp.float32), (block_in.reshape(N_DP, TOK_REP, D), seq_counts))
    return outputs.reshape(N_DP * TOK_REP, D)

def reference(block_in, seq_counts, norm1_gain, w_qkvg, conv_weight, w_gates, gate_params, out_gain, w_out, norm2_gain, w_gate_up, w_down, cotangent):
    float_args = [a.astype(jnp.float32) for a in (block_in, norm1_gain, w_qkvg, conv_weight, w_gates, gate_params, out_gain, w_out, norm2_gain, w_gate_up, w_down)]

    def wrapped(*values):
        return forward(values[0], seq_counts, *values[1:])
    result, pull_back = jax.vjp(wrapped, *float_args)
    gradients = pull_back(cotangent.astype(jnp.float32))
    return (result.astype(jnp.bfloat16), gradients[0], gradients[1], gradients[2], gradients[3], gradients[4], gradients[5], gradients[6], gradients[7], gradients[8], gradients[9], gradients[10])
```

```python
import functools
import jax
import jax.numpy as jnp
from jax import lax
from jax.experimental import pallas as pl
from jax.experimental.pallas import tpu as pltpu
from jax.sharding import PartitionSpec as P

SEQ_SHORT = 512
CHUNK = 256
HEAD = 128
EPS = 1e-06
F32 = jnp.float32
BF16 = jnp.bfloat16
LOW, MID, TOP = lax.Precision.DEFAULT, lax.Precision.HIGH, lax.Precision.HIGHEST
NN, NT, TN = ((1,), (0,)), ((1,), (1,)), ((0,), (0,))
P_INV, P_FWD, P_BWD = MID, MID, MID


def dot(left, right, dims, precision):
    if precision is LOW:
        left, right = left.astype(BF16), right.astype(BF16)
        return lax.dot_general(left, right, (dims, ((), ())), preferred_element_type=F32)
    return lax.dot_general(
        left, right, (dims, ((), ())), precision=precision, preferred_element_type=F32
    )


def grid_index(shape, axis):
    return lax.broadcasted_iota(jnp.int32, shape, axis)


def positions(longer, first_row, count):
    rows = grid_index((count, 1), 0) + first_row
    return jnp.where(longer > 0, rows, rows % SEQ_SHORT)


def keeps(longer, first_row):
    start = jnp.where(longer > 0, first_row, first_row % SEQ_SHORT)
    return jnp.where(start > 0, 1.0, 0.0).astype(F32)


def softplus(x):
    return jnp.maximum(x, 0.0) + jnp.log1p(jnp.exp(-jnp.abs(x)))


def gate_values(gates, params, heads):
    lane = grid_index(gates.shape, 1)
    rate = jnp.exp(params[0:1])
    shifted = gates + params[1:2]
    log_decay = jnp.where(lane < heads, -rate * softplus(shifted), 0.0)
    return rate, shifted, log_decay


def lane_column(values, index):
    return values[:, index : index + 1]


def decays(cumulative, cumulative_rows, head, masks):
    column = lane_column(cumulative, head)
    row = cumulative_rows[head : head + 1, :]
    inclusive = masks[0]
    ratio = jnp.where(inclusive, jnp.exp(jnp.where(inclusive, column - row, 0.0)), 0.0)
    last = column[CHUNK - 1 : CHUNK, :]
    return ratio, jnp.exp(column), jnp.exp(last - column), jnp.exp(last)


def unit(values):
    scale = lax.rsqrt(jnp.sum(values * values, axis=-1, keepdims=True) + EPS)
    return values * scale, scale


def inverse(link, row, col):
    apart = row ^ col

    def level(size):
        return (apart >= size) & (apart < 2 * size)

    out = jnp.where(row == col, 1.0, 0.0) - jnp.where(level(1), link, 0.0)
    size = 2
    while size < CHUNK // 2:
        part = jnp.where(level(size), link, 0.0)
        out = out - dot(out, dot(part, out, NN, P_INV), NN, P_INV)
        size *= 2
    half = CHUNK // 2
    corner = dot(link[half:, :half], out[:half, :half], NN, P_INV)
    corner = -dot(out[half:, half:], corner, NN, P_INV)
    return jnp.concatenate(
        [out[:half], jnp.concatenate([corner, out[half:, half:]], axis=1)], axis=0
    )


def forward_kernel(
    heads, longer_ref, main_ref, conv_ref, params_ref, gain_ref,
    mixed_ref, conv_out_ref, raw_ref, delta_ref, solve_ref, state_ref, state, tail_rows,
):
    step = pl.program_id(0)
    first_row = step * CHUNK
    longer = longer_ref[0]
    width = heads * HEAD

    @pl.when(step == 0)
    def _():
        state[...] = jnp.zeros_like(state)
        tail_rows[...] = jnp.zeros_like(tail_rows)

    position = positions(longer, first_row, CHUNK)
    keep = keeps(longer, first_row)
    triple = main_ref[:, : 3 * width]
    padded = jnp.concatenate([tail_rows[...], triple], axis=0)
    taps = conv_ref[...]
    convolved = triple * taps[0:1]
    for lag in range(1, 4):
        shifted = padded[8 - lag : 8 - lag + CHUNK]
        convolved = convolved + jnp.where(position >= lag, shifted, 0.0) * taps[lag : lag + 1]
    tail_rows[...] = triple[CHUNK - 8 :]
    conv_out_ref[...] = convolved
    active = convolved * jax.nn.sigmoid(convolved)
    gates = main_ref[:, 4 * width :]
    rate, shifted_gate, log_decay = gate_values(gates, params_ref[...], heads)
    beta_all = jax.nn.sigmoid(gates)
    row = grid_index((CHUNK, CHUNK), 0)
    col = grid_index((CHUNK, CHUNK), 1)
    masks = (row >= col, row > col)
    cumulative = dot(jnp.where(masks[0], 1.0, 0.0), log_decay, NN, TOP)
    cumulative_rows = jnp.transpose(cumulative)
    for head in range(heads):
        cols = slice(head * HEAD, (head + 1) * HEAD)
        query = unit(active[:, head * HEAD : (head + 1) * HEAD])[0] * HEAD**-0.5
        key = unit(active[:, width + head * HEAD : width + (head + 1) * HEAD])[0]
        value = active[:, 2 * width + head * HEAD : 2 * width + (head + 1) * HEAD]
        beta = lane_column(beta_all, heads + head)
        ratio, decay_in, decay_out, decay_all = decays(cumulative, cumulative_rows, head, masks)
        grams = dot(jnp.concatenate([key, query], axis=0), key, NT, P_FWD)
        link = jnp.where(masks[1], beta * ratio * grams[:CHUNK], 0.0)
        solve = inverse(link, row, col)
        solve_ref[head] = solve
        both = dot(
            solve, jnp.concatenate([beta * value, (beta * decay_in) * key], axis=1), NN, P_FWD
        )
        entry = state[head] * keep
        state_ref[0, head] = entry
        carried = dot(
            jnp.concatenate([both[:, HEAD:], decay_in * query], axis=0), entry, NT, P_FWD
        )
        delta = both[:, :HEAD] - carried[:CHUNK]
        delta_ref[:, cols] = delta
        raw = carried[CHUNK:] + dot(grams[CHUNK:] * ratio, delta, NN, P_FWD)
        state[head] = decay_all * entry + dot(delta * decay_out, key, TN, P_FWD)
        raw_ref[:, cols] = raw
        scale = lax.rsqrt(jnp.mean(raw * raw, axis=-1, keepdims=True) + EPS)
        gate = main_ref[:, 3 * width + head * HEAD : 3 * width + (head + 1) * HEAD]
        mixed = raw * scale * gain_ref[...] * (gate * jax.nn.sigmoid(gate))
        mixed_ref[:, cols] = mixed.astype(mixed_ref.dtype)


def backward_kernel(
    heads, chunks, longer_ref, grad_ref, main_ref, conv_out_ref, raw_ref, delta_ref,
    solve_ref, state_ref, conv_ref, params_ref, gain_ref,
    dmain_ref, dconv_ref, dparams_ref, dgain_ref, dstate, head_rows,
):
    step = pl.program_id(0)
    first_row = (chunks - 1 - step) * CHUNK
    longer = longer_ref[0]
    width = heads * HEAD

    @pl.when(step == 0)
    def _():
        dstate[...] = jnp.zeros_like(dstate)
        head_rows[...] = jnp.zeros_like(head_rows)
        dconv_ref[...] = jnp.zeros_like(dconv_ref)
        dparams_ref[...] = jnp.zeros_like(dparams_ref)
        dgain_ref[...] = jnp.zeros_like(dgain_ref)

    keep = keeps(longer, first_row)
    convolved = conv_out_ref[...]
    sigmoid_conv = jax.nn.sigmoid(convolved)
    active = convolved * sigmoid_conv
    slope = sigmoid_conv * (1.0 + convolved * (1.0 - sigmoid_conv))
    gates = main_ref[:, 4 * width :]
    params = params_ref[...]
    rate, shifted_gate, log_decay = gate_values(gates, params, heads)
    beta_all = jax.nn.sigmoid(gates)
    row = grid_index((CHUNK, CHUNK), 0)
    col = grid_index((CHUNK, CHUNK), 1)
    masks = (row >= col, row > col)
    cumulative = dot(jnp.where(masks[0], 1.0, 0.0), log_decay, NN, TOP)
    cumulative_rows = jnp.transpose(cumulative)
    lane = grid_index((CHUNK, 128), 1)
    last_row = grid_index((CHUNK, 1), 0) == CHUNK - 1
    dcumulative = jnp.zeros((CHUNK, 128), F32)
    dbeta_all = jnp.zeros((CHUNK, 128), F32)
    gain = gain_ref[...]
    dgain = jnp.zeros((1, HEAD), F32)
    dconv_parts = [[], [], []]
    for head in range(heads):
        cols = slice(head * HEAD, (head + 1) * HEAD)
        gate = main_ref[:, 3 * width + head * HEAD : 3 * width + (head + 1) * HEAD]
        raw = raw_ref[:, cols]
        grad = grad_ref[:, cols]
        scale = lax.rsqrt(jnp.mean(raw * raw, axis=-1, keepdims=True) + EPS)
        normed = raw * scale
        sigmoid_gate = jax.nn.sigmoid(gate)
        gated = gate * sigmoid_gate
        product = grad * normed
        dgain = dgain + jnp.sum(product * gated, axis=0, keepdims=True)
        dgate = product * gain * (sigmoid_gate * (1.0 + gate * (1.0 - sigmoid_gate)))
        dmain_ref[:, 3 * width + head * HEAD : 3 * width + (head + 1) * HEAD] = dgate.astype(
            dmain_ref.dtype
        )
        dnormed = grad * gain * gated
        draw = scale * (dnormed - normed * jnp.mean(dnormed * normed, axis=-1, keepdims=True))
        query_unit, query_scale = unit(active[:, head * HEAD : (head + 1) * HEAD])
        query = query_unit * HEAD**-0.5
        key, key_scale = unit(active[:, width + head * HEAD : width + (head + 1) * HEAD])
        value = active[:, 2 * width + head * HEAD : 2 * width + (head + 1) * HEAD]
        beta = lane_column(beta_all, heads + head)
        ratio, decay_in, decay_out, decay_all = decays(cumulative, cumulative_rows, head, masks)
        entry = state_ref[0, head]
        delta = delta_ref[:, cols]
        dlater = dstate[head]
        gram = dot(query, key, NT, P_BWD) * ratio
        key_dlater = dot(key, dlater, NT, P_BWD)
        ddelta = dot(gram, draw, TN, P_BWD) + decay_out * key_dlater
        dright = dot(solve_ref[head], ddelta, TN, P_BWD)
        pairs = dot(jnp.concatenate([dright, draw], axis=0), delta, NT, P_BWD)
        dlink = jnp.where(masks[1], -pairs[:CHUNK] * ratio, 0.0)
        dgram = pairs[CHUNK:] * ratio
        on_entry = dot(jnp.concatenate([dright, draw], axis=0), entry, NN, P_BWD)
        key_entry = dot(key, entry, NT, P_BWD)
        on_key = dot(jnp.concatenate([dlink, dgram], axis=0), key, NN, P_BWD)
        dquery = decay_in * on_entry[CHUNK:] + on_key[CHUNK:]
        link_key = on_key[:CHUNK]
        key_read = beta * (link_key - decay_in * on_entry[:CHUNK])
        key_tail = decay_out * dot(delta, dlater, NN, P_BWD)
        key_write = (
            dot(beta * dlink, key, TN, P_BWD) + dot(dgram, query, TN, P_BWD) + key_tail
        )
        dkey = key_read + key_write
        dvalue = beta * dright
        dbeta = jnp.sum(
            dright * (value - decay_in * key_entry) + key * link_key, axis=-1, keepdims=True
        )
        dlog = jnp.sum(query * dquery + key * (key_read - key_write), axis=-1, keepdims=True)
        ending = decay_all * jnp.sum(
            jnp.sum(entry * dlater, axis=-1, keepdims=True), axis=0, keepdims=True
        ) + jnp.sum(jnp.sum(key * key_tail, axis=-1, keepdims=True), axis=0, keepdims=True)
        dlog = dlog + jnp.where(last_row, ending, 0.0)
        dcumulative = jnp.where(lane == head, dlog, dcumulative)
        dbeta_all = jnp.where(lane == heads + head, dbeta, dbeta_all)
        dstate[head] = keep * (
            decay_all * dlater
            + dot(decay_in * draw, query, TN, P_BWD)
            - dot((beta * decay_in) * dright, key, TN, P_BWD)
        )
        dquery = (HEAD**-0.5 * query_scale) * (
            dquery - query_unit * jnp.sum(dquery * query_unit, axis=-1, keepdims=True)
        )
        dkey = key_scale * (dkey - key * jnp.sum(dkey * key, axis=-1, keepdims=True))
        for kind, part in enumerate((dquery, dkey, dvalue)):
            dconv_parts[kind].append(part)
    dactive = jnp.concatenate([p for parts in dconv_parts for p in parts], axis=1)
    dconvolved = dactive * slope
    padded = jnp.concatenate([dconvolved, head_rows[...]], axis=0)
    position = positions(longer, first_row, CHUNK + 8)
    taps = conv_ref[...]
    triple = main_ref[:, : 3 * width]
    dtriple = dconvolved * taps[0:1]
    dconv_ref[0:1] += jnp.sum(dconvolved * triple, axis=0, keepdims=True)
    for lag in range(1, 4):
        moved = jnp.where(position >= lag, padded, 0.0)[lag : lag + CHUNK]
        dtriple = dtriple + moved * taps[lag : lag + 1]
        dconv_ref[lag : lag + 1] += jnp.sum(moved * triple, axis=0, keepdims=True)
    head_rows[...] = dconvolved[:8]
    dmain_ref[:, : 3 * width] = dtriple.astype(dmain_ref.dtype)
    dlog_decay = dot(jnp.where(row <= col, 1.0, 0.0), dcumulative, NN, TOP)
    dshifted = -dlog_decay * rate * jax.nn.sigmoid(shifted_gate)
    dshifted = jnp.where(lane < heads, dshifted, 0.0)
    dparams_ref[0:1] += jnp.sum(dlog_decay * log_decay, axis=0, keepdims=True)
    dparams_ref[1:2] += jnp.sum(dshifted, axis=0, keepdims=True)
    dmain_ref[:, 4 * width :] = (dshifted + dbeta_all * beta_all * (1.0 - beta_all)).astype(
        dmain_ref.dtype
    )
    dgain_ref[...] += dgain


def row_block(width, chunks, backward):
    if backward:
        return pl.BlockSpec((CHUNK, width), lambda i: (chunks - 1 - i, 0))
    return pl.BlockSpec((CHUNK, width), lambda i: (i, 0))


def whole_block(shape):
    return pl.BlockSpec(shape, lambda i: (0,) * len(shape))


def mixer_forward(longer, main, conv, params, gain):
    rows, width = main.shape[0], conv.shape[1] // 3
    heads, chunks = width // HEAD, rows // CHUNK
    rowed = functools.partial(row_block, chunks=chunks, backward=False)
    shape = jax.ShapeDtypeStruct
    return pl.pallas_call(
        functools.partial(forward_kernel, heads),
        grid=(chunks,),
        in_specs=[
            pl.BlockSpec(memory_space=pltpu.SMEM),
            rowed(4 * width + 128),
            whole_block((4, 3 * width)),
            whole_block((2, 128)),
            whole_block((1, HEAD)),
        ],
        out_specs=[
            rowed(width),
            rowed(3 * width),
            rowed(width),
            rowed(width),
            pl.BlockSpec((heads, CHUNK, CHUNK), lambda i: (0, i, 0)),
            pl.BlockSpec((1, heads, HEAD, HEAD), lambda i: (i, 0, 0, 0)),
        ],
        out_shape=[
            shape((rows, width), BF16),
            shape((rows, 3 * width), F32),
            shape((rows, width), F32),
            shape((rows, width), F32),
            shape((heads, rows, CHUNK), F32),
            shape((chunks, heads, HEAD, HEAD), F32),
        ],
        scratch_shapes=[
            pltpu.VMEM((heads, HEAD, HEAD), F32),
            pltpu.VMEM((8, 3 * width), F32),
        ],
        compiler_params=pltpu.CompilerParams(vmem_limit_bytes=48 * 2**20),
        name="mixer_forward",
    )(longer, main, conv, params, gain)


def mixer_backward(longer, grad, main, saved, conv, params, gain):
    rows, width = main.shape[0], conv.shape[1] // 3
    heads, chunks = width // HEAD, rows // CHUNK
    rowed = functools.partial(row_block, chunks=chunks, backward=True)
    shape = jax.ShapeDtypeStruct
    return pl.pallas_call(
        functools.partial(backward_kernel, heads, chunks),
        grid=(chunks,),
        in_specs=[
            pl.BlockSpec(memory_space=pltpu.SMEM),
            rowed(width),
            rowed(4 * width + 128),
            rowed(3 * width),
            rowed(width),
            rowed(width),
            pl.BlockSpec((heads, CHUNK, CHUNK), lambda i: (0, chunks - 1 - i, 0)),
            pl.BlockSpec((1, heads, HEAD, HEAD), lambda i: (chunks - 1 - i, 0, 0, 0)),
            whole_block((4, 3 * width)),
            whole_block((2, 128)),
            whole_block((1, HEAD)),
        ],
        out_specs=[
            rowed(4 * width + 128),
            whole_block((4, 3 * width)),
            whole_block((2, 128)),
            whole_block((1, HEAD)),
        ],
        out_shape=[
            shape((rows, 4 * width + 128), BF16),
            shape((4, 3 * width), F32),
            shape((2, 128), F32),
            shape((1, HEAD), F32),
        ],
        scratch_shapes=[
            pltpu.VMEM((heads, HEAD, HEAD), F32),
            pltpu.VMEM((8, 3 * width), F32),
        ],
        compiler_params=pltpu.CompilerParams(vmem_limit_bytes=48 * 2**20),
        name="mixer_backward",
    )(longer, grad, main, *saved, conv, params, gain)


def rms_rows(values, gain):
    return values * lax.rsqrt(jnp.mean(values * values, axis=-1, keepdims=True) + EPS) * gain


def matmul(left, right, dims):
    return lax.dot_general(left, right, (dims, ((), ())), preferred_element_type=F32)


def gather_rows(values):
    return lax.all_gather(values, "heads", axis=0, tiled=True)


def scatter_rows(values):
    return lax.psum_scatter(
        values.astype(BF16), "heads", scatter_dimension=0, tiled=True
    ).astype(F32)


def sum_replicas(values):
    return lax.psum(values.astype(BF16), "dp").astype(F32)


def on_device(
    block_in,
    seq_counts,
    norm1_gain,
    w_qkvg,
    conv_weight,
    w_gates,
    gate_params,
    out_gain,
    w_out,
    norm2_gain,
    w_gate_up,
    w_down,
    cotangent,
):
    own_rows, features = block_in.shape
    all_rows = own_rows * lax.axis_size("heads")
    width = conv_weight.shape[2]
    heads = gate_params.shape[1]
    longer = seq_counts[0, 1:2]
    first_row = lax.axis_index("heads") * own_rows
    row_index = first_row + jnp.arange(own_rows, dtype=jnp.int32)
    live_own = jnp.where(longer[0] > 0, True, row_index < seq_counts[0, 0] * SEQ_SHORT)
    live_own = live_own.astype(F32)[:, None]
    input_rows = block_in.astype(F32)
    normed1, pull_norm1 = jax.vjp(rms_rows, input_rows, norm1_gain)
    full_normed1 = gather_rows(normed1.astype(BF16))
    weight = jnp.concatenate(
        [
            w_qkvg.reshape(features, 4 * width),
            w_gates.reshape(features, 2 * heads),
            jnp.zeros((features, 128 - 2 * heads), BF16),
        ],
        axis=1,
    )
    projected = matmul(full_normed1, weight, NN)
    taps = jnp.transpose(conv_weight, (1, 0, 2)).reshape(4, 3 * width)
    params = jnp.pad(gate_params, ((0, 0), (0, 128 - heads)))
    gain_row = out_gain[None]
    mixed, *saved = mixer_forward(longer, projected, taps, params, gain_row)
    branch = scatter_rows(matmul(mixed, w_out, NN))
    grad_top = cotangent.astype(F32)
    grad_feed = gather_rows((live_own * grad_top).astype(BF16))
    middle = input_rows + live_own * branch
    normed2, pull_norm2 = jax.vjp(rms_rows, middle, norm2_gain)
    full_normed2 = gather_rows(normed2.astype(BF16))
    feed_weight = w_gate_up.reshape(features, -1)
    hidden_cols = w_down.shape[0]
    gate_up = matmul(full_normed2, feed_weight, NN)
    gate_pre = gate_up[:, :hidden_cols]
    up_pre = gate_up[:, hidden_cols:]
    hidden = (jax.nn.silu(gate_pre) * up_pre).astype(BF16)
    grad_hidden = matmul(grad_feed, w_down, NT)
    sigmoid_gate = jax.nn.sigmoid(gate_pre)
    grad_gate = grad_hidden * up_pre * sigmoid_gate * (1.0 + gate_pre * (1.0 - sigmoid_gate))
    grad_up = grad_hidden * gate_pre * sigmoid_gate
    grad_gate_up = jnp.concatenate([grad_gate, grad_up], 1).astype(BF16)
    grad_normed2 = scatter_rows(matmul(grad_gate_up, feed_weight, NT))
    feed = scatter_rows(matmul(hidden, w_down, NN))
    layer_out = (middle + live_own * feed).astype(BF16)
    grad_middle_part, grad_gain2 = pull_norm2(grad_normed2)
    grad_middle = grad_top + grad_middle_part
    grad_mix = gather_rows((live_own * grad_middle).astype(BF16))
    grad_feed_weight = matmul(full_normed2, grad_gate_up, TN)
    grad_down = matmul(hidden, grad_feed, TN)
    grad_mixed = matmul(grad_mix, w_out, NT)
    grad_wout = matmul(mixed, grad_mix, TN)
    dprojected, dtaps, dparams, dgain = mixer_backward(
        longer, grad_mixed, projected, saved, taps, params, gain_row
    )
    grad_normed1 = scatter_rows(matmul(dprojected, weight, NT))
    grad_weight = matmul(full_normed1, dprojected, TN)
    grad_input_part, grad_gain1 = pull_norm1(grad_normed1)
    grad_in = grad_middle + grad_input_part
    grad_conv = jnp.transpose(dtaps.reshape(4, 3, width), (1, 0, 2))
    summed_ff = (
        sum_replicas(grad_feed_weight.reshape(w_gate_up.shape)),
        sum_replicas(grad_down),
    )
    summed_out = sum_replicas(grad_wout)
    small = lax.psum(
        (grad_conv, grad_weight[:, 4 * width : 4 * width + 2 * heads], dparams[:, :heads]), "dp"
    )
    gains = lax.psum((grad_gain1, grad_gain2, dgain[0]), ("dp", "heads"))
    return (
        layer_out,
        grad_in,
        gains[0],
        sum_replicas(grad_weight[:, : 4 * width]).reshape(w_qkvg.shape),
        small[0],
        small[1].reshape(w_gates.shape),
        small[2],
        gains[2],
        summed_out,
        gains[1],
        summed_ff[0],
        summed_ff[1],
    )


def solution(mesh):
    return jax.shard_map(
        on_device,
        mesh=mesh,
        in_specs=(
            P(("dp", "heads"), None),
            P("dp", None),
            P(),
            P(None, None, "heads"),
            P(None, None, "heads"),
            P(None, None, "heads"),
            P(None, "heads"),
            P(),
            P("heads", None),
            P(),
            P(None, None, "heads"),
            P("heads", None),
            P(("dp", "heads"), None),
        ),
        out_specs=(
            P(("dp", "heads"), None),
            P(("dp", "heads"), None),
            P(),
            P(None, None, "heads"),
            P(None, None, "heads"),
            P(None, None, "heads"),
            P(None, "heads"),
            P(),
            P("heads", None),
            P(),
            P(None, None, "heads"),
            P("heads", None),
        ),
        check_vma=False,
    )
```

```python
import functools
import jax
import jax.numpy as jnp
from jax import lax
from jax.experimental import pallas as pl
from jax.experimental.pallas import tpu as pltpu
from jax.sharding import PartitionSpec as P

SEQ_SHORT = 512
CHUNK = 256
HEAD = 128
EPS = 1e-06
F32 = jnp.float32
BF16 = jnp.bfloat16
LOW, MID, TOP = lax.Precision.DEFAULT, lax.Precision.HIGH, lax.Precision.HIGHEST
NN, NT, TN = ((1,), (0,)), ((1,), (1,)), ((0,), (0,))
P_INV, P_FWD, P_BWD = MID, MID, MID


def dot(left, right, dims, precision):
    if precision is LOW:
        left, right = left.astype(BF16), right.astype(BF16)
        return lax.dot_general(left, right, (dims, ((), ())), preferred_element_type=F32)
    return lax.dot_general(
        left, right, (dims, ((), ())), precision=precision, preferred_element_type=F32
    )


def grid_index(shape, axis):
    return lax.broadcasted_iota(jnp.int32, shape, axis)


def positions(longer, first_row, count):
    rows = grid_index((count, 1), 0) + first_row
    return jnp.where(longer > 0, rows, rows % SEQ_SHORT)


def keeps(longer, first_row):
    start = jnp.where(longer > 0, first_row, first_row % SEQ_SHORT)
    return jnp.where(start > 0, 1.0, 0.0).astype(F32)


def softplus(x):
    return jnp.maximum(x, 0.0) + jnp.log1p(jnp.exp(-jnp.abs(x)))


def gate_values(gates, params, heads):
    lane = grid_index(gates.shape, 1)
    rate = jnp.exp(params[0:1])
    shifted = gates + params[1:2]
    log_decay = jnp.where(lane < heads, -rate * softplus(shifted), 0.0)
    return rate, shifted, log_decay


def lane_column(values, index):
    return values[:, index : index + 1]


def decays(cumulative, cumulative_rows, head, masks):
    column = lane_column(cumulative, head)
    row = cumulative_rows[head : head + 1, :]
    inclusive = masks[0]
    ratio = jnp.where(inclusive, jnp.exp(jnp.where(inclusive, column - row, 0.0)), 0.0)
    last = column[CHUNK - 1 : CHUNK, :]
    return ratio, jnp.exp(column), jnp.exp(last - column), jnp.exp(last)


def unit(values):
    scale = lax.rsqrt(jnp.sum(values * values, axis=-1, keepdims=True) + EPS)
    return values * scale, scale


def inverse(link, row, col):
    apart = row ^ col

    def level(size):
        return (apart >= size) & (apart < 2 * size)

    out = jnp.where(row == col, 1.0, 0.0) - jnp.where(level(1), link, 0.0)
    size = 2
    while size < CHUNK // 2:
        part = jnp.where(level(size), link, 0.0)
        out = out - dot(out, dot(part, out, NN, P_INV), NN, P_INV)
        size *= 2
    half = CHUNK // 2
    corner = dot(link[half:, :half], out[:half, :half], NN, P_INV)
    corner = -dot(out[half:, half:], corner, NN, P_INV)
    return jnp.concatenate(
        [out[:half], jnp.concatenate([corner, out[half:, half:]], axis=1)], axis=0
    )


def forward_kernel(
    heads, longer_ref, main_ref, conv_ref, params_ref, gain_ref,
    mixed_ref, conv_out_ref, raw_ref, delta_ref, solve_ref, state_ref, state, tail_rows,
):
    step = pl.program_id(0)
    first_row = step * CHUNK
    longer = longer_ref[0]
    width = heads * HEAD

    @pl.when(step == 0)
    def _():
        state[...] = jnp.zeros_like(state)
        tail_rows[...] = jnp.zeros_like(tail_rows)

    position = positions(longer, first_row, CHUNK)
    keep = keeps(longer, first_row)
    triple = main_ref[:, : 3 * width]
    padded = jnp.concatenate([tail_rows[...], triple], axis=0)
    taps = conv_ref[...]
    convolved = triple * taps[0:1]
    for lag in range(1, 4):
        shifted = padded[8 - lag : 8 - lag + CHUNK]
        convolved = convolved + jnp.where(position >= lag, shifted, 0.0) * taps[lag : lag + 1]
    tail_rows[...] = triple[CHUNK - 8 :]
    conv_out_ref[...] = convolved
    active = convolved * jax.nn.sigmoid(convolved)
    gates = main_ref[:, 4 * width :]
    rate, shifted_gate, log_decay = gate_values(gates, params_ref[...], heads)
    beta_all = jax.nn.sigmoid(gates)
    row = grid_index((CHUNK, CHUNK), 0)
    col = grid_index((CHUNK, CHUNK), 1)
    masks = (row >= col, row > col)
    cumulative = dot(jnp.where(masks[0], 1.0, 0.0), log_decay, NN, TOP)
    cumulative_rows = jnp.transpose(cumulative)
    for head in range(heads):
        cols = slice(head * HEAD, (head + 1) * HEAD)
        query = unit(active[:, head * HEAD : (head + 1) * HEAD])[0] * HEAD**-0.5
        key = unit(active[:, width + head * HEAD : width + (head + 1) * HEAD])[0]
        value = active[:, 2 * width + head * HEAD : 2 * width + (head + 1) * HEAD]
        beta = lane_column(beta_all, heads + head)
        ratio, decay_in, decay_out, decay_all = decays(cumulative, cumulative_rows, head, masks)
        grams = dot(jnp.concatenate([key, query], axis=0), key, NT, P_FWD)
        link = jnp.where(masks[1], beta * ratio * grams[:CHUNK], 0.0)
        solve = inverse(link, row, col)
        solve_ref[head] = solve
        both = dot(
            solve, jnp.concatenate([beta * value, (beta * decay_in) * key], axis=1), NN, P_FWD
        )
        entry = state[head] * keep
        state_ref[0, head] = entry
        carried = dot(
            jnp.concatenate([both[:, HEAD:], decay_in * query], axis=0), entry, NT, P_FWD
        )
        delta = both[:, :HEAD] - carried[:CHUNK]
        delta_ref[:, cols] = delta
        raw = carried[CHUNK:] + dot(grams[CHUNK:] * ratio, delta, NN, P_FWD)
        state[head] = decay_all * entry + dot(delta * decay_out, key, TN, P_FWD)
        raw_ref[:, cols] = raw
        scale = lax.rsqrt(jnp.mean(raw * raw, axis=-1, keepdims=True) + EPS)
        gate = main_ref[:, 3 * width + head * HEAD : 3 * width + (head + 1) * HEAD]
        mixed = raw * scale * gain_ref[...] * (gate * jax.nn.sigmoid(gate))
        mixed_ref[:, cols] = mixed.astype(mixed_ref.dtype)


def backward_kernel(
    heads, chunks, longer_ref, grad_ref, main_ref, conv_out_ref, raw_ref, delta_ref,
    solve_ref, state_ref, conv_ref, params_ref, gain_ref,
    dmain_ref, dconv_ref, dparams_ref, dgain_ref, dstate, head_rows,
):
    step = pl.program_id(0)
    first_row = (chunks - 1 - step) * CHUNK
    longer = longer_ref[0]
    width = heads * HEAD

    @pl.when(step == 0)
    def _():
        dstate[...] = jnp.zeros_like(dstate)
        head_rows[...] = jnp.zeros_like(head_rows)
        dconv_ref[...] = jnp.zeros_like(dconv_ref)
        dparams_ref[...] = jnp.zeros_like(dparams_ref)
        dgain_ref[...] = jnp.zeros_like(dgain_ref)

    keep = keeps(longer, first_row)
    convolved = conv_out_ref[...]
    sigmoid_conv = jax.nn.sigmoid(convolved)
    active = convolved * sigmoid_conv
    slope = sigmoid_conv * (1.0 + convolved * (1.0 - sigmoid_conv))
    gates = main_ref[:, 4 * width :]
    params = params_ref[...]
    rate, shifted_gate, log_decay = gate_values(gates, params, heads)
    beta_all = jax.nn.sigmoid(gates)
    row = grid_index((CHUNK, CHUNK), 0)
    col = grid_index((CHUNK, CHUNK), 1)
    masks = (row >= col, row > col)
    cumulative = dot(jnp.where(masks[0], 1.0, 0.0), log_decay, NN, TOP)
    cumulative_rows = jnp.transpose(cumulative)
    lane = grid_index((CHUNK, 128), 1)
    last_row = grid_index((CHUNK, 1), 0) == CHUNK - 1
    dcumulative = jnp.zeros((CHUNK, 128), F32)
    dbeta_all = jnp.zeros((CHUNK, 128), F32)
    gain = gain_ref[...]
    dgain = jnp.zeros((1, HEAD), F32)
    dconv_parts = [[], [], []]
    for head in range(heads):
        cols = slice(head * HEAD, (head + 1) * HEAD)
        gate = main_ref[:, 3 * width + head * HEAD : 3 * width + (head + 1) * HEAD]
        raw = raw_ref[:, cols]
        grad = grad_ref[:, cols]
        scale = lax.rsqrt(jnp.mean(raw * raw, axis=-1, keepdims=True) + EPS)
        normed = raw * scale
        sigmoid_gate = jax.nn.sigmoid(gate)
        gated = gate * sigmoid_gate
        product = grad * normed
        dgain = dgain + jnp.sum(product * gated, axis=0, keepdims=True)
        dgate = product * gain * (sigmoid_gate * (1.0 + gate * (1.0 - sigmoid_gate)))
        dmain_ref[:, 3 * width + head * HEAD : 3 * width + (head + 1) * HEAD] = dgate.astype(
            dmain_ref.dtype
        )
        dnormed = grad * gain * gated
        draw = scale * (dnormed - normed * jnp.mean(dnormed * normed, axis=-1, keepdims=True))
        query_unit, query_scale = unit(active[:, head * HEAD : (head + 1) * HEAD])
        query = query_unit * HEAD**-0.5
        key, key_scale = unit(active[:, width + head * HEAD : width + (head + 1) * HEAD])
        value = active[:, 2 * width + head * HEAD : 2 * width + (head + 1) * HEAD]
        beta = lane_column(beta_all, heads + head)
        ratio, decay_in, decay_out, decay_all = decays(cumulative, cumulative_rows, head, masks)
        entry = state_ref[0, head]
        delta = delta_ref[:, cols]
        dlater = dstate[head]
        gram = dot(query, key, NT, P_BWD) * ratio
        key_dlater = dot(key, dlater, NT, P_BWD)
        ddelta = dot(gram, draw, TN, P_BWD) + decay_out * key_dlater
        dright = dot(solve_ref[head], ddelta, TN, P_BWD)
        pairs = dot(jnp.concatenate([dright, draw], axis=0), delta, NT, P_BWD)
        dlink = jnp.where(masks[1], -pairs[:CHUNK] * ratio, 0.0)
        dgram = pairs[CHUNK:] * ratio
        on_entry = dot(jnp.concatenate([dright, draw], axis=0), entry, NN, P_BWD)
        key_entry = dot(key, entry, NT, P_BWD)
        on_key = dot(jnp.concatenate([dlink, dgram], axis=0), key, NN, P_BWD)
        dquery = decay_in * on_entry[CHUNK:] + on_key[CHUNK:]
        link_key = on_key[:CHUNK]
        key_read = beta * (link_key - decay_in * on_entry[:CHUNK])
        key_tail = decay_out * dot(delta, dlater, NN, P_BWD)
        key_write = (
            dot(beta * dlink, key, TN, P_BWD) + dot(dgram, query, TN, P_BWD) + key_tail
        )
        dkey = key_read + key_write
        dvalue = beta * dright
        dbeta = jnp.sum(
            dright * (value - decay_in * key_entry) + key * link_key, axis=-1, keepdims=True
        )
        dlog = jnp.sum(query * dquery + key * (key_read - key_write), axis=-1, keepdims=True)
        ending = decay_all * jnp.sum(
            jnp.sum(entry * dlater, axis=-1, keepdims=True), axis=0, keepdims=True
        ) + jnp.sum(jnp.sum(key * key_tail, axis=-1, keepdims=True), axis=0, keepdims=True)
        dlog = dlog + jnp.where(last_row, ending, 0.0)
        dcumulative = jnp.where(lane == head, dlog, dcumulative)
        dbeta_all = jnp.where(lane == heads + head, dbeta, dbeta_all)
        dstate[head] = keep * (
            decay_all * dlater
            + dot(decay_in * draw, query, TN, P_BWD)
            - dot((beta * decay_in) * dright, key, TN, P_BWD)
        )
        dquery = (HEAD**-0.5 * query_scale) * (
            dquery - query_unit * jnp.sum(dquery * query_unit, axis=-1, keepdims=True)
        )
        dkey = key_scale * (dkey - key * jnp.sum(dkey * key, axis=-1, keepdims=True))
        for kind, part in enumerate((dquery, dkey, dvalue)):
            dconv_parts[kind].append(part)
    dactive = jnp.concatenate([p for parts in dconv_parts for p in parts], axis=1)
    dconvolved = dactive * slope
    padded = jnp.concatenate([dconvolved, head_rows[...]], axis=0)
    position = positions(longer, first_row, CHUNK + 8)
    taps = conv_ref[...]
    triple = main_ref[:, : 3 * width]
    dtriple = dconvolved * taps[0:1]
    dconv_ref[0:1] += jnp.sum(dconvolved * triple, axis=0, keepdims=True)
    for lag in range(1, 4):
        moved = jnp.where(position >= lag, padded, 0.0)[lag : lag + CHUNK]
        dtriple = dtriple + moved * taps[lag : lag + 1]
        dconv_ref[lag : lag + 1] += jnp.sum(moved * triple, axis=0, keepdims=True)
    head_rows[...] = dconvolved[:8]
    dmain_ref[:, : 3 * width] = dtriple.astype(dmain_ref.dtype)
    dlog_decay = dot(jnp.where(row <= col, 1.0, 0.0), dcumulative, NN, TOP)
    dshifted = -dlog_decay * rate * jax.nn.sigmoid(shifted_gate)
    dshifted = jnp.where(lane < heads, dshifted, 0.0)
    dparams_ref[0:1] += jnp.sum(dlog_decay * log_decay, axis=0, keepdims=True)
    dparams_ref[1:2] += jnp.sum(dshifted, axis=0, keepdims=True)
    dmain_ref[:, 4 * width :] = (dshifted + dbeta_all * beta_all * (1.0 - beta_all)).astype(
        dmain_ref.dtype
    )
    dgain_ref[...] += dgain


def row_block(width, chunks, backward):
    if backward:
        return pl.BlockSpec((CHUNK, width), lambda i: (chunks - 1 - i, 0))
    return pl.BlockSpec((CHUNK, width), lambda i: (i, 0))


def whole_block(shape):
    return pl.BlockSpec(shape, lambda i: (0,) * len(shape))


def mixer_forward(longer, main, conv, params, gain):
    rows, width = main.shape[0], conv.shape[1] // 3
    heads, chunks = width // HEAD, rows // CHUNK
    rowed = functools.partial(row_block, chunks=chunks, backward=False)
    shape = jax.ShapeDtypeStruct
    return pl.pallas_call(
        functools.partial(forward_kernel, heads),
        grid=(chunks,),
        in_specs=[
            pl.BlockSpec(memory_space=pltpu.SMEM),
            rowed(4 * width + 128),
            whole_block((4, 3 * width)),
            whole_block((2, 128)),
            whole_block((1, HEAD)),
        ],
        out_specs=[
            rowed(width),
            rowed(3 * width),
            rowed(width),
            rowed(width),
            pl.BlockSpec((heads, CHUNK, CHUNK), lambda i: (0, i, 0)),
            pl.BlockSpec((1, heads, HEAD, HEAD), lambda i: (i, 0, 0, 0)),
        ],
        out_shape=[
            shape((rows, width), BF16),
            shape((rows, 3 * width), F32),
            shape((rows, width), F32),
            shape((rows, width), F32),
            shape((heads, rows, CHUNK), F32),
            shape((chunks, heads, HEAD, HEAD), F32),
        ],
        scratch_shapes=[
            pltpu.VMEM((heads, HEAD, HEAD), F32),
            pltpu.VMEM((8, 3 * width), F32),
        ],
        compiler_params=pltpu.CompilerParams(vmem_limit_bytes=48 * 2**20),
        name="mixer_forward",
    )(longer, main, conv, params, gain)


def mixer_backward(longer, grad, main, saved, conv, params, gain):
    rows, width = main.shape[0], conv.shape[1] // 3
    heads, chunks = width // HEAD, rows // CHUNK
    rowed = functools.partial(row_block, chunks=chunks, backward=True)
    shape = jax.ShapeDtypeStruct
    return pl.pallas_call(
        functools.partial(backward_kernel, heads, chunks),
        grid=(chunks,),
        in_specs=[
            pl.BlockSpec(memory_space=pltpu.SMEM),
            rowed(width),
            rowed(4 * width + 128),
            rowed(3 * width),
            rowed(width),
            rowed(width),
            pl.BlockSpec((heads, CHUNK, CHUNK), lambda i: (0, chunks - 1 - i, 0)),
            pl.BlockSpec((1, heads, HEAD, HEAD), lambda i: (chunks - 1 - i, 0, 0, 0)),
            whole_block((4, 3 * width)),
            whole_block((2, 128)),
            whole_block((1, HEAD)),
        ],
        out_specs=[
            rowed(4 * width + 128),
            whole_block((4, 3 * width)),
            whole_block((2, 128)),
            whole_block((1, HEAD)),
        ],
        out_shape=[
            shape((rows, 4 * width + 128), BF16),
            shape((4, 3 * width), F32),
            shape((2, 128), F32),
            shape((1, HEAD), F32),
        ],
        scratch_shapes=[
            pltpu.VMEM((heads, HEAD, HEAD), F32),
            pltpu.VMEM((8, 3 * width), F32),
        ],
        compiler_params=pltpu.CompilerParams(vmem_limit_bytes=48 * 2**20),
        name="mixer_backward",
    )(longer, grad, main, *saved, conv, params, gain)


MESH = pl.DeviceIdType.MESH
PIECES = 4


class Group:
    def __init__(self, count, deep):
        self.nz = 4 if count % 4 == 0 else 1
        self.nx = count // self.nz
        self.deep = min(deep, self.nz)
        self.size = self.deep * self.nx
        me = lax.axis_index("heads")
        self.z, self.x = me // self.nx, me % self.nx
        self.base = (self.z // self.deep) * self.deep
        self.own = (self.z - self.base) * self.nx + self.x

    def along_z(self, k):
        return (self.z - self.base + k) % self.deep

    def along_x(self, j):
        return (self.x + j) % self.nx

    def slot(self, k, j):
        return self.along_z(k) * self.nx + self.along_x(j)

    def device(self, k, j):
        return {"heads": self.base * self.nx + self.slot(k, j)}


def meet(count, wide):
    me = lax.axis_index("heads")
    replica = lax.axis_index("dp")
    replicas = lax.axis_size("dp")
    barrier = pltpu.get_barrier_semaphore()

    def greet(k, _):
        pl.semaphore_signal(
            barrier, inc=1, device_id={"heads": (me + k) % count}, device_id_type=MESH
        )
        return 0

    def greet_replica(k, _):
        pl.semaphore_signal(
            barrier, inc=1, device_id={"dp": (replica + k) % replicas}, device_id_type=MESH
        )
        return 0

    lax.fori_loop(1, count, greet, 0)
    if wide:
        lax.fori_loop(1, replicas, greet_replica, 0)
    pl.semaphore_wait(barrier, count - 1 + (replicas - 1 if wide else 0))


def arrived(ref, sem):
    pltpu.make_async_copy(ref, ref, sem).wait()


class Gather:
    def __init__(self, group, full, send_sems, recv_sems):
        self.group, self.full = group, full
        self.part = full.shape[1] // PIECES
        self.send_sems, self.recv_sems = send_sems, recv_sems
        self.sent = []

    @staticmethod
    def scratch(deep, nx, rows, cols):
        size = deep * nx
        return [
            pltpu.VMEM((size, rows, cols), BF16),
            pltpu.SemaphoreType.DMA((PIECES, deep + deep * nx)),
            pltpu.SemaphoreType.DMA((PIECES, size)),
        ]

    def rows(self, piece):
        return pl.ds(piece * self.part, self.part)

    def send(self, slot, piece, which, target):
        place = self.full.at[slot, self.rows(piece)]
        copy = pltpu.make_async_remote_copy(
            place, place, self.send_sems.at[piece, which], self.recv_sems.at[piece, slot],
            device_id=target, device_id_type=MESH,
        )
        copy.start()
        self.sent.append(copy)

    def receive(self, slot, piece):
        arrived(self.full.at[slot, self.rows(piece)], self.recv_sems.at[piece, slot])

    def start(self, piece):
        group = self.group
        for k in range(1, group.deep):
            self.send(group.own, piece, k, group.device(k, 0))
        for j in range(1, group.nx):
            self.send(group.own, piece, group.deep + j, group.device(0, j))

    def relay(self, piece):
        group = self.group
        for k in range(1, group.deep):
            self.receive(group.slot(k, 0), piece)
            for j in range(1, group.nx):
                self.send(
                    group.slot(k, 0), piece, group.deep + k * group.nx + j, group.device(0, j)
                )

    def finish(self, piece):
        group = self.group
        for j in range(1, group.nx):
            for k in range(group.deep):
                self.receive(group.slot(k, j), piece)

    def drain(self):
        for copy in self.sent:
            copy.wait_send()


class Scatter:
    def __init__(self, group, parts, over_x, sums, over_z, sems):
        self.group, self.parts = group, parts
        self.over_x, self.sums, self.over_z = over_x, sums, over_z
        self.part = parts.shape[1] // PIECES
        self.x_send, self.x_recv, self.z_send, self.z_recv = sems
        self.sent = []

    @staticmethod
    def scratch(deep, nx, rows, cols):
        return [
            pltpu.VMEM((deep * nx, rows, cols), BF16),
            pltpu.VMEM((deep, max(nx - 1, 1), rows, cols), BF16),
            pltpu.VMEM((deep, rows, cols), BF16),
            pltpu.VMEM((max(deep - 1, 1), rows, cols), BF16),
            pltpu.SemaphoreType.DMA((PIECES, deep, nx)),
            pltpu.SemaphoreType.DMA((PIECES, deep, nx)),
            pltpu.SemaphoreType.DMA((PIECES, deep)),
            pltpu.SemaphoreType.DMA((PIECES, deep)),
        ]

    def rows(self, piece):
        return pl.ds(piece * self.part, self.part)

    def copy(self, source, target, send_sem, recv_sem, device):
        copy = pltpu.make_async_remote_copy(
            source, target, send_sem, recv_sem, device_id=device, device_id_type=MESH
        )
        copy.start()
        self.sent.append(copy)

    def start(self, piece):
        group, rows = self.group, self.rows(piece)
        for k in range(group.deep):
            for j in range(1, group.nx):
                self.copy(
                    self.parts.at[group.slot(k + 1, j), rows],
                    self.over_x.at[k, j - 1, rows],
                    self.x_send.at[piece, k, j],
                    self.x_recv.at[piece, k, j],
                    group.device(0, j),
                )

    def relay(self, piece):
        group, rows = self.group, self.rows(piece)
        for k in range(group.deep):
            total = self.parts[group.slot(k + 1, 0), rows].astype(F32)
            for j in range(1, group.nx):
                arrived(self.over_x.at[k, j - 1, rows], self.x_recv.at[piece, k, j])
                total = total + self.over_x[k, j - 1, rows].astype(F32)
            self.sums[k, rows] = total.astype(BF16)
            if k < group.deep - 1:
                self.copy(
                    self.sums.at[k, rows],
                    self.over_z.at[k, rows],
                    self.z_send.at[piece, k],
                    self.z_recv.at[piece, k],
                    group.device(k + 1, 0),
                )

    def finish(self, piece):
        group, rows = self.group, self.rows(piece)
        total = self.sums[group.deep - 1, rows].astype(F32)
        for k in range(group.deep - 1):
            arrived(self.over_z.at[k, rows], self.z_recv.at[piece, k])
            total = total + self.over_z[k, rows].astype(F32)
        return total

    def drain(self):
        for copy in self.sent:
            copy.wait_send()


def inverse_rms(rows):
    return lax.rsqrt(jnp.mean(rows * rows, axis=-1, keepdims=True) + EPS)


def wide_dot(left, right_ref, dims, tile, store):
    total = right_ref.shape[0] if dims is NT else right_ref.shape[1]
    for first in range(0, total, tile):
        cols = slice(first, min(first + tile, total))
        right = right_ref[cols, :] if dims is NT else right_ref[:, cols]
        store(cols, lax.dot_general(left, right, (dims, ((), ())), preferred_element_type=F32))


def project_kernel(
    count, rows_ref, gain_ref, weight_ref, full_out, projected_out,
    full, gather_send, gather_recv, staged, full_sems, staged_sems,
):
    group = Group(count, 4)
    gather = Gather(group, full, gather_send, gather_recv)
    part = gather.part
    meet(count, False)
    for piece in range(PIECES):
        rows = rows_ref[gather.rows(piece)].astype(F32)
        full[group.own, gather.rows(piece)] = (
            rows * inverse_rms(rows) * gain_ref[...]
        ).astype(BF16)
        gather.start(piece)
    outs = []
    for piece in range(PIECES):
        gather.relay(piece)
        gather.finish(piece)
        rows = gather.rows(piece)
        copy = pltpu.make_async_copy(full.at[:, rows], full_out.at[:, rows], full_sems.at[piece])
        copy.start()
        outs.append(copy)
        left = full[:, rows].reshape(count * part, full.shape[2])

        def store(cols, value, rows=rows):
            staged[:, rows, cols] = value.reshape(count, part, value.shape[1])

        wide_dot(left, weight_ref, NN, 256, store)
        copy = pltpu.make_async_copy(
            staged.at[:, rows], projected_out.at[:, rows], staged_sems.at[piece]
        )
        copy.start()
        outs.append(copy)
    gather.drain()
    for copy in outs:
        copy.wait()


VMEM_SPEC = pl.BlockSpec(memory_space=pltpu.VMEM)
ANY_SPEC = pl.BlockSpec(memory_space=pl.ANY)


def grid_sizes(count):
    nz = 4 if count % 4 == 0 else 1
    return nz, count // nz


def linked(collective):
    return pltpu.CompilerParams(
        collective_id=collective, has_side_effects=True, vmem_limit_bytes=60 * 2**20
    )


def project(rows, gain, weight, count):
    own, features = rows.shape
    cols = weight.shape[1]
    nz, nx = grid_sizes(count)
    return pl.pallas_call(
        functools.partial(project_kernel, count),
        out_shape=[
            jax.ShapeDtypeStruct((count, own, features), BF16),
            jax.ShapeDtypeStruct((count, own, cols), F32),
        ],
        in_specs=[VMEM_SPEC] * 3,
        out_specs=[ANY_SPEC] * 2,
        scratch_shapes=[
            *Gather.scratch(nz, nx, own, features),
            pltpu.VMEM((count, own, cols), F32),
            pltpu.SemaphoreType.DMA((PIECES,)),
            pltpu.SemaphoreType.DMA((PIECES,)),
        ],
        compiler_params=linked(0),
        name="project",
    )(rows, gain, weight)


def branch_kernel(
    count, deep, mixed_ref, weight_ref, input_ref, live_ref, gain_ref, middle_out, full_out,
    parts, over_x, sums, over_z, x_send, x_recv, z_send, z_recv,
    full, gather_send, gather_recv, out_sems,
):
    scatter = Scatter(
        Group(count, 4), parts, over_x, sums, over_z, (x_send, x_recv, z_send, z_recv)
    )
    near = Group(count, deep)
    gather = Gather(near, full, gather_send, gather_recv)
    part = gather.part
    meet(count, False)
    for piece in range(PIECES):
        rows = gather.rows(piece)
        left = mixed_ref[:, rows].reshape(count * part, mixed_ref.shape[2])

        def store(cols, value, rows=rows):
            parts[:, rows, cols] = value.astype(BF16).reshape(count, part, value.shape[1])

        wide_dot(left, weight_ref, NN, 512, store)
        scatter.start(piece)
    for piece in range(PIECES):
        scatter.relay(piece)
    outs = []

    def pass_on(piece):
        gather.relay(piece)

    for piece in range(PIECES):
        rows = gather.rows(piece)
        middle = input_ref[rows].astype(F32) + live_ref[rows] * scatter.finish(piece)
        middle_out[rows] = middle
        full[near.own, rows] = (middle * inverse_rms(middle) * gain_ref[...]).astype(BF16)
        gather.start(piece)
        if piece > 0:
            pass_on(piece - 1)
    pass_on(PIECES - 1)
    for piece in range(PIECES):
        gather.finish(piece)
        rows = gather.rows(piece)
        copy = pltpu.make_async_copy(full.at[:, rows], full_out.at[:, rows], out_sems.at[piece])
        copy.start()
        outs.append(copy)
    scatter.drain()
    gather.drain()
    for copy in outs:
        copy.wait()


def branch_and_norm(mixed, weight, rows, live, gain, count, deep):
    own, features = rows.shape
    nz, nx = grid_sizes(count)
    deep = min(deep, nz)
    return pl.pallas_call(
        functools.partial(branch_kernel, count, deep),
        out_shape=[
            jax.ShapeDtypeStruct((own, features), F32),
            jax.ShapeDtypeStruct((deep * nx, own, features), BF16),
        ],
        in_specs=[VMEM_SPEC] * 5,
        out_specs=[VMEM_SPEC, ANY_SPEC],
        scratch_shapes=[
            *Scatter.scratch(nz, nx, own, features),
            *Gather.scratch(deep, nx, own, features),
            pltpu.SemaphoreType.DMA((PIECES,)),
        ],
        compiler_params=linked(1),
        name="branch_and_norm",
    )(mixed.reshape(count, own, -1), weight, rows, live, gain)


def feed_back_kernel(
    count, deep, grad_ref, weight_ref, top_ref, middle_ref, live_ref, gain_ref, out_weight_ref,
    dmiddle_out, dgain_out, full_out, dmixed_out,
    parts, over_x, sums, over_z, x_send, x_recv, z_send, z_recv,
    full, gather_send, gather_recv, out_sems,
):
    near = Group(count, deep)
    scatter = Scatter(near, parts, over_x, sums, over_z, (x_send, x_recv, z_send, z_recv))
    group = Group(count, 4)
    gather = Gather(group, full, gather_send, gather_recv)
    part = gather.part
    meet(count, False)
    for piece in range(PIECES):
        rows = gather.rows(piece)
        left = grad_ref[:, rows].reshape(near.size * part, grad_ref.shape[2])

        def store(cols, value, rows=rows):
            parts[:, rows, cols] = value.astype(BF16).reshape(near.size, part, value.shape[1])

        wide_dot(left, weight_ref, NT, 256, store)
        scatter.start(piece)
    for piece in range(PIECES):
        scatter.relay(piece)
    dgain = jnp.zeros(dgain_out.shape, F32)
    gain = gain_ref[...]
    for piece in range(PIECES):
        rows = gather.rows(piece)
        dnormed = scatter.finish(piece)
        middle = middle_ref[rows]
        scale = inverse_rms(middle)
        normed = middle * scale
        dgain = dgain + jnp.sum(dnormed * normed, axis=0, keepdims=True)
        scaled = dnormed * gain
        dmiddle = top_ref[rows].astype(F32) + scale * (
            scaled - normed * jnp.mean(scaled * normed, axis=-1, keepdims=True)
        )
        dmiddle_out[rows] = dmiddle
        full[group.own, rows] = (live_ref[rows] * dmiddle).astype(BF16)
        gather.start(piece)
        if piece > 0:
            gather.relay(piece - 1)
    dgain_out[...] = dgain
    gather.relay(PIECES - 1)
    outs = []
    for piece in range(PIECES):
        gather.finish(piece)
        rows = gather.rows(piece)
        copy = pltpu.make_async_copy(full.at[:, rows], full_out.at[:, rows], out_sems.at[piece])
        copy.start()
        outs.append(copy)
        left = full[:, rows].reshape(count * part, full.shape[2])

        def store(cols, value, rows=rows):
            dmixed_out[:, rows, cols] = value.reshape(count, part, value.shape[1])

        wide_dot(left, out_weight_ref, NT, 256, store)
    scatter.drain()
    gather.drain()
    for copy in outs:
        copy.wait()


def feed_back(grad, weight, top, middle, live, gain, out_weight, count, deep):
    own, features = middle.shape
    nz, nx = grid_sizes(count)
    deep = min(deep, nz)
    width = out_weight.shape[0]
    return pl.pallas_call(
        functools.partial(feed_back_kernel, count, deep),
        out_shape=[
            jax.ShapeDtypeStruct((own, features), F32),
            jax.ShapeDtypeStruct((1, features), F32),
            jax.ShapeDtypeStruct((count, own, features), BF16),
            jax.ShapeDtypeStruct((count, own, width), F32),
        ],
        in_specs=[VMEM_SPEC] * 7,
        out_specs=[VMEM_SPEC, VMEM_SPEC, ANY_SPEC, VMEM_SPEC],
        scratch_shapes=[
            *Scatter.scratch(deep, nx, own, features),
            *Gather.scratch(nz, nx, own, features),
            pltpu.SemaphoreType.DMA((PIECES,)),
        ],
        compiler_params=linked(2),
        name="feed_back",
    )(grad.reshape(deep * nx, own, -1), weight, top, middle, live, gain, out_weight)


def input_back_kernel(
    count, grad_ref, weight_ref, later_ref, input_ref, gain_ref, grad_out, dgain_out,
    parts, over_x, sums, over_z, x_send, x_recv, z_send, z_recv,
):
    scatter = Scatter(
        Group(count, 4), parts, over_x, sums, over_z, (x_send, x_recv, z_send, z_recv)
    )
    part = scatter.part
    meet(count, False)
    for piece in range(PIECES):
        rows = scatter.rows(piece)
        left = grad_ref[:, rows].reshape(count * part, grad_ref.shape[2])

        def store(cols, value, rows=rows):
            parts[:, rows, cols] = value.astype(BF16).reshape(count, part, value.shape[1])

        wide_dot(left, weight_ref, NT, 256, store)
        scatter.start(piece)
    for piece in range(PIECES):
        scatter.relay(piece)
    dgain = jnp.zeros(dgain_out.shape, F32)
    gain = gain_ref[...]
    for piece in range(PIECES):
        rows = scatter.rows(piece)
        dnormed = scatter.finish(piece)
        values = input_ref[rows].astype(F32)
        scale = inverse_rms(values)
        normed = values * scale
        dgain = dgain + jnp.sum(dnormed * normed, axis=0, keepdims=True)
        scaled = dnormed * gain
        grad_out[rows] = later_ref[rows] + scale * (
            scaled - normed * jnp.mean(scaled * normed, axis=-1, keepdims=True)
        )
    dgain_out[...] = dgain
    scatter.drain()


def input_back(grad, weight, later, rows, gain, count):
    own, features = rows.shape
    nz, nx = grid_sizes(count)
    return pl.pallas_call(
        functools.partial(input_back_kernel, count),
        out_shape=[
            jax.ShapeDtypeStruct((own, features), F32),
            jax.ShapeDtypeStruct((1, features), F32),
        ],
        in_specs=[VMEM_SPEC] * 5,
        out_specs=[VMEM_SPEC, VMEM_SPEC],
        scratch_shapes=Scatter.scratch(nz, nx, own, features),
        compiler_params=linked(3),
        name="input_back",
    )(grad.reshape(count, own, -1), weight, later, rows, gain)


def matmul(left, right, dims):
    return lax.dot_general(left, right, (dims, ((), ())), preferred_element_type=F32)


def gather_rows(values):
    return lax.all_gather(values, "heads", axis=0, tiled=True)


def scatter_rows(values):
    return lax.psum_scatter(
        values.astype(BF16), "heads", scatter_dimension=0, tiled=True
    ).astype(F32)


def sum_replicas(values):
    return lax.psum(values.astype(BF16), "dp").astype(F32)


def on_device(
    block_in,
    seq_counts,
    norm1_gain,
    w_qkvg,
    conv_weight,
    w_gates,
    gate_params,
    out_gain,
    w_out,
    norm2_gain,
    w_gate_up,
    w_down,
    cotangent,
):
    own_rows, features = block_in.shape
    count = lax.axis_size("heads")
    all_rows = own_rows * count
    width = conv_weight.shape[2]
    heads = gate_params.shape[1]
    longer = seq_counts[0, 1:2]
    first_row = lax.axis_index("heads") * own_rows
    row_index = first_row + jnp.arange(own_rows, dtype=jnp.int32)
    live_own = jnp.where(longer[0] > 0, True, row_index < seq_counts[0, 0] * SEQ_SHORT)
    live_own = live_own.astype(F32)[:, None]
    grad_top = cotangent.astype(F32)
    grad_feed = gather_rows((live_own * grad_top).astype(BF16))
    weight = jnp.concatenate(
        [
            w_qkvg.reshape(features, 4 * width),
            w_gates.reshape(features, 2 * heads),
            jnp.zeros((features, 128 - 2 * heads), BF16),
        ],
        axis=1,
    )
    full_normed1, projected = project(block_in, norm1_gain[None], weight, count)
    full_normed1 = full_normed1.reshape(all_rows, features)
    projected = projected.reshape(all_rows, -1)
    taps = jnp.transpose(conv_weight, (1, 0, 2)).reshape(4, 3 * width)
    params = jnp.pad(gate_params, ((0, 0), (0, 128 - heads)))
    gain_row = out_gain[None]
    mixed, *saved = mixer_forward(longer, projected, taps, params, gain_row)
    mixed, grad_feed = lax.optimization_barrier((mixed, grad_feed))
    middle, full_normed2 = branch_and_norm(
        mixed, w_out, block_in, live_own, norm2_gain[None], count, 4
    )
    full_normed2 = full_normed2.reshape(all_rows, features)
    feed_weight = w_gate_up.reshape(features, -1)
    hidden_cols = w_down.shape[0]
    gate_up = matmul(full_normed2, feed_weight, NN)
    gate_pre = gate_up[:, :hidden_cols]
    up_pre = gate_up[:, hidden_cols:]
    hidden = (jax.nn.silu(gate_pre) * up_pre).astype(BF16)
    grad_hidden = matmul(grad_feed, w_down, NT)
    sigmoid_gate = jax.nn.sigmoid(gate_pre)
    grad_gate = grad_hidden * up_pre * sigmoid_gate * (1.0 + gate_pre * (1.0 - sigmoid_gate))
    grad_up = grad_hidden * gate_pre * sigmoid_gate
    grad_gate_up = jnp.concatenate([grad_gate, grad_up], 1).astype(BF16)
    grad_middle, grad_gain2, grad_mix, grad_mixed = feed_back(
        grad_gate_up,
        feed_weight,
        cotangent,
        middle,
        live_own,
        norm2_gain[None],
        w_out,
        count,
        4,
    )
    grad_mix = grad_mix.reshape(all_rows, features)
    feed = scatter_rows(matmul(hidden, w_down, NN))
    layer_out = (middle + live_own * feed).astype(BF16)
    grad_feed_weight = matmul(full_normed2, grad_gate_up, TN)
    grad_down = matmul(hidden, grad_feed, TN)
    grad_wout = matmul(mixed, grad_mix, TN)
    summed_ff = (
        sum_replicas(grad_feed_weight.reshape(w_gate_up.shape)),
        sum_replicas(grad_down),
        sum_replicas(grad_wout),
    )
    dprojected, dtaps, dparams, dgain = mixer_backward(
        longer, grad_mixed.reshape(all_rows, width), projected, saved, taps, params, gain_row
    )
    grad_weight = matmul(full_normed1, dprojected, TN)
    grad_in, grad_gain1 = input_back(
        dprojected, weight, grad_middle, block_in, norm1_gain[None], count
    )
    grad_conv = jnp.transpose(dtaps.reshape(4, 3, width), (1, 0, 2))
    small = lax.psum(
        (grad_conv, grad_weight[:, 4 * width : 4 * width + 2 * heads], dparams[:, :heads]), "dp"
    )
    gains = lax.psum((grad_gain1[0], grad_gain2[0], dgain[0]), ("dp", "heads"))
    return (
        layer_out,
        grad_in,
        gains[0],
        sum_replicas(grad_weight[:, : 4 * width]).reshape(w_qkvg.shape),
        small[0],
        small[1].reshape(w_gates.shape),
        small[2],
        gains[2],
        summed_ff[2],
        gains[1],
        summed_ff[0],
        summed_ff[1],
    )


def solution(mesh):
    return jax.shard_map(
        on_device,
        mesh=mesh,
        in_specs=(
            P(("dp", "heads"), None),
            P("dp", None),
            P(),
            P(None, None, "heads"),
            P(None, None, "heads"),
            P(None, None, "heads"),
            P(None, "heads"),
            P(),
            P("heads", None),
            P(),
            P(None, None, "heads"),
            P("heads", None),
            P(("dp", "heads"), None),
        ),
        out_specs=(
            P(("dp", "heads"), None),
            P(("dp", "heads"), None),
            P(),
            P(None, None, "heads"),
            P(None, None, "heads"),
            P(None, None, "heads"),
            P(None, "heads"),
            P(),
            P("heads", None),
            P(),
            P(None, None, "heads"),
            P("heads", None),
        ),
        check_vma=False,
    )
```

```python
import functools
import jax
import jax.numpy as jnp
from jax import lax
from jax.experimental import pallas as pl
from jax.experimental.pallas import tpu as pltpu
from jax.sharding import PartitionSpec as P

SEQ_SHORT = 512
CHUNK = 256
HEAD = 128
EPS = 1e-06
F32 = jnp.float32
BF16 = jnp.bfloat16
LOW, MID, TOP = lax.Precision.DEFAULT, lax.Precision.HIGH, lax.Precision.HIGHEST
NN, NT, TN = ((1,), (0,)), ((1,), (1,)), ((0,), (0,))
P_INV, P_FWD, P_BWD = MID, MID, MID


def dot(left, right, dims, precision):
    if precision is LOW:
        left, right = left.astype(BF16), right.astype(BF16)
        return lax.dot_general(left, right, (dims, ((), ())), preferred_element_type=F32)
    return lax.dot_general(
        left, right, (dims, ((), ())), precision=precision, preferred_element_type=F32
    )


def grid_index(shape, axis):
    return lax.broadcasted_iota(jnp.int32, shape, axis)


def positions(longer, first_row, count):
    rows = grid_index((count, 1), 0) + first_row
    return jnp.where(longer > 0, rows, rows % SEQ_SHORT)


def keeps(longer, first_row):
    start = jnp.where(longer > 0, first_row, first_row % SEQ_SHORT)
    return jnp.where(start > 0, 1.0, 0.0).astype(F32)


def softplus(x):
    return jnp.maximum(x, 0.0) + jnp.log1p(jnp.exp(-jnp.abs(x)))


def gate_values(gates, params, heads):
    lane = grid_index(gates.shape, 1)
    rate = jnp.exp(params[0:1])
    shifted = gates + params[1:2]
    log_decay = jnp.where(lane < heads, -rate * softplus(shifted), 0.0)
    return rate, shifted, log_decay


def lane_column(values, index):
    return values[:, index : index + 1]


def decays(cumulative, cumulative_rows, head, masks):
    column = lane_column(cumulative, head)
    row = cumulative_rows[head : head + 1, :]
    inclusive = masks[0]
    ratio = jnp.where(inclusive, jnp.exp(jnp.where(inclusive, column - row, 0.0)), 0.0)
    last = column[CHUNK - 1 : CHUNK, :]
    return ratio, jnp.exp(column), jnp.exp(last - column), jnp.exp(last)


def unit(values):
    scale = lax.rsqrt(jnp.sum(values * values, axis=-1, keepdims=True) + EPS)
    return values * scale, scale


def inverse(link, row, col):
    apart = row ^ col

    def level(size):
        return (apart >= size) & (apart < 2 * size)

    out = jnp.where(row == col, 1.0, 0.0) - jnp.where(level(1), link, 0.0)
    size = 2
    while size < CHUNK // 2:
        part = jnp.where(level(size), link, 0.0)
        out = out - dot(out, dot(part, out, NN, P_INV), NN, P_INV)
        size *= 2
    half = CHUNK // 2
    corner = dot(link[half:, :half], out[:half, :half], NN, P_INV)
    corner = -dot(out[half:, half:], corner, NN, P_INV)
    return jnp.concatenate(
        [out[:half], jnp.concatenate([corner, out[half:, half:]], axis=1)], axis=0
    )


def forward_kernel(
    heads, longer_ref, main_ref, conv_ref, params_ref, gain_ref,
    mixed_ref, conv_out_ref, raw_ref, delta_ref, solve_ref, state_ref, state, tail_rows,
):
    step = pl.program_id(0)
    first_row = step * CHUNK
    longer = longer_ref[0]
    width = heads * HEAD

    @pl.when(step == 0)
    def _():
        state[...] = jnp.zeros_like(state)
        tail_rows[...] = jnp.zeros_like(tail_rows)

    position = positions(longer, first_row, CHUNK)
    keep = keeps(longer, first_row)
    triple = main_ref[:, : 3 * width]
    padded = jnp.concatenate([tail_rows[...], triple], axis=0)
    taps = conv_ref[...]
    convolved = triple * taps[0:1]
    for lag in range(1, 4):
        shifted = padded[8 - lag : 8 - lag + CHUNK]
        convolved = convolved + jnp.where(position >= lag, shifted, 0.0) * taps[lag : lag + 1]
    tail_rows[...] = triple[CHUNK - 8 :]
    conv_out_ref[...] = convolved
    active = convolved * jax.nn.sigmoid(convolved)
    gates = main_ref[:, 4 * width :]
    rate, shifted_gate, log_decay = gate_values(gates, params_ref[...], heads)
    beta_all = jax.nn.sigmoid(gates)
    row = grid_index((CHUNK, CHUNK), 0)
    col = grid_index((CHUNK, CHUNK), 1)
    masks = (row >= col, row > col)
    cumulative = dot(jnp.where(masks[0], 1.0, 0.0), log_decay, NN, TOP)
    cumulative_rows = jnp.transpose(cumulative)
    for head in range(heads):
        cols = slice(head * HEAD, (head + 1) * HEAD)
        query = unit(active[:, head * HEAD : (head + 1) * HEAD])[0] * HEAD**-0.5
        key = unit(active[:, width + head * HEAD : width + (head + 1) * HEAD])[0]
        value = active[:, 2 * width + head * HEAD : 2 * width + (head + 1) * HEAD]
        beta = lane_column(beta_all, heads + head)
        ratio, decay_in, decay_out, decay_all = decays(cumulative, cumulative_rows, head, masks)
        grams = dot(jnp.concatenate([key, query], axis=0), key, NT, P_FWD)
        link = jnp.where(masks[1], beta * ratio * grams[:CHUNK], 0.0)
        solve = inverse(link, row, col)
        solve_ref[head] = solve
        both = dot(
            solve, jnp.concatenate([beta * value, (beta * decay_in) * key], axis=1), NN, P_FWD
        )
        entry = state[head] * keep
        state_ref[0, head] = entry
        carried = dot(
            jnp.concatenate([both[:, HEAD:], decay_in * query], axis=0), entry, NT, P_FWD
        )
        delta = both[:, :HEAD] - carried[:CHUNK]
        delta_ref[:, cols] = delta
        raw = carried[CHUNK:] + dot(grams[CHUNK:] * ratio, delta, NN, P_FWD)
        state[head] = decay_all * entry + dot(delta * decay_out, key, TN, P_FWD)
        raw_ref[:, cols] = raw
        scale = lax.rsqrt(jnp.mean(raw * raw, axis=-1, keepdims=True) + EPS)
        gate = main_ref[:, 3 * width + head * HEAD : 3 * width + (head + 1) * HEAD]
        mixed = raw * scale * gain_ref[...] * (gate * jax.nn.sigmoid(gate))
        mixed_ref[:, cols] = mixed.astype(mixed_ref.dtype)


def backward_kernel(
    heads, chunks, longer_ref, grad_ref, main_ref, conv_out_ref, raw_ref, delta_ref,
    solve_ref, state_ref, conv_ref, params_ref, gain_ref,
    dmain_ref, dconv_ref, dparams_ref, dgain_ref, dstate, head_rows,
):
    step = pl.program_id(0)
    first_row = (chunks - 1 - step) * CHUNK
    longer = longer_ref[0]
    width = heads * HEAD

    @pl.when(step == 0)
    def _():
        dstate[...] = jnp.zeros_like(dstate)
        head_rows[...] = jnp.zeros_like(head_rows)
        dconv_ref[...] = jnp.zeros_like(dconv_ref)
        dparams_ref[...] = jnp.zeros_like(dparams_ref)
        dgain_ref[...] = jnp.zeros_like(dgain_ref)

    keep = keeps(longer, first_row)
    convolved = conv_out_ref[...]
    sigmoid_conv = jax.nn.sigmoid(convolved)
    active = convolved * sigmoid_conv
    slope = sigmoid_conv * (1.0 + convolved * (1.0 - sigmoid_conv))
    gates = main_ref[:, 4 * width :]
    params = params_ref[...]
    rate, shifted_gate, log_decay = gate_values(gates, params, heads)
    beta_all = jax.nn.sigmoid(gates)
    row = grid_index((CHUNK, CHUNK), 0)
    col = grid_index((CHUNK, CHUNK), 1)
    masks = (row >= col, row > col)
    cumulative = dot(jnp.where(masks[0], 1.0, 0.0), log_decay, NN, TOP)
    cumulative_rows = jnp.transpose(cumulative)
    lane = grid_index((CHUNK, 128), 1)
    last_row = grid_index((CHUNK, 1), 0) == CHUNK - 1
    dcumulative = jnp.zeros((CHUNK, 128), F32)
    dbeta_all = jnp.zeros((CHUNK, 128), F32)
    gain = gain_ref[...]
    dgain = jnp.zeros((1, HEAD), F32)
    dconv_parts = [[], [], []]
    for head in range(heads):
        cols = slice(head * HEAD, (head + 1) * HEAD)
        gate = main_ref[:, 3 * width + head * HEAD : 3 * width + (head + 1) * HEAD]
        raw = raw_ref[:, cols]
        grad = grad_ref[:, cols]
        scale = lax.rsqrt(jnp.mean(raw * raw, axis=-1, keepdims=True) + EPS)
        normed = raw * scale
        sigmoid_gate = jax.nn.sigmoid(gate)
        gated = gate * sigmoid_gate
        product = grad * normed
        dgain = dgain + jnp.sum(product * gated, axis=0, keepdims=True)
        dgate = product * gain * (sigmoid_gate * (1.0 + gate * (1.0 - sigmoid_gate)))
        dmain_ref[:, 3 * width + head * HEAD : 3 * width + (head + 1) * HEAD] = dgate.astype(
            dmain_ref.dtype
        )
        dnormed = grad * gain * gated
        draw = scale * (dnormed - normed * jnp.mean(dnormed * normed, axis=-1, keepdims=True))
        query_unit, query_scale = unit(active[:, head * HEAD : (head + 1) * HEAD])
        query = query_unit * HEAD**-0.5
        key, key_scale = unit(active[:, width + head * HEAD : width + (head + 1) * HEAD])
        value = active[:, 2 * width + head * HEAD : 2 * width + (head + 1) * HEAD]
        beta = lane_column(beta_all, heads + head)
        ratio, decay_in, decay_out, decay_all = decays(cumulative, cumulative_rows, head, masks)
        entry = state_ref[0, head]
        delta = delta_ref[:, cols]
        dlater = dstate[head]
        gram = dot(query, key, NT, P_BWD) * ratio
        key_dlater = dot(key, dlater, NT, P_BWD)
        ddelta = dot(gram, draw, TN, P_BWD) + decay_out * key_dlater
        dright = dot(solve_ref[head], ddelta, TN, P_BWD)
        pairs = dot(jnp.concatenate([dright, draw], axis=0), delta, NT, P_BWD)
        dlink = jnp.where(masks[1], -pairs[:CHUNK] * ratio, 0.0)
        dgram = pairs[CHUNK:] * ratio
        on_entry = dot(jnp.concatenate([dright, draw], axis=0), entry, NN, P_BWD)
        key_entry = dot(key, entry, NT, P_BWD)
        on_key = dot(jnp.concatenate([dlink, dgram], axis=0), key, NN, P_BWD)
        dquery = decay_in * on_entry[CHUNK:] + on_key[CHUNK:]
        link_key = on_key[:CHUNK]
        key_read = beta * (link_key - decay_in * on_entry[:CHUNK])
        key_tail = decay_out * dot(delta, dlater, NN, P_BWD)
        key_write = (
            dot(beta * dlink, key, TN, P_BWD) + dot(dgram, query, TN, P_BWD) + key_tail
        )
        dkey = key_read + key_write
        dvalue = beta * dright
        dbeta = jnp.sum(
            dright * (value - decay_in * key_entry) + key * link_key, axis=-1, keepdims=True
        )
        dlog = jnp.sum(query * dquery + key * (key_read - key_write), axis=-1, keepdims=True)
        ending = decay_all * jnp.sum(
            jnp.sum(entry * dlater, axis=-1, keepdims=True), axis=0, keepdims=True
        ) + jnp.sum(jnp.sum(key * key_tail, axis=-1, keepdims=True), axis=0, keepdims=True)
        dlog = dlog + jnp.where(last_row, ending, 0.0)
        dcumulative = jnp.where(lane == head, dlog, dcumulative)
        dbeta_all = jnp.where(lane == heads + head, dbeta, dbeta_all)
        dstate[head] = keep * (
            decay_all * dlater
            + dot(decay_in * draw, query, TN, P_BWD)
            - dot((beta * decay_in) * dright, key, TN, P_BWD)
        )
        dquery = (HEAD**-0.5 * query_scale) * (
            dquery - query_unit * jnp.sum(dquery * query_unit, axis=-1, keepdims=True)
        )
        dkey = key_scale * (dkey - key * jnp.sum(dkey * key, axis=-1, keepdims=True))
        for kind, part in enumerate((dquery, dkey, dvalue)):
            dconv_parts[kind].append(part)
    dactive = jnp.concatenate([p for parts in dconv_parts for p in parts], axis=1)
    dconvolved = dactive * slope
    padded = jnp.concatenate([dconvolved, head_rows[...]], axis=0)
    position = positions(longer, first_row, CHUNK + 8)
    taps = conv_ref[...]
    triple = main_ref[:, : 3 * width]
    dtriple = dconvolved * taps[0:1]
    dconv_ref[0:1] += jnp.sum(dconvolved * triple, axis=0, keepdims=True)
    for lag in range(1, 4):
        moved = jnp.where(position >= lag, padded, 0.0)[lag : lag + CHUNK]
        dtriple = dtriple + moved * taps[lag : lag + 1]
        dconv_ref[lag : lag + 1] += jnp.sum(moved * triple, axis=0, keepdims=True)
    head_rows[...] = dconvolved[:8]
    dmain_ref[:, : 3 * width] = dtriple.astype(dmain_ref.dtype)
    dlog_decay = dot(jnp.where(row <= col, 1.0, 0.0), dcumulative, NN, TOP)
    dshifted = -dlog_decay * rate * jax.nn.sigmoid(shifted_gate)
    dshifted = jnp.where(lane < heads, dshifted, 0.0)
    dparams_ref[0:1] += jnp.sum(dlog_decay * log_decay, axis=0, keepdims=True)
    dparams_ref[1:2] += jnp.sum(dshifted, axis=0, keepdims=True)
    dmain_ref[:, 4 * width :] = (dshifted + dbeta_all * beta_all * (1.0 - beta_all)).astype(
        dmain_ref.dtype
    )
    dgain_ref[...] += dgain


def row_block(width, chunks, backward):
    if backward:
        return pl.BlockSpec((CHUNK, width), lambda i: (chunks - 1 - i, 0))
    return pl.BlockSpec((CHUNK, width), lambda i: (i, 0))


def whole_block(shape):
    return pl.BlockSpec(shape, lambda i: (0,) * len(shape))


def mixer_forward(longer, main, conv, params, gain):
    rows, width = main.shape[0], conv.shape[1] // 3
    heads, chunks = width // HEAD, rows // CHUNK
    rowed = functools.partial(row_block, chunks=chunks, backward=False)
    shape = jax.ShapeDtypeStruct
    return pl.pallas_call(
        functools.partial(forward_kernel, heads),
        grid=(chunks,),
        in_specs=[
            pl.BlockSpec(memory_space=pltpu.SMEM),
            rowed(4 * width + 128),
            whole_block((4, 3 * width)),
            whole_block((2, 128)),
            whole_block((1, HEAD)),
        ],
        out_specs=[
            rowed(width),
            rowed(3 * width),
            rowed(width),
            rowed(width),
            pl.BlockSpec((heads, CHUNK, CHUNK), lambda i: (0, i, 0)),
            pl.BlockSpec((1, heads, HEAD, HEAD), lambda i: (i, 0, 0, 0)),
        ],
        out_shape=[
            shape((rows, width), BF16),
            shape((rows, 3 * width), F32),
            shape((rows, width), F32),
            shape((rows, width), F32),
            shape((heads, rows, CHUNK), F32),
            shape((chunks, heads, HEAD, HEAD), F32),
        ],
        scratch_shapes=[
            pltpu.VMEM((heads, HEAD, HEAD), F32),
            pltpu.VMEM((8, 3 * width), F32),
        ],
        compiler_params=pltpu.CompilerParams(vmem_limit_bytes=48 * 2**20),
        cost_estimate=pl.CostEstimate(
            flops=10**11, bytes_accessed=2**20, transcendentals=0
        ),
        name="mixer_forward",
    )(longer, main, conv, params, gain)


def mixer_backward(longer, grad, main, saved, conv, params, gain):
    rows, width = main.shape[0], conv.shape[1] // 3
    heads, chunks = width // HEAD, rows // CHUNK
    rowed = functools.partial(row_block, chunks=chunks, backward=True)
    shape = jax.ShapeDtypeStruct
    return pl.pallas_call(
        functools.partial(backward_kernel, heads, chunks),
        grid=(chunks,),
        in_specs=[
            pl.BlockSpec(memory_space=pltpu.SMEM),
            rowed(width),
            rowed(4 * width + 128),
            rowed(3 * width),
            rowed(width),
            rowed(width),
            pl.BlockSpec((heads, CHUNK, CHUNK), lambda i: (0, chunks - 1 - i, 0)),
            pl.BlockSpec((1, heads, HEAD, HEAD), lambda i: (chunks - 1 - i, 0, 0, 0)),
            whole_block((4, 3 * width)),
            whole_block((2, 128)),
            whole_block((1, HEAD)),
        ],
        out_specs=[
            rowed(4 * width + 128),
            whole_block((4, 3 * width)),
            whole_block((2, 128)),
            whole_block((1, HEAD)),
        ],
        out_shape=[
            shape((rows, 4 * width + 128), BF16),
            shape((4, 3 * width), F32),
            shape((2, 128), F32),
            shape((1, HEAD), F32),
        ],
        scratch_shapes=[
            pltpu.VMEM((heads, HEAD, HEAD), F32),
            pltpu.VMEM((8, 3 * width), F32),
        ],
        compiler_params=pltpu.CompilerParams(vmem_limit_bytes=48 * 2**20),
        cost_estimate=pl.CostEstimate(
            flops=6 * 10**10, bytes_accessed=2**20, transcendentals=0
        ),
        name="mixer_backward",
    )(longer, grad, main, *saved, conv, params, gain)


MESH = pl.DeviceIdType.MESH
PIECES = 8


def grid_sizes(count):
    nz = 4 if count % 4 == 0 else 1
    return nz, count // nz


class Group:
    def __init__(self, count):
        self.deep, self.nx = grid_sizes(count)
        self.size = count
        me = lax.axis_index("heads")
        self.z, self.x = me // self.nx, me % self.nx
        self.own = me

    def slot(self, z, j):
        return z * self.nx + (self.x + j) % self.nx

    def device(self, z, j):
        return {"heads": self.slot(z, j)}


def meet(count, replicas=1):
    barrier = pltpu.get_barrier_semaphore()
    for axis, size in (("heads", count), ("dp", replicas)):
        me = lax.axis_index(axis)

        def greet(k, _, axis=axis, size=size, me=me):
            pl.semaphore_signal(
                barrier, inc=1, device_id={axis: (me + k) % size}, device_id_type=MESH
            )
            return 0

        lax.fori_loop(1, size, greet, 0)
    pl.semaphore_wait(barrier, count + replicas - 2)


def arrived(ref, sem):
    pltpu.make_async_copy(ref, ref, sem).wait()


def during(piece, work):
    pl.when((piece >= 0) & (piece < PIECES))(functools.partial(work, piece))


class Sender:
    draining = False

    def push(self, source, target, send_sem, recv_sem, device, condition=None):
        copy = pltpu.make_async_remote_copy(
            source, target, send_sem, recv_sem, device_id=device, device_id_type=MESH
        )
        act = copy.wait_send if self.draining else copy.start
        if condition is None:
            act()
        else:
            pl.when(condition)(act)

    def place(self, piece):
        rows = pl.ds(pl.multiple_of(piece * self.part, self.part), self.part)
        return rows, self.cols

    def drain(self):
        def one(piece, _):
            for step in range(self.last + 1):
                self.phase(piece, step)
            return 0

        self.draining = True
        lax.fori_loop(0, PIECES, one, 0)
        self.draining = False


class Gather(Sender):
    def __init__(self, group, full, cols, send_sems, recv_sems, x_first):
        self.group, self.full, self.cols, self.x_first = group, full, cols, x_first
        self.part = full.shape[1] // PIECES
        self.send_sems, self.recv_sems = send_sems, recv_sems
        self.last = group.deep

    @staticmethod
    def sems(size):
        return [
            pltpu.SemaphoreType.DMA((PIECES, 3, size)),
            pltpu.SemaphoreType.DMA((PIECES, size)),
        ]

    def send(self, piece, slot, way, mark, device, condition):
        place = self.full.at[slot, *self.place(piece)]
        self.push(
            place,
            place,
            self.send_sems.at[piece, way, mark],
            self.recv_sems.at[piece, slot],
            device,
            condition,
        )

    def receive(self, piece, slot):
        if not self.draining:
            arrived(self.full.at[slot, *self.place(piece)], self.recv_sems.at[piece, slot])

    def send_up(self, piece, slot, here=True):
        group = self.group
        self.send(
            piece, slot, 0, slot, group.device(group.z + 1, 0), here & (group.z + 1 < group.deep)
        )

    def send_down(self, piece, slot, here=True):
        group = self.group
        self.send(piece, slot, 1, slot, group.device(group.z - 1, 0), here & (group.z > 0))

    def send_x(self, piece, slot, here=None):
        group = self.group
        for j in range(1, group.nx):
            mark = (slot // group.nx) * group.nx + (slot + j) % group.nx
            self.send(piece, slot, 2, mark, group.device(group.z, j), here)

    def phase(self, piece, step):
        group = self.group
        if step == 0:
            self.send_up(piece, group.own)
            self.send_down(piece, group.own)
            self.send_x(piece, group.own)
            return
        if self.x_first and step == 1:
            for j in range(1, group.nx):
                slot = group.slot(group.z, j)
                self.receive(piece, slot)
                self.send_up(piece, slot)
                self.send_down(piece, slot)
        if step < group.deep:
            for j in range(group.nx if self.x_first else 1):
                below, above = group.z - step, group.z + step
                for z, here, forward in (
                    (below, below >= 0, self.send_up),
                    (above, above < group.deep, self.send_down),
                ):
                    slot = group.slot(z, j)
                    pl.when(here)(functools.partial(self.receive, piece, slot))
                    forward(piece, slot, here)
                    if not self.x_first:
                        self.send_x(piece, slot, here)
        elif not self.x_first:
            for j in range(1, group.nx):
                for z in range(group.deep):
                    self.receive(piece, group.slot(z, j))


class Scatter(Sender):
    last = 3

    def __init__(self, group, parts, cols, scratch, z_first):
        self.group, self.parts, self.cols, self.z_first = group, parts, cols, z_first
        self.part = parts.shape[1] // PIECES
        self.over_x, self.line, *sems = scratch
        self.x_send, self.x_recv, self.z_send, self.z_recv = sems

    @staticmethod
    def scratch(deep, nx, rows, cols, z_first):
        dma = pltpu.SemaphoreType.DMA
        return [
            pltpu.VMEM((1 if z_first else deep, max(nx - 1, 1), rows, cols), BF16),
            pltpu.VMEM((deep + 1, nx if z_first else 1, rows, cols), BF16),
            *[dma((PIECES, deep, nx))] * 2,
            *[dma((PIECES, 2, deep * nx))] * 2,
        ]

    def landing(self, piece):
        return self.place(piece)[0]

    def line_at(self, piece, slot, way):
        nx = self.group.nx
        z = slot // nx + (1 if way == 0 else 0)
        return self.line.at[z, slot % nx if self.z_first else 0, self.landing(piece)]

    def step_line(self, piece, slot, way, device, add):
        part = (slot, *self.place(piece))
        if add and not self.draining:
            landed = self.line_at(piece, slot, way)
            arrived(landed, self.z_recv.at[piece, way, slot])
            total = self.parts[part].astype(F32) + landed[...].astype(F32)
            self.parts[part] = total.astype(BF16)
        self.push(
            self.parts.at[part],
            self.line_at(piece, slot, way),
            self.z_send.at[piece, way, slot],
            self.z_recv.at[piece, way, slot],
            device,
        )

    def walk(self, piece, columns, ends):
        group = self.group
        deep = group.deep

        def one_way(way):
            for k in range(deep - 1, 0, -1):
                target = group.z + k if way == 0 else group.z - k
                inside = target < deep if way == 0 else target >= 0
                first = group.z == 0 if way == 0 else group.z == deep - 1
                condition = inside & (first if ends else jnp.logical_not(first))
                device = group.device(group.z + (1 if way == 0 else -1), 0)
                for j in range(columns):
                    slot = group.slot(target, j)
                    pl.when(condition)(
                        functools.partial(self.step_line, piece, slot, way, device, not ends)
                    )

        if ends or self.draining:
            one_way(0)
            one_way(1)
            return

        def both(first, second):
            one_way(first)
            one_way(second)

        low = group.z < deep // 2
        pl.when(low)(functools.partial(both, 0, 1))
        pl.when(jnp.logical_not(low))(functools.partial(both, 1, 0))

    def total_line(self, piece, slot):
        group = self.group
        total = self.parts[(slot, *self.place(piece))].astype(F32)
        for way, here in ((0, group.z > 0), (1, group.z + 1 < group.deep)):
            landed = self.line_at(piece, slot, way)
            pl.when(here)(
                functools.partial(arrived, landed, self.z_recv.at[piece, way, slot])
            )
            total = total + jnp.where(here, landed[...].astype(F32), 0.0)
        return total

    def send_x(self, piece, index, z, j):
        group = self.group
        self.push(
            self.parts.at[group.slot(z, j), *self.place(piece)],
            self.over_x.at[index, j - 1, self.landing(piece)],
            self.x_send.at[piece, index, j],
            self.x_recv.at[piece, index, j],
            group.device(group.z, j),
        )

    def add_x(self, piece, index, total):
        for j in range(1, self.group.nx):
            landed = self.over_x.at[index, j - 1, self.landing(piece)]
            arrived(landed, self.x_recv.at[piece, index, j])
            total = total + landed[...].astype(F32)
        return total

    def phase(self, piece, step):
        group = self.group
        if self.z_first:
            if step == 0:
                self.walk(piece, group.nx, True)
            elif step == 1:
                self.walk(piece, group.nx, False)
            elif step == 2:
                for j in range(1, group.nx):
                    slot = group.slot(group.z, j)
                    if not self.draining:
                        total = self.total_line(piece, slot)
                        self.parts[(slot, *self.place(piece))] = total.astype(BF16)
                    self.send_x(piece, 0, group.z, j)
            elif not self.draining:
                return self.add_x(piece, 0, self.total_line(piece, group.own))
        elif step == 0:
            for z in range(group.deep):
                for j in range(1, group.nx):
                    self.send_x(piece, z, z, j)
        elif step == 1:
            for z in range(group.deep):
                part = (group.slot(z, 0), *self.place(piece))
                if not self.draining:
                    total = self.add_x(piece, z, self.parts[part].astype(F32))
                    self.parts[part] = total.astype(BF16)
            self.walk(piece, 1, True)
        elif step == 2:
            self.walk(piece, 1, False)
        elif not self.draining:
            return self.total_line(piece, group.own)
        return None


class Both:
    def __init__(self, first, second):
        self.both = (first, second)
        self.part, self.last = first.part, first.last

    def rows(self, piece):
        return pl.ds(pl.multiple_of(piece * self.part, self.part), self.part)

    def phase(self, piece, step):
        out = [each.phase(piece, step) for each in self.both]
        return None if out[0] is None else jnp.concatenate(out, axis=1)

    def drain(self):
        for each in self.both:
            each.drain()


def cut(cols, share):
    edge = cols - cols * share // 8
    return pl.ds(0, edge), pl.ds(edge, cols - edge)


def gather_of(group, share, scratch):
    full, *sems = scratch
    first, second = cut(full.shape[2], share)
    return Both(
        Gather(group, full, first, *sems[:2], False), Gather(group, full, second, *sems[2:], True)
    )


def scatter_of(group, share, scratch):
    parts, *rest = scratch
    first, second = cut(parts.shape[2], share)
    return Both(
        Scatter(group, parts, first, rest[:6], False),
        Scatter(group, parts, second, rest[6:], True),
    )


def gather_scratch(nz, nx, rows, cols):
    return [pltpu.VMEM((nz * nx, rows, cols), BF16), *Gather.sems(nz * nx), *Gather.sems(nz * nx)]


def scatter_scratch(nz, nx, rows, cols, share):
    first, second = cut(cols, share)
    return [
        pltpu.VMEM((nz * nx, rows, cols), BF16),
        *Scatter.scratch(nz, nx, rows, first.size, False),
        *Scatter.scratch(nz, nx, rows, second.size, True),
    ]


SCATTER_COUNT, GATHER_COUNT = 13, 5


def inverse_rms(rows):
    return lax.rsqrt(jnp.mean(rows * rows, axis=-1, keepdims=True) + EPS)


def wide_dot(terms, dims, tile, store):
    total = terms[0][1].shape[0 if dims is NT else 1]
    for first in range(0, total, tile):
        cols = slice(first, min(first + tile, total))
        products = [
            lax.dot_general(
                left,
                right[cols, :] if dims is NT else right[:, cols],
                (dims, ((), ())),
                preferred_element_type=F32,
            )
            for left, right in terms
        ]
        store(cols, functools.reduce(jnp.add, products))


VMEM_SPEC = pl.BlockSpec(memory_space=pltpu.VMEM)
ANY_SPEC = pl.BlockSpec(memory_space=pl.ANY)
PAIR_SHARE, GATHER_SHARE, SCATTER_SHARE = 3, 1, 2


def lasting(microseconds):
    return pl.CostEstimate(
        flops=int(microseconds * 1.1e9), bytes_accessed=2**20, transcendentals=0
    )


def linked(collective):
    return pltpu.CompilerParams(
        collective_id=collective, has_side_effects=True, vmem_limit_bytes=62 * 2**20
    )


def joined(values):
    return values.reshape(values.shape[0] * values.shape[1], values.shape[2])


def split(values, parts):
    return values.reshape(parts, values.shape[0] // parts, values.shape[1])


def project_kernel(count, rows_ref, gain_ref, weight_ref, full_out, projected_out, *scratch):
    full, staged, full_sems, staged_sems = scratch[0], *scratch[GATHER_COUNT:]
    group = Group(count)
    gather = gather_of(group, GATHER_SHARE, scratch[:GATHER_COUNT])
    meet(count)

    shares, share = full_out.shape[0], full_out.shape[3]

    def full_copy(piece, index):
        rows = gather.rows(piece)
        return pltpu.make_async_copy(
            full.at[:, rows, pl.ds(index * share, share)],
            full_out.at[index, :, rows],
            full_sems.at[piece, index],
        )

    def staged_copy(piece):
        rows = gather.rows(piece)
        return pltpu.make_async_copy(
            staged.at[:, rows], projected_out.at[:, rows], staged_sems.at[piece]
        )

    def begin(piece):
        rows = rows_ref[gather.rows(piece)].astype(F32)
        full[group.own, gather.rows(piece)] = (
            rows * inverse_rms(rows) * gain_ref[...]
        ).astype(BF16)
        gather.phase(piece, 0)

    def ready(piece):
        gather.phase(piece, gather.last)
        rows = gather.rows(piece)
        for index in range(shares):
            full_copy(piece, index).start()

        def store(cols, value):
            staged[:, rows, cols] = split(value, count)

        wide_dot([(joined(full[:, rows]), weight_ref)], NN, 256, store)
        staged_copy(piece).start()

    def tick(time, _):
        during(time, begin)
        for step in range(1, gather.last):
            during(time - step, functools.partial(gather.phase, step=step))
        during(time - gather.last, ready)
        return 0

    lax.fori_loop(0, PIECES + gather.last, tick, 0)
    gather.drain()

    def finish(piece, _):
        for index in range(shares):
            full_copy(piece, index).wait()
        staged_copy(piece).wait()
        return 0

    lax.fori_loop(0, PIECES, finish, 0)


def project(rows, gain, weight, count, shares):
    own, features = rows.shape
    cols = weight.shape[1]
    nz, nx = grid_sizes(count)
    return pl.pallas_call(
        functools.partial(project_kernel, count),
        out_shape=[
            jax.ShapeDtypeStruct((shares, count, own, features // shares), BF16),
            jax.ShapeDtypeStruct((count, own, cols), F32),
        ],
        in_specs=[VMEM_SPEC] * 3,
        out_specs=[ANY_SPEC] * 2,
        scratch_shapes=[
            *gather_scratch(nz, nx, own, features),
            pltpu.VMEM((count, own, cols), F32),
            pltpu.SemaphoreType.DMA((PIECES, shares)),
            pltpu.SemaphoreType.DMA((PIECES,)),
        ],
        compiler_params=linked(0),
        cost_estimate=lasting(100),
        name="project",
    )(rows, gain, weight)


def sum_and_gather(scatter, gather, full, full_out, out_sems, prepare, middle, ready):
    own = lax.axis_index("heads")

    def out(piece):
        rows = gather.rows(piece)
        return pltpu.make_async_copy(full.at[:, rows], full_out.at[:, rows], out_sems.at[piece])

    def begin(piece):
        prepare(piece)
        scatter.phase(piece, 0)

    def turn(piece):
        total = scatter.phase(piece, scatter.last)
        full[own, gather.rows(piece)] = middle(piece, total).astype(BF16)
        gather.phase(piece, 0)

    def end(piece):
        gather.phase(piece, gather.last)
        out(piece).start()
        ready(piece)

    def tick(time, _):
        during(time + 1, begin)
        for step in range(1, scatter.last):
            during(time - step + 1, functools.partial(scatter.phase, step=step))
        during(time - scatter.last + 1, turn)
        for step in range(1, gather.last):
            during(
                time - scatter.last + 1 - step, functools.partial(gather.phase, step=step)
            )
        during(time - scatter.last + 1 - gather.last, end)
        return 0

    lax.fori_loop(-1, PIECES + scatter.last + gather.last - 1, tick, 0)
    scatter.drain()
    gather.drain()

    def finish(piece, _):
        out(piece).wait()
        return 0

    lax.fori_loop(0, PIECES, finish, 0)


def branch_kernel(
    count, mixed_ref, weight_ref, input_ref, live_ref, gain_ref, middle_out, full_out, *scratch
):
    group = Group(count)
    scatter = scatter_of(group, PAIR_SHARE, scratch[:SCATTER_COUNT])
    gather = gather_of(group, PAIR_SHARE, scratch[SCATTER_COUNT:-1])
    parts, full, out_sems = scratch[0], scratch[SCATTER_COUNT], scratch[-1]
    meet(count)

    def prepare(piece):
        rows = gather.rows(piece)

        def store(cols, value):
            parts[:, rows, cols] = split(value.astype(BF16), count)

        wide_dot([(joined(mixed_ref[:, rows]), weight_ref)], NN, 512, store)

    def middle(piece, total):
        rows = gather.rows(piece)
        values = input_ref[rows].astype(F32) + live_ref[rows] * total
        middle_out[rows] = values
        return values * inverse_rms(values) * gain_ref[...]

    sum_and_gather(
        scatter, gather, full, full_out, out_sems, prepare, middle, lambda piece: None
    )


def branch_and_norm(mixed, weight, rows, live, gain, count):
    own, features = rows.shape
    nz, nx = grid_sizes(count)
    return pl.pallas_call(
        functools.partial(branch_kernel, count),
        out_shape=[
            jax.ShapeDtypeStruct((own, features), F32),
            jax.ShapeDtypeStruct((count, own, features), BF16),
        ],
        in_specs=[VMEM_SPEC] * 5,
        out_specs=[VMEM_SPEC, ANY_SPEC],
        scratch_shapes=[
            *scatter_scratch(nz, nx, own, features, PAIR_SHARE),
            *gather_scratch(nz, nx, own, features),
            pltpu.SemaphoreType.DMA((PIECES,)),
        ],
        compiler_params=linked(1),
        cost_estimate=lasting(180),
        name="branch_and_norm",
    )(split(mixed, count), weight, rows, live, gain)


def feed_back_kernel(
    count, dgate_ref, dup_ref, gate_weight_ref, up_weight_ref, top_ref, middle_ref, live_ref,
    gain_ref, out_weight_ref, dmiddle_out, dgain_out, full_out, dmixed_out, *scratch
):
    group = Group(count)
    scatter = scatter_of(group, PAIR_SHARE, scratch[:SCATTER_COUNT])
    gather = gather_of(group, PAIR_SHARE, scratch[SCATTER_COUNT:-1])
    parts, full, out_sems = scratch[0], scratch[SCATTER_COUNT], scratch[-1]
    meet(count)
    dgain_out[...] = jnp.zeros(dgain_out.shape, F32)

    def prepare(piece):
        rows = gather.rows(piece)

        def store(cols, value):
            parts[:, rows, cols] = split(value.astype(BF16), count)

        wide_dot(
            [
                (joined(dgate_ref[:, rows]), gate_weight_ref),
                (joined(dup_ref[:, rows]), up_weight_ref),
            ],
            NT,
            256,
            store,
        )

    def middle(piece, dnormed):
        rows = gather.rows(piece)
        values = middle_ref[rows]
        scale = inverse_rms(values)
        normed = values * scale
        dgain_out[...] += jnp.sum(dnormed * normed, axis=0, keepdims=True)
        scaled = dnormed * gain_ref[...]
        dmiddle = top_ref[rows].astype(F32) + scale * (
            scaled - normed * jnp.mean(scaled * normed, axis=-1, keepdims=True)
        )
        dmiddle_out[rows] = dmiddle
        return live_ref[rows] * dmiddle

    def ready(piece):
        rows = gather.rows(piece)

        def store(cols, value):
            dmixed_out[:, rows, cols] = split(value, count)

        wide_dot([(joined(full[:, rows]), out_weight_ref)], NT, 256, store)

    sum_and_gather(scatter, gather, full, full_out, out_sems, prepare, middle, ready)


def feed_back(dgate, dup, gate_weight, up_weight, top, middle, live, gain, out_weight, count):
    own, features = middle.shape
    nz, nx = grid_sizes(count)
    width = out_weight.shape[0]
    return pl.pallas_call(
        functools.partial(feed_back_kernel, count),
        out_shape=[
            jax.ShapeDtypeStruct((own, features), F32),
            jax.ShapeDtypeStruct((1, features), F32),
            jax.ShapeDtypeStruct((count, own, features), BF16),
            jax.ShapeDtypeStruct((count, own, width), F32),
        ],
        in_specs=[VMEM_SPEC] * 9,
        out_specs=[VMEM_SPEC, VMEM_SPEC, ANY_SPEC, VMEM_SPEC],
        scratch_shapes=[
            *scatter_scratch(nz, nx, own, features, PAIR_SHARE),
            *gather_scratch(nz, nx, own, features),
            pltpu.SemaphoreType.DMA((PIECES,)),
        ],
        compiler_params=linked(2),
        cost_estimate=lasting(180),
        name="feed_back",
    )(
        split(dgate, count), split(dup, count), gate_weight, up_weight, top, middle, live, gain,
        out_weight,
    )


class Replicas(Sender):
    def __init__(self, values, from_core, from_y, over_back, over_home, sems):
        self.values, self.from_core, self.from_y = values, from_core, from_y
        self.over_back, self.over_home = over_back, over_home
        self.core_sems, self.y_sems, self.back_sems, self.home_sems = sems
        me = lax.axis_index("dp")
        self.lines = lax.axis_size("dp") // 2
        self.y, self.core = me // 2, me % 2

    @staticmethod
    def scratch(rows, cols, replicas):
        lines, share = replicas // 2, rows // replicas
        return [
            pltpu.VMEM((replicas, share, cols), BF16),
            pltpu.VMEM((lines, share, cols), BF16),
            pltpu.VMEM((max(lines - 1, 1), share, cols), BF16),
            pltpu.VMEM((max(lines - 1, 1), share, cols), BF16),
            pltpu.VMEM((lines, share, cols), BF16),
            *[pltpu.SemaphoreType.DMA((2, lines))] * 4,
        ]

    def share(self, core, y):
        return core * self.lines + y

    def peer(self, y, core):
        return {"dp": y * 2 + core}

    def line(self, k):
        return (self.y + k) % self.lines

    def drain(self):
        self.draining = True
        for k in range(self.lines):
            self.start(k)
            self.cores(k)
        self.over_y()
        self.back()
        self.draining = False

    def add(self, share, others):
        step = 64

        def some(block, _):
            rows = pl.ds(pl.multiple_of(block * step, step), step)
            total = self.values[share, rows].astype(F32)
            for ref, index in others:
                total = total + ref[index, rows].astype(F32)
            self.values[share, rows] = total.astype(BF16)
            return 0

        lax.fori_loop(0, self.values.shape[1] // step, some, 0)

    def start(self, k):
        y = self.line(k)
        self.push(
            self.values.at[self.share(1 - self.core, y)],
            self.from_core.at[y],
            self.core_sems.at[0, k],
            self.core_sems.at[1, k],
            self.peer(self.y, 1 - self.core),
        )

    def cores(self, k):
        y = self.line(k)
        share = self.share(self.core, y)
        if not self.draining:
            arrived(self.from_core.at[y], self.core_sems.at[1, k])
            self.add(share, [(self.from_core, y)])
        if k > 0:
            self.push(
                self.values.at[share],
                self.from_y.at[self.lines - k - 1],
                self.y_sems.at[0, k],
                self.y_sems.at[1, self.lines - k],
                self.peer(y, self.core),
            )

    def over_y(self):
        share = self.share(self.core, self.y)
        if not self.draining:
            for k in range(1, self.lines):
                arrived(self.from_y.at[k - 1], self.y_sems.at[1, k])
            self.add(share, [(self.from_y, k) for k in range(self.lines - 1)])
        for k in range(1, self.lines):
            self.push(
                self.values.at[share],
                self.over_back.at[self.lines - k - 1],
                self.back_sems.at[0, k],
                self.back_sems.at[1, self.lines - k],
                self.peer(self.line(k), self.core),
            )
        self.send_home(0)

    def own(self, k):
        return self.values.at[self.share(self.core, self.y)] if k == 0 else self.over_back.at[k - 1]

    def send_home(self, k):
        self.push(
            self.own(k),
            self.over_home.at[k],
            self.home_sems.at[0, k],
            self.home_sems.at[1, k],
            self.peer(self.y, 1 - self.core),
        )

    def back(self):
        for k in range(1, self.lines):
            if not self.draining:
                arrived(self.over_back.at[k - 1], self.back_sems.at[1, k])
            self.send_home(k)

    def home(self):
        for k in range(self.lines):
            arrived(self.over_home.at[k], self.home_sems.at[1, k])

    def totals(self):
        for k in range(self.lines):
            yield self.own(k), self.share(self.core, self.line(k))
            yield self.over_home.at[k], self.share(1 - self.core, self.line(k))


def sum_small(small, seen, send_sems, recv_sems, axis, rows):
    me, size = lax.axis_index(axis), lax.axis_size(axis)
    copies = []
    seen[me] = small[...]
    for k in range(1, size):
        copy = pltpu.make_async_remote_copy(
            seen.at[me], seen.at[me], send_sems.at[k], recv_sems.at[size - k],
            device_id={axis: (me + k) % size}, device_id_type=MESH,
        )
        copy.start()
        copies.append(copy)
    for k in range(1, size):
        arrived(seen.at[(me + k) % size], recv_sems.at[k])
    total = seen[0]
    for other in range(1, size):
        total = total + seen[other]
    small[...] = jnp.where(grid_index(total.shape, 0) < rows, total, small[...])
    return copies


def input_back_kernel(
    count, grad_ref, weight_ref, normed_ref, later_ref, input_ref, gain_ref, small_ref,
    wout_ref, grad_out, small_out, dweight_out, *scratch
):
    parts, rest = scratch[0], scratch[SCATTER_COUNT:]
    values = rest[0]
    near, near_send, near_recv, far, far_send, far_recv, staged, out_sems = rest[9:]
    scatter = scatter_of(Group(count), SCATTER_SHARE, scratch[:SCATTER_COUNT])
    replicas = Replicas(*rest[:5], rest[5:9])
    meet(count, lax.axis_size("dp"))
    small_out[...] = small_ref[...]
    width = grad_ref.shape[2]
    values[:, :, width:] = split(wout_ref[...], values.shape[0])

    def begin(piece):
        rows = scatter.rows(piece)

        def store(cols, value):
            parts[:, rows, cols] = split(value.astype(BF16), count)

        wide_dot([(joined(grad_ref[:, rows]), weight_ref)], NT, 256, store)
        scatter.phase(piece, 0)

    def end(piece):
        dnormed = scatter.phase(piece, scatter.last)
        rows = scatter.rows(piece)
        given = input_ref[rows].astype(F32)
        scale = inverse_rms(given)
        normed = given * scale
        small_out[0:1] += jnp.sum(dnormed * normed, axis=0, keepdims=True)
        scaled = dnormed * gain_ref[...]
        grad_out[rows] = later_ref[rows] + scale * (
            scaled - normed * jnp.mean(scaled * normed, axis=-1, keepdims=True)
        )

    def weight_share(core, y):
        share = replicas.share(core, y)
        left = joined(normed_ref[share])
        grads = joined(grad_ref[...])
        for first in range(0, width, 384):
            cols = slice(first, min(first + 384, width))
            staged[:, cols] = lax.dot_general(
                left, grads[:, cols], (TN, ((), ())), preferred_element_type=F32
            ).astype(BF16)

        def some(block, _):
            rows = pl.ds(pl.multiple_of(block * 64, 64), 64)
            values[share, rows, :width] = staged[rows]
            return 0

        lax.fori_loop(0, staged.shape[0] // 64, some, 0)

    def other_core(k):
        weight_share(1 - replicas.core, replicas.line(k))
        replicas.start(k)

    def this_core(k):
        weight_share(replicas.core, replicas.line(k))
        replicas.cores(k)

    order = range(replicas.lines - 1, -1, -1)
    steps = [functools.partial(other_core, k) for k in order]
    steps += [functools.partial(this_core, k) for k in order]
    steps += [replicas.over_y, replicas.back]

    def tick(time, _):
        during(time + 1, begin)
        for step in range(1, scatter.last):
            during(time - step + 1, functools.partial(scatter.phase, step=step))
        during(time - scatter.last + 1, end)
        for index, step in enumerate(steps):
            pl.when(time == index)(step)
        return 0

    lax.fori_loop(-1, max(PIECES + scatter.last - 1, len(steps)), tick, 0)
    copies = sum_small(small_out, near, near_send, near_recv, "heads", 3)
    copies += sum_small(small_out, far, far_send, far_recv, "dp", 8)
    replicas.home()
    outs = [
        pltpu.make_async_copy(total, dweight_out.at[share], out_sems.at[index])
        for index, (total, share) in enumerate(replicas.totals())
    ]
    for copy in outs:
        copy.start()
    scatter.drain()
    replicas.drain()
    for copy in copies:
        copy.wait_send()
    for copy in outs:
        copy.wait()


def input_back(
    grad, weight, normed, later, rows, gain, small, grad_wout, count, replica_count
):
    own, features = rows.shape
    nz, nx = grid_sizes(count)
    cols = weight.shape[1] + grad_wout.shape[1]
    dma = pltpu.SemaphoreType.DMA
    return pl.pallas_call(
        functools.partial(input_back_kernel, count),
        out_shape=[
            jax.ShapeDtypeStruct((own, features), F32),
            jax.ShapeDtypeStruct(small.shape, F32),
            jax.ShapeDtypeStruct((replica_count, features // replica_count, cols), BF16),
        ],
        in_specs=[VMEM_SPEC] * 8,
        out_specs=[VMEM_SPEC, VMEM_SPEC, ANY_SPEC],
        scratch_shapes=[
            *scatter_scratch(nz, nx, own, features, SCATTER_SHARE),
            *Replicas.scratch(features, cols, replica_count),
            pltpu.VMEM((count, *small.shape), F32),
            dma((count,)),
            dma((count,)),
            pltpu.VMEM((replica_count, *small.shape), F32),
            dma((replica_count,)),
            dma((replica_count,)),
            pltpu.VMEM((features // replica_count, weight.shape[1]), BF16),
            dma((replica_count,)),
        ],
        compiler_params=linked(3),
        cost_estimate=lasting(120),
        name="input_back",
    )(split(grad, count), weight, normed, later, rows, gain, small, grad_wout)


def matmul(left, right, dims):
    return lax.dot_general(left, right, (dims, ((), ())), preferred_element_type=F32)


def gather_rows(values):
    return lax.all_gather(values, "heads", axis=0, tiled=True)


def scatter_rows(values):
    return lax.psum_scatter(
        values.astype(BF16), "heads", scatter_dimension=0, tiled=True
    ).astype(F32)


def on_device(
    block_in,
    seq_counts,
    norm1_gain,
    w_qkvg,
    conv_weight,
    w_gates,
    gate_params,
    out_gain,
    w_out,
    norm2_gain,
    w_gate_up,
    w_down,
    cotangent,
):
    own_rows, features = block_in.shape
    count = lax.axis_size("heads")
    all_rows = own_rows * count
    width = conv_weight.shape[2]
    heads = gate_params.shape[1]
    longer = seq_counts[0, 1:2]
    first_row = lax.axis_index("heads") * own_rows
    row_index = first_row + jnp.arange(own_rows, dtype=jnp.int32)
    live_own = jnp.where(longer[0] > 0, True, row_index < seq_counts[0, 0] * SEQ_SHORT)
    live_own = live_own.astype(F32)[:, None]
    weight = jnp.concatenate(
        [
            w_qkvg.reshape(features, 4 * width),
            w_gates.reshape(features, 2 * heads),
            jnp.zeros((features, 128 - 2 * heads), BF16),
        ],
        axis=1,
    )
    full_normed1, projected = project(
        block_in, norm1_gain[None], weight, count, lax.axis_size("dp")
    )
    projected, grad_feed = lax.optimization_barrier(
        (projected, (live_own * cotangent.astype(F32)).astype(BF16))
    )
    grad_feed = gather_rows(grad_feed)
    projected = projected.reshape(all_rows, -1)
    taps = jnp.transpose(conv_weight, (1, 0, 2)).reshape(4, 3 * width)
    params = jnp.pad(gate_params, ((0, 0), (0, 128 - heads)))
    gain_row = out_gain[None]
    mixed, *saved = mixer_forward(longer, projected, taps, params, gain_row)
    mixed, grad_feed = lax.optimization_barrier((mixed, grad_feed))
    middle, full_normed2 = branch_and_norm(
        mixed, w_out, block_in, live_own, norm2_gain[None], count
    )
    full_normed2 = full_normed2.reshape(all_rows, features)
    gate_weight, up_weight = w_gate_up[:, 0], w_gate_up[:, 1]
    gate_pre = matmul(full_normed2, gate_weight, NN)
    up_pre = matmul(full_normed2, up_weight, NN)
    hidden = (jax.nn.silu(gate_pre) * up_pre).astype(BF16)
    grad_hidden = matmul(grad_feed, w_down, NT)
    sigmoid_gate = jax.nn.sigmoid(gate_pre)
    grad_gate = grad_hidden * up_pre * sigmoid_gate * (1.0 + gate_pre * (1.0 - sigmoid_gate))
    grad_gate = grad_gate.astype(BF16)
    grad_up = (grad_hidden * gate_pre * sigmoid_gate).astype(BF16)
    early = (
        matmul(full_normed2, grad_gate, TN).astype(BF16),
        matmul(full_normed2, grad_up, TN).astype(BF16),
        matmul(hidden, grad_feed, TN).astype(BF16),
    )
    grad_gate, grad_up, early, hidden = lax.optimization_barrier(
        (grad_gate, grad_up, early, hidden)
    )
    grad_middle, grad_gain2, grad_mix, grad_mixed = feed_back(
        grad_gate,
        grad_up,
        gate_weight,
        up_weight,
        cotangent,
        middle,
        live_own,
        norm2_gain[None],
        w_out,
        count,
    )
    early = lax.psum(early, "dp")
    hidden, grad_mixed, early = lax.optimization_barrier((hidden, grad_mixed, early))
    feed = scatter_rows(matmul(hidden, w_down, NN))
    grad_mix = grad_mix.reshape(all_rows, features)
    grad_wout = matmul(grad_mix, mixed, TN).astype(BF16)
    dprojected, dtaps, dparams, dgain = mixer_backward(
        longer, grad_mixed.reshape(all_rows, width), projected, saved, taps, params, gain_row
    )
    dprojected, feed = lax.optimization_barrier((dprojected, feed))
    layer_out = (middle + live_own * feed).astype(BF16)

    def row(values):
        return jnp.pad(values, ((0, 0), (0, features - values.shape[1])))

    small = jnp.concatenate(
        [
            jnp.zeros((1, features), F32),
            grad_gain2,
            row(dgain),
            row(dtaps),
            row(dparams.reshape(1, 256)),
        ],
        axis=0,
    )
    grad_in, small, grad_weight = input_back(
        dprojected,
        weight,
        full_normed1,
        grad_middle,
        block_in,
        norm1_gain[None],
        small,
        grad_wout,
        count,
        lax.axis_size("dp"),
    )
    cols = weight.shape[1]
    grad_weight = grad_weight.reshape(features, -1)
    grad_weight, grad_wout = grad_weight[:, :cols].astype(F32), grad_weight[:, cols:].T
    return (
        layer_out,
        grad_in,
        small[0],
        grad_weight[:, : 4 * width].reshape(w_qkvg.shape),
        jnp.transpose(small[3:7, : 3 * width].reshape(4, 3, width), (1, 0, 2)),
        grad_weight[:, 4 * width : 4 * width + 2 * heads].reshape(w_gates.shape),
        small[7, :256].reshape(2, 128)[:, :heads],
        small[2, : out_gain.shape[0]],
        grad_wout.astype(F32),
        small[1],
        jnp.stack([early[0], early[1]], axis=1).astype(F32),
        early[2].astype(F32),
    )


def solution(mesh):
    return jax.shard_map(
        on_device,
        mesh=mesh,
        in_specs=(
            P(("dp", "heads"), None),
            P("dp", None),
            P(),
            P(None, None, "heads"),
            P(None, None, "heads"),
            P(None, None, "heads"),
            P(None, "heads"),
            P(),
            P("heads", None),
            P(),
            P(None, None, "heads"),
            P("heads", None),
            P(("dp", "heads"), None),
        ),
        out_specs=(
            P(("dp", "heads"), None),
            P(("dp", "heads"), None),
            P(),
            P(None, None, "heads"),
            P(None, None, "heads"),
            P(None, None, "heads"),
            P(None, "heads"),
            P(),
            P("heads", None),
            P(),
            P(None, None, "heads"),
            P("heads", None),
        ),
        check_vma=False,
    )
```

```python
import functools
import jax
import jax.numpy as jnp
from jax import lax
from jax.experimental import pallas as pl
from jax.experimental.pallas import tpu as pltpu
from jax.sharding import PartitionSpec as P

SEQ_SHORT = 512
CHUNK = 256
HEAD = 128
EPS = 1e-06
F32 = jnp.float32
BF16 = jnp.bfloat16
LOW, MID, TOP = lax.Precision.DEFAULT, lax.Precision.HIGH, lax.Precision.HIGHEST
NN, NT, TN = ((1,), (0,)), ((1,), (1,)), ((0,), (0,))
P_FWD, P_BWD = MID, MID


def dot(left, right, dims, precision):
    if precision is LOW:
        left, right = left.astype(BF16), right.astype(BF16)
        return lax.dot_general(left, right, (dims, ((), ())), preferred_element_type=F32)
    return lax.dot_general(
        left, right, (dims, ((), ())), precision=precision, preferred_element_type=F32
    )


def grid_index(shape, axis):
    return lax.broadcasted_iota(jnp.int32, shape, axis)


def positions(longer, first_row, count):
    rows = grid_index((count, 1), 0) + first_row
    return jnp.where(longer > 0, rows, rows % SEQ_SHORT)


def keeps(longer, first_row):
    start = jnp.where(longer > 0, first_row, first_row % SEQ_SHORT)
    return jnp.where(start > 0, 1.0, 0.0).astype(F32)


def softplus(x):
    return jnp.maximum(x, 0.0) + jnp.log1p(jnp.exp(-jnp.abs(x)))


def gate_values(gates, params, heads):
    lane = grid_index(gates.shape, 1)
    rate = jnp.exp(params[0:1])
    shifted = gates + params[1:2]
    log_decay = jnp.where(lane < heads, -rate * softplus(shifted), 0.0)
    return rate, shifted, log_decay


def lane_column(values, index):
    return values[:, index : index + 1]


def decays(cumulative, cumulative_rows, head, masks):
    column = lane_column(cumulative, head)
    row = cumulative_rows[head : head + 1, :]
    inclusive = masks[0]
    ratio = jnp.where(inclusive, jnp.exp(jnp.where(inclusive, column - row, 0.0)), 0.0)
    last = column[CHUNK - 1 : CHUNK, :]
    return ratio, jnp.exp(column), jnp.exp(last - column), jnp.exp(last)


def unit(values):
    scale = lax.rsqrt(jnp.sum(values * values, axis=-1, keepdims=True) + EPS)
    return values * scale, scale


def pair_of(values):
    high = values.astype(BF16)
    return high, (values - high.astype(F32)).astype(BF16)


def pair_dot(left, right):
    def product(a, b):
        return lax.dot_general(a, b, (NN, ((), ())), preferred_element_type=F32)

    return product(left[0], right[0]) + (product(left[0], right[1]) + product(left[1], right[0]))


def inverses(links, row, col):
    apart = row ^ col
    size = links[0].shape[0]
    outs = [jnp.where(row == col, 1.0, 0.0) - jnp.where(apart == 1, link, 0.0) for link in links]
    pairs = [pair_of(link) for link in links]
    step = 2
    while step < size // 2:
        level = (apart >= step) & (apart < 2 * step)
        parts = [tuple(jnp.where(level, half, 0) for half in pair) for pair in pairs]
        out_pairs = [pair_of(out) for out in outs]
        inner = [pair_of(pair_dot(part, out)) for part, out in zip(parts, out_pairs)]
        outs = [out - pair_dot(pair, mid) for out, pair, mid in zip(outs, out_pairs, inner)]
        step *= 2
    half = size // 2
    uppers = [pair_of(out[:half, :half]) for out in outs]
    lowers = [pair_of(out[half:, half:]) for out in outs]
    corners = [tuple(each[half:, :half] for each in pair) for pair in pairs]
    inner = [pair_of(pair_dot(corner, upper)) for corner, upper in zip(corners, uppers)]
    corners = [pair_dot(lower, mid) for lower, mid in zip(lowers, inner)]
    return [
        jnp.concatenate(
            [out[:half], jnp.concatenate([-corner, out[half:, half:]], axis=1)], axis=0
        )
        for out, corner in zip(outs, corners)
    ]


def forward_kernel(
    heads, count, chunks, longer_ref, main_ref, conv_ref, params_ref, gain_ref, top_ref, live_ref,
    mixed_ref, conv_out_ref, raw_ref, delta_ref, solve_ref, state_ref, full_out,
    state, tail_rows, *scratch
):
    step = pl.program_id(0)
    first_row = step * CHUNK
    carry_along(step, chunks, count, top_ref, live_ref, full_out, scratch)
    longer = longer_ref[0]
    width = heads * HEAD

    @pl.when(step == 0)
    def _():
        state[...] = jnp.zeros_like(state)
        tail_rows[...] = jnp.zeros_like(tail_rows)

    position = positions(longer, first_row, CHUNK)
    keep = keeps(longer, first_row)
    triple = main_ref[:, : 3 * width]
    padded = jnp.concatenate([tail_rows[...], triple], axis=0)
    taps = conv_ref[...]
    convolved = triple * taps[0:1]
    for lag in range(1, 4):
        shifted = padded[8 - lag : 8 - lag + CHUNK]
        convolved = convolved + jnp.where(position >= lag, shifted, 0.0) * taps[lag : lag + 1]
    tail_rows[...] = triple[CHUNK - 8 :]
    conv_out_ref[...] = convolved
    active = convolved * jax.nn.sigmoid(convolved)
    gates = main_ref[:, 4 * width :]
    rate, shifted_gate, log_decay = gate_values(gates, params_ref[...], heads)
    beta_all = jax.nn.sigmoid(gates)
    row = grid_index((CHUNK, CHUNK), 0)
    col = grid_index((CHUNK, CHUNK), 1)
    masks = (row >= col, row > col)
    cumulative = dot(jnp.where(masks[0], 1.0, 0.0), log_decay, NN, TOP)
    cumulative_rows = jnp.transpose(cumulative)
    each = range(heads)
    columns = [slice(head * HEAD, (head + 1) * HEAD) for head in each]
    queries = [unit(active[:, cols])[0] * HEAD**-0.5 for cols in columns]
    keys = [unit(active[:, width + head * HEAD : width + (head + 1) * HEAD])[0] for head in each]
    values = [active[:, 2 * width + head * HEAD : 2 * width + (head + 1) * HEAD] for head in each]
    betas = [lane_column(beta_all, heads + head) for head in each]
    spans = [decays(cumulative, cumulative_rows, head, masks) for head in each]
    grams = [
        dot(jnp.concatenate([key, query], axis=0), key, NT, P_FWD)
        for key, query in zip(keys, queries)
    ]
    links = [
        jnp.where(masks[1], beta * span[0] * gram[:CHUNK], 0.0)
        for beta, span, gram in zip(betas, spans, grams)
    ]
    solves = inverses(links, row, col)
    boths = [
        dot(
            solve,
            jnp.concatenate([beta * value, (beta * span[1]) * key], axis=1),
            NN,
            P_FWD,
        )
        for solve, beta, value, key, span in zip(solves, betas, values, keys, spans)
    ]
    entries = [state[head] * keep for head in each]
    carried = [
        dot(jnp.concatenate([both[:, HEAD:], span[1] * query], axis=0), entry, NT, P_FWD)
        for both, span, query, entry in zip(boths, spans, queries, entries)
    ]
    deltas = [both[:, :HEAD] - carry[:CHUNK] for both, carry in zip(boths, carried)]
    states = [
        span[3] * entry + dot(delta * span[2], key, TN, P_FWD)
        for span, entry, delta, key in zip(spans, entries, deltas, keys)
    ]
    raws = [
        carry[CHUNK:] + dot(gram[CHUNK:] * span[0], delta, NN, P_FWD)
        for carry, gram, span, delta in zip(carried, grams, spans, deltas)
    ]
    for head, cols in zip(each, columns):
        solve_ref[head] = solves[head]
        state_ref[0, head] = entries[head]
        state[head] = states[head]
        delta_ref[:, cols] = deltas[head]
        raw = raws[head]
        raw_ref[:, cols] = raw
        scale = lax.rsqrt(jnp.mean(raw * raw, axis=-1, keepdims=True) + EPS)
        gate = main_ref[:, 3 * width + head * HEAD : 3 * width + (head + 1) * HEAD]
        mixed = raw * scale * gain_ref[...] * (gate * jax.nn.sigmoid(gate))
        mixed_ref[:, cols] = mixed.astype(mixed_ref.dtype)


def carry_along(step, chunks, count, top_ref, live_ref, full_out, scratch):
    *scratch, out_sems = scratch
    full = scratch[0]
    gather = gather_of(Group(count), GATHER_SHARE, scratch)

    def out(piece):
        rows = gather.rows(piece)
        return pltpu.make_async_copy(full.at[:, rows], full_out.at[:, rows], out_sems.at[piece])

    def begin(piece):
        rows = gather.rows(piece)
        full[lax.axis_index("heads"), rows] = (
            live_ref[rows] * top_ref[rows].astype(F32)
        ).astype(BF16)
        gather.phase(piece, 0)

    def end(piece):
        gather.phase(piece, gather.last)
        out(piece).start()

    def tick(time, _):
        during(time, begin)
        for phase in range(1, gather.last):
            during(time - phase, functools.partial(gather.phase, step=phase))
        during(time - gather.last, end)
        return 0

    ticks = PIECES + gather.last

    @pl.when(step == 0)
    def _():
        meet(count)

    lax.fori_loop(step * ticks // chunks, (step + 1) * ticks // chunks, tick, 0)

    @pl.when(step == chunks - 1)
    def _():
        gather.drain()

        def finish(piece, _):
            out(piece).wait()
            return 0

        lax.fori_loop(0, PIECES, finish, 0)


def backward_kernel(
    heads, chunks, longer_ref, grad_ref, main_ref, conv_out_ref, raw_ref, delta_ref,
    solve_ref, state_ref, conv_ref, params_ref, gain_ref,
    dmain_ref, dconv_ref, dparams_ref, dgain_ref, dstate, head_rows,
):
    step = pl.program_id(0)
    first_row = (chunks - 1 - step) * CHUNK
    longer = longer_ref[0]
    width = heads * HEAD

    @pl.when(step == 0)
    def _():
        dstate[...] = jnp.zeros_like(dstate)
        head_rows[...] = jnp.zeros_like(head_rows)
        dconv_ref[...] = jnp.zeros_like(dconv_ref)
        dparams_ref[...] = jnp.zeros_like(dparams_ref)
        dgain_ref[...] = jnp.zeros_like(dgain_ref)

    keep = keeps(longer, first_row)
    convolved = conv_out_ref[...]
    sigmoid_conv = jax.nn.sigmoid(convolved)
    active = convolved * sigmoid_conv
    slope = sigmoid_conv * (1.0 + convolved * (1.0 - sigmoid_conv))
    gates = main_ref[:, 4 * width :]
    params = params_ref[...]
    rate, shifted_gate, log_decay = gate_values(gates, params, heads)
    beta_all = jax.nn.sigmoid(gates)
    row = grid_index((CHUNK, CHUNK), 0)
    col = grid_index((CHUNK, CHUNK), 1)
    masks = (row >= col, row > col)
    cumulative = dot(jnp.where(masks[0], 1.0, 0.0), log_decay, NN, TOP)
    cumulative_rows = jnp.transpose(cumulative)
    lane = grid_index((CHUNK, 128), 1)
    last_row = grid_index((CHUNK, 1), 0) == CHUNK - 1
    gain = gain_ref[...]
    dgains, dlogs, dbetas, dparts = ([None] * heads for _ in range(4))

    def work(head):
        cols = slice(head * HEAD, (head + 1) * HEAD)
        gate = main_ref[:, 3 * width + head * HEAD : 3 * width + (head + 1) * HEAD]
        raw = raw_ref[:, cols]
        grad = grad_ref[:, cols]
        scale = lax.rsqrt(jnp.mean(raw * raw, axis=-1, keepdims=True) + EPS)
        normed = raw * scale
        sigmoid_gate = jax.nn.sigmoid(gate)
        gated = gate * sigmoid_gate
        product = grad * normed
        dgains[head] = jnp.sum(product * gated, axis=0, keepdims=True)
        dgate = product * gain * (sigmoid_gate * (1.0 + gate * (1.0 - sigmoid_gate)))
        dmain_ref[:, 3 * width + head * HEAD : 3 * width + (head + 1) * HEAD] = dgate.astype(
            dmain_ref.dtype
        )
        dnormed = grad * gain * gated
        draw = scale * (dnormed - normed * jnp.mean(dnormed * normed, axis=-1, keepdims=True))
        query_unit, query_scale = unit(active[:, head * HEAD : (head + 1) * HEAD])
        query = query_unit * HEAD**-0.5
        key, key_scale = unit(active[:, width + head * HEAD : width + (head + 1) * HEAD])
        value = active[:, 2 * width + head * HEAD : 2 * width + (head + 1) * HEAD]
        beta = lane_column(beta_all, heads + head)
        ratio, decay_in, decay_out, decay_all = decays(cumulative, cumulative_rows, head, masks)
        entry = state_ref[0, head]
        delta = delta_ref[:, cols]
        dlater = dstate[head]
        gram = dot(query, key, NT, P_BWD) * ratio
        yield
        key_dlater = dot(key, dlater, NT, P_BWD)
        yield
        ddelta = dot(gram, draw, TN, P_BWD) + decay_out * key_dlater
        yield
        dright = dot(solve_ref[head], ddelta, TN, P_BWD)
        yield
        pairs = dot(jnp.concatenate([dright, draw], axis=0), delta, NT, P_BWD)
        yield
        dlink = jnp.where(masks[1], -pairs[:CHUNK] * ratio, 0.0)
        dgram = pairs[CHUNK:] * ratio
        on_entry = dot(jnp.concatenate([dright, draw], axis=0), entry, NN, P_BWD)
        yield
        key_entry = dot(key, entry, NT, P_BWD)
        yield
        on_key = dot(jnp.concatenate([dlink, dgram], axis=0), key, NN, P_BWD)
        yield
        dquery = decay_in * on_entry[CHUNK:] + on_key[CHUNK:]
        link_key = on_key[:CHUNK]
        key_read = beta * (link_key - decay_in * on_entry[:CHUNK])
        key_tail = decay_out * dot(delta, dlater, NN, P_BWD)
        yield
        key_write = (
            dot(beta * dlink, key, TN, P_BWD) + dot(dgram, query, TN, P_BWD) + key_tail
        )
        yield
        dkey = key_read + key_write
        dvalue = beta * dright
        dbeta = jnp.sum(
            dright * (value - decay_in * key_entry) + key * link_key, axis=-1, keepdims=True
        )
        dlog = jnp.sum(query * dquery + key * (key_read - key_write), axis=-1, keepdims=True)
        ending = decay_all * jnp.sum(
            jnp.sum(entry * dlater, axis=-1, keepdims=True), axis=0, keepdims=True
        ) + jnp.sum(jnp.sum(key * key_tail, axis=-1, keepdims=True), axis=0, keepdims=True)
        dlog = dlog + jnp.where(last_row, ending, 0.0)
        dlogs[head], dbetas[head] = dlog, dbeta
        dstate[head] = keep * (
            decay_all * dlater
            + dot(decay_in * draw, query, TN, P_BWD)
            - dot((beta * decay_in) * dright, key, TN, P_BWD)
        )
        yield
        dquery = (HEAD**-0.5 * query_scale) * (
            dquery - query_unit * jnp.sum(dquery * query_unit, axis=-1, keepdims=True)
        )
        dkey = key_scale * (dkey - key * jnp.sum(dkey * key, axis=-1, keepdims=True))
        dparts[head] = (dquery, dkey, dvalue)

    works = [work(head) for head in range(heads)]
    while works:
        works = [each for each in works if next(each, "end") != "end"]
    dcumulative = jnp.zeros((CHUNK, 128), F32)
    dbeta_all = jnp.zeros((CHUNK, 128), F32)
    for head in range(heads):
        dcumulative = jnp.where(lane == head, dlogs[head], dcumulative)
        dbeta_all = jnp.where(lane == heads + head, dbetas[head], dbeta_all)
    dgain = functools.reduce(jnp.add, dgains)
    dconv_parts = [[dparts[head][kind] for head in range(heads)] for kind in range(3)]
    dactive = jnp.concatenate([p for parts in dconv_parts for p in parts], axis=1)
    dconvolved = dactive * slope
    padded = jnp.concatenate([dconvolved, head_rows[...]], axis=0)
    position = positions(longer, first_row, CHUNK + 8)
    taps = conv_ref[...]
    triple = main_ref[:, : 3 * width]
    dtriple = dconvolved * taps[0:1]
    dconv_ref[0:1] += jnp.sum(dconvolved * triple, axis=0, keepdims=True)
    for lag in range(1, 4):
        moved = jnp.where(position >= lag, padded, 0.0)[lag : lag + CHUNK]
        dtriple = dtriple + moved * taps[lag : lag + 1]
        dconv_ref[lag : lag + 1] += jnp.sum(moved * triple, axis=0, keepdims=True)
    head_rows[...] = dconvolved[:8]
    dmain_ref[:, : 3 * width] = dtriple.astype(dmain_ref.dtype)
    dlog_decay = dot(jnp.where(row <= col, 1.0, 0.0), dcumulative, NN, TOP)
    dshifted = -dlog_decay * rate * jax.nn.sigmoid(shifted_gate)
    dshifted = jnp.where(lane < heads, dshifted, 0.0)
    dparams_ref[0:1] += jnp.sum(dlog_decay * log_decay, axis=0, keepdims=True)
    dparams_ref[1:2] += jnp.sum(dshifted, axis=0, keepdims=True)
    dmain_ref[:, 4 * width :] = (dshifted + dbeta_all * beta_all * (1.0 - beta_all)).astype(
        dmain_ref.dtype
    )
    dgain_ref[...] += dgain


def row_block(width, chunks, backward):
    if backward:
        return pl.BlockSpec((CHUNK, width), lambda i: (chunks - 1 - i, 0))
    return pl.BlockSpec((CHUNK, width), lambda i: (i, 0))


def whole_block(shape):
    return pl.BlockSpec(shape, lambda i: (0,) * len(shape))


def mixer_forward(longer, main, conv, params, gain, top, live, count):
    rows, width = main.shape[0], conv.shape[1] // 3
    heads, chunks = width // HEAD, rows // CHUNK
    own, features = top.shape
    nz, nx = grid_sizes(count)
    rowed = functools.partial(row_block, chunks=chunks, backward=False)
    shape = jax.ShapeDtypeStruct
    return pl.pallas_call(
        functools.partial(forward_kernel, heads, count, chunks),
        grid=(chunks,),
        in_specs=[
            pl.BlockSpec(memory_space=pltpu.SMEM),
            rowed(4 * width + 128),
            whole_block((4, 3 * width)),
            whole_block((2, 128)),
            whole_block((1, HEAD)),
            whole_block((own, features)),
            whole_block((own, 1)),
        ],
        out_specs=[
            rowed(width),
            rowed(3 * width),
            rowed(width),
            rowed(width),
            pl.BlockSpec((heads, CHUNK, CHUNK), lambda i: (0, i, 0)),
            pl.BlockSpec((1, heads, HEAD, HEAD), lambda i: (i, 0, 0, 0)),
            pl.BlockSpec(memory_space=pl.ANY),
        ],
        out_shape=[
            shape((rows, width), BF16),
            shape((rows, 3 * width), F32),
            shape((rows, width), F32),
            shape((rows, width), F32),
            shape((heads, rows, CHUNK), F32),
            shape((chunks, heads, HEAD, HEAD), F32),
            shape((count, own, features), BF16),
        ],
        scratch_shapes=[
            pltpu.VMEM((heads, HEAD, HEAD), F32),
            pltpu.VMEM((8, 3 * width), F32),
            *gather_scratch(nz, nx, own, features),
            pltpu.SemaphoreType.DMA((PIECES,)),
        ],
        compiler_params=linked(4),
        cost_estimate=lasting(95),
        name="mixer_forward",
    )(longer, main, conv, params, gain, top, live)


def mixer_backward(longer, grad, main, saved, conv, params, gain):
    rows, width = main.shape[0], conv.shape[1] // 3
    heads, chunks = width // HEAD, rows // CHUNK
    rowed = functools.partial(row_block, chunks=chunks, backward=True)
    shape = jax.ShapeDtypeStruct
    return pl.pallas_call(
        functools.partial(backward_kernel, heads, chunks),
        grid=(chunks,),
        in_specs=[
            pl.BlockSpec(memory_space=pltpu.SMEM),
            rowed(width),
            rowed(4 * width + 128),
            rowed(3 * width),
            rowed(width),
            rowed(width),
            pl.BlockSpec((heads, CHUNK, CHUNK), lambda i: (0, chunks - 1 - i, 0)),
            pl.BlockSpec((1, heads, HEAD, HEAD), lambda i: (chunks - 1 - i, 0, 0, 0)),
            whole_block((4, 3 * width)),
            whole_block((2, 128)),
            whole_block((1, HEAD)),
        ],
        out_specs=[
            rowed(4 * width + 128),
            whole_block((4, 3 * width)),
            whole_block((2, 128)),
            whole_block((1, HEAD)),
        ],
        out_shape=[
            shape((rows, 4 * width + 128), BF16),
            shape((4, 3 * width), F32),
            shape((2, 128), F32),
            shape((1, HEAD), F32),
        ],
        scratch_shapes=[
            pltpu.VMEM((heads, HEAD, HEAD), F32),
            pltpu.VMEM((8, 3 * width), F32),
        ],
        compiler_params=pltpu.CompilerParams(vmem_limit_bytes=48 * 2**20),
        cost_estimate=pl.CostEstimate(
            flops=6 * 10**10, bytes_accessed=2**20, transcendentals=0
        ),
        name="mixer_backward",
    )(longer, grad, main, *saved, conv, params, gain)


MESH = pl.DeviceIdType.MESH
PIECES = 8


def grid_sizes(count):
    nz = 4 if count % 4 == 0 else 1
    return nz, count // nz


class Group:
    def __init__(self, count):
        self.deep, self.nx = grid_sizes(count)
        self.size = count
        me = lax.axis_index("heads")
        self.z, self.x = me // self.nx, me % self.nx
        self.own = me

    def slot(self, z, j):
        return z * self.nx + (self.x + j) % self.nx

    def device(self, z, j):
        return {"heads": self.slot(z, j)}


def meet(count, replicas=1):
    barrier = pltpu.get_barrier_semaphore()
    for axis, size in (("heads", count), ("dp", replicas)):
        me = lax.axis_index(axis)

        def greet(k, _, axis=axis, size=size, me=me):
            pl.semaphore_signal(
                barrier, inc=1, device_id={axis: (me + k) % size}, device_id_type=MESH
            )
            return 0

        lax.fori_loop(1, size, greet, 0)
    pl.semaphore_wait(barrier, count + replicas - 2)


def arrived(ref, sem):
    pltpu.make_async_copy(ref, ref, sem).wait()


def during(piece, work):
    pl.when((piece >= 0) & (piece < PIECES))(functools.partial(work, piece))


class Sender:
    draining = False

    def push(self, source, target, send_sem, recv_sem, device, condition=None):
        copy = pltpu.make_async_remote_copy(
            source, target, send_sem, recv_sem, device_id=device, device_id_type=MESH
        )
        act = copy.wait_send if self.draining else copy.start
        if condition is None:
            act()
        else:
            pl.when(condition)(act)

    def place(self, piece):
        rows = pl.ds(pl.multiple_of(piece * self.part, self.part), self.part)
        return rows, self.cols

    def drain(self):
        def one(piece, _):
            for step in range(self.last + 1):
                self.phase(piece, step)
            return 0

        self.draining = True
        lax.fori_loop(0, PIECES, one, 0)
        self.draining = False


class Gather(Sender):
    def __init__(self, group, full, cols, send_sems, recv_sems, x_first):
        self.group, self.full, self.cols, self.x_first = group, full, cols, x_first
        self.part = full.shape[1] // PIECES
        self.send_sems, self.recv_sems = send_sems, recv_sems
        self.last = group.deep

    @staticmethod
    def sems(size):
        return [
            pltpu.SemaphoreType.DMA((PIECES, 3, size)),
            pltpu.SemaphoreType.DMA((PIECES, size)),
        ]

    def send(self, piece, slot, way, mark, device, condition):
        place = self.full.at[slot, *self.place(piece)]
        self.push(
            place,
            place,
            self.send_sems.at[piece, way, mark],
            self.recv_sems.at[piece, slot],
            device,
            condition,
        )

    def receive(self, piece, slot):
        if not self.draining:
            arrived(self.full.at[slot, *self.place(piece)], self.recv_sems.at[piece, slot])

    def send_up(self, piece, slot, here=True):
        group = self.group
        self.send(
            piece, slot, 0, slot, group.device(group.z + 1, 0), here & (group.z + 1 < group.deep)
        )

    def send_down(self, piece, slot, here=True):
        group = self.group
        self.send(piece, slot, 1, slot, group.device(group.z - 1, 0), here & (group.z > 0))

    def send_x(self, piece, slot, here=None):
        group = self.group
        for j in range(1, group.nx):
            mark = (slot // group.nx) * group.nx + (slot + j) % group.nx
            self.send(piece, slot, 2, mark, group.device(group.z, j), here)

    def phase(self, piece, step):
        group = self.group
        if step == 0:
            self.send_up(piece, group.own)
            self.send_down(piece, group.own)
            self.send_x(piece, group.own)
            return
        if self.x_first and step == 1:
            for j in range(1, group.nx):
                slot = group.slot(group.z, j)
                self.receive(piece, slot)
                self.send_up(piece, slot)
                self.send_down(piece, slot)
        if step < group.deep:
            for j in range(group.nx if self.x_first else 1):
                below, above = group.z - step, group.z + step
                for z, here, forward in (
                    (below, below >= 0, self.send_up),
                    (above, above < group.deep, self.send_down),
                ):
                    slot = group.slot(z, j)
                    pl.when(here)(functools.partial(self.receive, piece, slot))
                    forward(piece, slot, here)
                    if not self.x_first:
                        self.send_x(piece, slot, here)
        elif not self.x_first:
            for j in range(1, group.nx):
                for z in range(group.deep):
                    self.receive(piece, group.slot(z, j))


class Scatter(Sender):
    last = 3

    def __init__(self, group, parts, cols, scratch, z_first):
        self.group, self.parts, self.cols, self.z_first = group, parts, cols, z_first
        self.part = parts.shape[1] // PIECES
        self.over_x, self.line, *sems = scratch
        self.x_send, self.x_recv, self.z_send, self.z_recv = sems

    @staticmethod
    def scratch(deep, nx, rows, cols, z_first):
        dma = pltpu.SemaphoreType.DMA
        return [
            pltpu.VMEM((1 if z_first else deep, max(nx - 1, 1), rows, cols), BF16),
            pltpu.VMEM((deep + 1, nx if z_first else 1, rows, cols), BF16),
            *[dma((PIECES, deep, nx))] * 2,
            *[dma((PIECES, 2, deep * nx))] * 2,
        ]

    def landing(self, piece):
        return self.place(piece)[0]

    def line_at(self, piece, slot, way):
        nx = self.group.nx
        z = slot // nx + (1 if way == 0 else 0)
        return self.line.at[z, slot % nx if self.z_first else 0, self.landing(piece)]

    def step_line(self, piece, slot, way, device, add):
        part = (slot, *self.place(piece))
        if add and not self.draining:
            landed = self.line_at(piece, slot, way)
            arrived(landed, self.z_recv.at[piece, way, slot])
            total = self.parts[part].astype(F32) + landed[...].astype(F32)
            self.parts[part] = total.astype(BF16)
        self.push(
            self.parts.at[part],
            self.line_at(piece, slot, way),
            self.z_send.at[piece, way, slot],
            self.z_recv.at[piece, way, slot],
            device,
        )

    def walk(self, piece, columns, ends):
        group = self.group
        deep = group.deep

        def one_way(way):
            for k in range(deep - 1, 0, -1):
                target = group.z + k if way == 0 else group.z - k
                inside = target < deep if way == 0 else target >= 0
                first = group.z == 0 if way == 0 else group.z == deep - 1
                condition = inside & (first if ends else jnp.logical_not(first))
                device = group.device(group.z + (1 if way == 0 else -1), 0)
                for j in range(columns):
                    slot = group.slot(target, j)
                    pl.when(condition)(
                        functools.partial(self.step_line, piece, slot, way, device, not ends)
                    )

        if ends or self.draining:
            one_way(0)
            one_way(1)
            return

        def both(first, second):
            one_way(first)
            one_way(second)

        low = group.z < deep // 2
        pl.when(low)(functools.partial(both, 0, 1))
        pl.when(jnp.logical_not(low))(functools.partial(both, 1, 0))

    def total_line(self, piece, slot):
        group = self.group
        total = self.parts[(slot, *self.place(piece))].astype(F32)
        for way, here in ((0, group.z > 0), (1, group.z + 1 < group.deep)):
            landed = self.line_at(piece, slot, way)
            pl.when(here)(
                functools.partial(arrived, landed, self.z_recv.at[piece, way, slot])
            )
            total = total + jnp.where(here, landed[...].astype(F32), 0.0)
        return total

    def send_x(self, piece, index, z, j):
        group = self.group
        self.push(
            self.parts.at[group.slot(z, j), *self.place(piece)],
            self.over_x.at[index, j - 1, self.landing(piece)],
            self.x_send.at[piece, index, j],
            self.x_recv.at[piece, index, j],
            group.device(group.z, j),
        )

    def add_x(self, piece, index, total):
        for j in range(1, self.group.nx):
            landed = self.over_x.at[index, j - 1, self.landing(piece)]
            arrived(landed, self.x_recv.at[piece, index, j])
            total = total + landed[...].astype(F32)
        return total

    def phase(self, piece, step):
        group = self.group
        if self.z_first:
            if step == 0:
                self.walk(piece, group.nx, True)
            elif step == 1:
                self.walk(piece, group.nx, False)
            elif step == 2:
                for j in range(1, group.nx):
                    slot = group.slot(group.z, j)
                    if not self.draining:
                        total = self.total_line(piece, slot)
                        self.parts[(slot, *self.place(piece))] = total.astype(BF16)
                    self.send_x(piece, 0, group.z, j)
            elif not self.draining:
                return self.add_x(piece, 0, self.total_line(piece, group.own))
        elif step == 0:
            for z in range(group.deep):
                for j in range(1, group.nx):
                    self.send_x(piece, z, z, j)
        elif step == 1:
            for z in range(group.deep):
                part = (group.slot(z, 0), *self.place(piece))
                if not self.draining:
                    total = self.add_x(piece, z, self.parts[part].astype(F32))
                    self.parts[part] = total.astype(BF16)
            self.walk(piece, 1, True)
        elif step == 2:
            self.walk(piece, 1, False)
        elif not self.draining:
            return self.total_line(piece, group.own)
        return None


class Both:
    def __init__(self, first, second):
        self.both = (first, second)
        self.part, self.last = first.part, first.last

    def rows(self, piece):
        return pl.ds(pl.multiple_of(piece * self.part, self.part), self.part)

    def phase(self, piece, step):
        out = [each.phase(piece, step) for each in self.both]
        return None if out[0] is None else jnp.concatenate(out, axis=1)

    def drain(self):
        for each in self.both:
            each.drain()


def cut(cols, share):
    edge = cols - cols * share // 8
    return pl.ds(0, edge), pl.ds(edge, cols - edge)


def gather_of(group, share, scratch):
    full, *sems = scratch
    first, second = cut(full.shape[2], share)
    return Both(
        Gather(group, full, first, *sems[:2], False), Gather(group, full, second, *sems[2:], True)
    )


def scatter_of(group, share, scratch):
    parts, *rest = scratch
    first, second = cut(parts.shape[2], share)
    return Both(
        Scatter(group, parts, first, rest[:6], False),
        Scatter(group, parts, second, rest[6:], True),
    )


def gather_scratch(nz, nx, rows, cols):
    return [pltpu.VMEM((nz * nx, rows, cols), BF16), *Gather.sems(nz * nx), *Gather.sems(nz * nx)]


def scatter_scratch(nz, nx, rows, cols, share):
    first, second = cut(cols, share)
    return [
        pltpu.VMEM((nz * nx, rows, cols), BF16),
        *Scatter.scratch(nz, nx, rows, first.size, False),
        *Scatter.scratch(nz, nx, rows, second.size, True),
    ]


SCATTER_COUNT, GATHER_COUNT = 13, 5


def inverse_rms(rows):
    return lax.rsqrt(jnp.mean(rows * rows, axis=-1, keepdims=True) + EPS)


def wide_dot(terms, dims, tile, store):
    total = terms[0][1].shape[0 if dims is NT else 1]
    for first in range(0, total, tile):
        cols = slice(first, min(first + tile, total))
        products = [
            lax.dot_general(
                left,
                right[cols, :] if dims is NT else right[:, cols],
                (dims, ((), ())),
                preferred_element_type=F32,
            )
            for left, right in terms
        ]
        store(cols, functools.reduce(jnp.add, products))


VMEM_SPEC = pl.BlockSpec(memory_space=pltpu.VMEM)
ANY_SPEC = pl.BlockSpec(memory_space=pl.ANY)
PAIR_SHARE, GATHER_SHARE, SCATTER_SHARE = 3, 1, 2


def lasting(microseconds):
    return pl.CostEstimate(
        flops=int(microseconds * 1.1e9), bytes_accessed=2**20, transcendentals=0
    )


def linked(collective):
    return pltpu.CompilerParams(
        collective_id=collective, has_side_effects=True, vmem_limit_bytes=62 * 2**20
    )


def joined(values):
    return values.reshape(values.shape[0] * values.shape[1], values.shape[2])


def split(values, parts):
    return values.reshape(parts, values.shape[0] // parts, values.shape[1])


def project_kernel(count, rows_ref, gain_ref, weight_ref, full_out, projected_out, *scratch):
    full, staged, full_sems, staged_sems = scratch[0], *scratch[GATHER_COUNT:]
    group = Group(count)
    gather = gather_of(group, GATHER_SHARE, scratch[:GATHER_COUNT])
    meet(count)

    shares, share = full_out.shape[0], full_out.shape[3]

    def full_copy(piece, index):
        rows = gather.rows(piece)
        return pltpu.make_async_copy(
            full.at[:, rows, pl.ds(index * share, share)],
            full_out.at[index, :, rows],
            full_sems.at[piece, index],
        )

    def staged_copy(piece):
        rows = gather.rows(piece)
        return pltpu.make_async_copy(
            staged.at[:, rows], projected_out.at[:, rows], staged_sems.at[piece]
        )

    def begin(piece):
        rows = rows_ref[gather.rows(piece)].astype(F32)
        full[group.own, gather.rows(piece)] = (
            rows * inverse_rms(rows) * gain_ref[...]
        ).astype(BF16)
        gather.phase(piece, 0)

    def ready(piece):
        gather.phase(piece, gather.last)
        rows = gather.rows(piece)
        for index in range(shares):
            full_copy(piece, index).start()

        def store(cols, value):
            staged[:, rows, cols] = split(value, count)

        wide_dot([(joined(full[:, rows]), weight_ref)], NN, 256, store)
        staged_copy(piece).start()

    def tick(time, _):
        during(time, begin)
        for step in range(1, gather.last):
            during(time - step, functools.partial(gather.phase, step=step))
        during(time - gather.last, ready)
        return 0

    lax.fori_loop(0, PIECES + gather.last, tick, 0)
    gather.drain()

    def finish(piece, _):
        for index in range(shares):
            full_copy(piece, index).wait()
        staged_copy(piece).wait()
        return 0

    lax.fori_loop(0, PIECES, finish, 0)


def project(rows, gain, weight, count, shares):
    own, features = rows.shape
    cols = weight.shape[1]
    nz, nx = grid_sizes(count)
    return pl.pallas_call(
        functools.partial(project_kernel, count),
        out_shape=[
            jax.ShapeDtypeStruct((shares, count, own, features // shares), BF16),
            jax.ShapeDtypeStruct((count, own, cols), F32),
        ],
        in_specs=[VMEM_SPEC] * 3,
        out_specs=[ANY_SPEC] * 2,
        scratch_shapes=[
            *gather_scratch(nz, nx, own, features),
            pltpu.VMEM((count, own, cols), F32),
            pltpu.SemaphoreType.DMA((PIECES, shares)),
            pltpu.SemaphoreType.DMA((PIECES,)),
        ],
        compiler_params=linked(0),
        cost_estimate=lasting(100),
        name="project",
    )(rows, gain, weight)


def sum_and_gather(scatter, gather, full, full_out, out_sems, prepare, middle, ready):
    own = lax.axis_index("heads")

    def out(piece):
        rows = gather.rows(piece)
        return pltpu.make_async_copy(full.at[:, rows], full_out.at[:, rows], out_sems.at[piece])

    def begin(piece):
        prepare(piece)
        scatter.phase(piece, 0)

    def turn(piece):
        total = scatter.phase(piece, scatter.last)
        full[own, gather.rows(piece)] = middle(piece, total).astype(BF16)
        gather.phase(piece, 0)

    def end(piece):
        gather.phase(piece, gather.last)
        out(piece).start()
        ready(piece)

    def tick(time, _):
        during(time + 1, begin)
        for step in range(1, scatter.last):
            during(time - step + 1, functools.partial(scatter.phase, step=step))
        during(time - scatter.last + 1, turn)
        for step in range(1, gather.last):
            during(
                time - scatter.last + 1 - step, functools.partial(gather.phase, step=step)
            )
        during(time - scatter.last + 1 - gather.last, end)
        return 0

    lax.fori_loop(-1, PIECES + scatter.last + gather.last - 1, tick, 0)
    scatter.drain()
    gather.drain()

    def finish(piece, _):
        out(piece).wait()
        return 0

    lax.fori_loop(0, PIECES, finish, 0)


def branch_kernel(
    count, mixed_ref, weight_ref, input_ref, live_ref, gain_ref, gate_weight_ref, up_weight_ref,
    down_weight_ref, grad_ref, middle_out, full_out, dgate_out, dup_out, hidden_out, *scratch
):
    *scratch, grads, grad_sems, dgate, dup, hidden, feed_sems = scratch
    group = Group(count)
    scatter = scatter_of(group, PAIR_SHARE, scratch[:SCATTER_COUNT])
    gather = gather_of(group, PAIR_SHARE, scratch[SCATTER_COUNT:-1])
    parts, full, out_sems = scratch[0], scratch[SCATTER_COUNT], scratch[-1]

    def fetch(piece):
        slot = piece % 2
        return pltpu.make_async_copy(
            grad_ref.at[:, gather.rows(piece)], grads.at[slot], grad_sems.at[slot]
        )

    fetch(0).start()
    meet(count)

    def prepare(piece):
        rows = gather.rows(piece)

        def store(cols, value):
            parts[:, rows, cols] = split(value.astype(BF16), count)

        wide_dot([(joined(mixed_ref[:, rows]), weight_ref)], NN, 512, store)

    def middle(piece, total):
        rows = gather.rows(piece)
        values = input_ref[rows].astype(F32) + live_ref[rows] * total
        middle_out[rows] = values
        return values * inverse_rms(values) * gain_ref[...]

    def copies(piece):
        rows = gather.rows(piece)
        return [
            pltpu.make_async_copy(ref.at[:, rows], out.at[:, rows], feed_sems.at[piece, index])
            for index, (ref, out) in enumerate(
                ((dgate, dgate_out), (dup, dup_out), (hidden, hidden_out))
            )
        ]

    def ready(piece):
        rows = gather.rows(piece)
        fetch(piece).wait()
        pl.when(piece + 1 < PIECES)(lambda: fetch(piece + 1).start())
        left, grad = joined(full[:, rows]), joined(grads[piece % 2])
        total = gate_weight_ref.shape[1]
        for first in range(0, total, 256):
            cols = slice(first, min(first + 256, total))

            def product(a, b, dims):
                return lax.dot_general(a, b, (dims, ((), ())), preferred_element_type=F32)

            gate = product(left, gate_weight_ref[:, cols], NN)
            up = product(left, up_weight_ref[:, cols], NN)
            dhidden = product(grad, down_weight_ref[cols, :], NT)
            sigmoid = jax.nn.sigmoid(gate)
            active = gate * sigmoid
            hidden[:, rows, cols] = split((active * up).astype(BF16), count)
            dup[:, rows, cols] = split((dhidden * active).astype(BF16), count)
            slope = sigmoid * (1.0 + gate * (1.0 - sigmoid))
            dgate[:, rows, cols] = split((dhidden * up * slope).astype(BF16), count)
        for copy in copies(piece):
            copy.start()

    sum_and_gather(scatter, gather, full, full_out, out_sems, prepare, middle, ready)

    def finish(piece, _):
        for copy in copies(piece):
            copy.wait()
        return 0

    lax.fori_loop(0, PIECES, finish, 0)


def branch_and_feed(
    mixed, weight, rows, live, gain, gate_weight, up_weight, down_weight, grad, count
):
    own, features = rows.shape
    hidden = gate_weight.shape[1]
    nz, nx = grid_sizes(count)
    return pl.pallas_call(
        functools.partial(branch_kernel, count),
        out_shape=[
            jax.ShapeDtypeStruct((own, features), F32),
            jax.ShapeDtypeStruct((count, own, features), BF16),
            *[jax.ShapeDtypeStruct((count, own, hidden), BF16)] * 3,
        ],
        in_specs=[VMEM_SPEC] * 8 + [ANY_SPEC],
        out_specs=[VMEM_SPEC] + [ANY_SPEC] * 4,
        scratch_shapes=[
            *scatter_scratch(nz, nx, own, features, PAIR_SHARE),
            *gather_scratch(nz, nx, own, features),
            pltpu.SemaphoreType.DMA((PIECES,)),
            pltpu.VMEM((2, count, own // PIECES, features), BF16),
            pltpu.SemaphoreType.DMA((2,)),
            *[pltpu.VMEM((count, own, hidden), BF16)] * 3,
            pltpu.SemaphoreType.DMA((PIECES, 3)),
        ],
        compiler_params=linked(1),
        cost_estimate=lasting(180),
        name="branch_and_feed",
    )(
        split(mixed, count), weight, rows, live, gain, gate_weight, up_weight, down_weight, grad
    )


def feed_back_kernel(
    count, dgate_ref, dup_ref, gate_weight_ref, up_weight_ref, top_ref, middle_ref, live_ref,
    gain_ref, out_weight_ref, dmiddle_out, dgain_out, full_out, dmixed_out, *scratch
):
    group = Group(count)
    scatter = scatter_of(group, PAIR_SHARE, scratch[:SCATTER_COUNT])
    gather = gather_of(group, PAIR_SHARE, scratch[SCATTER_COUNT:-1])
    parts, full, out_sems = scratch[0], scratch[SCATTER_COUNT], scratch[-1]
    meet(count)
    dgain_out[...] = jnp.zeros(dgain_out.shape, F32)

    def prepare(piece):
        rows = gather.rows(piece)

        def store(cols, value):
            parts[:, rows, cols] = split(value.astype(BF16), count)

        wide_dot(
            [
                (joined(dgate_ref[:, rows]), gate_weight_ref),
                (joined(dup_ref[:, rows]), up_weight_ref),
            ],
            NT,
            256,
            store,
        )

    def middle(piece, dnormed):
        rows = gather.rows(piece)
        values = middle_ref[rows]
        scale = inverse_rms(values)
        normed = values * scale
        dgain_out[...] += jnp.sum(dnormed * normed, axis=0, keepdims=True)
        scaled = dnormed * gain_ref[...]
        dmiddle = top_ref[rows].astype(F32) + scale * (
            scaled - normed * jnp.mean(scaled * normed, axis=-1, keepdims=True)
        )
        dmiddle_out[rows] = dmiddle
        return live_ref[rows] * dmiddle

    def ready(piece):
        rows = gather.rows(piece)

        def store(cols, value):
            dmixed_out[:, rows, cols] = split(value, count)

        wide_dot([(joined(full[:, rows]), out_weight_ref)], NT, 256, store)

    sum_and_gather(scatter, gather, full, full_out, out_sems, prepare, middle, ready)


def feed_back(dgate, dup, gate_weight, up_weight, top, middle, live, gain, out_weight, count):
    own, features = middle.shape
    nz, nx = grid_sizes(count)
    width = out_weight.shape[0]
    return pl.pallas_call(
        functools.partial(feed_back_kernel, count),
        out_shape=[
            jax.ShapeDtypeStruct((own, features), F32),
            jax.ShapeDtypeStruct((1, features), F32),
            jax.ShapeDtypeStruct((count, own, features), BF16),
            jax.ShapeDtypeStruct((count, own, width), F32),
        ],
        in_specs=[VMEM_SPEC] * 9,
        out_specs=[VMEM_SPEC, VMEM_SPEC, ANY_SPEC, VMEM_SPEC],
        scratch_shapes=[
            *scatter_scratch(nz, nx, own, features, PAIR_SHARE),
            *gather_scratch(nz, nx, own, features),
            pltpu.SemaphoreType.DMA((PIECES,)),
        ],
        compiler_params=linked(2),
        cost_estimate=lasting(180),
        name="feed_back",
    )(
        dgate, dup, gate_weight, up_weight, top, middle, live, gain,
        out_weight,
    )


class Replicas(Sender):
    def __init__(self, values, from_core, from_y, over_back, over_home, sems):
        self.values, self.from_core, self.from_y = values, from_core, from_y
        self.over_back, self.over_home = over_back, over_home
        self.core_sems, self.y_sems, self.back_sems, self.home_sems = sems
        me = lax.axis_index("dp")
        self.lines = lax.axis_size("dp") // 2
        self.y, self.core = me // 2, me % 2

    @staticmethod
    def scratch(rows, cols, replicas):
        lines, share = replicas // 2, rows // replicas
        return [
            pltpu.VMEM((replicas, share, cols), BF16),
            pltpu.VMEM((lines, share, cols), BF16),
            pltpu.VMEM((max(lines - 1, 1), share, cols), BF16),
            pltpu.VMEM((max(lines - 1, 1), share, cols), BF16),
            pltpu.VMEM((lines, share, cols), BF16),
            *[pltpu.SemaphoreType.DMA((2, lines))] * 4,
        ]

    def share(self, core, y):
        return core * self.lines + y

    def peer(self, y, core):
        return {"dp": y * 2 + core}

    def line(self, k):
        return (self.y + k) % self.lines

    def drain(self):
        self.draining = True
        for k in range(self.lines):
            self.start(k)
            self.cores(k)
        self.over_y()
        self.back()
        self.draining = False

    def add(self, share, others):
        step = 64

        def some(block, _):
            rows = pl.ds(pl.multiple_of(block * step, step), step)
            total = self.values[share, rows].astype(F32)
            for ref, index in others:
                total = total + ref[index, rows].astype(F32)
            self.values[share, rows] = total.astype(BF16)
            return 0

        lax.fori_loop(0, self.values.shape[1] // step, some, 0)

    def start(self, k):
        y = self.line(k)
        self.push(
            self.values.at[self.share(1 - self.core, y)],
            self.from_core.at[y],
            self.core_sems.at[0, k],
            self.core_sems.at[1, k],
            self.peer(self.y, 1 - self.core),
        )

    def cores(self, k):
        y = self.line(k)
        share = self.share(self.core, y)
        if not self.draining:
            arrived(self.from_core.at[y], self.core_sems.at[1, k])
            self.add(share, [(self.from_core, y)])
        if k > 0:
            self.push(
                self.values.at[share],
                self.from_y.at[self.lines - k - 1],
                self.y_sems.at[0, k],
                self.y_sems.at[1, self.lines - k],
                self.peer(y, self.core),
            )

    def over_y(self):
        share = self.share(self.core, self.y)
        if not self.draining:
            for k in range(1, self.lines):
                arrived(self.from_y.at[k - 1], self.y_sems.at[1, k])
            self.add(share, [(self.from_y, k) for k in range(self.lines - 1)])
        for k in range(1, self.lines):
            self.push(
                self.values.at[share],
                self.over_back.at[self.lines - k - 1],
                self.back_sems.at[0, k],
                self.back_sems.at[1, self.lines - k],
                self.peer(self.line(k), self.core),
            )
        self.send_home(0)

    def own(self, k):
        return self.values.at[self.share(self.core, self.y)] if k == 0 else self.over_back.at[k - 1]

    def send_home(self, k):
        self.push(
            self.own(k),
            self.over_home.at[k],
            self.home_sems.at[0, k],
            self.home_sems.at[1, k],
            self.peer(self.y, 1 - self.core),
        )

    def back(self):
        for k in range(1, self.lines):
            if not self.draining:
                arrived(self.over_back.at[k - 1], self.back_sems.at[1, k])
            self.send_home(k)

    def home(self):
        for k in range(self.lines):
            arrived(self.over_home.at[k], self.home_sems.at[1, k])

    def totals(self):
        for k in range(self.lines):
            yield self.own(k), self.share(self.core, self.line(k))
            yield self.over_home.at[k], self.share(1 - self.core, self.line(k))


def sum_small(small, seen, send_sems, recv_sems, axis, rows):
    me, size = lax.axis_index(axis), lax.axis_size(axis)
    copies = []
    seen[me] = small[...]
    for k in range(1, size):
        copy = pltpu.make_async_remote_copy(
            seen.at[me], seen.at[me], send_sems.at[k], recv_sems.at[size - k],
            device_id={axis: (me + k) % size}, device_id_type=MESH,
        )
        copy.start()
        copies.append(copy)
    for k in range(1, size):
        arrived(seen.at[(me + k) % size], recv_sems.at[k])
    total = seen[0]
    for other in range(1, size):
        total = total + seen[other]
    small[...] = jnp.where(grid_index(total.shape, 0) < rows, total, small[...])
    return copies


def input_back_kernel(
    count, grad_ref, weight_ref, normed_ref, later_ref, input_ref, gain_ref, small_ref,
    wout_ref, grad_out, small_out, dmain_out, drest_out, *scratch
):
    parts, rest = scratch[0], scratch[SCATTER_COUNT:]
    values = rest[0]
    near, near_send, near_recv, far, far_send, far_recv, staged, out_sems = rest[9:]
    scatter = scatter_of(Group(count), SCATTER_SHARE, scratch[:SCATTER_COUNT])
    replicas = Replicas(*rest[:5], rest[5:9])
    meet(count, lax.axis_size("dp"))
    small_out[...] = small_ref[...]
    width = grad_ref.shape[2]
    values[:, :, width:] = split(wout_ref[...], values.shape[0])

    def begin(piece):
        rows = scatter.rows(piece)

        def store(cols, value):
            parts[:, rows, cols] = split(value.astype(BF16), count)

        wide_dot([(joined(grad_ref[:, rows]), weight_ref)], NT, 256, store)
        scatter.phase(piece, 0)

    def end(piece):
        dnormed = scatter.phase(piece, scatter.last)
        rows = scatter.rows(piece)
        given = input_ref[rows].astype(F32)
        scale = inverse_rms(given)
        normed = given * scale
        small_out[0:1] += jnp.sum(dnormed * normed, axis=0, keepdims=True)
        scaled = dnormed * gain_ref[...]
        grad_out[rows] = later_ref[rows] + scale * (
            scaled - normed * jnp.mean(scaled * normed, axis=-1, keepdims=True)
        )

    def weight_share(core, y):
        share = replicas.share(core, y)
        left = joined(normed_ref[share])
        grads = joined(grad_ref[...])
        for first in range(0, width, 384):
            cols = slice(first, min(first + 384, width))
            staged[:, cols] = lax.dot_general(
                left, grads[:, cols], (TN, ((), ())), preferred_element_type=F32
            ).astype(BF16)

        def some(block, _):
            rows = pl.ds(pl.multiple_of(block * 64, 64), 64)
            values[share, rows, :width] = staged[rows]
            return 0

        lax.fori_loop(0, staged.shape[0] // 64, some, 0)

    def other_core(k):
        weight_share(1 - replicas.core, replicas.line(k))
        replicas.start(k)

    def this_core(k):
        weight_share(replicas.core, replicas.line(k))
        replicas.cores(k)

    steps = []
    for k in range(replicas.lines - 1, -1, -1):
        steps += [functools.partial(other_core, k), functools.partial(this_core, k)]
    while len(steps) < PIECES - 1:
        steps.append(lambda: None)
    steps.append(replicas.over_y)

    def tick(time, _):
        during(time + 1, begin)
        for step in range(1, scatter.last):
            during(time - step + 1, functools.partial(scatter.phase, step=step))
        during(time - scatter.last + 1, end)
        for index, step in enumerate(steps):
            pl.when(time == index)(step)
        return 0

    lax.fori_loop(-1, max(PIECES + scatter.last - 1, len(steps)), tick, 0)
    replicas.back()
    copies = sum_small(small_out, near, near_send, near_recv, "heads", 3)
    copies += sum_small(small_out, far, far_send, far_recv, "dp", 8)
    replicas.home()
    part = dmain_out.shape[3]
    outs = []
    for index, (total, share) in enumerate(replicas.totals()):
        for kind in range(4):
            outs.append((total.at[:, pl.ds(kind * part, part)], dmain_out.at[kind, share], index))
        rest_cols = pl.ds(4 * part, drest_out.shape[2])
        outs.append((total.at[:, rest_cols], drest_out.at[share], index))
    outs = [
        pltpu.make_async_copy(source, target, out_sems.at[index, place % 5])
        for place, (source, target, index) in enumerate(outs)
    ]
    for copy in outs:
        copy.start()
    scatter.drain()
    replicas.drain()
    for copy in copies:
        copy.wait_send()
    for copy in outs:
        copy.wait()


def input_back(
    grad, weight, normed, later, rows, gain, small, grad_wout, count, replica_count
):
    own, features = rows.shape
    nz, nx = grid_sizes(count)
    width, share = grad_wout.shape[1], features // replica_count
    cols = weight.shape[1] + width
    dma = pltpu.SemaphoreType.DMA
    return pl.pallas_call(
        functools.partial(input_back_kernel, count),
        out_shape=[
            jax.ShapeDtypeStruct((own, features), F32),
            jax.ShapeDtypeStruct(small.shape, F32),
            jax.ShapeDtypeStruct((4, replica_count, share, width), BF16),
            jax.ShapeDtypeStruct((replica_count, share, cols - 4 * width), BF16),
        ],
        in_specs=[VMEM_SPEC] * 8,
        out_specs=[VMEM_SPEC, VMEM_SPEC, ANY_SPEC, ANY_SPEC],
        scratch_shapes=[
            *scatter_scratch(nz, nx, own, features, SCATTER_SHARE),
            *Replicas.scratch(features, cols, replica_count),
            pltpu.VMEM((count, *small.shape), F32),
            dma((count,)),
            dma((count,)),
            pltpu.VMEM((replica_count, *small.shape), F32),
            dma((replica_count,)),
            dma((replica_count,)),
            pltpu.VMEM((features // replica_count, weight.shape[1]), BF16),
            dma((replica_count, 5)),
        ],
        compiler_params=linked(3),
        cost_estimate=lasting(120),
        name="input_back",
    )(split(grad, count), weight, normed, later, rows, gain, small, grad_wout)


def matmul(left, right, dims):
    return lax.dot_general(left, right, (dims, ((), ())), preferred_element_type=F32)


def scatter_rows(values):
    return lax.psum_scatter(values, "heads", scatter_dimension=0, tiled=True).astype(F32)


def on_device(
    block_in,
    seq_counts,
    norm1_gain,
    w_qkvg,
    conv_weight,
    w_gates,
    gate_params,
    out_gain,
    w_out,
    norm2_gain,
    w_gate_up,
    w_down,
    cotangent,
):
    own_rows, features = block_in.shape
    count = lax.axis_size("heads")
    all_rows = own_rows * count
    width = conv_weight.shape[2]
    heads = gate_params.shape[1]
    longer = seq_counts[0, 1:2]
    first_row = lax.axis_index("heads") * own_rows
    row_index = first_row + jnp.arange(own_rows, dtype=jnp.int32)
    live_own = jnp.where(longer[0] > 0, True, row_index < seq_counts[0, 0] * SEQ_SHORT)
    live_own = live_own.astype(F32)[:, None]
    weight = jnp.concatenate(
        [
            w_qkvg.reshape(features, 4 * width),
            w_gates.reshape(features, 2 * heads),
            jnp.zeros((features, 128 - 2 * heads), BF16),
        ],
        axis=1,
    )
    full_normed1, projected = project(
        block_in, norm1_gain[None], weight, count, lax.axis_size("dp")
    )
    projected = projected.reshape(all_rows, -1)
    taps = jnp.transpose(conv_weight, (1, 0, 2)).reshape(4, 3 * width)
    params = jnp.pad(gate_params, ((0, 0), (0, 128 - heads)))
    gain_row = out_gain[None]
    mixed, *saved, grad_feed = mixer_forward(
        longer, projected, taps, params, gain_row, cotangent, live_own, count
    )
    gate_weight, up_weight = w_gate_up[:, 0], w_gate_up[:, 1]
    middle, full_normed2, grad_gate, grad_up, hidden = branch_and_feed(
        mixed,
        w_out,
        block_in,
        live_own,
        norm2_gain[None],
        gate_weight,
        up_weight,
        w_down,
        grad_feed,
        count,
    )
    early = (
        matmul(joined(full_normed2), joined(grad_gate), TN).astype(BF16),
        matmul(joined(full_normed2), joined(grad_up), TN).astype(BF16),
        matmul(joined(hidden), joined(grad_feed), TN).astype(BF16),
    )
    grad_gate, grad_up, early, hidden = lax.optimization_barrier(
        (grad_gate, grad_up, early, hidden)
    )
    grad_middle, grad_gain2, grad_mix, grad_mixed = feed_back(
        grad_gate,
        grad_up,
        gate_weight,
        up_weight,
        cotangent,
        middle,
        live_own,
        norm2_gain[None],
        w_out,
        count,
    )
    early = lax.psum(early, "dp")
    hidden, grad_mixed, early = lax.optimization_barrier((hidden, grad_mixed, early))
    feed = matmul(joined(hidden), w_down, NN).astype(BF16)
    feed, grad_mixed = lax.optimization_barrier((feed, grad_mixed))
    feed = scatter_rows(feed)
    grad_mix = grad_mix.reshape(all_rows, features)
    grad_wout = matmul(grad_mix, mixed, TN).astype(BF16)
    dprojected, dtaps, dparams, dgain = mixer_backward(
        longer, grad_mixed.reshape(all_rows, width), projected, saved, taps, params, gain_row
    )
    layer_out = (middle + live_own * feed).astype(BF16)

    def row(values):
        return jnp.pad(values, ((0, 0), (0, features - values.shape[1])))

    small = jnp.concatenate(
        [
            jnp.zeros((1, features), F32),
            grad_gain2,
            row(dgain),
            row(dtaps),
            row(dparams.reshape(1, 256)),
        ],
        axis=0,
    )
    grad_in, small, grad_main, grad_rest = input_back(
        dprojected,
        weight,
        full_normed1,
        grad_middle,
        block_in,
        norm1_gain[None],
        small,
        grad_wout,
        count,
        lax.axis_size("dp"),
    )
    grad_main = grad_main.reshape(4, features, width)
    grad_rest = grad_rest.reshape(features, -1)
    return (
        layer_out,
        grad_in,
        small[0],
        jnp.transpose(grad_main, (1, 0, 2)).astype(F32),
        jnp.transpose(small[3:7, : 3 * width].reshape(4, 3, width), (1, 0, 2)),
        grad_rest[:, : 2 * heads].reshape(w_gates.shape).astype(F32),
        small[7, :256].reshape(2, 128)[:, :heads],
        small[2, : out_gain.shape[0]],
        grad_rest[:, 128:].T.astype(F32),
        small[1],
        jnp.stack([early[0], early[1]], axis=1).astype(F32),
        early[2].astype(F32),
    )


def solution(mesh):
    return jax.shard_map(
        on_device,
        mesh=mesh,
        in_specs=(
            P(("dp", "heads"), None),
            P("dp", None),
            P(),
            P(None, None, "heads"),
            P(None, None, "heads"),
            P(None, None, "heads"),
            P(None, "heads"),
            P(),
            P("heads", None),
            P(),
            P(None, None, "heads"),
            P("heads", None),
            P(("dp", "heads"), None),
        ),
        out_specs=(
            P(("dp", "heads"), None),
            P(("dp", "heads"), None),
            P(),
            P(None, None, "heads"),
            P(None, None, "heads"),
            P(None, None, "heads"),
            P(None, "heads"),
            P(),
            P("heads", None),
            P(),
            P(None, None, "heads"),
            P("heads", None),
        ),
        check_vma=False,
    )
```

```python
import functools
import jax
import jax.numpy as jnp
from jax import lax
from jax.experimental import pallas as pl
from jax.experimental.pallas import tpu as pltpu
from jax.sharding import PartitionSpec as P

SEQ_SHORT = 512
CHUNK = 256
HEAD = 128
EPS = 1e-06
F32 = jnp.float32
BF16 = jnp.bfloat16
LOW, MID, TOP = lax.Precision.DEFAULT, lax.Precision.HIGH, lax.Precision.HIGHEST
NN, NT, TN = ((1,), (0,)), ((1,), (1,)), ((0,), (0,))
P_FWD, P_BWD = MID, MID


def dot(left, right, dims, precision):
    if precision is LOW:
        left, right = left.astype(BF16), right.astype(BF16)
        return lax.dot_general(left, right, (dims, ((), ())), preferred_element_type=F32)
    return lax.dot_general(
        left, right, (dims, ((), ())), precision=precision, preferred_element_type=F32
    )


def grid_index(shape, axis):
    return lax.broadcasted_iota(jnp.int32, shape, axis)


def positions(longer, first_row, count):
    rows = grid_index((count, 1), 0) + first_row
    return jnp.where(longer > 0, rows, rows % SEQ_SHORT)


def keeps(longer, first_row):
    start = jnp.where(longer > 0, first_row, first_row % SEQ_SHORT)
    return jnp.where(start > 0, 1.0, 0.0).astype(F32)


def softplus(x):
    return jnp.maximum(x, 0.0) + jnp.log1p(jnp.exp(-jnp.abs(x)))


def gate_values(gates, params, heads):
    lane = grid_index(gates.shape, 1)
    rate = jnp.exp(params[0:1])
    shifted = gates + params[1:2]
    log_decay = jnp.where(lane < heads, -rate * softplus(shifted), 0.0)
    return rate, shifted, log_decay


def lane_column(values, index):
    return values[:, index : index + 1]


def decays(cumulative, cumulative_rows, head, masks):
    column = lane_column(cumulative, head)
    row = cumulative_rows[head : head + 1, :]
    inclusive = masks[0]
    ratio = jnp.where(inclusive, jnp.exp(jnp.where(inclusive, column - row, 0.0)), 0.0)
    last = column[CHUNK - 1 : CHUNK, :]
    return ratio, jnp.exp(column), jnp.exp(last - column), jnp.exp(last)


def unit(values):
    scale = lax.rsqrt(jnp.sum(values * values, axis=-1, keepdims=True) + EPS)
    return values * scale, scale


def pair_of(values):
    high = values.astype(BF16)
    return high, (values - high.astype(F32)).astype(BF16)


def pair_dot(left, right):
    def product(a, b):
        return lax.dot_general(a, b, (NN, ((), ())), preferred_element_type=F32)

    return product(left[0], right[0]) + (product(left[0], right[1]) + product(left[1], right[0]))


def inverses(links, row, col):
    apart = row ^ col
    size = links[0].shape[0]
    outs = [jnp.where(row == col, 1.0, 0.0) - jnp.where(apart == 1, link, 0.0) for link in links]
    pairs = [pair_of(link) for link in links]
    step = 2
    while step < size // 2:
        level = (apart >= step) & (apart < 2 * step)
        parts = [tuple(jnp.where(level, half, 0) for half in pair) for pair in pairs]
        out_pairs = [pair_of(out) for out in outs]
        inner = [pair_of(pair_dot(part, out)) for part, out in zip(parts, out_pairs)]
        outs = [out - pair_dot(pair, mid) for out, pair, mid in zip(outs, out_pairs, inner)]
        step *= 2
    half = size // 2
    uppers = [pair_of(out[:half, :half]) for out in outs]
    lowers = [pair_of(out[half:, half:]) for out in outs]
    corners = [tuple(each[half:, :half] for each in pair) for pair in pairs]
    inner = [pair_of(pair_dot(corner, upper)) for corner, upper in zip(corners, uppers)]
    corners = [pair_dot(lower, mid) for lower, mid in zip(lowers, inner)]
    return [
        jnp.concatenate(
            [out[:half], jnp.concatenate([-corner, out[half:, half:]], axis=1)], axis=0
        )
        for out, corner in zip(outs, corners)
    ]


def forward_kernel(
    heads, count, chunks, longer_ref, main_ref, conv_ref, params_ref, gain_ref, top_ref, live_ref,
    mixed_ref, conv_out_ref, raw_ref, delta_ref, solve_ref, state_ref, full_out,
    state, tail_rows, *scratch
):
    step = pl.program_id(0)
    first_row = step * CHUNK
    run, close = gather_along(step, chunks, count, top_ref, live_ref, full_out, scratch)
    run(2 * step)
    longer = longer_ref[0]
    width = heads * HEAD

    @pl.when(step == 0)
    def _():
        state[...] = jnp.zeros_like(state)
        tail_rows[...] = jnp.zeros_like(tail_rows)

    position = positions(longer, first_row, CHUNK)
    keep = keeps(longer, first_row)
    triple = main_ref[:, : 3 * width]
    padded = jnp.concatenate([tail_rows[...], triple], axis=0)
    taps = conv_ref[...]
    convolved = triple * taps[0:1]
    for lag in range(1, 4):
        shifted = padded[8 - lag : 8 - lag + CHUNK]
        convolved = convolved + jnp.where(position >= lag, shifted, 0.0) * taps[lag : lag + 1]
    tail_rows[...] = triple[CHUNK - 8 :]
    conv_out_ref[...] = convolved
    active = convolved * jax.nn.sigmoid(convolved)
    gates = main_ref[:, 4 * width :]
    rate, shifted_gate, log_decay = gate_values(gates, params_ref[...], heads)
    beta_all = jax.nn.sigmoid(gates)
    row = grid_index((CHUNK, CHUNK), 0)
    col = grid_index((CHUNK, CHUNK), 1)
    masks = (row >= col, row > col)
    cumulative = dot(jnp.where(masks[0], 1.0, 0.0), log_decay, NN, TOP)
    cumulative_rows = jnp.transpose(cumulative)
    each = range(heads)
    columns = [slice(head * HEAD, (head + 1) * HEAD) for head in each]
    queries = [unit(active[:, cols])[0] * HEAD**-0.5 for cols in columns]
    keys = [unit(active[:, width + head * HEAD : width + (head + 1) * HEAD])[0] for head in each]
    values = [active[:, 2 * width + head * HEAD : 2 * width + (head + 1) * HEAD] for head in each]
    betas = [lane_column(beta_all, heads + head) for head in each]
    spans = [decays(cumulative, cumulative_rows, head, masks) for head in each]
    grams = [
        dot(jnp.concatenate([key, query], axis=0), key, NT, P_FWD)
        for key, query in zip(keys, queries)
    ]
    links = [
        jnp.where(masks[1], beta * span[0] * gram[:CHUNK], 0.0)
        for beta, span, gram in zip(betas, spans, grams)
    ]
    solves = inverses(links, row, col)
    run(2 * step + 1)
    boths = [
        dot(
            solve,
            jnp.concatenate([beta * value, (beta * span[1]) * key], axis=1),
            NN,
            P_FWD,
        )
        for solve, beta, value, key, span in zip(solves, betas, values, keys, spans)
    ]
    entries = [state[head] * keep for head in each]
    carried = [
        dot(jnp.concatenate([both[:, HEAD:], span[1] * query], axis=0), entry, NT, P_FWD)
        for both, span, query, entry in zip(boths, spans, queries, entries)
    ]
    deltas = [both[:, :HEAD] - carry[:CHUNK] for both, carry in zip(boths, carried)]
    states = [
        span[3] * entry + dot(delta * span[2], key, TN, P_FWD)
        for span, entry, delta, key in zip(spans, entries, deltas, keys)
    ]
    raws = [
        carry[CHUNK:] + dot(gram[CHUNK:] * span[0], delta, NN, P_FWD)
        for carry, gram, span, delta in zip(carried, grams, spans, deltas)
    ]
    for head, cols in zip(each, columns):
        solve_ref[head] = solves[head]
        state_ref[0, head] = entries[head]
        state[head] = states[head]
        delta_ref[:, cols] = deltas[head]
        raw = raws[head]
        raw_ref[:, cols] = raw
        scale = lax.rsqrt(jnp.mean(raw * raw, axis=-1, keepdims=True) + EPS)
        gate = main_ref[:, 3 * width + head * HEAD : 3 * width + (head + 1) * HEAD]
        mixed = raw * scale * gain_ref[...] * (gate * jax.nn.sigmoid(gate))
        mixed_ref[:, cols] = mixed.astype(mixed_ref.dtype)
    pl.when(step == chunks - 1)(close)


def spread_ticks(tick, first, ticks, halves):
    def run(half):
        def one(index, _):
            tick(first + index)
            return 0

        lax.fori_loop(half * ticks // halves, (half + 1) * ticks // halves, one, 0)

    return run


def gather_along(step, chunks, count, top_ref, live_ref, full_out, scratch):
    *scratch, out_sems = scratch
    full = scratch[0]
    gather = gather_of(Group(count), GATHER_SHARE, scratch)

    def out(piece):
        rows = gather.rows(piece)
        return pltpu.make_async_copy(full.at[:, rows], full_out.at[:, rows], out_sems.at[piece])

    def begin(piece):
        rows = gather.rows(piece)
        full[lax.axis_index("heads"), rows] = (
            live_ref[rows] * top_ref[rows].astype(F32)
        ).astype(BF16)
        gather.phase(piece, 0)

    def end(piece):
        gather.phase(piece, gather.last)
        out(piece).start()

    def tick(time):
        during(time, begin)
        for phase in range(1, gather.last):
            during(time - phase, functools.partial(gather.phase, step=phase))
        during(time - gather.last, end)

    def close():
        gather.drain()

        def finish(piece, _):
            out(piece).wait()
            return 0

        lax.fori_loop(0, PIECES, finish, 0)

    pl.when(step == 0)(functools.partial(meet, count))
    return spread_ticks(tick, 0, PIECES + gather.last, 2 * chunks), close


def scatter_along(step, chunks, count, hidden_ref, weight_ref, middle_ref, live_ref, out, scratch):
    parts = scratch[0]
    scatter = scatter_of(Group(count), SCATTER_SHARE, scratch)

    def begin(piece):
        rows = scatter.rows(piece)

        def store(cols, value):
            parts[:, rows, cols] = split(value.astype(BF16), count)

        wide_dot([(joined(hidden_ref[:, rows]), weight_ref)], NN, 512, store)
        scatter.phase(piece, 0)

    def end(piece):
        total = scatter.phase(piece, scatter.last)
        rows = scatter.rows(piece)
        out[rows] = (middle_ref[rows] + live_ref[rows] * total).astype(BF16)

    def tick(time):
        during(time + 1, begin)
        for phase in range(1, scatter.last):
            during(time - phase + 1, functools.partial(scatter.phase, step=phase))
        during(time - scatter.last + 1, end)

    pl.when(step == 0)(functools.partial(meet, count))
    return spread_ticks(tick, -1, PIECES + scatter.last, 2 * chunks), scatter.drain


def backward_kernel(
    heads, chunks, count, longer_ref, grad_ref, main_ref, conv_out_ref, raw_ref, delta_ref,
    solve_ref, state_ref, conv_ref, params_ref, gain_ref, hidden_ref, down_ref, middle_ref, live_ref,
    dmain_ref, dconv_ref, dparams_ref, dgain_ref, layer_ref, dstate, head_rows, *scratch
):
    step = pl.program_id(0)
    first_row = (chunks - 1 - step) * CHUNK
    run, close = scatter_along(
        step, chunks, count, hidden_ref, down_ref, middle_ref, live_ref, layer_ref, scratch
    )
    run(2 * step)
    longer = longer_ref[0]
    width = heads * HEAD

    @pl.when(step == 0)
    def _():
        dstate[...] = jnp.zeros_like(dstate)
        head_rows[...] = jnp.zeros_like(head_rows)
        dconv_ref[...] = jnp.zeros_like(dconv_ref)
        dparams_ref[...] = jnp.zeros_like(dparams_ref)
        dgain_ref[...] = jnp.zeros_like(dgain_ref)

    keep = keeps(longer, first_row)
    convolved = conv_out_ref[...]
    sigmoid_conv = jax.nn.sigmoid(convolved)
    active = convolved * sigmoid_conv
    slope = sigmoid_conv * (1.0 + convolved * (1.0 - sigmoid_conv))
    gates = main_ref[:, 4 * width :]
    params = params_ref[...]
    rate, shifted_gate, log_decay = gate_values(gates, params, heads)
    beta_all = jax.nn.sigmoid(gates)
    row = grid_index((CHUNK, CHUNK), 0)
    col = grid_index((CHUNK, CHUNK), 1)
    masks = (row >= col, row > col)
    cumulative = dot(jnp.where(masks[0], 1.0, 0.0), log_decay, NN, TOP)
    cumulative_rows = jnp.transpose(cumulative)
    lane = grid_index((CHUNK, 128), 1)
    last_row = grid_index((CHUNK, 1), 0) == CHUNK - 1
    gain = gain_ref[...]
    dgains, dlogs, dbetas, dparts = ([None] * heads for _ in range(4))

    def work(head):
        cols = slice(head * HEAD, (head + 1) * HEAD)
        gate = main_ref[:, 3 * width + head * HEAD : 3 * width + (head + 1) * HEAD]
        raw = raw_ref[:, cols]
        grad = grad_ref[:, cols]
        scale = lax.rsqrt(jnp.mean(raw * raw, axis=-1, keepdims=True) + EPS)
        normed = raw * scale
        sigmoid_gate = jax.nn.sigmoid(gate)
        gated = gate * sigmoid_gate
        product = grad * normed
        dgains[head] = jnp.sum(product * gated, axis=0, keepdims=True)
        dgate = product * gain * (sigmoid_gate * (1.0 + gate * (1.0 - sigmoid_gate)))
        dmain_ref[:, 3 * width + head * HEAD : 3 * width + (head + 1) * HEAD] = dgate.astype(
            dmain_ref.dtype
        )
        dnormed = grad * gain * gated
        draw = scale * (dnormed - normed * jnp.mean(dnormed * normed, axis=-1, keepdims=True))
        query_unit, query_scale = unit(active[:, head * HEAD : (head + 1) * HEAD])
        query = query_unit * HEAD**-0.5
        key, key_scale = unit(active[:, width + head * HEAD : width + (head + 1) * HEAD])
        value = active[:, 2 * width + head * HEAD : 2 * width + (head + 1) * HEAD]
        beta = lane_column(beta_all, heads + head)
        ratio, decay_in, decay_out, decay_all = decays(cumulative, cumulative_rows, head, masks)
        entry = state_ref[0, head]
        delta = delta_ref[:, cols]
        dlater = dstate[head]
        gram = dot(query, key, NT, P_BWD) * ratio
        yield
        key_dlater = dot(key, dlater, NT, P_BWD)
        yield
        ddelta = dot(gram, draw, TN, P_BWD) + decay_out * key_dlater
        yield
        dright = dot(solve_ref[head], ddelta, TN, P_BWD)
        yield
        pairs = dot(jnp.concatenate([dright, draw], axis=0), delta, NT, P_BWD)
        yield
        dlink = jnp.where(masks[1], -pairs[:CHUNK] * ratio, 0.0)
        dgram = pairs[CHUNK:] * ratio
        on_entry = dot(jnp.concatenate([dright, draw], axis=0), entry, NN, P_BWD)
        yield
        key_entry = dot(key, entry, NT, P_BWD)
        yield
        on_key = dot(jnp.concatenate([dlink, dgram], axis=0), key, NN, P_BWD)
        yield
        dquery = decay_in * on_entry[CHUNK:] + on_key[CHUNK:]
        link_key = on_key[:CHUNK]
        key_read = beta * (link_key - decay_in * on_entry[:CHUNK])
        key_tail = decay_out * dot(delta, dlater, NN, P_BWD)
        yield
        key_write = (
            dot(beta * dlink, key, TN, P_BWD) + dot(dgram, query, TN, P_BWD) + key_tail
        )
        yield
        dkey = key_read + key_write
        dvalue = beta * dright
        dbeta = jnp.sum(
            dright * (value - decay_in * key_entry) + key * link_key, axis=-1, keepdims=True
        )
        dlog = jnp.sum(query * dquery + key * (key_read - key_write), axis=-1, keepdims=True)
        ending = decay_all * jnp.sum(
            jnp.sum(entry * dlater, axis=-1, keepdims=True), axis=0, keepdims=True
        ) + jnp.sum(jnp.sum(key * key_tail, axis=-1, keepdims=True), axis=0, keepdims=True)
        dlog = dlog + jnp.where(last_row, ending, 0.0)
        dlogs[head], dbetas[head] = dlog, dbeta
        dstate[head] = keep * (
            decay_all * dlater
            + dot(decay_in * draw, query, TN, P_BWD)
            - dot((beta * decay_in) * dright, key, TN, P_BWD)
        )
        yield
        dquery = (HEAD**-0.5 * query_scale) * (
            dquery - query_unit * jnp.sum(dquery * query_unit, axis=-1, keepdims=True)
        )
        dkey = key_scale * (dkey - key * jnp.sum(dkey * key, axis=-1, keepdims=True))
        dparts[head] = (dquery, dkey, dvalue)

    works = [work(head) for head in range(heads)]
    turns = 0
    while works:
        works = [each for each in works if next(each, "end") != "end"]
        turns += 1
        if turns == 6:
            run(2 * step + 1)
    dcumulative = jnp.zeros((CHUNK, 128), F32)
    dbeta_all = jnp.zeros((CHUNK, 128), F32)
    for head in range(heads):
        dcumulative = jnp.where(lane == head, dlogs[head], dcumulative)
        dbeta_all = jnp.where(lane == heads + head, dbetas[head], dbeta_all)
    dgain = functools.reduce(jnp.add, dgains)
    dconv_parts = [[dparts[head][kind] for head in range(heads)] for kind in range(3)]
    dactive = jnp.concatenate([p for parts in dconv_parts for p in parts], axis=1)
    dconvolved = dactive * slope
    padded = jnp.concatenate([dconvolved, head_rows[...]], axis=0)
    position = positions(longer, first_row, CHUNK + 8)
    taps = conv_ref[...]
    triple = main_ref[:, : 3 * width]
    dtriple = dconvolved * taps[0:1]
    dconv_ref[0:1] += jnp.sum(dconvolved * triple, axis=0, keepdims=True)
    for lag in range(1, 4):
        moved = jnp.where(position >= lag, padded, 0.0)[lag : lag + CHUNK]
        dtriple = dtriple + moved * taps[lag : lag + 1]
        dconv_ref[lag : lag + 1] += jnp.sum(moved * triple, axis=0, keepdims=True)
    head_rows[...] = dconvolved[:8]
    dmain_ref[:, : 3 * width] = dtriple.astype(dmain_ref.dtype)
    dlog_decay = dot(jnp.where(row <= col, 1.0, 0.0), dcumulative, NN, TOP)
    dshifted = -dlog_decay * rate * jax.nn.sigmoid(shifted_gate)
    dshifted = jnp.where(lane < heads, dshifted, 0.0)
    dparams_ref[0:1] += jnp.sum(dlog_decay * log_decay, axis=0, keepdims=True)
    dparams_ref[1:2] += jnp.sum(dshifted, axis=0, keepdims=True)
    dmain_ref[:, 4 * width :] = (dshifted + dbeta_all * beta_all * (1.0 - beta_all)).astype(
        dmain_ref.dtype
    )
    dgain_ref[...] += dgain
    pl.when(step == chunks - 1)(close)


def row_block(width, chunks, backward):
    if backward:
        return pl.BlockSpec((CHUNK, width), lambda i: (chunks - 1 - i, 0))
    return pl.BlockSpec((CHUNK, width), lambda i: (i, 0))


def whole_block(shape):
    return pl.BlockSpec(shape, lambda i: (0,) * len(shape))


def mixer_forward(longer, main, conv, params, gain, top, live, count):
    rows, width = main.shape[0], conv.shape[1] // 3
    heads, chunks = width // HEAD, rows // CHUNK
    own, features = top.shape
    nz, nx = grid_sizes(count)
    rowed = functools.partial(row_block, chunks=chunks, backward=False)
    shape = jax.ShapeDtypeStruct
    return pl.pallas_call(
        functools.partial(forward_kernel, heads, count, chunks),
        grid=(chunks,),
        in_specs=[
            pl.BlockSpec(memory_space=pltpu.SMEM),
            rowed(4 * width + 128),
            whole_block((4, 3 * width)),
            whole_block((2, 128)),
            whole_block((1, HEAD)),
            whole_block((own, features)),
            whole_block((own, 1)),
        ],
        out_specs=[
            rowed(width),
            rowed(3 * width),
            rowed(width),
            rowed(width),
            pl.BlockSpec((heads, CHUNK, CHUNK), lambda i: (0, i, 0)),
            pl.BlockSpec((1, heads, HEAD, HEAD), lambda i: (i, 0, 0, 0)),
            pl.BlockSpec(memory_space=pl.ANY),
        ],
        out_shape=[
            shape((rows, width), BF16),
            shape((rows, 3 * width), F32),
            shape((rows, width), F32),
            shape((rows, width), F32),
            shape((heads, rows, CHUNK), F32),
            shape((chunks, heads, HEAD, HEAD), F32),
            shape((count, own, features), BF16),
        ],
        scratch_shapes=[
            pltpu.VMEM((heads, HEAD, HEAD), F32),
            pltpu.VMEM((8, 3 * width), F32),
            *gather_scratch(nz, nx, own, features),
            pltpu.SemaphoreType.DMA((PIECES,)),
        ],
        compiler_params=linked(4),
        cost_estimate=lasting(95),
        name="mixer_forward",
    )(longer, main, conv, params, gain, top, live)


def mixer_backward(
    longer, grad, main, saved, conv, params, gain, hidden, down_weight, middle, live, count
):
    rows, width = main.shape[0], conv.shape[1] // 3
    heads, chunks = width // HEAD, rows // CHUNK
    own, features = middle.shape
    nz, nx = grid_sizes(count)
    rowed = functools.partial(row_block, chunks=chunks, backward=True)
    shape = jax.ShapeDtypeStruct
    return pl.pallas_call(
        functools.partial(backward_kernel, heads, chunks, count),
        grid=(chunks,),
        in_specs=[
            pl.BlockSpec(memory_space=pltpu.SMEM),
            rowed(width),
            rowed(4 * width + 128),
            rowed(3 * width),
            rowed(width),
            rowed(width),
            pl.BlockSpec((heads, CHUNK, CHUNK), lambda i: (0, chunks - 1 - i, 0)),
            pl.BlockSpec((1, heads, HEAD, HEAD), lambda i: (chunks - 1 - i, 0, 0, 0)),
            whole_block((4, 3 * width)),
            whole_block((2, 128)),
            whole_block((1, HEAD)),
            whole_block(hidden.shape),
            whole_block(down_weight.shape),
            whole_block((own, features)),
            whole_block((own, 1)),
        ],
        out_specs=[
            rowed(4 * width + 128),
            whole_block((4, 3 * width)),
            whole_block((2, 128)),
            whole_block((1, HEAD)),
            whole_block((own, features)),
        ],
        out_shape=[
            shape((rows, 4 * width + 128), BF16),
            shape((4, 3 * width), F32),
            shape((2, 128), F32),
            shape((1, HEAD), F32),
            shape((own, features), BF16),
        ],
        scratch_shapes=[
            pltpu.VMEM((heads, HEAD, HEAD), F32),
            pltpu.VMEM((8, 3 * width), F32),
            *scatter_scratch(nz, nx, own, features, SCATTER_SHARE),
        ],
        compiler_params=linked(5),
        cost_estimate=lasting(100),
        name="mixer_backward",
    )(
        longer, grad, main, *saved, conv, params, gain, hidden, down_weight, middle, live
    )


MESH = pl.DeviceIdType.MESH
PIECES = 8


def grid_sizes(count):
    nz = 4 if count % 4 == 0 else 1
    return nz, count // nz


class Group:
    def __init__(self, count):
        self.deep, self.nx = grid_sizes(count)
        self.size = count
        me = lax.axis_index("heads")
        self.z, self.x = me // self.nx, me % self.nx
        self.own = me

    def slot(self, z, j):
        return z * self.nx + (self.x + j) % self.nx

    def device(self, z, j):
        return {"heads": self.slot(z, j)}


def meet(count, replicas=1):
    barrier = pltpu.get_barrier_semaphore()
    for axis, size in (("heads", count), ("dp", replicas)):
        me = lax.axis_index(axis)

        def greet(k, _, axis=axis, size=size, me=me):
            pl.semaphore_signal(
                barrier, inc=1, device_id={axis: (me + k) % size}, device_id_type=MESH
            )
            return 0

        lax.fori_loop(1, size, greet, 0)
    pl.semaphore_wait(barrier, count + replicas - 2)


def arrived(ref, sem):
    pltpu.make_async_copy(ref, ref, sem).wait()


def during(piece, work):
    pl.when((piece >= 0) & (piece < PIECES))(functools.partial(work, piece))


class Sender:
    draining = False

    def push(self, source, target, send_sem, recv_sem, device, condition=None):
        copy = pltpu.make_async_remote_copy(
            source, target, send_sem, recv_sem, device_id=device, device_id_type=MESH
        )
        act = copy.wait_send if self.draining else copy.start
        if condition is None:
            act()
        else:
            pl.when(condition)(act)

    def place(self, piece):
        rows = pl.ds(pl.multiple_of(piece * self.part, self.part), self.part)
        return rows, self.cols

    def drain(self):
        def one(piece, _):
            for step in range(self.last + 1):
                self.phase(piece, step)
            return 0

        self.draining = True
        lax.fori_loop(0, PIECES, one, 0)
        self.draining = False


class Gather(Sender):
    def __init__(self, group, full, cols, send_sems, recv_sems, x_first):
        self.group, self.full, self.cols, self.x_first = group, full, cols, x_first
        self.part = full.shape[1] // PIECES
        self.send_sems, self.recv_sems = send_sems, recv_sems
        self.last = group.deep

    @staticmethod
    def sems(size):
        return [
            pltpu.SemaphoreType.DMA((PIECES, 3, size)),
            pltpu.SemaphoreType.DMA((PIECES, size)),
        ]

    def send(self, piece, slot, way, mark, device, condition):
        place = self.full.at[slot, *self.place(piece)]
        self.push(
            place,
            place,
            self.send_sems.at[piece, way, mark],
            self.recv_sems.at[piece, slot],
            device,
            condition,
        )

    def receive(self, piece, slot):
        if not self.draining:
            arrived(self.full.at[slot, *self.place(piece)], self.recv_sems.at[piece, slot])

    def send_up(self, piece, slot, here=True):
        group = self.group
        self.send(
            piece, slot, 0, slot, group.device(group.z + 1, 0), here & (group.z + 1 < group.deep)
        )

    def send_down(self, piece, slot, here=True):
        group = self.group
        self.send(piece, slot, 1, slot, group.device(group.z - 1, 0), here & (group.z > 0))

    def send_x(self, piece, slot, here=None):
        group = self.group
        for j in range(1, group.nx):
            mark = (slot // group.nx) * group.nx + (slot + j) % group.nx
            self.send(piece, slot, 2, mark, group.device(group.z, j), here)

    def phase(self, piece, step):
        group = self.group
        if step == 0:
            self.send_up(piece, group.own)
            self.send_down(piece, group.own)
            self.send_x(piece, group.own)
            return
        if self.x_first and step == 1:
            for j in range(1, group.nx):
                slot = group.slot(group.z, j)
                self.receive(piece, slot)
                self.send_up(piece, slot)
                self.send_down(piece, slot)
        if step < group.deep:
            for j in range(group.nx if self.x_first else 1):
                below, above = group.z - step, group.z + step
                for z, here, forward in (
                    (below, below >= 0, self.send_up),
                    (above, above < group.deep, self.send_down),
                ):
                    slot = group.slot(z, j)
                    pl.when(here)(functools.partial(self.receive, piece, slot))
                    forward(piece, slot, here)
                    if not self.x_first:
                        self.send_x(piece, slot, here)
        elif not self.x_first:
            for j in range(1, group.nx):
                for z in range(group.deep):
                    self.receive(piece, group.slot(z, j))


class Scatter(Sender):
    last = 3

    def __init__(self, group, parts, cols, scratch, z_first):
        self.group, self.parts, self.cols, self.z_first = group, parts, cols, z_first
        self.part = parts.shape[1] // PIECES
        self.over_x, self.line, *sems = scratch
        self.x_send, self.x_recv, self.z_send, self.z_recv = sems

    @staticmethod
    def scratch(deep, nx, rows, cols, z_first):
        dma = pltpu.SemaphoreType.DMA
        return [
            pltpu.VMEM((1 if z_first else deep, max(nx - 1, 1), rows, cols), BF16),
            pltpu.VMEM((deep + 1, nx if z_first else 1, rows, cols), BF16),
            *[dma((PIECES, deep, nx))] * 2,
            *[dma((PIECES, 2, deep * nx))] * 2,
        ]

    def landing(self, piece):
        return self.place(piece)[0]

    def line_at(self, piece, slot, way):
        nx = self.group.nx
        z = slot // nx + (1 if way == 0 else 0)
        return self.line.at[z, slot % nx if self.z_first else 0, self.landing(piece)]

    def step_line(self, piece, slot, way, device, add):
        part = (slot, *self.place(piece))
        if add and not self.draining:
            landed = self.line_at(piece, slot, way)
            arrived(landed, self.z_recv.at[piece, way, slot])
            total = self.parts[part].astype(F32) + landed[...].astype(F32)
            self.parts[part] = total.astype(BF16)
        self.push(
            self.parts.at[part],
            self.line_at(piece, slot, way),
            self.z_send.at[piece, way, slot],
            self.z_recv.at[piece, way, slot],
            device,
        )

    def walk(self, piece, columns, ends):
        group = self.group
        deep = group.deep

        def one_way(way):
            for k in range(deep - 1, 0, -1):
                target = group.z + k if way == 0 else group.z - k
                inside = target < deep if way == 0 else target >= 0
                first = group.z == 0 if way == 0 else group.z == deep - 1
                condition = inside & (first if ends else jnp.logical_not(first))
                device = group.device(group.z + (1 if way == 0 else -1), 0)
                for j in range(columns):
                    slot = group.slot(target, j)
                    pl.when(condition)(
                        functools.partial(self.step_line, piece, slot, way, device, not ends)
                    )

        if ends or self.draining:
            one_way(0)
            one_way(1)
            return

        def both(first, second):
            one_way(first)
            one_way(second)

        low = group.z < deep // 2
        pl.when(low)(functools.partial(both, 0, 1))
        pl.when(jnp.logical_not(low))(functools.partial(both, 1, 0))

    def total_line(self, piece, slot):
        group = self.group
        total = self.parts[(slot, *self.place(piece))].astype(F32)
        for way, here in ((0, group.z > 0), (1, group.z + 1 < group.deep)):
            landed = self.line_at(piece, slot, way)
            pl.when(here)(
                functools.partial(arrived, landed, self.z_recv.at[piece, way, slot])
            )
            total = total + jnp.where(here, landed[...].astype(F32), 0.0)
        return total

    def send_x(self, piece, index, z, j):
        group = self.group
        self.push(
            self.parts.at[group.slot(z, j), *self.place(piece)],
            self.over_x.at[index, j - 1, self.landing(piece)],
            self.x_send.at[piece, index, j],
            self.x_recv.at[piece, index, j],
            group.device(group.z, j),
        )

    def add_x(self, piece, index, total):
        for j in range(1, self.group.nx):
            landed = self.over_x.at[index, j - 1, self.landing(piece)]
            arrived(landed, self.x_recv.at[piece, index, j])
            total = total + landed[...].astype(F32)
        return total

    def phase(self, piece, step):
        group = self.group
        if self.z_first:
            if step == 0:
                self.walk(piece, group.nx, True)
            elif step == 1:
                self.walk(piece, group.nx, False)
            elif step == 2:
                for j in range(1, group.nx):
                    slot = group.slot(group.z, j)
                    if not self.draining:
                        total = self.total_line(piece, slot)
                        self.parts[(slot, *self.place(piece))] = total.astype(BF16)
                    self.send_x(piece, 0, group.z, j)
            elif not self.draining:
                return self.add_x(piece, 0, self.total_line(piece, group.own))
        elif step == 0:
            for z in range(group.deep):
                for j in range(1, group.nx):
                    self.send_x(piece, z, z, j)
        elif step == 1:
            for z in range(group.deep):
                part = (group.slot(z, 0), *self.place(piece))
                if not self.draining:
                    total = self.add_x(piece, z, self.parts[part].astype(F32))
                    self.parts[part] = total.astype(BF16)
            self.walk(piece, 1, True)
        elif step == 2:
            self.walk(piece, 1, False)
        elif not self.draining:
            return self.total_line(piece, group.own)
        return None


class Both:
    def __init__(self, first, second):
        self.both = (first, second)
        self.part, self.last = first.part, first.last

    def rows(self, piece):
        return pl.ds(pl.multiple_of(piece * self.part, self.part), self.part)

    def phase(self, piece, step):
        out = [each.phase(piece, step) for each in self.both]
        return None if out[0] is None else jnp.concatenate(out, axis=1)

    def drain(self):
        for each in self.both:
            each.drain()


def cut(cols, share):
    edge = cols - cols * share // 8
    return pl.ds(0, edge), pl.ds(edge, cols - edge)


def gather_of(group, share, scratch):
    full, *sems = scratch
    first, second = cut(full.shape[2], share)
    return Both(
        Gather(group, full, first, *sems[:2], False), Gather(group, full, second, *sems[2:], True)
    )


def scatter_of(group, share, scratch):
    parts, *rest = scratch
    first, second = cut(parts.shape[2], share)
    return Both(
        Scatter(group, parts, first, rest[:6], False),
        Scatter(group, parts, second, rest[6:], True),
    )


def gather_scratch(nz, nx, rows, cols):
    return [pltpu.VMEM((nz * nx, rows, cols), BF16), *Gather.sems(nz * nx), *Gather.sems(nz * nx)]


def scatter_scratch(nz, nx, rows, cols, share):
    first, second = cut(cols, share)
    return [
        pltpu.VMEM((nz * nx, rows, cols), BF16),
        *Scatter.scratch(nz, nx, rows, first.size, False),
        *Scatter.scratch(nz, nx, rows, second.size, True),
    ]


SCATTER_COUNT, GATHER_COUNT = 13, 5


def inverse_rms(rows):
    return lax.rsqrt(jnp.mean(rows * rows, axis=-1, keepdims=True) + EPS)


def wide_dot(terms, dims, tile, store):
    total = terms[0][1].shape[0 if dims is NT else 1]
    for first in range(0, total, tile):
        cols = slice(first, min(first + tile, total))
        products = [
            lax.dot_general(
                left,
                right[cols, :] if dims is NT else right[:, cols],
                (dims, ((), ())),
                preferred_element_type=F32,
            )
            for left, right in terms
        ]
        store(cols, functools.reduce(jnp.add, products))


VMEM_SPEC = pl.BlockSpec(memory_space=pltpu.VMEM)
ANY_SPEC = pl.BlockSpec(memory_space=pl.ANY)
PAIR_SHARE, GATHER_SHARE, SCATTER_SHARE = 2, 1, 2


def lasting(microseconds):
    return pl.CostEstimate(
        flops=int(microseconds * 1.1e9), bytes_accessed=2**20, transcendentals=0
    )


def linked(collective):
    return pltpu.CompilerParams(
        collective_id=collective, has_side_effects=True, vmem_limit_bytes=62 * 2**20
    )


def joined(values):
    return values.reshape(values.shape[0] * values.shape[1], values.shape[2])


def split(values, parts):
    return values.reshape(parts, values.shape[0] // parts, values.shape[1])


def project_kernel(
    count, rows_ref, gain_ref, weight_ref, gates_ref, full_out, projected_out, *scratch
):
    full, staged, full_sems, staged_sems = scratch[0], *scratch[GATHER_COUNT:]
    group = Group(count)
    gather = gather_of(group, GATHER_SHARE, scratch[:GATHER_COUNT])
    meet(count)

    shares, share = full_out.shape[0], full_out.shape[3]

    def full_copy(piece, index):
        rows = gather.rows(piece)
        return pltpu.make_async_copy(
            full.at[:, rows, pl.ds(index * share, share)],
            full_out.at[index, :, rows],
            full_sems.at[piece, index],
        )

    def staged_copy(piece):
        rows = gather.rows(piece)
        return pltpu.make_async_copy(
            staged.at[:, rows], projected_out.at[:, rows], staged_sems.at[piece]
        )

    def begin(piece):
        rows = rows_ref[gather.rows(piece)].astype(F32)
        full[group.own, gather.rows(piece)] = (
            rows * inverse_rms(rows) * gain_ref[...]
        ).astype(BF16)
        gather.phase(piece, 0)

    def ready(piece):
        gather.phase(piece, gather.last)
        rows = gather.rows(piece)
        for index in range(shares):
            full_copy(piece, index).start()

        def store(cols, value):
            staged[:, rows, cols] = split(value, count)

        left = joined(full[:, rows])
        wide_dot([(left, weight_ref)], NN, 256, store)
        value = lax.dot_general(
            left, gates_ref[...], (NN, ((), ())), preferred_element_type=F32
        )
        staged[:, rows, weight_ref.shape[1] :] = split(value, count)
        staged_copy(piece).start()

    def tick(time, _):
        during(time, begin)
        for step in range(1, gather.last):
            during(time - step, functools.partial(gather.phase, step=step))
        during(time - gather.last, ready)
        return 0

    lax.fori_loop(0, PIECES + gather.last, tick, 0)
    gather.drain()

    def finish(piece, _):
        for index in range(shares):
            full_copy(piece, index).wait()
        staged_copy(piece).wait()
        return 0

    lax.fori_loop(0, PIECES, finish, 0)


def project(rows, gain, weight, gates, count, shares):
    own, features = rows.shape
    cols = weight.shape[1] + gates.shape[1]
    nz, nx = grid_sizes(count)
    return pl.pallas_call(
        functools.partial(project_kernel, count),
        out_shape=[
            jax.ShapeDtypeStruct((shares, count, own, features // shares), BF16),
            jax.ShapeDtypeStruct((count, own, cols), F32),
        ],
        in_specs=[VMEM_SPEC] * 4,
        out_specs=[ANY_SPEC] * 2,
        scratch_shapes=[
            *gather_scratch(nz, nx, own, features),
            pltpu.VMEM((count, own, cols), F32),
            pltpu.SemaphoreType.DMA((PIECES, shares)),
            pltpu.SemaphoreType.DMA((PIECES,)),
        ],
        compiler_params=linked(0),
        cost_estimate=lasting(100),
        name="project",
    )(rows, gain, weight, gates)


def sum_and_gather(scatter, gather, full, prepare, middle, ready, job=None):
    own = lax.axis_index("heads")

    def begin(piece):
        prepare(piece)
        scatter.phase(piece, 0)

    def turn(piece):
        total = scatter.phase(piece, scatter.last)
        full[own, gather.rows(piece)] = middle(piece, total).astype(BF16)
        gather.phase(piece, 0)

    def end(piece):
        gather.phase(piece, gather.last)
        ready(piece)

    def tick(time, _):
        during(time + 1, begin)
        if job is not None:
            job(time + 1)
        for step in range(1, scatter.last):
            during(time - step + 1, functools.partial(scatter.phase, step=step))
        during(time - scatter.last + 1, turn)
        for step in range(1, gather.last):
            during(
                time - scatter.last + 1 - step, functools.partial(gather.phase, step=step)
            )
        during(time - scatter.last + 1 - gather.last, end)
        return 0

    lax.fori_loop(-1, PIECES + scatter.last + gather.last - 1, tick, 0)
    scatter.drain()
    gather.drain()


def branch_kernel(
    count, mixed_ref, weight_ref, input_ref, live_ref, gain_ref, gate_weight_ref, up_weight_ref,
    down_weight_ref, grad_ref, middle_out, full_out, dgate_out, dup_out, hidden_out, *scratch
):
    *scratch, grads, grad_sems, dgate, dup, hidden, feed_sems = scratch
    group = Group(count)
    scatter = scatter_of(group, PAIR_SHARE, scratch[:SCATTER_COUNT])
    gather = gather_of(group, PAIR_SHARE, scratch[SCATTER_COUNT:])
    parts, full = scratch[0], scratch[SCATTER_COUNT]

    def fetch(piece):
        slot = piece % 2
        return pltpu.make_async_copy(
            grad_ref.at[:, gather.rows(piece)], grads.at[slot], grad_sems.at[slot]
        )

    fetch(0).start()
    meet(count)

    def prepare(piece):
        rows = gather.rows(piece)

        def store(cols, value):
            parts[:, rows, cols] = split(value.astype(BF16), count)

        wide_dot([(joined(mixed_ref[:, rows]), weight_ref)], NN, 512, store)

    def middle(piece, total):
        rows = gather.rows(piece)
        values = input_ref[rows].astype(F32) + live_ref[rows] * total
        middle_out[rows] = values
        return values * inverse_rms(values) * gain_ref[...]

    def copies(piece):
        rows = gather.rows(piece)
        return [
            pltpu.make_async_copy(ref.at[:, rows], out.at[:, rows], feed_sems.at[piece, index])
            for index, (ref, out) in enumerate(
                ((dgate, dgate_out), (dup, dup_out), (hidden, hidden_out), (full, full_out))
            )
        ]

    def ready(piece):
        rows = gather.rows(piece)
        fetch(piece).wait()
        pl.when(piece + 1 < PIECES)(lambda: fetch(piece + 1).start())
        left, grad = joined(full[:, rows]), joined(grads[piece % 2])
        total = gate_weight_ref.shape[1]
        for first in range(0, total, 256):
            cols = slice(first, min(first + 256, total))

            def product(a, b, dims):
                return lax.dot_general(a, b, (dims, ((), ())), preferred_element_type=F32)

            gate = product(left, gate_weight_ref[:, cols], NN)
            up = product(left, up_weight_ref[:, cols], NN)
            dhidden = product(grad, down_weight_ref[cols, :], NT)
            sigmoid = jax.nn.sigmoid(gate)
            active = gate * sigmoid
            hidden[:, rows, cols] = split((active * up).astype(BF16), count)
            dup[:, rows, cols] = split((dhidden * active).astype(BF16), count)
            slope = sigmoid * (1.0 + gate * (1.0 - sigmoid))
            dgate[:, rows, cols] = split((dhidden * up * slope).astype(BF16), count)
        for copy in copies(piece):
            copy.start()

    sum_and_gather(scatter, gather, full, prepare, middle, ready)

    def finish(piece, _):
        for copy in copies(piece):
            copy.wait()
        return 0

    lax.fori_loop(0, PIECES, finish, 0)


def branch_and_feed(
    mixed, weight, rows, live, gain, gate_weight, up_weight, down_weight, grad, count
):
    own, features = rows.shape
    hidden = gate_weight.shape[1]
    nz, nx = grid_sizes(count)
    return pl.pallas_call(
        functools.partial(branch_kernel, count),
        out_shape=[
            jax.ShapeDtypeStruct((own, features), F32),
            jax.ShapeDtypeStruct((count, own, features), BF16),
            *[jax.ShapeDtypeStruct((count, own, hidden), BF16)] * 3,
        ],
        in_specs=[VMEM_SPEC] * 8 + [ANY_SPEC],
        out_specs=[VMEM_SPEC] + [ANY_SPEC] * 4,
        scratch_shapes=[
            *scatter_scratch(nz, nx, own, features, PAIR_SHARE),
            *gather_scratch(nz, nx, own, features),
            pltpu.VMEM((2, count, own // PIECES, features), BF16),
            pltpu.SemaphoreType.DMA((2,)),
            *[pltpu.VMEM((count, own, hidden), BF16)] * 3,
            pltpu.SemaphoreType.DMA((PIECES, 4)),
        ],
        compiler_params=linked(1),
        cost_estimate=lasting(180),
        name="branch_and_feed",
    )(
        split(mixed, count), weight, rows, live, gain, gate_weight, up_weight, down_weight, grad
    )


TILE = 256


class TileJob:
    def __init__(self, rows_ref, tile, factors, staged, outs, fetch_sem, out_sems):
        self.rows_ref, self.tile, self.factors = rows_ref, tile, factors
        self.staged, self.outs = staged, outs
        self.fetch_sem, self.out_sems = fetch_sem, out_sems
        self.count = rows_ref.shape[2] // TILE

    def span(self, index):
        return pl.ds(pl.multiple_of(index * TILE, TILE), TILE)

    def fetch(self, index):
        return pltpu.make_async_copy(
            self.rows_ref.at[:, :, self.span(index)], self.tile, self.fetch_sem
        )

    def results(self, index):
        return [
            pltpu.make_async_copy(
                self.staged.at[which], out.at[self.span(index)], self.out_sems.at[which]
            )
            for which, out in enumerate(self.outs)
        ]

    def wait_results(self, index):
        for copy in self.results(index):
            copy.wait()

    def run(self, index):
        self.fetch(index).wait()
        left = joined(self.tile[...])
        pl.when(index > 0)(lambda: self.wait_results(index - 1))
        for which, factor in enumerate(self.factors):
            self.staged[which] = lax.dot_general(
                left, joined(factor[...]), (TN, ((), ())), preferred_element_type=F32
            ).astype(BF16)
        for copy in self.results(index):
            copy.start()
        pl.when(index + 1 < self.count)(lambda: self.fetch(index + 1).start())


def feed_back_kernel(
    count, dgate_ref, dup_ref, gate_weight_ref, up_weight_ref, top_ref, middle_ref, live_ref,
    gain_ref, out_weight_ref, mixed_ref, hidden_ref, normed_ref, grad_feed_ref,
    dmiddle_out, dgain_out, dmixed_out, dweight_out, dgate_weight, dup_weight, ddown_weight,
    *scratch
):
    *scratch, total_out, tile, grad_tile, staged, grad_staged, fetch_sems, out_sems = scratch
    group = Group(count)
    scatter = scatter_of(group, PAIR_SHARE, scratch[:SCATTER_COUNT])
    gather = gather_of(group, PAIR_SHARE, scratch[SCATTER_COUNT:])
    parts, full = scratch[0], scratch[SCATTER_COUNT]
    jobs = (
        TileJob(
            normed_ref, tile, (dgate_ref, dup_ref), staged, (dgate_weight, dup_weight),
            fetch_sems.at[0], out_sems.at[0],
        ),
        TileJob(
            grad_feed_ref, grad_tile, (hidden_ref,), grad_staged, (ddown_weight,),
            fetch_sems.at[1], out_sems.at[1],
        ),
    )
    for each in jobs:
        each.fetch(0).start()
    meet(count)
    dgain_out[...] = jnp.zeros(dgain_out.shape, F32)
    total_out[...] = jnp.zeros(total_out.shape, F32)

    def prepare(piece):
        rows = gather.rows(piece)

        def store(cols, value):
            parts[:, rows, cols] = split(value.astype(BF16), count)

        wide_dot(
            [
                (joined(dgate_ref[:, rows]), gate_weight_ref),
                (joined(dup_ref[:, rows]), up_weight_ref),
            ],
            NT,
            256,
            store,
        )

    def middle(piece, dnormed):
        rows = gather.rows(piece)
        values = middle_ref[rows]
        scale = inverse_rms(values)
        normed = values * scale
        dgain_out[...] += jnp.sum(dnormed * normed, axis=0, keepdims=True)
        scaled = dnormed * gain_ref[...]
        dmiddle = top_ref[rows].astype(F32) + scale * (
            scaled - normed * jnp.mean(scaled * normed, axis=-1, keepdims=True)
        )
        dmiddle_out[rows] = dmiddle
        return live_ref[rows] * dmiddle

    def ready(piece):
        rows = gather.rows(piece)
        left, mixed = joined(full[:, rows]), joined(mixed_ref[:, rows])

        def store(cols, value):
            dmixed_out[:, rows, cols] = split(value, count)

        wide_dot([(left, out_weight_ref)], NT, 256, store)
        for first in range(0, left.shape[1], 256):
            total_out[first : first + 256] += lax.dot_general(
                left[:, first : first + 256], mixed, (TN, ((), ())), preferred_element_type=F32
            )

    def job(time):
        for which, each in enumerate(jobs):
            pl.when((time % 2 == which) & (time < 2 * each.count))(
                functools.partial(each.run, time // 2)
            )

    sum_and_gather(scatter, gather, full, prepare, middle, ready, job)
    last = PIECES + scatter.last + gather.last
    lax.fori_loop(last, max(2 * jobs[0].count, last), lambda time, _: (job(time), 0)[1], 0)
    for each in jobs:
        each.wait_results(each.count - 1)
    dweight_out[...] = total_out[...].astype(BF16)


def feed_back(
    dgate, dup, gate_weight, up_weight, top, middle, live, gain, out_weight, mixed, hidden,
    normed, grad_feed, count,
):
    own, features = middle.shape
    nz, nx = grid_sizes(count)
    width, units = out_weight.shape[0], gate_weight.shape[1]
    return pl.pallas_call(
        functools.partial(feed_back_kernel, count),
        out_shape=[
            jax.ShapeDtypeStruct((own, features), F32),
            jax.ShapeDtypeStruct((1, features), F32),
            jax.ShapeDtypeStruct((count, own, width), F32),
            jax.ShapeDtypeStruct((features, width), BF16),
            *[jax.ShapeDtypeStruct((features, units), BF16)] * 3,
        ],
        in_specs=[VMEM_SPEC] * 11 + [ANY_SPEC] * 2,
        out_specs=[VMEM_SPEC] * 4 + [ANY_SPEC] * 3,
        scratch_shapes=[
            *scatter_scratch(nz, nx, own, features, PAIR_SHARE),
            *gather_scratch(nz, nx, own, features),
            pltpu.VMEM((features, width), F32),
            pltpu.VMEM((count, own, TILE), BF16),
            pltpu.VMEM((count, own, TILE), BF16),
            pltpu.VMEM((2, TILE, units), BF16),
            pltpu.VMEM((1, TILE, units), BF16),
            pltpu.SemaphoreType.DMA((2,)),
            pltpu.SemaphoreType.DMA((2, 2)),
        ],
        compiler_params=linked(2),
        cost_estimate=lasting(180),
        name="feed_back",
    )(
        dgate, dup, gate_weight, up_weight, top, middle, live, gain, out_weight,
        split(mixed, count), hidden, normed, grad_feed,
    )


class Replicas(Sender):
    def __init__(self, values, from_core, from_y, over_back, over_home, sems):
        self.values, self.from_core, self.from_y = values, from_core, from_y
        self.over_back, self.over_home = over_back, over_home
        self.core_sems, self.y_sems, self.back_sems, self.home_sems = sems
        me = lax.axis_index("dp")
        self.lines = lax.axis_size("dp") // 2
        self.y, self.core = me // 2, me % 2

    @staticmethod
    def scratch(rows, cols, replicas):
        lines, share = replicas // 2, rows // replicas
        return [
            pltpu.VMEM((replicas, share, cols), BF16),
            pltpu.VMEM((lines, share, cols), BF16),
            pltpu.VMEM((max(lines - 1, 1), share, cols), BF16),
            pltpu.VMEM((max(lines - 1, 1), share, cols), BF16),
            pltpu.VMEM((lines, share, cols), BF16),
            *[pltpu.SemaphoreType.DMA((2, lines))] * 4,
        ]

    def share(self, core, y):
        return core * self.lines + y

    def peer(self, y, core):
        return {"dp": y * 2 + core}

    def line(self, k):
        return (self.y + k) % self.lines

    def drain(self):
        self.draining = True
        for k in range(self.lines):
            self.start(k)
            self.cores(k)
        self.over_y()
        self.back()
        self.draining = False

    def add(self, share, others):
        step = 64

        def some(block, _):
            rows = pl.ds(pl.multiple_of(block * step, step), step)
            total = self.values[share, rows].astype(F32)
            for ref, index in others:
                total = total + ref[index, rows].astype(F32)
            self.values[share, rows] = total.astype(BF16)
            return 0

        lax.fori_loop(0, self.values.shape[1] // step, some, 0)

    def start(self, k):
        y = self.line(k)
        self.push(
            self.values.at[self.share(1 - self.core, y)],
            self.from_core.at[y],
            self.core_sems.at[0, k],
            self.core_sems.at[1, k],
            self.peer(self.y, 1 - self.core),
        )

    def cores(self, k):
        y = self.line(k)
        share = self.share(self.core, y)
        if not self.draining:
            arrived(self.from_core.at[y], self.core_sems.at[1, k])
            self.add(share, [(self.from_core, y)])
        if k > 0:
            self.push(
                self.values.at[share],
                self.from_y.at[self.lines - k - 1],
                self.y_sems.at[0, k],
                self.y_sems.at[1, self.lines - k],
                self.peer(y, self.core),
            )

    def over_y(self):
        share = self.share(self.core, self.y)
        if not self.draining:
            for k in range(1, self.lines):
                arrived(self.from_y.at[k - 1], self.y_sems.at[1, k])
            self.add(share, [(self.from_y, k) for k in range(self.lines - 1)])
        for k in range(1, self.lines):
            self.push(
                self.values.at[share],
                self.over_back.at[self.lines - k - 1],
                self.back_sems.at[0, k],
                self.back_sems.at[1, self.lines - k],
                self.peer(self.line(k), self.core),
            )
        self.send_home(0)

    def own(self, k):
        return self.values.at[self.share(self.core, self.y)] if k == 0 else self.over_back.at[k - 1]

    def send_home(self, k):
        self.push(
            self.own(k),
            self.over_home.at[k],
            self.home_sems.at[0, k],
            self.home_sems.at[1, k],
            self.peer(self.y, 1 - self.core),
        )

    def back(self):
        for k in range(1, self.lines):
            if not self.draining:
                arrived(self.over_back.at[k - 1], self.back_sems.at[1, k])
            self.send_home(k)

    def home(self):
        for k in range(self.lines):
            arrived(self.over_home.at[k], self.home_sems.at[1, k])

    def totals(self):
        for k in range(self.lines):
            yield self.own(k), self.share(self.core, self.line(k))
            yield self.over_home.at[k], self.share(1 - self.core, self.line(k))


def sum_small(small, seen, send_sems, recv_sems, axis, rows):
    me, size = lax.axis_index(axis), lax.axis_size(axis)
    copies = []
    seen[me] = small[...]
    for k in range(1, size):
        copy = pltpu.make_async_remote_copy(
            seen.at[me], seen.at[me], send_sems.at[k], recv_sems.at[size - k],
            device_id={axis: (me + k) % size}, device_id_type=MESH,
        )
        copy.start()
        copies.append(copy)
    for k in range(1, size):
        arrived(seen.at[(me + k) % size], recv_sems.at[k])
    total = seen[0]
    for other in range(1, size):
        total = total + seen[other]
    small[...] = jnp.where(grid_index(total.shape, 0) < rows, total, small[...])
    return copies


def input_back_kernel(
    count, grad_ref, weight_ref, gates_ref, normed_ref, later_ref, input_ref, gain_ref, small_ref,
    wout_ref, grad_out, small_out, dmain_out, drest_out, *scratch
):
    parts, rest = scratch[0], scratch[SCATTER_COUNT:]
    values = rest[0]
    near, near_send, near_recv, far, far_send, far_recv, staged, out_sems = rest[9:]
    scatter = scatter_of(Group(count), SCATTER_SHARE, scratch[:SCATTER_COUNT])
    replicas = Replicas(*rest[:5], rest[5:9])
    meet(count, lax.axis_size("dp"))
    small_out[...] = small_ref[...]
    width = grad_ref.shape[2]
    values[:, :, width:] = split(wout_ref[...], values.shape[0])

    def begin(piece):
        rows = scatter.rows(piece)

        def store(cols, value):
            parts[:, rows, cols] = split(value.astype(BF16), count)

        left, edge = joined(grad_ref[:, rows]), weight_ref.shape[1]
        wide_dot(
            [(left[:, :edge], weight_ref), (left[:, edge:], gates_ref)], NT, 256, store
        )
        scatter.phase(piece, 0)

    def end(piece):
        dnormed = scatter.phase(piece, scatter.last)
        rows = scatter.rows(piece)
        given = input_ref[rows].astype(F32)
        scale = inverse_rms(given)
        normed = given * scale
        small_out[0:1] += jnp.sum(dnormed * normed, axis=0, keepdims=True)
        scaled = dnormed * gain_ref[...]
        grad_out[rows] = later_ref[rows] + scale * (
            scaled - normed * jnp.mean(scaled * normed, axis=-1, keepdims=True)
        )

    def weight_share(core, y):
        share = replicas.share(core, y)
        left = joined(normed_ref[share])
        grads = joined(grad_ref[...])
        for first in range(0, width, 384):
            cols = slice(first, min(first + 384, width))
            staged[:, cols] = lax.dot_general(
                left, grads[:, cols], (TN, ((), ())), preferred_element_type=F32
            ).astype(BF16)

        def some(block, _):
            rows = pl.ds(pl.multiple_of(block * 64, 64), 64)
            values[share, rows, :width] = staged[rows]
            return 0

        lax.fori_loop(0, staged.shape[0] // 64, some, 0)

    def other_core(k):
        weight_share(1 - replicas.core, replicas.line(k))
        replicas.start(k)

    def this_core(k):
        weight_share(replicas.core, replicas.line(k))
        replicas.cores(k)

    steps = []
    for k in range(replicas.lines - 1, -1, -1):
        steps += [functools.partial(other_core, k), functools.partial(this_core, k)]
    while len(steps) < PIECES - 1:
        steps.append(lambda: None)
    steps.append(replicas.over_y)

    def tick(time, _):
        during(time + 1, begin)
        for step in range(1, scatter.last):
            during(time - step + 1, functools.partial(scatter.phase, step=step))
        during(time - scatter.last + 1, end)
        for index, step in enumerate(steps):
            pl.when(time == index)(step)
        return 0

    lax.fori_loop(-1, max(PIECES + scatter.last - 1, len(steps)), tick, 0)
    replicas.back()
    copies = sum_small(small_out, near, near_send, near_recv, "heads", 3)
    copies += sum_small(small_out, far, far_send, far_recv, "dp", 8)
    replicas.home()
    part = dmain_out.shape[3]
    outs = []
    for index, (total, share) in enumerate(replicas.totals()):
        for kind in range(4):
            outs.append((total.at[:, pl.ds(kind * part, part)], dmain_out.at[kind, share], index))
        rest_cols = pl.ds(4 * part, drest_out.shape[2])
        outs.append((total.at[:, rest_cols], drest_out.at[share], index))
    outs = [
        pltpu.make_async_copy(source, target, out_sems.at[index, place % 5])
        for place, (source, target, index) in enumerate(outs)
    ]
    for copy in outs:
        copy.start()
    scatter.drain()
    replicas.drain()
    for copy in copies:
        copy.wait_send()
    for copy in outs:
        copy.wait()


def input_back(
    grad, weight, gates, normed, later, rows, gain, small, grad_wout, count, replica_count
):
    own, features = rows.shape
    nz, nx = grid_sizes(count)
    width, share = grad_wout.shape[1], features // replica_count
    cols = grad.shape[1] + width
    dma = pltpu.SemaphoreType.DMA
    return pl.pallas_call(
        functools.partial(input_back_kernel, count),
        out_shape=[
            jax.ShapeDtypeStruct((own, features), F32),
            jax.ShapeDtypeStruct(small.shape, F32),
            jax.ShapeDtypeStruct((4, replica_count, share, width), BF16),
            jax.ShapeDtypeStruct((replica_count, share, cols - 4 * width), BF16),
        ],
        in_specs=[VMEM_SPEC] * 9,
        out_specs=[VMEM_SPEC, VMEM_SPEC, ANY_SPEC, ANY_SPEC],
        scratch_shapes=[
            *scatter_scratch(nz, nx, own, features, SCATTER_SHARE),
            *Replicas.scratch(features, cols, replica_count),
            pltpu.VMEM((count, *small.shape), F32),
            dma((count,)),
            dma((count,)),
            pltpu.VMEM((replica_count, *small.shape), F32),
            dma((replica_count,)),
            dma((replica_count,)),
            pltpu.VMEM((share, grad.shape[1]), BF16),
            dma((replica_count, 5)),
        ],
        compiler_params=linked(3),
        cost_estimate=lasting(120),
        name="input_back",
    )(split(grad, count), weight, gates, normed, later, rows, gain, small, grad_wout)


def spread_kernel(given_ref, out_ref):
    for kind in range(given_ref.shape[0]):
        out_ref[:, kind, :] = given_ref[kind].astype(F32)


def by_rows(values):
    kinds, rows, cols = values.shape
    return pl.pallas_call(
        spread_kernel,
        grid=(rows // 256,),
        in_specs=[pl.BlockSpec((kinds, 256, cols), lambda i: (0, i, 0))],
        out_specs=pl.BlockSpec((256, kinds, cols), lambda i: (i, 0, 0)),
        out_shape=jax.ShapeDtypeStruct((rows, kinds, cols), F32),
        name="by_rows",
    )(values)


def on_device(
    block_in,
    seq_counts,
    norm1_gain,
    w_qkvg,
    conv_weight,
    w_gates,
    gate_params,
    out_gain,
    w_out,
    norm2_gain,
    w_gate_up,
    w_down,
    cotangent,
):
    own_rows, features = block_in.shape
    count = lax.axis_size("heads")
    all_rows = own_rows * count
    width = conv_weight.shape[2]
    heads = gate_params.shape[1]
    longer = seq_counts[0, 1:2]
    first_row = lax.axis_index("heads") * own_rows
    row_index = first_row + jnp.arange(own_rows, dtype=jnp.int32)
    live_own = jnp.where(longer[0] > 0, True, row_index < seq_counts[0, 0] * SEQ_SHORT)
    live_own = live_own.astype(F32)[:, None]
    weight = w_qkvg.reshape(features, 4 * width)
    gates_weight = jnp.pad(
        w_gates.reshape(features, 2 * heads), ((0, 0), (0, 128 - 2 * heads))
    )
    full_normed1, projected = project(
        block_in, norm1_gain[None], weight, gates_weight, count, lax.axis_size("dp")
    )
    projected = projected.reshape(all_rows, -1)
    taps = jnp.transpose(conv_weight, (1, 0, 2)).reshape(4, 3 * width)
    params = jnp.pad(gate_params, ((0, 0), (0, 128 - heads)))
    gain_row = out_gain[None]
    mixed, *saved, grad_feed = mixer_forward(
        longer, projected, taps, params, gain_row, cotangent, live_own, count
    )
    gate_weight, up_weight = w_gate_up[:, 0], w_gate_up[:, 1]
    middle, full_normed2, grad_gate, grad_up, hidden = branch_and_feed(
        mixed,
        w_out,
        block_in,
        live_own,
        norm2_gain[None],
        gate_weight,
        up_weight,
        w_down,
        grad_feed,
        count,
    )
    grad_middle, grad_gain2, grad_mixed, grad_wout, *early = feed_back(
        grad_gate,
        grad_up,
        gate_weight,
        up_weight,
        cotangent,
        middle,
        live_own,
        norm2_gain[None],
        w_out,
        mixed,
        hidden,
        full_normed2,
        grad_feed,
        count,
    )
    early = lax.optimization_barrier(lax.psum(lax.optimization_barrier(early), "dp"))
    dprojected, dtaps, dparams, dgain, layer_out = mixer_backward(
        longer,
        grad_mixed.reshape(all_rows, width),
        projected,
        saved,
        taps,
        params,
        gain_row,
        hidden,
        w_down,
        middle,
        live_own,
        count,
    )

    def row(values):
        return jnp.pad(values, ((0, 0), (0, features - values.shape[1])))

    small = jnp.concatenate(
        [
            jnp.zeros((1, features), F32),
            grad_gain2,
            row(dgain),
            row(dtaps),
            row(dparams.reshape(1, 256)),
        ],
        axis=0,
    )
    grad_in, small, grad_main, grad_rest = input_back(
        dprojected,
        weight,
        gates_weight,
        full_normed1,
        grad_middle,
        block_in,
        norm1_gain[None],
        small,
        grad_wout,
        count,
        lax.axis_size("dp"),
    )
    grad_main = grad_main.reshape(4, features, width)
    grad_rest = grad_rest.reshape(features, -1)
    return (
        layer_out,
        grad_in,
        small[0],
        by_rows(grad_main),
        jnp.transpose(small[3:7, : 3 * width].reshape(4, 3, width), (1, 0, 2)),
        grad_rest[:, : 2 * heads].reshape(w_gates.shape).astype(F32),
        small[7, :256].reshape(2, 128)[:, :heads],
        small[2, : out_gain.shape[0]],
        grad_rest[:, 128:].T.astype(F32),
        small[1],
        jnp.stack([early[0], early[1]], axis=1).astype(F32),
        early[2].T.astype(F32),
    )


def solution(mesh):
    return jax.shard_map(
        on_device,
        mesh=mesh,
        in_specs=(
            P(("dp", "heads"), None),
            P("dp", None),
            P(),
            P(None, None, "heads"),
            P(None, None, "heads"),
            P(None, None, "heads"),
            P(None, "heads"),
            P(),
            P("heads", None),
            P(),
            P(None, None, "heads"),
            P("heads", None),
            P(("dp", "heads"), None),
        ),
        out_specs=(
            P(("dp", "heads"), None),
            P(("dp", "heads"), None),
            P(),
            P(None, None, "heads"),
            P(None, None, "heads"),
            P(None, None, "heads"),
            P(None, "heads"),
            P(),
            P("heads", None),
            P(),
            P(None, None, "heads"),
            P("heads", None),
        ),
        check_vma=False,
    )
```

```python
import functools
import math
import jax
import jax.numpy as jnp
from jax import lax
from jax.experimental import pallas as pl
from jax.experimental.pallas import tpu as pltpu
from jax.sharding import PartitionSpec as P

SEQ_SHORT = 512
CHUNK = 256
HEAD = 128
EPS = 1e-06
F32 = jnp.float32
BF16 = jnp.bfloat16
LOW, MID, TOP = lax.Precision.DEFAULT, lax.Precision.HIGH, lax.Precision.HIGHEST
NN, NT, TN = ((1,), (0,)), ((1,), (1,)), ((0,), (0,))
P_FWD, P_BWD = MID, MID


def dot(left, right, dims, precision):
    if precision is LOW:
        left, right = left.astype(BF16), right.astype(BF16)
        return lax.dot_general(left, right, (dims, ((), ())), preferred_element_type=F32)
    return lax.dot_general(
        left, right, (dims, ((), ())), precision=precision, preferred_element_type=F32
    )


def grid_index(shape, axis):
    return lax.broadcasted_iota(jnp.int32, shape, axis)


def positions(longer, first_row, count):
    rows = grid_index((count, 1), 0) + first_row
    return jnp.where(longer > 0, rows, rows % SEQ_SHORT)


def keeps(longer, first_row):
    start = jnp.where(longer > 0, first_row, first_row % SEQ_SHORT)
    return jnp.where(start > 0, 1.0, 0.0).astype(F32)


def softplus(x):
    return jnp.maximum(x, 0.0) + jnp.log1p(jnp.exp(-jnp.abs(x)))


def gate_values(gates, params, heads):
    lane = grid_index(gates.shape, 1)
    rate = jnp.exp(params[0:1])
    shifted = gates + params[1:2]
    log_decay = jnp.where(lane < heads, -rate * softplus(shifted), 0.0)
    return rate, shifted, log_decay


def lane_column(values, index):
    return values[:, index : index + 1]


def decays(cumulative, cumulative_rows, head, masks):
    column = lane_column(cumulative, head)
    row = cumulative_rows[head : head + 1, :]
    inclusive = masks[0]
    ratio = jnp.where(inclusive, jnp.exp(jnp.where(inclusive, column - row, 0.0)), 0.0)
    last = column[CHUNK - 1 : CHUNK, :]
    return ratio, jnp.exp(column), jnp.exp(last - column), jnp.exp(last)


def unit(values):
    scale = lax.rsqrt(jnp.sum(values * values, axis=-1, keepdims=True) + EPS)
    return values * scale, scale


def pair_of(values):
    high = values.astype(BF16)
    return high, (values - high.astype(F32)).astype(BF16)


def pair_dot(left, right):
    def product(a, b):
        return lax.dot_general(a, b, (NN, ((), ())), preferred_element_type=F32)

    return product(left[0], right[0]) + (product(left[0], right[1]) + product(left[1], right[0]))


def inverses(links, row, col):
    apart = row ^ col
    size = links[0].shape[0]
    outs = [jnp.where(row == col, 1.0, 0.0) - jnp.where(apart == 1, link, 0.0) for link in links]
    pairs = [pair_of(link) for link in links]
    step = 2
    while step < size // 2:
        level = (apart >= step) & (apart < 2 * step)
        parts = [tuple(jnp.where(level, half, 0) for half in pair) for pair in pairs]
        out_pairs = [pair_of(out) for out in outs]
        inner = [pair_of(pair_dot(part, out)) for part, out in zip(parts, out_pairs)]
        outs = [out - pair_dot(pair, mid) for out, pair, mid in zip(outs, out_pairs, inner)]
        step *= 2
    half = size // 2
    uppers = [pair_of(out[:half, :half]) for out in outs]
    lowers = [pair_of(out[half:, half:]) for out in outs]
    corners = [tuple(each[half:, :half] for each in pair) for pair in pairs]
    inner = [pair_of(pair_dot(corner, upper)) for corner, upper in zip(corners, uppers)]
    corners = [pair_dot(lower, mid) for lower, mid in zip(lowers, inner)]
    return [
        jnp.concatenate(
            [out[:half], jnp.concatenate([-corner, out[half:, half:]], axis=1)], axis=0
        )
        for out, corner in zip(outs, corners)
    ]


def forward_kernel(
    heads, count, chunks, longer_ref, main_ref, conv_ref, params_ref, gain_ref, top_ref, live_ref,
    mixed_ref, conv_out_ref, raw_ref, delta_ref, solve_ref, state_ref, full_out,
    state, tail_rows, *scratch
):
    step = pl.program_id(0)
    first_row = step * CHUNK
    run, close = gather_along(step, chunks, count, top_ref, live_ref, full_out, scratch)
    run(2 * step)
    longer = longer_ref[0]
    width = heads * HEAD

    @pl.when(step == 0)
    def _():
        state[...] = jnp.zeros_like(state)
        tail_rows[...] = jnp.zeros_like(tail_rows)

    position = positions(longer, first_row, CHUNK)
    keep = keeps(longer, first_row)
    triple = main_ref[:, : 3 * width]
    padded = jnp.concatenate([tail_rows[...], triple], axis=0)
    taps = conv_ref[...]
    convolved = triple * taps[0:1]
    for lag in range(1, 4):
        shifted = padded[8 - lag : 8 - lag + CHUNK]
        convolved = convolved + jnp.where(position >= lag, shifted, 0.0) * taps[lag : lag + 1]
    tail_rows[...] = triple[CHUNK - 8 :]
    conv_out_ref[...] = convolved
    active = convolved * jax.nn.sigmoid(convolved)
    gates = main_ref[:, 4 * width :]
    rate, shifted_gate, log_decay = gate_values(gates, params_ref[...], heads)
    beta_all = jax.nn.sigmoid(gates)
    row = grid_index((CHUNK, CHUNK), 0)
    col = grid_index((CHUNK, CHUNK), 1)
    masks = (row >= col, row > col)
    cumulative = dot(jnp.where(masks[0], 1.0, 0.0), log_decay, NN, TOP)
    cumulative_rows = jnp.transpose(cumulative)
    each = range(heads)
    columns = [slice(head * HEAD, (head + 1) * HEAD) for head in each]
    queries = [unit(active[:, cols])[0] * HEAD**-0.5 for cols in columns]
    keys = [unit(active[:, width + head * HEAD : width + (head + 1) * HEAD])[0] for head in each]
    values = [active[:, 2 * width + head * HEAD : 2 * width + (head + 1) * HEAD] for head in each]
    betas = [lane_column(beta_all, heads + head) for head in each]
    spans = [decays(cumulative, cumulative_rows, head, masks) for head in each]
    grams = [
        dot(jnp.concatenate([key, query], axis=0), key, NT, P_FWD)
        for key, query in zip(keys, queries)
    ]
    links = [
        jnp.where(masks[1], beta * span[0] * gram[:CHUNK], 0.0)
        for beta, span, gram in zip(betas, spans, grams)
    ]
    solves = inverses(links, row, col)
    run(2 * step + 1)
    boths = [
        dot(
            solve,
            jnp.concatenate([beta * value, (beta * span[1]) * key], axis=1),
            NN,
            P_FWD,
        )
        for solve, beta, value, key, span in zip(solves, betas, values, keys, spans)
    ]
    entries = [state[head] * keep for head in each]
    carried = [
        dot(jnp.concatenate([both[:, HEAD:], span[1] * query], axis=0), entry, NT, P_FWD)
        for both, span, query, entry in zip(boths, spans, queries, entries)
    ]
    deltas = [both[:, :HEAD] - carry[:CHUNK] for both, carry in zip(boths, carried)]
    states = [
        span[3] * entry + dot(delta * span[2], key, TN, P_FWD)
        for span, entry, delta, key in zip(spans, entries, deltas, keys)
    ]
    raws = [
        carry[CHUNK:] + dot(gram[CHUNK:] * span[0], delta, NN, P_FWD)
        for carry, gram, span, delta in zip(carried, grams, spans, deltas)
    ]
    for head, cols in zip(each, columns):
        solve_ref[head] = solves[head]
        state_ref[0, head] = entries[head]
        state[head] = states[head]
        delta_ref[:, cols] = deltas[head]
        raw = raws[head]
        raw_ref[:, cols] = raw
        scale = lax.rsqrt(jnp.mean(raw * raw, axis=-1, keepdims=True) + EPS)
        gate = main_ref[:, 3 * width + head * HEAD : 3 * width + (head + 1) * HEAD]
        mixed = raw * scale * gain_ref[...] * (gate * jax.nn.sigmoid(gate))
        mixed_ref[:, cols] = mixed.astype(mixed_ref.dtype)
    pl.when(step == chunks - 1)(close)


def spread_ticks(tick, first, ticks, halves):
    def run(half):
        def one(index, _):
            tick(first + index)
            return 0

        lax.fori_loop(half * ticks // halves, (half + 1) * ticks // halves, one, 0)

    return run


def gather_along(step, chunks, count, top_ref, live_ref, full_out, scratch):
    *scratch, out_sems = scratch
    full = scratch[0]
    group = Group(count)
    gather = gather_of(group, GATHER_SHARE, scratch)

    def out(piece):
        rows = gather.rows(piece)
        return pltpu.make_async_copy(
            full.at[:, :, rows], full_out.at[:, :, rows], out_sems.at[piece]
        )

    def prepare(piece):
        rows = gather.rows(piece)
        full[group.z, group.x, rows] = (live_ref[rows] * top_ref[rows].astype(F32)).astype(BF16)

    before, within, behind = gather_ticks(gather, prepare, lambda piece: out(piece).start())

    def tick(time):
        before(time)
        at_each_z(group, functools.partial(within, time))
        behind(time)

    def close():
        gather.drain()

        def finish(piece, _):
            out(piece).wait()
            return 0

        lax.fori_loop(0, PIECES, finish, 0)

    pl.when(step == 0)(functools.partial(meet, count))
    return spread_ticks(tick, 0, PIECES + gather.last, 2 * chunks), close


def scatter_along(step, chunks, count, hidden_ref, weight_ref, middle_ref, live_ref, out, scratch):
    parts = scratch[0]
    group = Group(count)
    scatter = scatter_of(group, SCATTER_SHARE, scratch)

    def prepare(piece):
        rows = scatter.rows(piece)

        def store(cols, value):
            parts[:, :, rows, cols] = split(value.astype(BF16), group.deep, group.nx)

        wide_dot([(joined(hidden_ref[:, rows]), weight_ref)], NN, 512, store)

    def end(piece, total):
        rows = scatter.rows(piece)
        out[rows] = (middle_ref[rows] + live_ref[rows] * total).astype(BF16)

    before, within, behind = scatter_ticks(scatter, prepare, end)

    def tick(time):
        before(time)
        at_each_z(group, functools.partial(within, time))
        behind(time)

    pl.when(step == 0)(functools.partial(meet, count))
    return spread_ticks(tick, -1, PIECES + scatter.last, 2 * chunks), scatter.drain


def backward_kernel(
    heads, chunks, count, longer_ref, grad_ref, main_ref, conv_out_ref, raw_ref, delta_ref,
    solve_ref, state_ref, conv_ref, params_ref, gain_ref, hidden_ref, down_ref, middle_ref, live_ref,
    dmain_ref, dconv_ref, dparams_ref, dgain_ref, layer_ref, dstate, head_rows, *scratch
):
    step = pl.program_id(0)
    first_row = (chunks - 1 - step) * CHUNK
    run, close = scatter_along(
        step, chunks, count, hidden_ref, down_ref, middle_ref, live_ref, layer_ref, scratch
    )
    run(2 * step)
    longer = longer_ref[0]
    width = heads * HEAD

    @pl.when(step == 0)
    def _():
        dstate[...] = jnp.zeros_like(dstate)
        head_rows[...] = jnp.zeros_like(head_rows)
        dconv_ref[...] = jnp.zeros_like(dconv_ref)
        dparams_ref[...] = jnp.zeros_like(dparams_ref)
        dgain_ref[...] = jnp.zeros_like(dgain_ref)

    keep = keeps(longer, first_row)
    convolved = conv_out_ref[...]
    sigmoid_conv = jax.nn.sigmoid(convolved)
    active = convolved * sigmoid_conv
    slope = sigmoid_conv * (1.0 + convolved * (1.0 - sigmoid_conv))
    gates = main_ref[:, 4 * width :]
    params = params_ref[...]
    rate, shifted_gate, log_decay = gate_values(gates, params, heads)
    beta_all = jax.nn.sigmoid(gates)
    row = grid_index((CHUNK, CHUNK), 0)
    col = grid_index((CHUNK, CHUNK), 1)
    masks = (row >= col, row > col)
    cumulative = dot(jnp.where(masks[0], 1.0, 0.0), log_decay, NN, TOP)
    cumulative_rows = jnp.transpose(cumulative)
    lane = grid_index((CHUNK, 128), 1)
    last_row = grid_index((CHUNK, 1), 0) == CHUNK - 1
    gain = gain_ref[...]
    dgains, dlogs, dbetas, dparts = ([None] * heads for _ in range(4))

    def work(head):
        cols = slice(head * HEAD, (head + 1) * HEAD)
        gate = main_ref[:, 3 * width + head * HEAD : 3 * width + (head + 1) * HEAD]
        raw = raw_ref[:, cols]
        grad = grad_ref[:, cols]
        scale = lax.rsqrt(jnp.mean(raw * raw, axis=-1, keepdims=True) + EPS)
        normed = raw * scale
        sigmoid_gate = jax.nn.sigmoid(gate)
        gated = gate * sigmoid_gate
        product = grad * normed
        dgains[head] = jnp.sum(product * gated, axis=0, keepdims=True)
        dgate = product * gain * (sigmoid_gate * (1.0 + gate * (1.0 - sigmoid_gate)))
        dmain_ref[:, 3 * width + head * HEAD : 3 * width + (head + 1) * HEAD] = dgate.astype(
            dmain_ref.dtype
        )
        dnormed = grad * gain * gated
        draw = scale * (dnormed - normed * jnp.mean(dnormed * normed, axis=-1, keepdims=True))
        query_unit, query_scale = unit(active[:, head * HEAD : (head + 1) * HEAD])
        query = query_unit * HEAD**-0.5
        key, key_scale = unit(active[:, width + head * HEAD : width + (head + 1) * HEAD])
        value = active[:, 2 * width + head * HEAD : 2 * width + (head + 1) * HEAD]
        beta = lane_column(beta_all, heads + head)
        ratio, decay_in, decay_out, decay_all = decays(cumulative, cumulative_rows, head, masks)
        entry = state_ref[0, head]
        delta = delta_ref[:, cols]
        dlater = dstate[head]
        gram = dot(query, key, NT, P_BWD) * ratio
        yield
        key_dlater = dot(key, dlater, NT, P_BWD)
        yield
        ddelta = dot(gram, draw, TN, P_BWD) + decay_out * key_dlater
        yield
        dright = dot(solve_ref[head], ddelta, TN, P_BWD)
        yield
        pairs = dot(jnp.concatenate([dright, draw], axis=0), delta, NT, P_BWD)
        yield
        dlink = jnp.where(masks[1], -pairs[:CHUNK] * ratio, 0.0)
        dgram = pairs[CHUNK:] * ratio
        on_entry = dot(jnp.concatenate([dright, draw], axis=0), entry, NN, P_BWD)
        yield
        key_entry = dot(key, entry, NT, P_BWD)
        yield
        on_key = dot(jnp.concatenate([dlink, dgram], axis=0), key, NN, P_BWD)
        yield
        dquery = decay_in * on_entry[CHUNK:] + on_key[CHUNK:]
        link_key = on_key[:CHUNK]
        key_read = beta * (link_key - decay_in * on_entry[:CHUNK])
        key_tail = decay_out * dot(delta, dlater, NN, P_BWD)
        yield
        key_write = (
            dot(beta * dlink, key, TN, P_BWD) + dot(dgram, query, TN, P_BWD) + key_tail
        )
        yield
        dkey = key_read + key_write
        dvalue = beta * dright
        dbeta = jnp.sum(
            dright * (value - decay_in * key_entry) + key * link_key, axis=-1, keepdims=True
        )
        dlog = jnp.sum(query * dquery + key * (key_read - key_write), axis=-1, keepdims=True)
        ending = decay_all * jnp.sum(
            jnp.sum(entry * dlater, axis=-1, keepdims=True), axis=0, keepdims=True
        ) + jnp.sum(jnp.sum(key * key_tail, axis=-1, keepdims=True), axis=0, keepdims=True)
        dlog = dlog + jnp.where(last_row, ending, 0.0)
        dlogs[head], dbetas[head] = dlog, dbeta
        dstate[head] = keep * (
            decay_all * dlater
            + dot(decay_in * draw, query, TN, P_BWD)
            - dot((beta * decay_in) * dright, key, TN, P_BWD)
        )
        yield
        dquery = (HEAD**-0.5 * query_scale) * (
            dquery - query_unit * jnp.sum(dquery * query_unit, axis=-1, keepdims=True)
        )
        dkey = key_scale * (dkey - key * jnp.sum(dkey * key, axis=-1, keepdims=True))
        dparts[head] = (dquery, dkey, dvalue)

    works = [work(head) for head in range(heads)]
    turns = 0
    while works:
        works = [each for each in works if next(each, "end") != "end"]
        turns += 1
        if turns == 6:
            run(2 * step + 1)
    dcumulative = jnp.zeros((CHUNK, 128), F32)
    dbeta_all = jnp.zeros((CHUNK, 128), F32)
    for head in range(heads):
        dcumulative = jnp.where(lane == head, dlogs[head], dcumulative)
        dbeta_all = jnp.where(lane == heads + head, dbetas[head], dbeta_all)
    dgain = functools.reduce(jnp.add, dgains)
    dconv_parts = [[dparts[head][kind] for head in range(heads)] for kind in range(3)]
    dactive = jnp.concatenate([p for parts in dconv_parts for p in parts], axis=1)
    dconvolved = dactive * slope
    padded = jnp.concatenate([dconvolved, head_rows[...]], axis=0)
    position = positions(longer, first_row, CHUNK + 8)
    taps = conv_ref[...]
    triple = main_ref[:, : 3 * width]
    dtriple = dconvolved * taps[0:1]
    dconv_ref[0:1] += jnp.sum(dconvolved * triple, axis=0, keepdims=True)
    for lag in range(1, 4):
        moved = jnp.where(position >= lag, padded, 0.0)[lag : lag + CHUNK]
        dtriple = dtriple + moved * taps[lag : lag + 1]
        dconv_ref[lag : lag + 1] += jnp.sum(moved * triple, axis=0, keepdims=True)
    head_rows[...] = dconvolved[:8]
    dmain_ref[:, : 3 * width] = dtriple.astype(dmain_ref.dtype)
    dlog_decay = dot(jnp.where(row <= col, 1.0, 0.0), dcumulative, NN, TOP)
    dshifted = -dlog_decay * rate * jax.nn.sigmoid(shifted_gate)
    dshifted = jnp.where(lane < heads, dshifted, 0.0)
    dparams_ref[0:1] += jnp.sum(dlog_decay * log_decay, axis=0, keepdims=True)
    dparams_ref[1:2] += jnp.sum(dshifted, axis=0, keepdims=True)
    dmain_ref[:, 4 * width :] = (dshifted + dbeta_all * beta_all * (1.0 - beta_all)).astype(
        dmain_ref.dtype
    )
    dgain_ref[...] += dgain
    pl.when(step == chunks - 1)(close)


def row_block(width, chunks, backward):
    if backward:
        return pl.BlockSpec((CHUNK, width), lambda i: (chunks - 1 - i, 0))
    return pl.BlockSpec((CHUNK, width), lambda i: (i, 0))


def whole_block(shape):
    return pl.BlockSpec(shape, lambda i: (0,) * len(shape))


def mixer_forward(longer, main, conv, params, gain, top, live, count):
    rows, width = main.shape[0], conv.shape[1] // 3
    heads, chunks = width // HEAD, rows // CHUNK
    own, features = top.shape
    nz, nx = grid_sizes(count)
    rowed = functools.partial(row_block, chunks=chunks, backward=False)
    shape = jax.ShapeDtypeStruct
    return pl.pallas_call(
        functools.partial(forward_kernel, heads, count, chunks),
        grid=(chunks,),
        in_specs=[
            pl.BlockSpec(memory_space=pltpu.SMEM),
            rowed(4 * width + 128),
            whole_block((4, 3 * width)),
            whole_block((2, 128)),
            whole_block((1, HEAD)),
            whole_block((own, features)),
            whole_block((own, 1)),
        ],
        out_specs=[
            rowed(width),
            rowed(3 * width),
            rowed(width),
            rowed(width),
            pl.BlockSpec((heads, CHUNK, CHUNK), lambda i: (0, i, 0)),
            pl.BlockSpec((1, heads, HEAD, HEAD), lambda i: (i, 0, 0, 0)),
            pl.BlockSpec(memory_space=pl.ANY),
        ],
        out_shape=[
            shape((rows, width), BF16),
            shape((rows, 3 * width), F32),
            shape((rows, width), F32),
            shape((rows, width), F32),
            shape((heads, rows, CHUNK), F32),
            shape((chunks, heads, HEAD, HEAD), F32),
            shape((nz, nx, own, features), BF16),
        ],
        scratch_shapes=[
            pltpu.VMEM((heads, HEAD, HEAD), F32),
            pltpu.VMEM((8, 3 * width), F32),
            *gather_scratch(nz, nx, own, features),
            pltpu.SemaphoreType.DMA((PIECES,)),
        ],
        compiler_params=linked(4),
        cost_estimate=lasting(95),
        name="mixer_forward",
    )(longer, main, conv, params, gain, top, live)


def mixer_backward(
    longer, grad, main, saved, conv, params, gain, hidden, down_weight, middle, live, count
):
    rows, width = main.shape[0], conv.shape[1] // 3
    heads, chunks = width // HEAD, rows // CHUNK
    own, features = middle.shape
    nz, nx = grid_sizes(count)
    rowed = functools.partial(row_block, chunks=chunks, backward=True)
    shape = jax.ShapeDtypeStruct
    return pl.pallas_call(
        functools.partial(backward_kernel, heads, chunks, count),
        grid=(chunks,),
        in_specs=[
            pl.BlockSpec(memory_space=pltpu.SMEM),
            rowed(width),
            rowed(4 * width + 128),
            rowed(3 * width),
            rowed(width),
            rowed(width),
            pl.BlockSpec((heads, CHUNK, CHUNK), lambda i: (0, chunks - 1 - i, 0)),
            pl.BlockSpec((1, heads, HEAD, HEAD), lambda i: (chunks - 1 - i, 0, 0, 0)),
            whole_block((4, 3 * width)),
            whole_block((2, 128)),
            whole_block((1, HEAD)),
            whole_block(hidden.shape),
            whole_block(down_weight.shape),
            whole_block((own, features)),
            whole_block((own, 1)),
        ],
        out_specs=[
            rowed(4 * width + 128),
            whole_block((4, 3 * width)),
            whole_block((2, 128)),
            whole_block((1, HEAD)),
            whole_block((own, features)),
        ],
        out_shape=[
            shape((rows, 4 * width + 128), BF16),
            shape((4, 3 * width), F32),
            shape((2, 128), F32),
            shape((1, HEAD), F32),
            shape((own, features), BF16),
        ],
        scratch_shapes=[
            pltpu.VMEM((heads, HEAD, HEAD), F32),
            pltpu.VMEM((8, 3 * width), F32),
            *scatter_scratch(nz, nx, own, features, SCATTER_SHARE),
        ],
        compiler_params=linked(5),
        cost_estimate=lasting(100),
        name="mixer_backward",
    )(
        longer, grad, main, *saved, conv, params, gain, hidden, down_weight, middle, live
    )


MESH = pl.DeviceIdType.MESH
PIECES = 8


def grid_sizes(count):
    nz = 4 if count % 4 == 0 else 1
    return nz, count // nz


class Group:
    def __init__(self, count):
        self.deep, self.nx = grid_sizes(count)
        me = lax.axis_index("heads")
        self.z, self.x = me // self.nx, me % self.nx

    def column(self, j):
        return (self.x + j) % self.nx

    def over_x(self, j):
        return {"heads": self.z * self.nx + self.column(j)}

    def along_z(self, z):
        return {"heads": z * self.nx + self.x}


def meet(count, replicas=1):
    barrier = pltpu.get_barrier_semaphore()
    for axis, size in (("heads", count), ("dp", replicas)):
        me = lax.axis_index(axis)

        def greet(k, _, axis=axis, size=size, me=me):
            pl.semaphore_signal(
                barrier, inc=1, device_id={axis: (me + k) % size}, device_id_type=MESH
            )
            return 0

        lax.fori_loop(1, size, greet, 0)
    pl.semaphore_wait(barrier, count + replicas - 2)


def arrived(ref, sem):
    pltpu.make_async_copy(ref, ref, sem).wait()


def during(piece, work):
    pl.when((piece >= 0) & (piece < PIECES))(functools.partial(work, piece))


def push(source, target, send_sem, recv_sem, device):
    pltpu.make_async_remote_copy(
        source, target, send_sem, recv_sem, device_id=device, device_id_type=MESH
    ).start()


class Gather:
    def __init__(self, group, full, cols, sems, x_first):
        self.group, self.full, self.cols, self.x_first = group, full, cols, x_first
        self.part = full.shape[2] // PIECES
        self.line_send, self.line_recv, self.x_send, self.x_recv = sems
        self.last = group.deep

    @staticmethod
    def sems(deep, nx):
        dma = pltpu.SemaphoreType.DMA
        return [dma((PIECES, 2)), dma((PIECES, deep)), dma((PIECES, nx)), dma((PIECES, nx))]

    def at(self, piece, z, column):
        rows = pl.ds(pl.multiple_of(piece * self.part, self.part), self.part)
        return self.full.at[z, column, rows, self.cols]

    def columns(self):
        return slice(None) if self.x_first else self.group.x

    def push_line(self, piece, z, way, zz):
        place = self.at(piece, z, self.columns())
        push(
            place,
            place,
            self.line_send.at[piece, way],
            self.line_recv.at[piece, z],
            self.group.along_z(zz + (1 if way == 0 else -1)),
        )

    def push_x(self, piece, z):
        place = self.at(piece, z, self.group.x)
        for j in range(1, self.group.nx):
            push(
                place,
                place,
                self.x_send.at[piece, j],
                self.x_recv.at[piece, self.group.nx - j],
                self.group.over_x(j),
            )

    def own_line(self, piece, zz):
        if zz + 1 < self.group.deep:
            self.push_line(piece, zz, 0, zz)
        if zz > 0:
            self.push_line(piece, zz, 1, zz)

    def begin(self, piece):
        self.push_x(piece, self.group.z)
        if not self.x_first:
            group = self.group
            pl.when(group.z + 1 < group.deep)(lambda: self.push_line(piece, group.z, 0, group.z))
            pl.when(group.z > 0)(lambda: self.push_line(piece, group.z, 1, group.z))

    def phase(self, piece, step, zz):
        deep, nx = self.group.deep, self.group.nx
        if self.x_first:
            if step == 1:
                for j in range(1, nx):
                    arrived(self.at(piece, zz, self.group.column(j)), self.x_recv.at[piece, j])
                self.own_line(piece, zz)
                return
            step -= 1
        elif step == deep:
            for j in range(1, nx):
                place = self.at(piece, slice(None), self.group.column(j))
                arrived(place, self.x_recv.at[piece, j])
            return
        for z, way in ((zz - step, 0), (zz + step, 1)):
            if 0 <= z < deep:
                arrived(self.at(piece, z, self.columns()), self.line_recv.at[piece, z])
                if 0 <= zz + (1 if way == 0 else -1) < deep:
                    self.push_line(piece, z, way, zz)
                if not self.x_first:
                    self.push_x(piece, z)

    def drain(self, piece, zz):
        deep, nx = self.group.deep, self.group.nx
        if zz + 1 < deep:
            place = self.at(piece, pl.ds(0, zz + 1), self.columns())
            arrived(place, self.line_send.at[piece, 0])
        if zz > 0:
            place = self.at(piece, pl.ds(zz, deep - zz), self.columns())
            arrived(place, self.line_send.at[piece, 1])
        z = zz if self.x_first else slice(None)
        for j in range(1, nx):
            arrived(self.at(piece, z, self.group.x), self.x_send.at[piece, j])


class Scatter:
    last = 4

    def __init__(self, group, parts, cols, scratch, z_first):
        self.group, self.parts, self.cols, self.z_first = group, parts, cols, z_first
        self.part = parts.shape[2] // PIECES
        self.landed_x, self.line, *sems = scratch
        self.x_send, self.x_recv, self.z_send, self.z_recv = sems

    @staticmethod
    def scratch(deep, nx, rows, cols, z_first):
        dma = pltpu.SemaphoreType.DMA
        return [
            pltpu.VMEM((max(nx - 1, 1), 1 if z_first else deep, rows, cols), BF16),
            pltpu.VMEM((deep + 1, nx if z_first else 1, rows, cols), BF16),
            *[dma((PIECES, nx))] * 2,
            *[dma((PIECES, 2))] * 2,
        ]

    def rows(self, piece):
        return pl.ds(pl.multiple_of(piece * self.part, self.part), self.part)

    def columns(self):
        return slice(None) if self.z_first else pl.ds(self.group.x, 1)

    def at(self, piece, z, column):
        return self.parts.at[z, column, self.rows(piece), self.cols]

    def line_at(self, piece, way, zz):
        first, size = (zz + 1, self.group.deep - zz) if way == 0 else (0, zz + 1)
        return self.line.at[pl.ds(first, size), :, self.rows(piece)]

    def push_line(self, piece, way, zz):
        deep = self.group.deep
        first, size = (zz + 1, deep - 1 - zz) if way == 0 else (0, zz)
        if size == 0:
            return
        after = zz + 1 if way == 0 else zz - 1
        push(
            self.at(piece, pl.ds(first, size), self.columns()),
            self.line_at(piece, way, after),
            self.z_send.at[piece, way],
            self.z_recv.at[piece, way],
            self.group.along_z(after),
        )

    def ends(self, piece, zz):
        if zz == 0:
            self.push_line(piece, 0, zz)
        if zz == self.group.deep - 1:
            self.push_line(piece, 1, zz)

    def hand_on(self, piece, near, zz):
        deep = self.group.deep
        if zz == 0 or zz == deep - 1:
            return
        way = 0 if (zz < deep // 2) == near else 1
        arrived(self.line_at(piece, way, zz), self.z_recv.at[piece, way])
        first, size = (zz + 1, deep - 1 - zz) if way == 0 else (0, zz)
        shift = 1 if way == 0 else 0
        ours = self.at(piece, pl.ds(first, size), self.columns())
        landed = self.line.at[pl.ds(first + shift, size), :, self.rows(piece)]
        ours[...] = (ours[...].astype(F32) + landed[...].astype(F32)).astype(BF16)
        self.push_line(piece, way, zz)

    def wait_ends(self, piece, zz):
        deep = self.group.deep
        if deep == 1:
            return
        if zz == 0:
            arrived(self.line_at(piece, 1, zz), self.z_recv.at[piece, 1])
        if zz == deep - 1:
            arrived(self.line_at(piece, 0, zz), self.z_recv.at[piece, 0])

    def total_line(self, piece, column):
        group, rows = self.group, self.rows(piece)
        total = self.parts[group.z, column, rows, self.cols].astype(F32)
        index = column if self.z_first else 0
        for here, place in ((group.z > 0, group.z + 1), (group.z + 1 < group.deep, group.z)):
            landed = self.line[place, index, rows]
            total = total + jnp.where(here, landed.astype(F32), 0.0)
        return total

    def begin(self, piece):
        if not self.z_first:
            for j in range(1, self.group.nx):
                push(
                    self.at(piece, slice(None), self.group.column(j)),
                    self.landed_x.at[self.group.nx - j - 1, :, self.rows(piece)],
                    self.x_send.at[piece, j],
                    self.x_recv.at[piece, self.group.nx - j],
                    self.group.over_x(j),
                )

    def begin_line(self, piece, zz):
        if self.z_first:
            self.ends(piece, zz)

    def wait_x(self, piece, j):
        landed = self.landed_x.at[j - 1, :, self.rows(piece)]
        arrived(landed, self.x_recv.at[piece, j])
        return landed[...].astype(F32)

    def phase(self, piece, step, zz):
        nx = self.group.nx
        if self.z_first:
            if step < 3:
                self.hand_on(piece, step == 1, zz)
            elif step == 3:
                self.wait_ends(piece, zz)
            return
        if step == 1:
            ours = self.at(piece, slice(None), self.group.x)
            total = ours[...].astype(F32)
            for j in range(1, nx):
                total = total + self.wait_x(piece, j)
            ours[...] = total.astype(BF16)
            self.ends(piece, zz)
        elif step < 4:
            self.hand_on(piece, step == 2, zz)
        else:
            self.wait_ends(piece, zz)

    def third(self, piece):
        if not self.z_first:
            return
        group, rows = self.group, self.rows(piece)
        for j in range(1, group.nx):
            column = group.column(j)
            total = self.total_line(piece, column).astype(BF16)
            self.parts[group.z, column, rows, self.cols] = total
            push(
                self.at(piece, pl.ds(group.z, 1), column),
                self.landed_x.at[group.nx - j - 1, :, rows],
                self.x_send.at[piece, j],
                self.x_recv.at[piece, group.nx - j],
                group.over_x(j),
            )

    def total(self, piece):
        total = self.total_line(piece, self.group.x)
        if self.z_first:
            for j in range(1, self.group.nx):
                total = total + self.wait_x(piece, j)[0]
        return total

    def drain(self, piece, zz):
        deep = self.group.deep
        for way, size in ((0, deep - 1 - zz), (1, zz)):
            if size > 0:
                place = self.at(piece, pl.ds(0, size), self.columns())
                arrived(place, self.z_send.at[piece, way])
        z = pl.ds(0, 1 if self.z_first else deep)
        for j in range(1, self.group.nx):
            arrived(self.at(piece, z, self.group.x), self.x_send.at[piece, j])


class Both:
    def __init__(self, first, second):
        self.both = (first, second)
        self.group = first.group
        self.part, self.last = first.part, first.last

    def rows(self, piece):
        return pl.ds(pl.multiple_of(piece * self.part, self.part), self.part)

    def begin(self, piece):
        for each in self.both:
            each.begin(piece)

    def begin_line(self, piece, zz):
        for each in self.both:
            each.begin_line(piece, zz)

    def phase(self, piece, step, zz):
        for each in self.both:
            each.phase(piece, step, zz)

    def third(self, piece):
        for each in self.both:
            each.third(piece)

    def total(self, piece):
        return jnp.concatenate([each.total(piece) for each in self.both], axis=1)

    def drain(self):
        def at(zz):
            def one(piece, _):
                for each in self.both:
                    each.drain(piece, zz)
                return 0

            lax.fori_loop(0, PIECES, one, 0)

        at_each_z(self.group, at)


def at_each_z(group, work):
    for zz in range(group.deep):
        pl.when(group.z == zz)(functools.partial(work, zz))


def scatter_ticks(scatter, prepare, finish, after=None):
    def before(time):
        def begin(piece):
            prepare(piece)
            scatter.begin(piece)

        during(time + 1, begin)

    def within(time, zz):
        for step in range(scatter.last, 0, -1):
            during(time - step + 1, functools.partial(scatter.phase, step=step, zz=zz))
        during(time + 1, functools.partial(scatter.begin_line, zz=zz))

    def behind(time):
        during(time - 2, scatter.third)
        during(time - scatter.last + 1, lambda piece: finish(piece, scatter.total(piece)))

    return before, within, behind


def gather_ticks(gather, prepare, ready):
    def before(time):
        if prepare is not None:

            def begin(piece):
                prepare(piece)
                gather.begin(piece)

            during(time, begin)

    def within(time, zz):
        for step in range(gather.last, 0, -1):
            during(time - step, functools.partial(gather.phase, step=step, zz=zz))

    def behind(time):
        during(time - gather.last, ready)

    return before, within, behind


def cut(cols, share):
    edge = cols - cols * share // 8
    return pl.ds(0, edge), pl.ds(edge, cols - edge)


def gather_of(group, share, scratch):
    full, *sems = scratch
    first, second = cut(full.shape[3], share)
    return Both(
        Gather(group, full, first, sems[:4], False), Gather(group, full, second, sems[4:], True)
    )


def scatter_of(group, share, scratch):
    parts, *rest = scratch
    first, second = cut(parts.shape[3], share)
    return Both(
        Scatter(group, parts, first, rest[:6], False),
        Scatter(group, parts, second, rest[6:], True),
    )


def gather_scratch(nz, nx, rows, cols):
    return [pltpu.VMEM((nz, nx, rows, cols), BF16), *Gather.sems(nz, nx), *Gather.sems(nz, nx)]


def scatter_scratch(nz, nx, rows, cols, share):
    first, second = cut(cols, share)
    return [
        pltpu.VMEM((nz, nx, rows, cols), BF16),
        *Scatter.scratch(nz, nx, rows, first.size, False),
        *Scatter.scratch(nz, nx, rows, second.size, True),
    ]


SCATTER_COUNT, GATHER_COUNT = 13, 9


def inverse_rms(rows):
    return lax.rsqrt(jnp.mean(rows * rows, axis=-1, keepdims=True) + EPS)


def wide_dot(terms, dims, tile, store):
    total = terms[0][1].shape[0 if dims is NT else 1]
    for first in range(0, total, tile):
        cols = slice(first, min(first + tile, total))
        products = [
            lax.dot_general(
                left,
                right[cols, :] if dims is NT else right[:, cols],
                (dims, ((), ())),
                preferred_element_type=F32,
            )
            for left, right in terms
        ]
        store(cols, functools.reduce(jnp.add, products))


VMEM_SPEC = pl.BlockSpec(memory_space=pltpu.VMEM)
ANY_SPEC = pl.BlockSpec(memory_space=pl.ANY)
PAIR_SHARE, GATHER_SHARE, SCATTER_SHARE = 2, 1, 2


def lasting(microseconds):
    return pl.CostEstimate(
        flops=int(microseconds * 1.1e9), bytes_accessed=2**20, transcendentals=0
    )


def linked(collective):
    return pltpu.CompilerParams(
        collective_id=collective, has_side_effects=True, vmem_limit_bytes=62 * 2**20
    )


def joined(values):
    return values.reshape(-1, values.shape[-1])


def split(values, *parts):
    return values.reshape(*parts, values.shape[0] // math.prod(parts), values.shape[1])


def project_kernel(
    count, rows_ref, gain_ref, weight_ref, gates_ref, full_out, projected_out, *scratch
):
    full, staged, full_sems, staged_sems = scratch[0], *scratch[GATHER_COUNT:]
    group = Group(count)
    gather = gather_of(group, GATHER_SHARE, scratch[:GATHER_COUNT])
    meet(count)
    shares, share = full_out.shape[0], full_out.shape[4]

    def full_copy(piece, index):
        rows = gather.rows(piece)
        return pltpu.make_async_copy(
            full.at[:, :, rows, pl.ds(index * share, share)],
            full_out.at[index, :, :, rows],
            full_sems.at[piece, index],
        )

    def staged_copy(piece):
        rows = gather.rows(piece)
        return pltpu.make_async_copy(
            staged.at[:, rows], projected_out.at[:, rows], staged_sems.at[piece]
        )

    def prepare(piece):
        rows = rows_ref[gather.rows(piece)].astype(F32)
        full[group.z, group.x, gather.rows(piece)] = (
            rows * inverse_rms(rows) * gain_ref[...]
        ).astype(BF16)

    def ready(piece):
        rows = gather.rows(piece)
        for index in range(shares):
            full_copy(piece, index).start()

        def store(cols, value):
            staged[:, rows, cols] = split(value, count)

        left = joined(full[:, :, rows])
        wide_dot([(left, weight_ref)], NN, 256, store)
        value = lax.dot_general(
            left, gates_ref[...], (NN, ((), ())), preferred_element_type=F32
        )
        staged[:, rows, weight_ref.shape[1] :] = split(value, count)
        staged_copy(piece).start()

    before, within, behind = gather_ticks(gather, prepare, ready)

    def tick(time, _):
        before(time)
        at_each_z(group, functools.partial(within, time))
        behind(time)
        return 0

    lax.fori_loop(0, PIECES + gather.last, tick, 0)
    gather.drain()

    def finish(piece, _):
        for index in range(shares):
            full_copy(piece, index).wait()
        staged_copy(piece).wait()
        return 0

    lax.fori_loop(0, PIECES, finish, 0)


def project(rows, gain, weight, gates, count, shares):
    own, features = rows.shape
    cols = weight.shape[1] + gates.shape[1]
    nz, nx = grid_sizes(count)
    return pl.pallas_call(
        functools.partial(project_kernel, count),
        out_shape=[
            jax.ShapeDtypeStruct((shares, nz, nx, own, features // shares), BF16),
            jax.ShapeDtypeStruct((count, own, cols), F32),
        ],
        in_specs=[VMEM_SPEC] * 4,
        out_specs=[ANY_SPEC] * 2,
        scratch_shapes=[
            *gather_scratch(nz, nx, own, features),
            pltpu.VMEM((count, own, cols), F32),
            pltpu.SemaphoreType.DMA((PIECES, shares)),
            pltpu.SemaphoreType.DMA((PIECES,)),
        ],
        compiler_params=linked(0),
        cost_estimate=lasting(100),
        name="project",
    )(rows, gain, weight, gates)


def sum_and_gather(scatter, gather, prepare, middle, ready, job=None):
    group = gather.group
    full = gather.both[0].full

    def turn(piece, total):
        full[group.z, group.x, gather.rows(piece)] = middle(piece, total).astype(BF16)
        gather.begin(piece)

    late = scatter.last - 1
    before, sum_within, sum_behind = scatter_ticks(scatter, prepare, turn)
    _, gather_within, gather_behind = gather_ticks(gather, None, ready)

    def tick(time, _):
        before(time)

        def within(zz):
            gather_within(time - late, zz)
            sum_within(time, zz)

        at_each_z(group, within)
        sum_behind(time)
        gather_behind(time - late)
        if job is not None:
            job(time + 1)
        return 0

    lax.fori_loop(-1, PIECES + late + gather.last, tick, 0)
    scatter.drain()
    gather.drain()


def branch_kernel(
    count, mixed_ref, weight_ref, input_ref, live_ref, gain_ref, feed_weight_ref,
    down_weight_ref, grad_ref, middle_out, full_out, dgate_out, dup_out, hidden_out, *scratch
):
    *scratch, grads, grad_sems, dgate, dup, hidden, feed_sems = scratch
    group = Group(count)
    scatter = scatter_of(group, PAIR_SHARE, scratch[:SCATTER_COUNT])
    gather = gather_of(group, PAIR_SHARE, scratch[SCATTER_COUNT:])
    parts, full = scratch[0], scratch[SCATTER_COUNT]

    def fetch(piece):
        slot = piece % 2
        return pltpu.make_async_copy(
            grad_ref.at[:, :, gather.rows(piece)], grads.at[slot], grad_sems.at[slot]
        )

    fetch(0).start()
    meet(count)

    def prepare(piece):
        rows = gather.rows(piece)

        def store(cols, value):
            parts[:, :, rows, cols] = split(value.astype(BF16), group.deep, group.nx)

        wide_dot([(joined(mixed_ref[:, rows]), weight_ref)], NN, 512, store)

    def middle(piece, total):
        rows = gather.rows(piece)
        values = input_ref[rows].astype(F32) + live_ref[rows] * total
        middle_out[rows] = values
        return values * inverse_rms(values) * gain_ref[...]

    def copies(piece):
        rows = gather.rows(piece)
        return [
            pltpu.make_async_copy(ref.at[:, rows], out.at[:, rows], feed_sems.at[piece, index])
            for index, (ref, out) in enumerate(
                ((dgate, dgate_out), (dup, dup_out), (hidden, hidden_out))
            )
        ] + [
            pltpu.make_async_copy(
                full.at[:, :, rows], full_out.at[:, :, rows], feed_sems.at[piece, 3]
            )
        ]

    def ready(piece):
        rows = gather.rows(piece)
        fetch(piece).wait()
        pl.when(piece + 1 < PIECES)(lambda: fetch(piece + 1).start())
        left, grad = joined(full[:, :, rows]), joined(grads[piece % 2])
        total = feed_weight_ref.shape[1]
        for first in range(0, total, 256):
            cols = slice(first, min(first + 256, total))

            def product(a, b, dims):
                return lax.dot_general(a, b, (dims, ((), ())), preferred_element_type=F32)

            gate = product(left, feed_weight_ref[0, cols], NT)
            up = product(left, feed_weight_ref[1, cols], NT)
            dhidden = product(grad, down_weight_ref[cols, :], NT)
            sigmoid = jax.nn.sigmoid(gate)
            active = gate * sigmoid
            hidden[:, rows, cols] = split((active * up).astype(BF16), count)
            dup[:, rows, cols] = split((dhidden * active).astype(BF16), count)
            slope = sigmoid * (1.0 + gate * (1.0 - sigmoid))
            dgate[:, rows, cols] = split((dhidden * up * slope).astype(BF16), count)
        for copy in copies(piece):
            copy.start()

    sum_and_gather(scatter, gather, prepare, middle, ready)

    def finish(piece, _):
        for copy in copies(piece):
            copy.wait()
        return 0

    lax.fori_loop(0, PIECES, finish, 0)


def branch_and_feed(mixed, weight, rows, live, gain, feed_weight, down_weight, grad, count):
    own, features = rows.shape
    hidden = feed_weight.shape[1]
    nz, nx = grid_sizes(count)
    return pl.pallas_call(
        functools.partial(branch_kernel, count),
        out_shape=[
            jax.ShapeDtypeStruct((own, features), F32),
            jax.ShapeDtypeStruct((nz, nx, own, features), BF16),
            *[jax.ShapeDtypeStruct((count, own, hidden), BF16)] * 3,
        ],
        in_specs=[VMEM_SPEC] * 7 + [ANY_SPEC],
        out_specs=[VMEM_SPEC] + [ANY_SPEC] * 4,
        scratch_shapes=[
            *scatter_scratch(nz, nx, own, features, PAIR_SHARE),
            *gather_scratch(nz, nx, own, features),
            pltpu.VMEM((2, nz, nx, own // PIECES, features), BF16),
            pltpu.SemaphoreType.DMA((2,)),
            *[pltpu.VMEM((count, own, hidden), BF16)] * 3,
            pltpu.SemaphoreType.DMA((PIECES, 4)),
        ],
        compiler_params=linked(1),
        cost_estimate=lasting(180),
        name="branch_and_feed",
    )(split(mixed, count), weight, rows, live, gain, feed_weight, down_weight, grad)


TILE = 256


class TileJob:
    def __init__(self, rows_ref, tile, factors, staged, outs, fetch_sem, out_sems):
        self.rows_ref, self.tile, self.factors = rows_ref, tile, factors
        self.staged, self.outs = staged, outs
        self.fetch_sem, self.out_sems = fetch_sem, out_sems
        self.count = rows_ref.shape[3] // TILE

    def span(self, index):
        return pl.ds(pl.multiple_of(index * TILE, TILE), TILE)

    def fetch(self, index):
        return pltpu.make_async_copy(
            self.rows_ref.at[:, :, :, self.span(index)], self.tile, self.fetch_sem
        )

    def results(self, index):
        return [
            pltpu.make_async_copy(
                self.staged.at[which], out.at[:, self.span(index)], self.out_sems.at[which]
            )
            for which, out in enumerate(self.outs)
        ]

    def wait_results(self, index):
        for copy in self.results(index):
            copy.wait()

    def run(self, index):
        self.fetch(index).wait()
        left = joined(self.tile[...])
        pl.when(index > 0)(lambda: self.wait_results(index - 1))
        for which, factor in enumerate(self.factors):
            product = lax.dot_general(
                left, joined(factor[...]), (TN, ((), ())), preferred_element_type=F32
            )
            self.staged[which] = jnp.transpose(product).astype(BF16)
        for copy in self.results(index):
            copy.start()
        pl.when(index + 1 < self.count)(lambda: self.fetch(index + 1).start())


def feed_back_kernel(
    count, dgate_ref, dup_ref, feed_weight_ref, top_ref, middle_ref, live_ref,
    gain_ref, out_weight_ref, mixed_ref, hidden_ref, normed_ref, grad_feed_ref,
    dmiddle_out, dgain_out, dmixed_out, dweight_out, dfeed_out, *scratch
):
    *scratch, total_out, tile, grad_tile, staged, grad_staged, fetch_sems, out_sems = scratch
    group = Group(count)
    scatter = scatter_of(group, PAIR_SHARE, scratch[:SCATTER_COUNT])
    gather = gather_of(group, PAIR_SHARE, scratch[SCATTER_COUNT:])
    parts, full = scratch[0], scratch[SCATTER_COUNT]
    jobs = (
        TileJob(
            normed_ref, tile, (dgate_ref, dup_ref), staged, (dfeed_out.at[0], dfeed_out.at[1]),
            fetch_sems.at[0], out_sems.at[0],
        ),
        TileJob(
            grad_feed_ref, grad_tile, (hidden_ref,), grad_staged, (dfeed_out.at[2],),
            fetch_sems.at[1], out_sems.at[1],
        ),
    )
    for each in jobs:
        each.fetch(0).start()
    meet(count)
    dgain_out[...] = jnp.zeros(dgain_out.shape, F32)
    total_out[...] = jnp.zeros(total_out.shape, F32)

    def prepare(piece):
        rows = gather.rows(piece)

        def store(cols, value):
            parts[:, :, rows, cols] = split(value.astype(BF16), group.deep, group.nx)

        wide_dot(
            [
                (joined(dgate_ref[:, rows]), feed_weight_ref.at[0]),
                (joined(dup_ref[:, rows]), feed_weight_ref.at[1]),
            ],
            NN,
            256,
            store,
        )

    def middle(piece, dnormed):
        rows = gather.rows(piece)
        values = middle_ref[rows]
        scale = inverse_rms(values)
        normed = values * scale
        dgain_out[...] += jnp.sum(dnormed * normed, axis=0, keepdims=True)
        scaled = dnormed * gain_ref[...]
        dmiddle = top_ref[rows].astype(F32) + scale * (
            scaled - normed * jnp.mean(scaled * normed, axis=-1, keepdims=True)
        )
        dmiddle_out[rows] = dmiddle
        return live_ref[rows] * dmiddle

    def ready(piece):
        rows = gather.rows(piece)
        left, mixed = joined(full[:, :, rows]), joined(mixed_ref[:, rows])

        def store(cols, value):
            dmixed_out[:, rows, cols] = split(value, count)

        wide_dot([(left, out_weight_ref)], NT, 256, store)
        for first in range(0, left.shape[1], 256):
            total_out[first : first + 256] += lax.dot_general(
                left[:, first : first + 256], mixed, (TN, ((), ())), preferred_element_type=F32
            )

    def job(time):
        for which, each in enumerate(jobs):
            pl.when((time % 2 == which) & (time < 2 * each.count))(
                functools.partial(each.run, time // 2)
            )

    sum_and_gather(scatter, gather, prepare, middle, ready, job)
    last = PIECES + scatter.last + gather.last
    lax.fori_loop(last, max(2 * jobs[0].count, last), lambda time, _: (job(time), 0)[1], 0)
    for each in jobs:
        each.wait_results(each.count - 1)
    dweight_out[...] = total_out[...].astype(BF16)


def feed_back(
    dgate, dup, feed_weight, top, middle, live, gain, out_weight, mixed, hidden, normed, grad_feed,
    count,
):
    own, features = middle.shape
    nz, nx = grid_sizes(count)
    width, units = out_weight.shape[0], feed_weight.shape[1]
    return pl.pallas_call(
        functools.partial(feed_back_kernel, count),
        out_shape=[
            jax.ShapeDtypeStruct((own, features), F32),
            jax.ShapeDtypeStruct((1, features), F32),
            jax.ShapeDtypeStruct((count, own, width), F32),
            jax.ShapeDtypeStruct((features, width), BF16),
            jax.ShapeDtypeStruct((3, units, features), BF16),
        ],
        in_specs=[VMEM_SPEC] * 10 + [ANY_SPEC] * 2,
        out_specs=[VMEM_SPEC] * 4 + [ANY_SPEC],
        scratch_shapes=[
            *scatter_scratch(nz, nx, own, features, PAIR_SHARE),
            *gather_scratch(nz, nx, own, features),
            pltpu.VMEM((features, width), F32),
            pltpu.VMEM((nz, nx, own, TILE), BF16),
            pltpu.VMEM((nz, nx, own, TILE), BF16),
            pltpu.VMEM((2, units, TILE), BF16),
            pltpu.VMEM((1, units, TILE), BF16),
            pltpu.SemaphoreType.DMA((2,)),
            pltpu.SemaphoreType.DMA((2, 2)),
        ],
        compiler_params=linked(2),
        cost_estimate=lasting(180),
        name="feed_back",
    )(
        dgate, dup, feed_weight, top, middle, live, gain, out_weight,
        split(mixed, count), hidden, normed, grad_feed,
    )


class Replicas:
    def __init__(self, values, from_core, from_y, over_back, over_home, sems):
        self.values, self.from_core, self.from_y = values, from_core, from_y
        self.over_back, self.over_home = over_back, over_home
        self.core_sems, self.y_sems, self.back_sems, self.home_sems = sems
        me = lax.axis_index("dp")
        self.lines = lax.axis_size("dp") // 2
        self.y, self.core = me // 2, me % 2

    @staticmethod
    def scratch(rows, cols, replicas):
        lines, share = replicas // 2, rows // replicas
        return [
            pltpu.VMEM((replicas, share, cols), BF16),
            pltpu.VMEM((lines, share, cols), BF16),
            pltpu.VMEM((max(lines - 1, 1), share, cols), BF16),
            pltpu.VMEM((max(lines - 1, 1), share, cols), BF16),
            pltpu.VMEM((lines, share, cols), BF16),
            *[pltpu.SemaphoreType.DMA((2, lines))] * 4,
        ]

    def share(self, core, y):
        return core * self.lines + y

    def peer(self, y, core):
        return {"dp": y * 2 + core}

    def line(self, k):
        return (self.y + k) % self.lines

    draining = False

    def push(self, source, target, send_sem, recv_sem, device):
        copy = pltpu.make_async_remote_copy(
            source, target, send_sem, recv_sem, device_id=device, device_id_type=MESH
        )
        if self.draining:
            copy.wait_send()
        else:
            copy.start()

    def drain(self):
        self.draining = True
        for k in range(self.lines):
            self.start(k)
            self.cores(k)
        self.over_y()
        self.back()
        self.draining = False

    def add(self, share, others):
        step = 64

        def some(block, _):
            rows = pl.ds(pl.multiple_of(block * step, step), step)
            total = self.values[share, rows].astype(F32)
            for ref, index in others:
                total = total + ref[index, rows].astype(F32)
            self.values[share, rows] = total.astype(BF16)
            return 0

        lax.fori_loop(0, self.values.shape[1] // step, some, 0)

    def start(self, k):
        y = self.line(k)
        self.push(
            self.values.at[self.share(1 - self.core, y)],
            self.from_core.at[y],
            self.core_sems.at[0, k],
            self.core_sems.at[1, k],
            self.peer(self.y, 1 - self.core),
        )

    def cores(self, k):
        y = self.line(k)
        share = self.share(self.core, y)
        if not self.draining:
            arrived(self.from_core.at[y], self.core_sems.at[1, k])
            self.add(share, [(self.from_core, y)])
        if k > 0:
            self.push(
                self.values.at[share],
                self.from_y.at[self.lines - k - 1],
                self.y_sems.at[0, k],
                self.y_sems.at[1, self.lines - k],
                self.peer(y, self.core),
            )

    def over_y(self):
        share = self.share(self.core, self.y)
        if not self.draining:
            for k in range(1, self.lines):
                arrived(self.from_y.at[k - 1], self.y_sems.at[1, k])
            self.add(share, [(self.from_y, k) for k in range(self.lines - 1)])
        for k in range(1, self.lines):
            self.push(
                self.values.at[share],
                self.over_back.at[self.lines - k - 1],
                self.back_sems.at[0, k],
                self.back_sems.at[1, self.lines - k],
                self.peer(self.line(k), self.core),
            )
        self.send_home(0)

    def own(self, k):
        return self.values.at[self.share(self.core, self.y)] if k == 0 else self.over_back.at[k - 1]

    def send_home(self, k):
        self.push(
            self.own(k),
            self.over_home.at[k],
            self.home_sems.at[0, k],
            self.home_sems.at[1, k],
            self.peer(self.y, 1 - self.core),
        )

    def back(self):
        for k in range(1, self.lines):
            if not self.draining:
                arrived(self.over_back.at[k - 1], self.back_sems.at[1, k])
            self.send_home(k)

    def home(self):
        for k in range(self.lines):
            arrived(self.over_home.at[k], self.home_sems.at[1, k])

    def totals(self):
        for k in range(self.lines):
            yield self.own(k), self.share(self.core, self.line(k))
            yield self.over_home.at[k], self.share(1 - self.core, self.line(k))


def sum_small(small, seen, send_sems, recv_sems, axis, rows):
    me, size = lax.axis_index(axis), lax.axis_size(axis)
    copies = []
    seen[me] = small[...]
    for k in range(1, size):
        copy = pltpu.make_async_remote_copy(
            seen.at[me], seen.at[me], send_sems.at[k], recv_sems.at[size - k],
            device_id={axis: (me + k) % size}, device_id_type=MESH,
        )
        copy.start()
        copies.append(copy)
    for k in range(1, size):
        arrived(seen.at[(me + k) % size], recv_sems.at[k])
    total = seen[0]
    for other in range(1, size):
        total = total + seen[other]
    small[...] = jnp.where(grid_index(total.shape, 0) < rows, total, small[...])
    return copies


def input_back_kernel(
    count, grad_ref, weight_ref, gates_ref, normed_ref, later_ref, input_ref, gain_ref, small_ref,
    wout_ref, grad_out, small_out, dmain_out, drest_out, *scratch
):
    parts, rest = scratch[0], scratch[SCATTER_COUNT:]
    values = rest[0]
    near, near_send, near_recv, far, far_send, far_recv, staged, out_sems = rest[9:]
    group = Group(count)
    scatter = scatter_of(group, SCATTER_SHARE, scratch[:SCATTER_COUNT])
    replicas = Replicas(*rest[:5], rest[5:9])
    meet(count, lax.axis_size("dp"))
    small_out[...] = small_ref[...]
    width = grad_ref.shape[2]
    values[:, :, width:] = split(wout_ref[...], values.shape[0])

    def prepare(piece):
        rows = scatter.rows(piece)

        def store(cols, value):
            parts[:, :, rows, cols] = split(value.astype(BF16), group.deep, group.nx)

        left, edge = joined(grad_ref[:, rows]), weight_ref.shape[1]
        wide_dot(
            [(left[:, :edge], weight_ref), (left[:, edge:], gates_ref)], NT, 256, store
        )

    def end(piece, dnormed):
        rows = scatter.rows(piece)
        given = input_ref[rows].astype(F32)
        scale = inverse_rms(given)
        normed = given * scale
        small_out[0:1] += jnp.sum(dnormed * normed, axis=0, keepdims=True)
        scaled = dnormed * gain_ref[...]
        grad_out[rows] = later_ref[rows] + scale * (
            scaled - normed * jnp.mean(scaled * normed, axis=-1, keepdims=True)
        )

    def weight_share(core, y):
        share = replicas.share(core, y)
        left = joined(normed_ref[share])
        grads = joined(grad_ref[...])
        for first in range(0, width, 384):
            cols = slice(first, min(first + 384, width))
            staged[:, cols] = lax.dot_general(
                left, grads[:, cols], (TN, ((), ())), preferred_element_type=F32
            ).astype(BF16)

        def some(block, _):
            rows = pl.ds(pl.multiple_of(block * 64, 64), 64)
            values[share, rows, :width] = staged[rows]
            return 0

        lax.fori_loop(0, staged.shape[0] // 64, some, 0)

    def other_core(k):
        weight_share(1 - replicas.core, replicas.line(k))
        replicas.start(k)

    def this_core(k):
        weight_share(replicas.core, replicas.line(k))
        replicas.cores(k)

    steps = []
    for k in range(replicas.lines - 1, -1, -1):
        steps += [functools.partial(other_core, k), functools.partial(this_core, k)]
    while len(steps) < PIECES - 1:
        steps.append(lambda: None)
    steps.append(replicas.over_y)

    before, within, behind = scatter_ticks(scatter, prepare, end)

    def tick(time, _):
        before(time)
        at_each_z(group, functools.partial(within, time))
        behind(time)
        for index, step in enumerate(steps):
            pl.when(time == index)(step)
        return 0

    lax.fori_loop(-1, max(PIECES + scatter.last - 1, len(steps)), tick, 0)
    replicas.back()
    copies = sum_small(small_out, near, near_send, near_recv, "heads", 3)
    copies += sum_small(small_out, far, far_send, far_recv, "dp", 8)
    replicas.home()
    part = dmain_out.shape[3]
    outs = []
    for index, (total, share) in enumerate(replicas.totals()):
        for kind in range(4):
            outs.append((total.at[:, pl.ds(kind * part, part)], dmain_out.at[kind, share], index))
        rest_cols = pl.ds(4 * part, drest_out.shape[2])
        outs.append((total.at[:, rest_cols], drest_out.at[share], index))
    outs = [
        pltpu.make_async_copy(source, target, out_sems.at[index, place % 5])
        for place, (source, target, index) in enumerate(outs)
    ]
    for copy in outs:
        copy.start()
    scatter.drain()
    replicas.drain()
    for copy in copies:
        copy.wait_send()
    for copy in outs:
        copy.wait()


def input_back(
    grad, weight, gates, normed, later, rows, gain, small, grad_wout, count, replica_count
):
    own, features = rows.shape
    nz, nx = grid_sizes(count)
    width, share = grad_wout.shape[1], features // replica_count
    cols = grad.shape[1] + width
    dma = pltpu.SemaphoreType.DMA
    return pl.pallas_call(
        functools.partial(input_back_kernel, count),
        out_shape=[
            jax.ShapeDtypeStruct((own, features), F32),
            jax.ShapeDtypeStruct(small.shape, F32),
            jax.ShapeDtypeStruct((4, replica_count, share, width), BF16),
            jax.ShapeDtypeStruct((replica_count, share, cols - 4 * width), BF16),
        ],
        in_specs=[VMEM_SPEC] * 9,
        out_specs=[VMEM_SPEC, VMEM_SPEC, ANY_SPEC, ANY_SPEC],
        scratch_shapes=[
            *scatter_scratch(nz, nx, own, features, SCATTER_SHARE),
            *Replicas.scratch(features, cols, replica_count),
            pltpu.VMEM((count, *small.shape), F32),
            dma((count,)),
            dma((count,)),
            pltpu.VMEM((replica_count, *small.shape), F32),
            dma((replica_count,)),
            dma((replica_count,)),
            pltpu.VMEM((share, grad.shape[1]), BF16),
            dma((replica_count, 5)),
        ],
        compiler_params=linked(3),
        cost_estimate=lasting(120),
        name="input_back",
    )(split(grad, count), weight, gates, normed, later, rows, gain, small, grad_wout)


def spread_kernel(given_ref, out_ref):
    for kind in range(given_ref.shape[0]):
        out_ref[:, kind, :] = given_ref[kind].astype(F32)


def by_rows(values):
    kinds, rows, cols = values.shape
    return pl.pallas_call(
        spread_kernel,
        grid=(rows // 256,),
        in_specs=[pl.BlockSpec((kinds, 256, cols), lambda i: (0, i, 0))],
        out_specs=pl.BlockSpec((256, kinds, cols), lambda i: (i, 0, 0)),
        out_shape=jax.ShapeDtypeStruct((rows, kinds, cols), F32),
        name="by_rows",
    )(values)


def on_device(
    block_in,
    seq_counts,
    norm1_gain,
    w_qkvg,
    conv_weight,
    w_gates,
    gate_params,
    out_gain,
    w_out,
    norm2_gain,
    w_gate_up,
    w_down,
    cotangent,
):
    own_rows, features = block_in.shape
    count = lax.axis_size("heads")
    all_rows = own_rows * count
    width = conv_weight.shape[2]
    heads = gate_params.shape[1]
    longer = seq_counts[0, 1:2]
    first_row = lax.axis_index("heads") * own_rows
    row_index = first_row + jnp.arange(own_rows, dtype=jnp.int32)
    live_own = jnp.where(longer[0] > 0, True, row_index < seq_counts[0, 0] * SEQ_SHORT)
    live_own = live_own.astype(F32)[:, None]
    weight = w_qkvg.reshape(features, 4 * width)
    gates_weight = jnp.pad(
        w_gates.reshape(features, 2 * heads), ((0, 0), (0, 128 - 2 * heads))
    )
    full_normed1, projected = project(
        block_in, norm1_gain[None], weight, gates_weight, count, lax.axis_size("dp")
    )
    projected = projected.reshape(all_rows, -1)
    taps = jnp.transpose(conv_weight, (1, 0, 2)).reshape(4, 3 * width)
    params = jnp.pad(gate_params, ((0, 0), (0, 128 - heads)))
    gain_row = out_gain[None]
    mixed, *saved, grad_feed = mixer_forward(
        longer, projected, taps, params, gain_row, cotangent, live_own, count
    )
    feed_weight = jnp.transpose(w_gate_up, (1, 2, 0))
    middle, full_normed2, grad_gate, grad_up, hidden = branch_and_feed(
        mixed,
        w_out,
        block_in,
        live_own,
        norm2_gain[None],
        feed_weight,
        w_down,
        grad_feed,
        count,
    )
    grad_middle, grad_gain2, grad_mixed, grad_wout, early = feed_back(
        grad_gate,
        grad_up,
        feed_weight,
        cotangent,
        middle,
        live_own,
        norm2_gain[None],
        w_out,
        mixed,
        hidden,
        full_normed2,
        grad_feed,
        count,
    )
    early = lax.psum(early, "dp")
    dprojected, dtaps, dparams, dgain, layer_out = mixer_backward(
        longer,
        grad_mixed.reshape(all_rows, width),
        projected,
        saved,
        taps,
        params,
        gain_row,
        hidden,
        w_down,
        middle,
        live_own,
        count,
    )

    def row(values):
        return jnp.pad(values, ((0, 0), (0, features - values.shape[1])))

    small = jnp.concatenate(
        [
            jnp.zeros((1, features), F32),
            grad_gain2,
            row(dgain),
            row(dtaps),
            row(dparams.reshape(1, 256)),
        ],
        axis=0,
    )
    grad_in, small, grad_main, grad_rest = input_back(
        dprojected,
        weight,
        gates_weight,
        full_normed1,
        grad_middle,
        block_in,
        norm1_gain[None],
        small,
        grad_wout,
        count,
        lax.axis_size("dp"),
    )
    grad_main = grad_main.reshape(4, features, width)
    grad_rest = grad_rest.reshape(features, -1)
    return (
        layer_out,
        grad_in,
        small[0],
        by_rows(grad_main),
        jnp.transpose(small[3:7, : 3 * width].reshape(4, 3, width), (1, 0, 2)),
        grad_rest[:, : 2 * heads].reshape(w_gates.shape).astype(F32),
        small[7, :256].reshape(2, 128)[:, :heads],
        small[2, : out_gain.shape[0]],
        grad_rest[:, 128:].T.astype(F32),
        small[1],
        jnp.transpose(early[:2].astype(F32), (2, 0, 1)),
        early[2].astype(F32),
    )


def solution(mesh):
    return jax.shard_map(
        on_device,
        mesh=mesh,
        in_specs=(
            P(("dp", "heads"), None),
            P("dp", None),
            P(),
            P(None, None, "heads"),
            P(None, None, "heads"),
            P(None, None, "heads"),
            P(None, "heads"),
            P(),
            P("heads", None),
            P(),
            P(None, None, "heads"),
            P("heads", None),
            P(("dp", "heads"), None),
        ),
        out_specs=(
            P(("dp", "heads"), None),
            P(("dp", "heads"), None),
            P(),
            P(None, None, "heads"),
            P(None, None, "heads"),
            P(None, None, "heads"),
            P(None, "heads"),
            P(),
            P("heads", None),
            P(),
            P(None, None, "heads"),
            P("heads", None),
        ),
        check_vma=False,
    )
```

```python
import functools
import math
import jax
import jax.numpy as jnp
from jax import lax
from jax.experimental import pallas as pl
from jax.experimental.pallas import tpu as pltpu
from jax.sharding import PartitionSpec as P

SEQ_SHORT = 512
CHUNK = 256
HEAD = 128
EPS = 1e-06
F32 = jnp.float32
BF16 = jnp.bfloat16
LOW, MID, TOP = lax.Precision.DEFAULT, lax.Precision.HIGH, lax.Precision.HIGHEST
NN, NT, TN = ((1,), (0,)), ((1,), (1,)), ((0,), (0,))
P_FWD, P_BWD = MID, MID


def dot(left, right, dims, precision):
    if precision is LOW:
        left, right = left.astype(BF16), right.astype(BF16)
        return lax.dot_general(left, right, (dims, ((), ())), preferred_element_type=F32)
    return lax.dot_general(
        left, right, (dims, ((), ())), precision=precision, preferred_element_type=F32
    )


def grid_index(shape, axis):
    return lax.broadcasted_iota(jnp.int32, shape, axis)


def positions(longer, first_row, count):
    rows = grid_index((count, 1), 0) + first_row
    return jnp.where(longer > 0, rows, rows % SEQ_SHORT)


def keeps(longer, first_row):
    start = jnp.where(longer > 0, first_row, first_row % SEQ_SHORT)
    return jnp.where(start > 0, 1.0, 0.0).astype(F32)


def softplus(x):
    return jnp.maximum(x, 0.0) + jnp.log1p(jnp.exp(-jnp.abs(x)))


def gate_values(gates, params, heads):
    lane = grid_index(gates.shape, 1)
    rate = jnp.exp(params[0:1])
    shifted = gates + params[1:2]
    log_decay = jnp.where(lane < heads, -rate * softplus(shifted), 0.0)
    return rate, shifted, log_decay


def lane_column(values, index):
    return values[:, index : index + 1]


def decays(cumulative, cumulative_rows, head, masks):
    column = lane_column(cumulative, head)
    row = cumulative_rows[head : head + 1, :]
    inclusive = masks[0]
    ratio = jnp.where(inclusive, jnp.exp(jnp.where(inclusive, column - row, 0.0)), 0.0)
    last = column[CHUNK - 1 : CHUNK, :]
    return ratio, jnp.exp(column), jnp.exp(last - column), jnp.exp(last)


def unit(values):
    scale = lax.rsqrt(jnp.sum(values * values, axis=-1, keepdims=True) + EPS)
    return values * scale, scale


def pair_of(values):
    high = values.astype(BF16)
    return high, (values - high.astype(F32)).astype(BF16)


def pair_dot(left, right):
    def product(a, b):
        return lax.dot_general(a, b, (NN, ((), ())), preferred_element_type=F32)

    return product(left[0], right[0]) + (product(left[0], right[1]) + product(left[1], right[0]))


def inverses(links, row, col):
    apart = row ^ col
    size = links[0].shape[0]
    outs = [jnp.where(row == col, 1.0, 0.0) - jnp.where(apart == 1, link, 0.0) for link in links]
    pairs = [pair_of(link) for link in links]
    step = 2
    while step < size // 2:
        level = (apart >= step) & (apart < 2 * step)
        parts = [tuple(jnp.where(level, half, 0) for half in pair) for pair in pairs]
        out_pairs = [pair_of(out) for out in outs]
        inner = [pair_of(pair_dot(part, out)) for part, out in zip(parts, out_pairs)]
        outs = [out - pair_dot(pair, mid) for out, pair, mid in zip(outs, out_pairs, inner)]
        step *= 2
    half = size // 2
    uppers = [pair_of(out[:half, :half]) for out in outs]
    lowers = [pair_of(out[half:, half:]) for out in outs]
    corners = [tuple(each[half:, :half] for each in pair) for pair in pairs]
    inner = [pair_of(pair_dot(corner, upper)) for corner, upper in zip(corners, uppers)]
    corners = [pair_dot(lower, mid) for lower, mid in zip(lowers, inner)]
    return [
        jnp.concatenate(
            [out[:half], jnp.concatenate([-corner, out[half:, half:]], axis=1)], axis=0
        )
        for out, corner in zip(outs, corners)
    ]


def forward_kernel(
    heads, count, chunks, longer_ref, main_ref, conv_ref, params_ref, gain_ref, top_ref, live_ref,
    mixed_ref, conv_out_ref, raw_ref, delta_ref, solve_ref, state_ref, full_out,
    state, tail_rows, *scratch
):
    step = pl.program_id(0)
    first_row = step * CHUNK
    run, close = gather_along(step, chunks, count, top_ref, live_ref, full_out, scratch)
    run(2 * step)
    longer = longer_ref[0]
    width = heads * HEAD

    @pl.when(step == 0)
    def _():
        state[...] = jnp.zeros_like(state)
        tail_rows[...] = jnp.zeros_like(tail_rows)

    position = positions(longer, first_row, CHUNK)
    keep = keeps(longer, first_row)
    triple = main_ref[:, : 3 * width]
    padded = jnp.concatenate([tail_rows[...], triple], axis=0)
    taps = conv_ref[...]
    convolved = triple * taps[0:1]
    for lag in range(1, 4):
        shifted = padded[8 - lag : 8 - lag + CHUNK]
        convolved = convolved + jnp.where(position >= lag, shifted, 0.0) * taps[lag : lag + 1]
    tail_rows[...] = triple[CHUNK - 8 :]
    conv_out_ref[...] = convolved
    active = convolved * jax.nn.sigmoid(convolved)
    gates = main_ref[:, 4 * width :]
    rate, shifted_gate, log_decay = gate_values(gates, params_ref[...], heads)
    beta_all = jax.nn.sigmoid(gates)
    row = grid_index((CHUNK, CHUNK), 0)
    col = grid_index((CHUNK, CHUNK), 1)
    masks = (row >= col, row > col)
    cumulative = dot(jnp.where(masks[0], 1.0, 0.0), log_decay, NN, TOP)
    cumulative_rows = jnp.transpose(cumulative)
    each = range(heads)
    columns = [slice(head * HEAD, (head + 1) * HEAD) for head in each]
    queries = [unit(active[:, cols])[0] * HEAD**-0.5 for cols in columns]
    keys = [unit(active[:, width + head * HEAD : width + (head + 1) * HEAD])[0] for head in each]
    values = [active[:, 2 * width + head * HEAD : 2 * width + (head + 1) * HEAD] for head in each]
    betas = [lane_column(beta_all, heads + head) for head in each]
    spans = [decays(cumulative, cumulative_rows, head, masks) for head in each]
    grams = [
        dot(jnp.concatenate([key, query], axis=0), key, NT, P_FWD)
        for key, query in zip(keys, queries)
    ]
    links = [
        jnp.where(masks[1], beta * span[0] * gram[:CHUNK], 0.0)
        for beta, span, gram in zip(betas, spans, grams)
    ]
    solves = inverses(links, row, col)
    run(2 * step + 1)
    boths = [
        dot(
            solve,
            jnp.concatenate([beta * value, (beta * span[1]) * key], axis=1),
            NN,
            P_FWD,
        )
        for solve, beta, value, key, span in zip(solves, betas, values, keys, spans)
    ]
    entries = [state[head] * keep for head in each]
    carried = [
        dot(jnp.concatenate([both[:, HEAD:], span[1] * query], axis=0), entry, NT, P_FWD)
        for both, span, query, entry in zip(boths, spans, queries, entries)
    ]
    deltas = [both[:, :HEAD] - carry[:CHUNK] for both, carry in zip(boths, carried)]
    states = [
        span[3] * entry + dot(delta * span[2], key, TN, P_FWD)
        for span, entry, delta, key in zip(spans, entries, deltas, keys)
    ]
    raws = [
        carry[CHUNK:] + dot(gram[CHUNK:] * span[0], delta, NN, P_FWD)
        for carry, gram, span, delta in zip(carried, grams, spans, deltas)
    ]
    for head, cols in zip(each, columns):
        solve_ref[head] = solves[head]
        state_ref[0, head] = entries[head]
        state[head] = states[head]
        delta_ref[:, cols] = deltas[head]
        raw = raws[head]
        raw_ref[:, cols] = raw
        scale = lax.rsqrt(jnp.mean(raw * raw, axis=-1, keepdims=True) + EPS)
        gate = main_ref[:, 3 * width + head * HEAD : 3 * width + (head + 1) * HEAD]
        mixed = raw * scale * gain_ref[...] * (gate * jax.nn.sigmoid(gate))
        mixed_ref[:, cols] = mixed.astype(mixed_ref.dtype)
    pl.when(step == chunks - 1)(close)


def spread_ticks(tick, first, ticks, halves):
    def run(half):
        def one(index, _):
            tick(first + index)
            return 0

        lax.fori_loop(half * ticks // halves, (half + 1) * ticks // halves, one, 0)

    return run


def gather_along(step, chunks, count, top_ref, live_ref, full_out, scratch):
    *scratch, out_sems = scratch
    full = scratch[0]
    group = Group(count)
    gather = gather_of(group, GATHER_SHARE, scratch)

    def out(piece):
        rows = gather.rows(piece)
        return pltpu.make_async_copy(
            full.at[:, :, rows], full_out.at[:, :, rows], out_sems.at[piece]
        )

    def prepare(piece):
        rows = gather.rows(piece)
        full[group.z, group.x, rows] = (live_ref[rows] * top_ref[rows].astype(F32)).astype(BF16)

    before, within, behind = gather_ticks(gather, prepare, lambda piece: out(piece).start())

    def tick(time):
        before(time)
        at_each_z(group, functools.partial(within, time))
        behind(time)

    def close():
        gather.drain()

        def finish(piece, _):
            out(piece).wait()
            return 0

        lax.fori_loop(0, PIECES, finish, 0)

    pl.when(step == 0)(functools.partial(meet, count))
    return spread_ticks(tick, 0, PIECES + gather.last, 2 * chunks), close


def scatter_along(step, chunks, count, hidden_ref, weight_ref, middle_ref, live_ref, out, scratch):
    parts = scratch[0]
    group = Group(count)
    scatter = scatter_of(group, SCATTER_SHARE, scratch)

    def prepare(piece):
        rows = scatter.rows(piece)

        def store(cols, value):
            parts[:, :, rows, cols] = split(value.astype(BF16), group.deep, group.nx)

        wide_dot([(joined(hidden_ref[:, rows]), weight_ref)], NN, 512, store)

    def end(piece, total):
        rows = scatter.rows(piece)
        out[rows] = (middle_ref[rows] + live_ref[rows] * total).astype(BF16)

    before, within, behind = scatter_ticks(scatter, prepare, end)

    def tick(time):
        before(time)
        at_each_z(group, functools.partial(within, time))
        behind(time)

    pl.when(step == 0)(functools.partial(meet, count))
    return spread_ticks(tick, -1, PIECES + scatter.last, 2 * chunks), scatter.drain


def backward_kernel(
    heads, chunks, count, longer_ref, grad_ref, main_ref, conv_out_ref, raw_ref, delta_ref,
    solve_ref, state_ref, conv_ref, params_ref, gain_ref, hidden_ref, down_ref, middle_ref, live_ref,
    dmain_ref, dconv_ref, dparams_ref, dgain_ref, layer_ref, dstate, head_rows, *scratch
):
    step = pl.program_id(0)
    first_row = (chunks - 1 - step) * CHUNK
    run, close = scatter_along(
        step, chunks, count, hidden_ref, down_ref, middle_ref, live_ref, layer_ref, scratch
    )
    run(2 * step)
    longer = longer_ref[0]
    width = heads * HEAD

    @pl.when(step == 0)
    def _():
        dstate[...] = jnp.zeros_like(dstate)
        head_rows[...] = jnp.zeros_like(head_rows)
        dconv_ref[...] = jnp.zeros_like(dconv_ref)
        dparams_ref[...] = jnp.zeros_like(dparams_ref)
        dgain_ref[...] = jnp.zeros_like(dgain_ref)

    keep = keeps(longer, first_row)
    convolved = conv_out_ref[...]
    sigmoid_conv = jax.nn.sigmoid(convolved)
    active = convolved * sigmoid_conv
    slope = sigmoid_conv * (1.0 + convolved * (1.0 - sigmoid_conv))
    gates = main_ref[:, 4 * width :]
    params = params_ref[...]
    rate, shifted_gate, log_decay = gate_values(gates, params, heads)
    beta_all = jax.nn.sigmoid(gates)
    row = grid_index((CHUNK, CHUNK), 0)
    col = grid_index((CHUNK, CHUNK), 1)
    masks = (row >= col, row > col)
    cumulative = dot(jnp.where(masks[0], 1.0, 0.0), log_decay, NN, TOP)
    cumulative_rows = jnp.transpose(cumulative)
    lane = grid_index((CHUNK, 128), 1)
    last_row = grid_index((CHUNK, 1), 0) == CHUNK - 1
    gain = gain_ref[...]
    dgains, dlogs, dbetas, dparts = ([None] * heads for _ in range(4))

    def work(head):
        cols = slice(head * HEAD, (head + 1) * HEAD)
        gate = main_ref[:, 3 * width + head * HEAD : 3 * width + (head + 1) * HEAD]
        raw = raw_ref[:, cols]
        grad = grad_ref[:, cols]
        scale = lax.rsqrt(jnp.mean(raw * raw, axis=-1, keepdims=True) + EPS)
        normed = raw * scale
        sigmoid_gate = jax.nn.sigmoid(gate)
        gated = gate * sigmoid_gate
        product = grad * normed
        dgains[head] = jnp.sum(product * gated, axis=0, keepdims=True)
        dgate = product * gain * (sigmoid_gate * (1.0 + gate * (1.0 - sigmoid_gate)))
        dmain_ref[:, 3 * width + head * HEAD : 3 * width + (head + 1) * HEAD] = dgate.astype(
            dmain_ref.dtype
        )
        dnormed = grad * gain * gated
        draw = scale * (dnormed - normed * jnp.mean(dnormed * normed, axis=-1, keepdims=True))
        query_unit, query_scale = unit(active[:, head * HEAD : (head + 1) * HEAD])
        query = query_unit * HEAD**-0.5
        key, key_scale = unit(active[:, width + head * HEAD : width + (head + 1) * HEAD])
        value = active[:, 2 * width + head * HEAD : 2 * width + (head + 1) * HEAD]
        beta = lane_column(beta_all, heads + head)
        ratio, decay_in, decay_out, decay_all = decays(cumulative, cumulative_rows, head, masks)
        entry = state_ref[0, head]
        delta = delta_ref[:, cols]
        dlater = dstate[head]
        gram = dot(query, key, NT, P_BWD) * ratio
        yield
        key_dlater = dot(key, dlater, NT, P_BWD)
        yield
        ddelta = dot(gram, draw, TN, P_BWD) + decay_out * key_dlater
        yield
        dright = dot(solve_ref[head], ddelta, TN, P_BWD)
        yield
        pairs = dot(jnp.concatenate([dright, draw], axis=0), delta, NT, P_BWD)
        yield
        dlink = jnp.where(masks[1], -pairs[:CHUNK] * ratio, 0.0)
        dgram = pairs[CHUNK:] * ratio
        on_entry = dot(jnp.concatenate([dright, draw], axis=0), entry, NN, P_BWD)
        yield
        key_entry = dot(key, entry, NT, P_BWD)
        yield
        on_key = dot(jnp.concatenate([dlink, dgram], axis=0), key, NN, P_BWD)
        yield
        dquery = decay_in * on_entry[CHUNK:] + on_key[CHUNK:]
        link_key = on_key[:CHUNK]
        key_read = beta * (link_key - decay_in * on_entry[:CHUNK])
        key_tail = decay_out * dot(delta, dlater, NN, P_BWD)
        yield
        key_write = (
            dot(beta * dlink, key, TN, P_BWD) + dot(dgram, query, TN, P_BWD) + key_tail
        )
        yield
        dkey = key_read + key_write
        dvalue = beta * dright
        dbeta = jnp.sum(
            dright * (value - decay_in * key_entry) + key * link_key, axis=-1, keepdims=True
        )
        dlog = jnp.sum(query * dquery + key * (key_read - key_write), axis=-1, keepdims=True)
        ending = decay_all * jnp.sum(
            jnp.sum(entry * dlater, axis=-1, keepdims=True), axis=0, keepdims=True
        ) + jnp.sum(jnp.sum(key * key_tail, axis=-1, keepdims=True), axis=0, keepdims=True)
        dlog = dlog + jnp.where(last_row, ending, 0.0)
        dlogs[head], dbetas[head] = dlog, dbeta
        dstate[head] = keep * (
            decay_all * dlater
            + dot(decay_in * draw, query, TN, P_BWD)
            - dot((beta * decay_in) * dright, key, TN, P_BWD)
        )
        yield
        dquery = (HEAD**-0.5 * query_scale) * (
            dquery - query_unit * jnp.sum(dquery * query_unit, axis=-1, keepdims=True)
        )
        dkey = key_scale * (dkey - key * jnp.sum(dkey * key, axis=-1, keepdims=True))
        dparts[head] = (dquery, dkey, dvalue)

    works = [work(head) for head in range(heads)]
    turns = 0
    while works:
        works = [each for each in works if next(each, "end") != "end"]
        turns += 1
        if turns == 6:
            run(2 * step + 1)
    dcumulative = jnp.zeros((CHUNK, 128), F32)
    dbeta_all = jnp.zeros((CHUNK, 128), F32)
    for head in range(heads):
        dcumulative = jnp.where(lane == head, dlogs[head], dcumulative)
        dbeta_all = jnp.where(lane == heads + head, dbetas[head], dbeta_all)
    dgain = functools.reduce(jnp.add, dgains)
    dconv_parts = [[dparts[head][kind] for head in range(heads)] for kind in range(3)]
    dactive = jnp.concatenate([p for parts in dconv_parts for p in parts], axis=1)
    dconvolved = dactive * slope
    padded = jnp.concatenate([dconvolved, head_rows[...]], axis=0)
    position = positions(longer, first_row, CHUNK + 8)
    taps = conv_ref[...]
    triple = main_ref[:, : 3 * width]
    dtriple = dconvolved * taps[0:1]
    dconv_ref[0:1] += jnp.sum(dconvolved * triple, axis=0, keepdims=True)
    for lag in range(1, 4):
        moved = jnp.where(position >= lag, padded, 0.0)[lag : lag + CHUNK]
        dtriple = dtriple + moved * taps[lag : lag + 1]
        dconv_ref[lag : lag + 1] += jnp.sum(moved * triple, axis=0, keepdims=True)
    head_rows[...] = dconvolved[:8]
    dmain_ref[:, : 3 * width] = dtriple.astype(dmain_ref.dtype)
    dlog_decay = dot(jnp.where(row <= col, 1.0, 0.0), dcumulative, NN, TOP)
    dshifted = -dlog_decay * rate * jax.nn.sigmoid(shifted_gate)
    dshifted = jnp.where(lane < heads, dshifted, 0.0)
    dparams_ref[0:1] += jnp.sum(dlog_decay * log_decay, axis=0, keepdims=True)
    dparams_ref[1:2] += jnp.sum(dshifted, axis=0, keepdims=True)
    dmain_ref[:, 4 * width :] = (dshifted + dbeta_all * beta_all * (1.0 - beta_all)).astype(
        dmain_ref.dtype
    )
    dgain_ref[...] += dgain
    pl.when(step == chunks - 1)(close)


def row_block(width, chunks, backward):
    if backward:
        return pl.BlockSpec((CHUNK, width), lambda i: (chunks - 1 - i, 0))
    return pl.BlockSpec((CHUNK, width), lambda i: (i, 0))


def whole_block(shape):
    return pl.BlockSpec(shape, lambda i: (0,) * len(shape))


def mixer_forward(longer, main, conv, params, gain, top, live, count):
    rows, width = main.shape[0], conv.shape[1] // 3
    heads, chunks = width // HEAD, rows // CHUNK
    own, features = top.shape
    nz, nx = grid_sizes(count)
    rowed = functools.partial(row_block, chunks=chunks, backward=False)
    shape = jax.ShapeDtypeStruct
    return pl.pallas_call(
        functools.partial(forward_kernel, heads, count, chunks),
        grid=(chunks,),
        in_specs=[
            pl.BlockSpec(memory_space=pltpu.SMEM),
            rowed(4 * width + 128),
            whole_block((4, 3 * width)),
            whole_block((2, 128)),
            whole_block((1, HEAD)),
            whole_block((own, features)),
            whole_block((own, 1)),
        ],
        out_specs=[
            rowed(width),
            rowed(3 * width),
            rowed(width),
            rowed(width),
            pl.BlockSpec((heads, CHUNK, CHUNK), lambda i: (0, i, 0)),
            pl.BlockSpec((1, heads, HEAD, HEAD), lambda i: (i, 0, 0, 0)),
            pl.BlockSpec(memory_space=pl.ANY),
        ],
        out_shape=[
            shape((rows, width), BF16),
            shape((rows, 3 * width), F32),
            shape((rows, width), F32),
            shape((rows, width), F32),
            shape((heads, rows, CHUNK), F32),
            shape((chunks, heads, HEAD, HEAD), F32),
            shape((nz, nx, own, features), BF16),
        ],
        scratch_shapes=[
            pltpu.VMEM((heads, HEAD, HEAD), F32),
            pltpu.VMEM((8, 3 * width), F32),
            *gather_scratch(nz, nx, own, features),
            pltpu.SemaphoreType.DMA((PIECES,)),
        ],
        compiler_params=linked(4),
        cost_estimate=lasting(95),
        name="mixer_forward",
    )(longer, main, conv, params, gain, top, live)


def mixer_backward(
    longer, grad, main, saved, conv, params, gain, hidden, down_weight, middle, live, count
):
    rows, width = main.shape[0], conv.shape[1] // 3
    heads, chunks = width // HEAD, rows // CHUNK
    own, features = middle.shape
    nz, nx = grid_sizes(count)
    rowed = functools.partial(row_block, chunks=chunks, backward=True)
    shape = jax.ShapeDtypeStruct
    return pl.pallas_call(
        functools.partial(backward_kernel, heads, chunks, count),
        grid=(chunks,),
        in_specs=[
            pl.BlockSpec(memory_space=pltpu.SMEM),
            rowed(width),
            rowed(4 * width + 128),
            rowed(3 * width),
            rowed(width),
            rowed(width),
            pl.BlockSpec((heads, CHUNK, CHUNK), lambda i: (0, chunks - 1 - i, 0)),
            pl.BlockSpec((1, heads, HEAD, HEAD), lambda i: (chunks - 1 - i, 0, 0, 0)),
            whole_block((4, 3 * width)),
            whole_block((2, 128)),
            whole_block((1, HEAD)),
            whole_block(hidden.shape),
            whole_block(down_weight.shape),
            whole_block((own, features)),
            whole_block((own, 1)),
        ],
        out_specs=[
            rowed(4 * width + 128),
            whole_block((4, 3 * width)),
            whole_block((2, 128)),
            whole_block((1, HEAD)),
            whole_block((own, features)),
        ],
        out_shape=[
            shape((rows, 4 * width + 128), BF16),
            shape((4, 3 * width), F32),
            shape((2, 128), F32),
            shape((1, HEAD), F32),
            shape((own, features), BF16),
        ],
        scratch_shapes=[
            pltpu.VMEM((heads, HEAD, HEAD), F32),
            pltpu.VMEM((8, 3 * width), F32),
            *scatter_scratch(nz, nx, own, features, SCATTER_SHARE),
        ],
        compiler_params=linked(5),
        cost_estimate=lasting(100),
        name="mixer_backward",
    )(
        longer, grad, main, *saved, conv, params, gain, hidden, down_weight, middle, live
    )


MESH = pl.DeviceIdType.MESH
PIECES = 8


def grid_sizes(count):
    nz = 4 if count % 4 == 0 else 1
    return nz, count // nz


class Group:
    def __init__(self, count):
        self.deep, self.nx = grid_sizes(count)
        me = lax.axis_index("heads")
        self.z, self.x = me // self.nx, me % self.nx

    def column(self, j):
        return (self.x + j) % self.nx

    def over_x(self, j):
        return {"heads": self.z * self.nx + self.column(j)}

    def along_z(self, z):
        return {"heads": z * self.nx + self.x}


def meet(count, replicas=1):
    barrier = pltpu.get_barrier_semaphore()
    for axis, size in (("heads", count), ("dp", replicas)):
        me = lax.axis_index(axis)

        def greet(k, _, axis=axis, size=size, me=me):
            pl.semaphore_signal(
                barrier, inc=1, device_id={axis: (me + k) % size}, device_id_type=MESH
            )
            return 0

        lax.fori_loop(1, size, greet, 0)
    pl.semaphore_wait(barrier, count + replicas - 2)


def arrived(ref, sem):
    pltpu.make_async_copy(ref, ref, sem).wait()


def during(piece, work):
    pl.when((piece >= 0) & (piece < PIECES))(functools.partial(work, piece))


def push(source, target, send_sem, recv_sem, device):
    pltpu.make_async_remote_copy(
        source, target, send_sem, recv_sem, device_id=device, device_id_type=MESH
    ).start()


class Gather:
    def __init__(self, group, full, cols, sems, x_first):
        self.group, self.full, self.cols, self.x_first = group, full, cols, x_first
        self.part = full.shape[2] // PIECES
        self.line_send, self.line_recv, self.x_send, self.x_recv = sems
        self.last = group.deep

    @staticmethod
    def sems(deep, nx):
        dma = pltpu.SemaphoreType.DMA
        return [dma((PIECES, 2)), dma((PIECES, deep)), dma((PIECES, nx)), dma((PIECES, nx))]

    def at(self, piece, z, column):
        rows = pl.ds(pl.multiple_of(piece * self.part, self.part), self.part)
        return self.full.at[z, column, rows, self.cols]

    def columns(self):
        return slice(None) if self.x_first else self.group.x

    def push_line(self, piece, z, way, zz):
        place = self.at(piece, z, self.columns())
        push(
            place,
            place,
            self.line_send.at[piece, way],
            self.line_recv.at[piece, z],
            self.group.along_z(zz + (1 if way == 0 else -1)),
        )

    def push_x(self, piece, z):
        place = self.at(piece, z, self.group.x)
        for j in range(1, self.group.nx):
            push(
                place,
                place,
                self.x_send.at[piece, j],
                self.x_recv.at[piece, self.group.nx - j],
                self.group.over_x(j),
            )

    def own_line(self, piece, zz):
        if zz + 1 < self.group.deep:
            self.push_line(piece, zz, 0, zz)
        if zz > 0:
            self.push_line(piece, zz, 1, zz)

    def begin(self, piece):
        self.push_x(piece, self.group.z)
        if not self.x_first:
            group = self.group
            pl.when(group.z + 1 < group.deep)(lambda: self.push_line(piece, group.z, 0, group.z))
            pl.when(group.z > 0)(lambda: self.push_line(piece, group.z, 1, group.z))

    def phase(self, piece, step, zz):
        deep, nx = self.group.deep, self.group.nx
        if self.x_first:
            if step == 1:
                for j in range(1, nx):
                    arrived(self.at(piece, zz, self.group.column(j)), self.x_recv.at[piece, j])
                self.own_line(piece, zz)
                return
            step -= 1
        elif step == deep:
            for j in range(1, nx):
                place = self.at(piece, slice(None), self.group.column(j))
                arrived(place, self.x_recv.at[piece, j])
            return
        for z, way in ((zz - step, 0), (zz + step, 1)):
            if 0 <= z < deep:
                arrived(self.at(piece, z, self.columns()), self.line_recv.at[piece, z])
                if 0 <= zz + (1 if way == 0 else -1) < deep:
                    self.push_line(piece, z, way, zz)
                if not self.x_first:
                    self.push_x(piece, z)

    def drain(self, piece, zz):
        deep, nx = self.group.deep, self.group.nx
        if zz + 1 < deep:
            place = self.at(piece, pl.ds(0, zz + 1), self.columns())
            arrived(place, self.line_send.at[piece, 0])
        if zz > 0:
            place = self.at(piece, pl.ds(zz, deep - zz), self.columns())
            arrived(place, self.line_send.at[piece, 1])
        z = zz if self.x_first else slice(None)
        for j in range(1, nx):
            arrived(self.at(piece, z, self.group.x), self.x_send.at[piece, j])


class Scatter:
    last = 4

    def __init__(self, group, parts, cols, scratch, z_first):
        self.group, self.parts, self.cols, self.z_first = group, parts, cols, z_first
        self.part = parts.shape[2] // PIECES
        self.landed_x, self.line, *sems = scratch
        self.x_send, self.x_recv, self.z_send, self.z_recv = sems

    @staticmethod
    def scratch(deep, nx, rows, cols, z_first):
        dma = pltpu.SemaphoreType.DMA
        return [
            pltpu.VMEM((max(nx - 1, 1), 1 if z_first else deep, rows, cols), BF16),
            pltpu.VMEM((deep + 1, nx if z_first else 1, rows, cols), BF16),
            *[dma((PIECES, nx))] * 2,
            *[dma((PIECES, 2))] * 2,
        ]

    def rows(self, piece):
        return pl.ds(pl.multiple_of(piece * self.part, self.part), self.part)

    def columns(self):
        return slice(None) if self.z_first else pl.ds(self.group.x, 1)

    def at(self, piece, z, column):
        return self.parts.at[z, column, self.rows(piece), self.cols]

    def line_at(self, piece, way, zz):
        first, size = (zz + 1, self.group.deep - zz) if way == 0 else (0, zz + 1)
        return self.line.at[pl.ds(first, size), :, self.rows(piece)]

    def push_line(self, piece, way, zz):
        deep = self.group.deep
        first, size = (zz + 1, deep - 1 - zz) if way == 0 else (0, zz)
        if size == 0:
            return
        after = zz + 1 if way == 0 else zz - 1
        push(
            self.at(piece, pl.ds(first, size), self.columns()),
            self.line_at(piece, way, after),
            self.z_send.at[piece, way],
            self.z_recv.at[piece, way],
            self.group.along_z(after),
        )

    def ends(self, piece, zz):
        if zz == 0:
            self.push_line(piece, 0, zz)
        if zz == self.group.deep - 1:
            self.push_line(piece, 1, zz)

    def hand_on(self, piece, near, zz):
        deep = self.group.deep
        if zz == 0 or zz == deep - 1:
            return
        way = 0 if (zz < deep // 2) == near else 1
        arrived(self.line_at(piece, way, zz), self.z_recv.at[piece, way])
        first, size = (zz + 1, deep - 1 - zz) if way == 0 else (0, zz)
        shift = 1 if way == 0 else 0
        ours = self.at(piece, pl.ds(first, size), self.columns())
        landed = self.line.at[pl.ds(first + shift, size), :, self.rows(piece)]
        ours[...] = (ours[...].astype(F32) + landed[...].astype(F32)).astype(BF16)
        self.push_line(piece, way, zz)

    def wait_ends(self, piece, zz):
        deep = self.group.deep
        if deep == 1:
            return
        if zz == 0:
            arrived(self.line_at(piece, 1, zz), self.z_recv.at[piece, 1])
        if zz == deep - 1:
            arrived(self.line_at(piece, 0, zz), self.z_recv.at[piece, 0])

    def total_line(self, piece, column):
        group, rows = self.group, self.rows(piece)
        total = self.parts[group.z, column, rows, self.cols].astype(F32)
        index = column if self.z_first else 0
        for here, place in ((group.z > 0, group.z + 1), (group.z + 1 < group.deep, group.z)):
            landed = self.line[place, index, rows]
            total = total + jnp.where(here, landed.astype(F32), 0.0)
        return total

    def begin(self, piece):
        if not self.z_first:
            for j in range(1, self.group.nx):
                push(
                    self.at(piece, slice(None), self.group.column(j)),
                    self.landed_x.at[self.group.nx - j - 1, :, self.rows(piece)],
                    self.x_send.at[piece, j],
                    self.x_recv.at[piece, self.group.nx - j],
                    self.group.over_x(j),
                )

    def begin_line(self, piece, zz):
        if self.z_first:
            self.ends(piece, zz)

    def wait_x(self, piece, j):
        landed = self.landed_x.at[j - 1, :, self.rows(piece)]
        arrived(landed, self.x_recv.at[piece, j])
        return landed[...].astype(F32)

    def phase(self, piece, step, zz):
        nx = self.group.nx
        if self.z_first:
            if step < 3:
                self.hand_on(piece, step == 1, zz)
            elif step == 3:
                self.wait_ends(piece, zz)
            return
        if step == 1:
            ours = self.at(piece, slice(None), self.group.x)
            total = ours[...].astype(F32)
            for j in range(1, nx):
                total = total + self.wait_x(piece, j)
            ours[...] = total.astype(BF16)
            self.ends(piece, zz)
        elif step < 4:
            self.hand_on(piece, step == 2, zz)
        else:
            self.wait_ends(piece, zz)

    def third(self, piece):
        if not self.z_first:
            return
        group, rows = self.group, self.rows(piece)
        for j in range(1, group.nx):
            column = group.column(j)
            total = self.total_line(piece, column).astype(BF16)
            self.parts[group.z, column, rows, self.cols] = total
            push(
                self.at(piece, pl.ds(group.z, 1), column),
                self.landed_x.at[group.nx - j - 1, :, rows],
                self.x_send.at[piece, j],
                self.x_recv.at[piece, group.nx - j],
                group.over_x(j),
            )

    def total(self, piece):
        total = self.total_line(piece, self.group.x)
        if self.z_first:
            for j in range(1, self.group.nx):
                total = total + self.wait_x(piece, j)[0]
        return total

    def drain(self, piece, zz):
        deep = self.group.deep
        for way, size in ((0, deep - 1 - zz), (1, zz)):
            if size > 0:
                place = self.at(piece, pl.ds(0, size), self.columns())
                arrived(place, self.z_send.at[piece, way])
        z = pl.ds(0, 1 if self.z_first else deep)
        for j in range(1, self.group.nx):
            arrived(self.at(piece, z, self.group.x), self.x_send.at[piece, j])


class Both:
    def __init__(self, first, second):
        self.both = (first, second)
        self.group = first.group
        self.part, self.last = first.part, first.last

    def rows(self, piece):
        return pl.ds(pl.multiple_of(piece * self.part, self.part), self.part)

    def begin(self, piece):
        for each in self.both:
            each.begin(piece)

    def begin_line(self, piece, zz):
        for each in self.both:
            each.begin_line(piece, zz)

    def phase(self, piece, step, zz):
        for each in self.both:
            each.phase(piece, step, zz)

    def third(self, piece):
        for each in self.both:
            each.third(piece)

    def total(self, piece):
        return jnp.concatenate([each.total(piece) for each in self.both], axis=1)

    def drain(self):
        def at(zz):
            def one(piece, _):
                for each in self.both:
                    each.drain(piece, zz)
                return 0

            lax.fori_loop(0, PIECES, one, 0)

        at_each_z(self.group, at)


def at_each_z(group, work):
    for zz in range(group.deep):
        pl.when(group.z == zz)(functools.partial(work, zz))


def scatter_ticks(scatter, prepare, finish, after=None):
    def before(time):
        def begin(piece):
            prepare(piece)
            scatter.begin(piece)

        during(time + 1, begin)

    def within(time, zz):
        for step in range(scatter.last, 0, -1):
            during(time - step + 1, functools.partial(scatter.phase, step=step, zz=zz))
        during(time + 1, functools.partial(scatter.begin_line, zz=zz))

    def behind(time):
        during(time - 2, scatter.third)
        during(time - scatter.last + 1, lambda piece: finish(piece, scatter.total(piece)))

    return before, within, behind


def gather_ticks(gather, prepare, ready):
    def before(time):
        if prepare is not None:

            def begin(piece):
                prepare(piece)
                gather.begin(piece)

            during(time, begin)

    def within(time, zz):
        for step in range(gather.last, 0, -1):
            during(time - step, functools.partial(gather.phase, step=step, zz=zz))

    def behind(time):
        during(time - gather.last, ready)

    return before, within, behind


def cut(cols, share):
    edge = cols - cols * share // 8
    return pl.ds(0, edge), pl.ds(edge, cols - edge)


def gather_of(group, share, scratch):
    full, *sems = scratch
    first, second = cut(full.shape[3], share)
    return Both(
        Gather(group, full, first, sems[:4], False), Gather(group, full, second, sems[4:], True)
    )


def scatter_of(group, share, scratch):
    parts, *rest = scratch
    first, second = cut(parts.shape[3], share)
    return Both(
        Scatter(group, parts, first, rest[:6], False),
        Scatter(group, parts, second, rest[6:], True),
    )


def gather_scratch(nz, nx, rows, cols):
    return [pltpu.VMEM((nz, nx, rows, cols), BF16), *Gather.sems(nz, nx), *Gather.sems(nz, nx)]


def scatter_scratch(nz, nx, rows, cols, share):
    first, second = cut(cols, share)
    return [
        pltpu.VMEM((nz, nx, rows, cols), BF16),
        *Scatter.scratch(nz, nx, rows, first.size, False),
        *Scatter.scratch(nz, nx, rows, second.size, True),
    ]


SCATTER_COUNT, GATHER_COUNT = 13, 9


def inverse_rms(rows):
    return lax.rsqrt(jnp.mean(rows * rows, axis=-1, keepdims=True) + EPS)


def wide_dot(terms, dims, tile, store):
    total = terms[0][1].shape[0 if dims is NT else 1]
    for first in range(0, total, tile):
        cols = slice(first, min(first + tile, total))
        products = [
            lax.dot_general(
                left,
                right[cols, :] if dims is NT else right[:, cols],
                (dims, ((), ())),
                preferred_element_type=F32,
            )
            for left, right in terms
        ]
        store(cols, functools.reduce(jnp.add, products))


VMEM_SPEC = pl.BlockSpec(memory_space=pltpu.VMEM)
ANY_SPEC = pl.BlockSpec(memory_space=pl.ANY)
PAIR_SHARE, GATHER_SHARE, SCATTER_SHARE = 2, 1, 2


class Late:
    def __init__(self, given, held, sem):
        self.held = held
        self.copy = pltpu.make_async_copy(given, held, sem)
        self.copy.start()

    def wait(self):
        self.copy.wait()


def late_all(given, scratch):
    return [
        Late(ref, held, sem)
        for ref, held, sem in zip(given, scratch[: len(given)], scratch[len(given) :])
    ]


def late_scratch(*values):
    return [
        *[pltpu.VMEM(value.shape, value.dtype) for value in values],
        *[pltpu.SemaphoreType.DMA] * len(values),
    ]


def lasting(microseconds):
    return pl.CostEstimate(
        flops=int(microseconds * 1.1e9), bytes_accessed=2**20, transcendentals=0
    )


def linked(collective):
    return pltpu.CompilerParams(
        collective_id=collective, has_side_effects=True, vmem_limit_bytes=62 * 2**20
    )


def joined(values):
    return values.reshape(-1, values.shape[-1])


def split(values, *parts):
    return values.reshape(*parts, values.shape[0] // math.prod(parts), values.shape[1])


def project_kernel(
    count, rows_ref, gain_ref, weight_ref, gates_ref, full_out, projected_out, weight_out, *scratch
):
    full = scratch[0]
    staged, full_sems, staged_sems, given, weight, given_sem, out_sem = scratch[GATHER_COUNT:]
    late = Late(weight_ref, given, given_sem)
    group = Group(count)
    gather = gather_of(group, GATHER_SHARE, scratch[:GATHER_COUNT])
    meet(count)
    weight_copy = pltpu.make_async_copy(weight, weight_out, out_sem)
    kinds, width = given.shape[1:]
    blocks = given.shape[0] // 256
    shares, share = full_out.shape[0], full_out.shape[4]

    def full_copy(piece, index):
        rows = gather.rows(piece)
        return pltpu.make_async_copy(
            full.at[:, :, rows, pl.ds(index * share, share)],
            full_out.at[index, :, :, rows],
            full_sems.at[piece, index],
        )

    def staged_copy(piece):
        rows = gather.rows(piece)
        return pltpu.make_async_copy(
            staged.at[:, rows], projected_out.at[:, rows], staged_sems.at[piece]
        )

    def prepare(piece):
        rows = rows_ref[gather.rows(piece)].astype(F32)
        full[group.z, group.x, gather.rows(piece)] = (
            rows * inverse_rms(rows) * gain_ref[...]
        ).astype(BF16)

    def ready(piece):
        rows = gather.rows(piece)
        for index in range(shares):
            full_copy(piece, index).start()

        def store(cols, value):
            staged[:, rows, cols] = split(value, count)

        left = joined(full[:, :, rows])
        wide_dot([(left, weight)], NN, 256, store)
        value = lax.dot_general(
            left, gates_ref[...], (NN, ((), ())), preferred_element_type=F32
        )
        staged[:, rows, kinds * width :] = split(value, count)
        staged_copy(piece).start()

    before, within, behind = gather_ticks(gather, prepare, ready)

    def lay_out(block, _):
        rows = pl.ds(pl.multiple_of(block * 256, 256), 256)
        for kind in range(kinds):
            weight[rows, kind * width : (kind + 1) * width] = given[rows, kind, :]
        return 0

    def tick(time, _):
        before(time)
        pl.when(time == 0)(late.wait)
        lax.fori_loop(
            jnp.minimum(time * 2, blocks), jnp.minimum(time * 2 + 2, blocks), lay_out, 0
        )
        pl.when(time == 4)(weight_copy.start)
        at_each_z(group, functools.partial(within, time))
        behind(time)
        return 0

    lax.fori_loop(0, PIECES + gather.last, tick, 0)
    gather.drain()
    weight_copy.wait()

    def finish(piece, _):
        for index in range(shares):
            full_copy(piece, index).wait()
        staged_copy(piece).wait()
        return 0

    lax.fori_loop(0, PIECES, finish, 0)


def project(rows, gain, weight, gates, count, shares):
    own, features = rows.shape
    kinds, width = weight.shape[1:]
    cols = kinds * width + gates.shape[1]
    nz, nx = grid_sizes(count)
    return pl.pallas_call(
        functools.partial(project_kernel, count),
        out_shape=[
            jax.ShapeDtypeStruct((shares, nz, nx, own, features // shares), BF16),
            jax.ShapeDtypeStruct((count, own, cols), F32),
            jax.ShapeDtypeStruct((features, kinds * width), BF16),
        ],
        in_specs=[VMEM_SPEC, VMEM_SPEC, ANY_SPEC, VMEM_SPEC],
        out_specs=[ANY_SPEC] * 3,
        scratch_shapes=[
            *gather_scratch(nz, nx, own, features),
            pltpu.VMEM((count, own, cols), F32),
            pltpu.SemaphoreType.DMA((PIECES, shares)),
            pltpu.SemaphoreType.DMA((PIECES,)),
            pltpu.VMEM(weight.shape, BF16),
            pltpu.VMEM((features, kinds * width), BF16),
            *[pltpu.SemaphoreType.DMA] * 2,
        ],
        compiler_params=linked(0),
        cost_estimate=lasting(100),
        name="project",
    )(rows, gain, weight, gates)


def sum_and_gather(scatter, gather, prepare, middle, ready, job=None):
    group = gather.group
    full = gather.both[0].full

    def turn(piece, total):
        full[group.z, group.x, gather.rows(piece)] = middle(piece, total).astype(BF16)
        gather.begin(piece)

    late = scatter.last - 1
    before, sum_within, sum_behind = scatter_ticks(scatter, prepare, turn)
    _, gather_within, gather_behind = gather_ticks(gather, None, ready)

    def tick(time, _):
        before(time)

        def within(zz):
            gather_within(time - late, zz)
            sum_within(time, zz)

        at_each_z(group, within)
        sum_behind(time)
        gather_behind(time - late)
        if job is not None:
            job(time + 1)
        return 0

    lax.fori_loop(-1, PIECES + late + gather.last, tick, 0)
    scatter.drain()
    gather.drain()


def branch_kernel(
    count, mixed_ref, weight_ref, input_ref, live_ref, gain_ref, feed_weight_ref,
    down_weight_ref, grad_ref, middle_out, full_out, dgate_out, dup_out, hidden_out, *all_scratch
):
    *scratch, grads, grad_sems, dgate, dup, hidden, feed_sems = all_scratch[:-4]
    lates = late_all((feed_weight_ref, down_weight_ref), all_scratch[-4:])
    feed_weight_ref, down_weight_ref = (late.held for late in lates)
    group = Group(count)
    scatter = scatter_of(group, PAIR_SHARE, scratch[:SCATTER_COUNT])
    gather = gather_of(group, PAIR_SHARE, scratch[SCATTER_COUNT:])
    parts, full = scratch[0], scratch[SCATTER_COUNT]

    def fetch(piece):
        slot = piece % 2
        return pltpu.make_async_copy(
            grad_ref.at[:, :, gather.rows(piece)], grads.at[slot], grad_sems.at[slot]
        )

    fetch(0).start()
    meet(count)

    def prepare(piece):
        rows = gather.rows(piece)

        def store(cols, value):
            parts[:, :, rows, cols] = split(value.astype(BF16), group.deep, group.nx)

        wide_dot([(joined(mixed_ref[:, rows]), weight_ref)], NN, 512, store)

    def middle(piece, total):
        rows = gather.rows(piece)
        values = input_ref[rows].astype(F32) + live_ref[rows] * total
        middle_out[rows] = values
        return values * inverse_rms(values) * gain_ref[...]

    def copies(piece):
        rows = gather.rows(piece)
        return [
            pltpu.make_async_copy(ref.at[:, rows], out.at[:, rows], feed_sems.at[piece, index])
            for index, (ref, out) in enumerate(
                ((dgate, dgate_out), (dup, dup_out), (hidden, hidden_out))
            )
        ] + [
            pltpu.make_async_copy(
                full.at[:, :, rows], full_out.at[:, :, rows], feed_sems.at[piece, 3]
            )
        ]

    def ready(piece):
        rows = gather.rows(piece)
        for late in lates:
            pl.when(piece == 0)(late.wait)
        fetch(piece).wait()
        pl.when(piece + 1 < PIECES)(lambda: fetch(piece + 1).start())
        left, grad = joined(full[:, :, rows]), joined(grads[piece % 2])
        total = feed_weight_ref.shape[1]
        for first in range(0, total, 256):
            cols = slice(first, min(first + 256, total))

            def product(a, b, dims):
                return lax.dot_general(a, b, (dims, ((), ())), preferred_element_type=F32)

            gate = product(left, feed_weight_ref[0, cols], NT)
            up = product(left, feed_weight_ref[1, cols], NT)
            dhidden = product(grad, down_weight_ref[cols, :], NT)
            sigmoid = jax.nn.sigmoid(gate)
            active = gate * sigmoid
            hidden[:, rows, cols] = split((active * up).astype(BF16), count)
            dup[:, rows, cols] = split((dhidden * active).astype(BF16), count)
            slope = sigmoid * (1.0 + gate * (1.0 - sigmoid))
            dgate[:, rows, cols] = split((dhidden * up * slope).astype(BF16), count)
        for copy in copies(piece):
            copy.start()

    sum_and_gather(scatter, gather, prepare, middle, ready)

    def finish(piece, _):
        for copy in copies(piece):
            copy.wait()
        return 0

    lax.fori_loop(0, PIECES, finish, 0)


def branch_and_feed(mixed, weight, rows, live, gain, feed_weight, down_weight, grad, count):
    own, features = rows.shape
    hidden = feed_weight.shape[1]
    nz, nx = grid_sizes(count)
    return pl.pallas_call(
        functools.partial(branch_kernel, count),
        out_shape=[
            jax.ShapeDtypeStruct((own, features), F32),
            jax.ShapeDtypeStruct((nz, nx, own, features), BF16),
            *[jax.ShapeDtypeStruct((count, own, hidden), BF16)] * 3,
        ],
        in_specs=[VMEM_SPEC] * 5 + [ANY_SPEC] * 3,
        out_specs=[VMEM_SPEC] + [ANY_SPEC] * 4,
        scratch_shapes=[
            *scatter_scratch(nz, nx, own, features, PAIR_SHARE),
            *gather_scratch(nz, nx, own, features),
            pltpu.VMEM((2, nz, nx, own // PIECES, features), BF16),
            pltpu.SemaphoreType.DMA((2,)),
            *[pltpu.VMEM((count, own, hidden), BF16)] * 3,
            pltpu.SemaphoreType.DMA((PIECES, 4)),
            *late_scratch(feed_weight, down_weight),
        ],
        compiler_params=linked(1),
        cost_estimate=lasting(180),
        name="branch_and_feed",
    )(split(mixed, count), weight, rows, live, gain, feed_weight, down_weight, grad)


TILE = 256


class TileJob:
    def __init__(self, rows_ref, tile, factors, staged, outs, fetch_sem, out_sems):
        self.rows_ref, self.tile, self.factors = rows_ref, tile, factors
        self.staged, self.outs = staged, outs
        self.fetch_sem, self.out_sems = fetch_sem, out_sems
        self.count = rows_ref.shape[3] // TILE

    def span(self, index):
        return pl.ds(pl.multiple_of(index * TILE, TILE), TILE)

    def fetch(self, index):
        return pltpu.make_async_copy(
            self.rows_ref.at[:, :, :, self.span(index)], self.tile, self.fetch_sem
        )

    def results(self, index):
        return [
            pltpu.make_async_copy(
                self.staged.at[which], out.at[:, self.span(index)], self.out_sems.at[which]
            )
            for which, out in enumerate(self.outs)
        ]

    def wait_results(self, index):
        for copy in self.results(index):
            copy.wait()

    def run(self, index):
        self.fetch(index).wait()
        left = joined(self.tile[...])
        pl.when(index > 0)(lambda: self.wait_results(index - 1))
        for which, factor in enumerate(self.factors):
            product = lax.dot_general(
                left, joined(factor[...]), (TN, ((), ())), preferred_element_type=F32
            )
            self.staged[which] = jnp.transpose(product).astype(BF16)
        for copy in self.results(index):
            copy.start()
        pl.when(index + 1 < self.count)(lambda: self.fetch(index + 1).start())


def feed_back_kernel(
    count, dgate_ref, dup_ref, feed_weight_ref, top_ref, middle_ref, live_ref,
    gain_ref, out_weight_ref, mixed_ref, hidden_ref, normed_ref, grad_feed_ref,
    dmiddle_out, dgain_out, dmixed_out, dweight_out, dfeed_out, *all_scratch
):
    lates = late_all((out_weight_ref, mixed_ref, hidden_ref), all_scratch[-6:])
    out_weight_ref, mixed_ref, hidden_ref = (late.held for late in lates)
    *scratch, total_out, tile, grad_tile, staged, grad_staged, fetch_sems, out_sems = (
        all_scratch[:-6]
    )
    group = Group(count)
    scatter = scatter_of(group, PAIR_SHARE, scratch[:SCATTER_COUNT])
    gather = gather_of(group, PAIR_SHARE, scratch[SCATTER_COUNT:])
    parts, full = scratch[0], scratch[SCATTER_COUNT]
    jobs = (
        TileJob(
            normed_ref, tile, (dgate_ref, dup_ref), staged, (dfeed_out.at[0], dfeed_out.at[1]),
            fetch_sems.at[0], out_sems.at[0],
        ),
        TileJob(
            grad_feed_ref, grad_tile, (hidden_ref,), grad_staged, (dfeed_out.at[2],),
            fetch_sems.at[1], out_sems.at[1],
        ),
    )
    for each in jobs:
        each.fetch(0).start()
    meet(count)
    dgain_out[...] = jnp.zeros(dgain_out.shape, F32)
    total_out[...] = jnp.zeros(total_out.shape, F32)

    def prepare(piece):
        rows = gather.rows(piece)

        def store(cols, value):
            parts[:, :, rows, cols] = split(value.astype(BF16), group.deep, group.nx)

        wide_dot(
            [
                (joined(dgate_ref[:, rows]), feed_weight_ref.at[0]),
                (joined(dup_ref[:, rows]), feed_weight_ref.at[1]),
            ],
            NN,
            256,
            store,
        )

    def middle(piece, dnormed):
        rows = gather.rows(piece)
        values = middle_ref[rows]
        scale = inverse_rms(values)
        normed = values * scale
        dgain_out[...] += jnp.sum(dnormed * normed, axis=0, keepdims=True)
        scaled = dnormed * gain_ref[...]
        dmiddle = top_ref[rows].astype(F32) + scale * (
            scaled - normed * jnp.mean(scaled * normed, axis=-1, keepdims=True)
        )
        dmiddle_out[rows] = dmiddle
        return live_ref[rows] * dmiddle

    def ready(piece):
        rows = gather.rows(piece)
        for late in lates[:2]:
            pl.when(piece == 0)(late.wait)
        left, mixed = joined(full[:, :, rows]), joined(mixed_ref[:, rows])

        def store(cols, value):
            dmixed_out[:, rows, cols] = split(value, count)

        wide_dot([(left, out_weight_ref)], NT, 256, store)
        for first in range(0, left.shape[1], 256):
            total_out[first : first + 256] += lax.dot_general(
                left[:, first : first + 256], mixed, (TN, ((), ())), preferred_element_type=F32
            )

    def job(time):
        pl.when(time == 1)(lates[2].wait)
        for which, each in enumerate(jobs):
            pl.when((time % 2 == which) & (time < 2 * each.count))(
                functools.partial(each.run, time // 2)
            )

    sum_and_gather(scatter, gather, prepare, middle, ready, job)
    last = PIECES + scatter.last + gather.last
    lax.fori_loop(last, max(2 * jobs[0].count, last), lambda time, _: (job(time), 0)[1], 0)
    for each in jobs:
        each.wait_results(each.count - 1)
    dweight_out[...] = total_out[...].astype(BF16)


def feed_back(
    dgate, dup, feed_weight, top, middle, live, gain, out_weight, mixed, hidden, normed, grad_feed,
    count,
):
    own, features = middle.shape
    nz, nx = grid_sizes(count)
    width, units = out_weight.shape[0], feed_weight.shape[1]
    return pl.pallas_call(
        functools.partial(feed_back_kernel, count),
        out_shape=[
            jax.ShapeDtypeStruct((own, features), F32),
            jax.ShapeDtypeStruct((1, features), F32),
            jax.ShapeDtypeStruct((count, own, width), F32),
            jax.ShapeDtypeStruct((features, width), BF16),
            jax.ShapeDtypeStruct((3, units, features), BF16),
        ],
        in_specs=[VMEM_SPEC] * 7 + [ANY_SPEC] * 5,
        out_specs=[VMEM_SPEC] * 4 + [ANY_SPEC],
        scratch_shapes=[
            *scatter_scratch(nz, nx, own, features, PAIR_SHARE),
            *gather_scratch(nz, nx, own, features),
            pltpu.VMEM((features, width), F32),
            pltpu.VMEM((nz, nx, own, TILE), BF16),
            pltpu.VMEM((nz, nx, own, TILE), BF16),
            pltpu.VMEM((2, units, TILE), BF16),
            pltpu.VMEM((1, units, TILE), BF16),
            pltpu.SemaphoreType.DMA((2,)),
            pltpu.SemaphoreType.DMA((2, 2)),
            *late_scratch(out_weight, split(mixed, count), hidden),
        ],
        compiler_params=linked(2),
        cost_estimate=lasting(180),
        name="feed_back",
    )(
        dgate, dup, feed_weight, top, middle, live, gain, out_weight,
        split(mixed, count), hidden, normed, grad_feed,
    )


class Replicas:
    def __init__(self, values, from_core, from_y, over_back, over_home, sems):
        self.values, self.from_core, self.from_y = values, from_core, from_y
        self.over_back, self.over_home = over_back, over_home
        self.core_sems, self.y_sems, self.back_sems, self.home_sems = sems
        me = lax.axis_index("dp")
        self.lines = lax.axis_size("dp") // 2
        self.y, self.core = me // 2, me % 2

    @staticmethod
    def scratch(rows, cols, replicas):
        lines, share = replicas // 2, rows // replicas
        return [
            pltpu.VMEM((replicas, share, cols), BF16),
            pltpu.VMEM((lines, share, cols), BF16),
            pltpu.VMEM((max(lines - 1, 1), share, cols), BF16),
            pltpu.VMEM((max(lines - 1, 1), share, cols), BF16),
            pltpu.VMEM((lines, share, cols), BF16),
            *[pltpu.SemaphoreType.DMA((2, lines))] * 4,
        ]

    def share(self, core, y):
        return core * self.lines + y

    def peer(self, y, core):
        return {"dp": y * 2 + core}

    def line(self, k):
        return (self.y + k) % self.lines

    draining = False

    def push(self, source, target, send_sem, recv_sem, device):
        copy = pltpu.make_async_remote_copy(
            source, target, send_sem, recv_sem, device_id=device, device_id_type=MESH
        )
        if self.draining:
            copy.wait_send()
        else:
            copy.start()

    def drain(self):
        self.draining = True
        for k in range(self.lines):
            self.start(k)
            self.cores(k)
        self.over_y()
        self.back()
        self.draining = False

    def add(self, share, others):
        step = 64

        def some(block, _):
            rows = pl.ds(pl.multiple_of(block * step, step), step)
            total = self.values[share, rows].astype(F32)
            for ref, index in others:
                total = total + ref[index, rows].astype(F32)
            self.values[share, rows] = total.astype(BF16)
            return 0

        lax.fori_loop(0, self.values.shape[1] // step, some, 0)

    def start(self, k):
        y = self.line(k)
        self.push(
            self.values.at[self.share(1 - self.core, y)],
            self.from_core.at[y],
            self.core_sems.at[0, k],
            self.core_sems.at[1, k],
            self.peer(self.y, 1 - self.core),
        )

    def cores(self, k):
        y = self.line(k)
        share = self.share(self.core, y)
        if not self.draining:
            arrived(self.from_core.at[y], self.core_sems.at[1, k])
            self.add(share, [(self.from_core, y)])
        if k > 0:
            self.push(
                self.values.at[share],
                self.from_y.at[self.lines - k - 1],
                self.y_sems.at[0, k],
                self.y_sems.at[1, self.lines - k],
                self.peer(y, self.core),
            )

    def over_y(self):
        share = self.share(self.core, self.y)
        if not self.draining:
            for k in range(1, self.lines):
                arrived(self.from_y.at[k - 1], self.y_sems.at[1, k])
            self.add(share, [(self.from_y, k) for k in range(self.lines - 1)])
        for k in range(1, self.lines):
            self.push(
                self.values.at[share],
                self.over_back.at[self.lines - k - 1],
                self.back_sems.at[0, k],
                self.back_sems.at[1, self.lines - k],
                self.peer(self.line(k), self.core),
            )
        self.send_home(0)

    def own(self, k):
        return self.values.at[self.share(self.core, self.y)] if k == 0 else self.over_back.at[k - 1]

    def send_home(self, k):
        self.push(
            self.own(k),
            self.over_home.at[k],
            self.home_sems.at[0, k],
            self.home_sems.at[1, k],
            self.peer(self.y, 1 - self.core),
        )

    def back(self):
        for k in range(1, self.lines):
            if not self.draining:
                arrived(self.over_back.at[k - 1], self.back_sems.at[1, k])
            self.send_home(k)

    def home(self):
        for k in range(self.lines):
            arrived(self.over_home.at[k], self.home_sems.at[1, k])

    def totals(self):
        for k in range(self.lines):
            yield self.own(k), self.share(self.core, self.line(k))
            yield self.over_home.at[k], self.share(1 - self.core, self.line(k))


def sum_small(small, seen, send_sems, recv_sems, axis, rows):
    me, size = lax.axis_index(axis), lax.axis_size(axis)
    copies = []
    seen[me] = small[...]
    for k in range(1, size):
        copy = pltpu.make_async_remote_copy(
            seen.at[me], seen.at[me], send_sems.at[k], recv_sems.at[size - k],
            device_id={axis: (me + k) % size}, device_id_type=MESH,
        )
        copy.start()
        copies.append(copy)
    for k in range(1, size):
        arrived(seen.at[(me + k) % size], recv_sems.at[k])
    total = seen[0]
    for other in range(1, size):
        total = total + seen[other]
    small[...] = jnp.where(grid_index(total.shape, 0) < rows, total, small[...])
    return copies


def input_back_kernel(
    count, grad_ref, weight_ref, gates_ref, later_ref, input_ref, gain_ref, dgain_ref, dnorm_ref,
    dtaps_ref, dparams_ref, wout_ref, normed_ref, grad_out, norm1_out, norm2_out, gain_out,
    taps_out, params_out, dmain_out, drest_out, *scratch
):
    *scratch, small_out, normed, normed_sem = scratch
    late = Late(normed_ref, normed, normed_sem)
    normed_ref = normed
    parts, rest = scratch[0], scratch[SCATTER_COUNT:]
    values = rest[0]
    near, near_send, near_recv, far, far_send, far_recv, staged, out_sems = rest[9:]
    group = Group(count)
    scatter = scatter_of(group, SCATTER_SHARE, scratch[:SCATTER_COUNT])
    replicas = Replicas(*rest[:5], rest[5:9])
    meet(count, lax.axis_size("dp"))
    small_out[...] = jnp.zeros(small_out.shape, F32)
    small_out[1:2] = dnorm_ref[...]
    small_out[2:3, : dgain_ref.shape[1]] = dgain_ref[...]
    small_out[3:7, : dtaps_ref.shape[1]] = dtaps_ref[...]
    for row in range(2):
        small_out[7:8, 128 * row : 128 * (row + 1)] = dparams_ref[row : row + 1]
    width = grad_ref.shape[2]
    values[:, :, width:] = split(wout_ref[...], values.shape[0])

    def prepare(piece):
        rows = scatter.rows(piece)

        def store(cols, value):
            parts[:, :, rows, cols] = split(value.astype(BF16), group.deep, group.nx)

        left, edge = joined(grad_ref[:, rows]), weight_ref.shape[1]
        wide_dot(
            [(left[:, :edge], weight_ref), (left[:, edge:], gates_ref)], NT, 256, store
        )

    def end(piece, dnormed):
        rows = scatter.rows(piece)
        given = input_ref[rows].astype(F32)
        scale = inverse_rms(given)
        normed = given * scale
        small_out[0:1] += jnp.sum(dnormed * normed, axis=0, keepdims=True)
        scaled = dnormed * gain_ref[...]
        grad_out[rows] = later_ref[rows] + scale * (
            scaled - normed * jnp.mean(scaled * normed, axis=-1, keepdims=True)
        )

    def weight_share(core, y, first=False):
        if first:
            late.wait()
        share = replicas.share(core, y)
        left = joined(normed_ref[share])
        grads = joined(grad_ref[...])
        for first in range(0, width, 384):
            cols = slice(first, min(first + 384, width))
            staged[:, cols] = lax.dot_general(
                left, grads[:, cols], (TN, ((), ())), preferred_element_type=F32
            ).astype(BF16)

        def some(block, _):
            rows = pl.ds(pl.multiple_of(block * 64, 64), 64)
            values[share, rows, :width] = staged[rows]
            return 0

        lax.fori_loop(0, staged.shape[0] // 64, some, 0)

    def other_core(k):
        weight_share(1 - replicas.core, replicas.line(k), k == replicas.lines - 1)
        replicas.start(k)

    def this_core(k):
        weight_share(replicas.core, replicas.line(k))
        replicas.cores(k)

    steps = []
    for k in range(replicas.lines - 1, -1, -1):
        steps += [functools.partial(other_core, k), functools.partial(this_core, k)]
    while len(steps) < 5:
        steps.append(lambda: None)
    steps.append(replicas.over_y)

    before, within, behind = scatter_ticks(scatter, prepare, end)

    def tick(time, _):
        before(time)
        at_each_z(group, functools.partial(within, time))
        behind(time)
        for index, step in enumerate(steps):
            pl.when(time == index)(step)
        return 0

    lax.fori_loop(-1, max(PIECES + scatter.last - 1, len(steps)), tick, 0)
    replicas.back()
    copies = sum_small(small_out, near, near_send, near_recv, "heads", 3)
    copies += sum_small(small_out, far, far_send, far_recv, "dp", 8)
    norm1_out[...] = small_out[0:1]
    norm2_out[...] = small_out[1:2]
    gain_out[...] = small_out[2:3, : gain_out.shape[1]]
    kind_width = taps_out.shape[2]
    for kind in range(taps_out.shape[0]):
        taps_out[kind] = small_out[3:7, kind * kind_width : (kind + 1) * kind_width]
    for row in range(2):
        params_out[row : row + 1] = small_out[7:8, 128 * row : 128 * (row + 1)]
    replicas.home()
    part = dmain_out.shape[3]
    outs = []
    for index, (total, share) in enumerate(replicas.totals()):
        for kind in range(4):
            outs.append((total.at[:, pl.ds(kind * part, part)], dmain_out.at[kind, share], index))
        rest_cols = pl.ds(4 * part, drest_out.shape[2])
        outs.append((total.at[:, rest_cols], drest_out.at[share], index))
    outs = [
        pltpu.make_async_copy(source, target, out_sems.at[index, place % 5])
        for place, (source, target, index) in enumerate(outs)
    ]
    for copy in outs:
        copy.start()
    scatter.drain()
    replicas.drain()
    for copy in copies:
        copy.wait_send()
    for copy in outs:
        copy.wait()


def input_back(
    grad, weight, gates, later, rows, gain, dgain, dnorm, dtaps, dparams, grad_wout, normed, count,
    replica_count,
):
    own, features = rows.shape
    nz, nx = grid_sizes(count)
    width, share = grad_wout.shape[1], features // replica_count
    cols = grad.shape[1] + width
    dma = pltpu.SemaphoreType.DMA
    return pl.pallas_call(
        functools.partial(input_back_kernel, count),
        out_shape=[
            jax.ShapeDtypeStruct((own, features), F32),
            *[jax.ShapeDtypeStruct((1, features), F32)] * 2,
            jax.ShapeDtypeStruct(dgain.shape, F32),
            jax.ShapeDtypeStruct((3, 4, width), F32),
            jax.ShapeDtypeStruct(dparams.shape, F32),
            jax.ShapeDtypeStruct((4, replica_count, share, width), BF16),
            jax.ShapeDtypeStruct((replica_count, share, cols - 4 * width), BF16),
        ],
        in_specs=[VMEM_SPEC] * 11 + [ANY_SPEC],
        out_specs=[VMEM_SPEC] * 6 + [ANY_SPEC] * 2,
        scratch_shapes=[
            *scatter_scratch(nz, nx, own, features, SCATTER_SHARE),
            *Replicas.scratch(features, cols, replica_count),
            pltpu.VMEM((count, 8, features), F32),
            dma((count,)),
            dma((count,)),
            pltpu.VMEM((replica_count, 8, features), F32),
            dma((replica_count,)),
            dma((replica_count,)),
            pltpu.VMEM((share, grad.shape[1]), BF16),
            dma((replica_count, 5)),
            pltpu.VMEM((8, features), F32),
            pltpu.VMEM(normed.shape, BF16),
            dma,
        ],
        compiler_params=linked(3),
        cost_estimate=lasting(120),
        name="input_back",
    )(
        split(grad, count), weight, gates, later, rows, gain, dgain, dnorm, dtaps, dparams,
        grad_wout, normed,
    )


def spread_kernel(given_ref, out_ref):
    for kind in range(given_ref.shape[0]):
        out_ref[:, kind, :] = given_ref[kind].astype(F32)


def by_rows(values):
    kinds, rows, cols = values.shape
    return pl.pallas_call(
        spread_kernel,
        grid=(rows // 256,),
        in_specs=[pl.BlockSpec((kinds, 256, cols), lambda i: (0, i, 0))],
        out_specs=pl.BlockSpec((256, kinds, cols), lambda i: (i, 0, 0)),
        out_shape=jax.ShapeDtypeStruct((rows, kinds, cols), F32),
        name="by_rows",
    )(values)


def on_device(
    block_in,
    seq_counts,
    norm1_gain,
    w_qkvg,
    conv_weight,
    w_gates,
    gate_params,
    out_gain,
    w_out,
    norm2_gain,
    w_gate_up,
    w_down,
    cotangent,
):
    own_rows, features = block_in.shape
    count = lax.axis_size("heads")
    all_rows = own_rows * count
    width = conv_weight.shape[2]
    heads = gate_params.shape[1]
    longer = seq_counts[0, 1:2]
    first_row = lax.axis_index("heads") * own_rows
    row_index = first_row + jnp.arange(own_rows, dtype=jnp.int32)
    live_own = jnp.where(longer[0] > 0, True, row_index < seq_counts[0, 0] * SEQ_SHORT)
    live_own = live_own.astype(F32)[:, None]
    gates_weight = jnp.pad(
        w_gates.reshape(features, 2 * heads), ((0, 0), (0, 128 - 2 * heads))
    )
    full_normed1, projected, weight = project(
        block_in, norm1_gain[None], w_qkvg, gates_weight, count, lax.axis_size("dp")
    )
    projected = projected.reshape(all_rows, -1)
    taps = jnp.transpose(conv_weight, (1, 0, 2)).reshape(4, 3 * width)
    params = jnp.pad(gate_params, ((0, 0), (0, 128 - heads)))
    gain_row = out_gain[None]
    mixed, *saved, grad_feed = mixer_forward(
        longer, projected, taps, params, gain_row, cotangent, live_own, count
    )
    feed_weight = jnp.transpose(w_gate_up, (1, 2, 0))
    middle, full_normed2, grad_gate, grad_up, hidden = branch_and_feed(
        mixed,
        w_out,
        block_in,
        live_own,
        norm2_gain[None],
        feed_weight,
        w_down,
        grad_feed,
        count,
    )
    grad_middle, grad_gain2, grad_mixed, grad_wout, early = feed_back(
        grad_gate,
        grad_up,
        feed_weight,
        cotangent,
        middle,
        live_own,
        norm2_gain[None],
        w_out,
        mixed,
        hidden,
        full_normed2,
        grad_feed,
        count,
    )
    early = lax.psum(early, "dp")
    dprojected, dtaps, dparams, dgain, layer_out = mixer_backward(
        longer,
        grad_mixed.reshape(all_rows, width),
        projected,
        saved,
        taps,
        params,
        gain_row,
        hidden,
        w_down,
        middle,
        live_own,
        count,
    )

    grad_in, grad_gain1, grad_gain2, dgain, grad_conv, dparams, grad_main, grad_rest = input_back(
        dprojected,
        weight,
        gates_weight,
        grad_middle,
        block_in,
        norm1_gain[None],
        dgain,
        grad_gain2,
        dtaps,
        dparams,
        grad_wout,
        full_normed1,
        count,
        lax.axis_size("dp"),
    )
    grad_main = grad_main.reshape(4, features, width)
    grad_rest = grad_rest.reshape(features, -1)
    return (
        layer_out,
        grad_in,
        grad_gain1[0],
        by_rows(grad_main),
        grad_conv,
        grad_rest[:, : 2 * heads].reshape(w_gates.shape).astype(F32),
        dparams[:, :heads],
        dgain[0],
        grad_rest[:, 128:].T.astype(F32),
        grad_gain2[0],
        jnp.transpose(early[:2].astype(F32), (2, 0, 1)),
        early[2].astype(F32),
    )


def solution(mesh):
    return jax.shard_map(
        on_device,
        mesh=mesh,
        in_specs=(
            P(("dp", "heads"), None),
            P("dp", None),
            P(),
            P(None, None, "heads"),
            P(None, None, "heads"),
            P(None, None, "heads"),
            P(None, "heads"),
            P(),
            P("heads", None),
            P(),
            P(None, None, "heads"),
            P("heads", None),
            P(("dp", "heads"), None),
        ),
        out_specs=(
            P(("dp", "heads"), None),
            P(("dp", "heads"), None),
            P(),
            P(None, None, "heads"),
            P(None, None, "heads"),
            P(None, None, "heads"),
            P(None, "heads"),
            P(),
            P("heads", None),
            P(),
            P(None, None, "heads"),
            P("heads", None),
        ),
        check_vma=False,
    )
```

```python
import functools
import math
import jax
import jax.numpy as jnp
from jax import lax
from jax.experimental import pallas as pl
from jax.experimental.pallas import tpu as pltpu
from jax.sharding import PartitionSpec as P

SEQ_SHORT = 512
CHUNK = 256
HEAD = 128
EPS = 1e-06
F32 = jnp.float32
BF16 = jnp.bfloat16
LOW, MID, TOP = lax.Precision.DEFAULT, lax.Precision.HIGH, lax.Precision.HIGHEST
NN, NT, TN = ((1,), (0,)), ((1,), (1,)), ((0,), (0,))
P_FWD, P_BWD = MID, MID


def dot(left, right, dims, precision):
    if precision is LOW:
        left, right = left.astype(BF16), right.astype(BF16)
        return lax.dot_general(left, right, (dims, ((), ())), preferred_element_type=F32)
    return lax.dot_general(
        left, right, (dims, ((), ())), precision=precision, preferred_element_type=F32
    )


def grid_index(shape, axis):
    return lax.broadcasted_iota(jnp.int32, shape, axis)


def positions(longer, first_row, count):
    rows = grid_index((count, 1), 0) + first_row
    return jnp.where(longer > 0, rows, rows % SEQ_SHORT)


def keeps(longer, first_row):
    start = jnp.where(longer > 0, first_row, first_row % SEQ_SHORT)
    return jnp.where(start > 0, 1.0, 0.0).astype(F32)


def softplus(x):
    return jnp.maximum(x, 0.0) + jnp.log1p(jnp.exp(-jnp.abs(x)))


def gate_values(gates, params, heads):
    lane = grid_index(gates.shape, 1)
    rate = jnp.exp(params[0:1])
    shifted = gates + params[1:2]
    log_decay = jnp.where(lane < heads, -rate * softplus(shifted), 0.0)
    return rate, shifted, log_decay


def lane_column(values, index):
    return values[:, index : index + 1]


def decays(cumulative, cumulative_rows, head, masks):
    column = lane_column(cumulative, head)
    row = cumulative_rows[head : head + 1, :]
    inclusive = masks[0]
    ratio = jnp.where(inclusive, jnp.exp(jnp.where(inclusive, column - row, 0.0)), 0.0)
    last = column[CHUNK - 1 : CHUNK, :]
    return ratio, jnp.exp(column), jnp.exp(last - column), jnp.exp(last)


def unit(values):
    scale = lax.rsqrt(jnp.sum(values * values, axis=-1, keepdims=True) + EPS)
    return values * scale, scale


def pair_of(values):
    high = values.astype(BF16)
    return high, (values - high.astype(F32)).astype(BF16)


def pair_dot(left, right):
    def product(a, b):
        return lax.dot_general(a, b, (NN, ((), ())), preferred_element_type=F32)

    return product(left[0], right[0]) + (product(left[0], right[1]) + product(left[1], right[0]))


def inverses(links, row, col):
    apart = row ^ col
    size = links[0].shape[0]
    outs = [jnp.where(row == col, 1.0, 0.0) - jnp.where(apart == 1, link, 0.0) for link in links]
    pairs = [pair_of(link) for link in links]
    step = 2
    while step < size // 2:
        level = (apart >= step) & (apart < 2 * step)
        parts = [tuple(jnp.where(level, half, 0) for half in pair) for pair in pairs]
        out_pairs = [pair_of(out) for out in outs]
        inner = [pair_of(pair_dot(part, out)) for part, out in zip(parts, out_pairs)]
        outs = [out - pair_dot(pair, mid) for out, pair, mid in zip(outs, out_pairs, inner)]
        step *= 2
    half = size // 2
    uppers = [pair_of(out[:half, :half]) for out in outs]
    lowers = [pair_of(out[half:, half:]) for out in outs]
    corners = [tuple(each[half:, :half] for each in pair) for pair in pairs]
    inner = [pair_of(pair_dot(corner, upper)) for corner, upper in zip(corners, uppers)]
    corners = [pair_dot(lower, mid) for lower, mid in zip(lowers, inner)]
    return [
        jnp.concatenate(
            [out[:half], jnp.concatenate([-corner, out[half:, half:]], axis=1)], axis=0
        )
        for out, corner in zip(outs, corners)
    ]


def forward_kernel(
    heads, count, chunks, longer_ref, main_ref, conv_ref, params_ref, gain_ref, top_ref, live_ref,
    mixed_ref, conv_out_ref, raw_ref, delta_ref, solve_ref, state_ref, full_out,
    state, tail_rows, *scratch
):
    step = pl.program_id(0)
    first_row = step * CHUNK
    run, close = gather_along(step, chunks, count, top_ref, live_ref, full_out, scratch)
    run(2 * step)
    longer = longer_ref[0]
    width = heads * HEAD

    @pl.when(step == 0)
    def _():
        state[...] = jnp.zeros_like(state)
        tail_rows[...] = jnp.zeros_like(tail_rows)

    position = positions(longer, first_row, CHUNK)
    keep = keeps(longer, first_row)
    triple = main_ref[:, : 3 * width]
    padded = jnp.concatenate([tail_rows[...], triple], axis=0)
    taps = conv_ref[...]
    convolved = triple * taps[0:1]
    for lag in range(1, 4):
        shifted = padded[8 - lag : 8 - lag + CHUNK]
        convolved = convolved + jnp.where(position >= lag, shifted, 0.0) * taps[lag : lag + 1]
    tail_rows[...] = triple[CHUNK - 8 :]
    conv_out_ref[...] = convolved
    active = convolved * jax.nn.sigmoid(convolved)
    gates = main_ref[:, 4 * width :]
    rate, shifted_gate, log_decay = gate_values(gates, params_ref[...], heads)
    beta_all = jax.nn.sigmoid(gates)
    row = grid_index((CHUNK, CHUNK), 0)
    col = grid_index((CHUNK, CHUNK), 1)
    masks = (row >= col, row > col)
    cumulative = dot(jnp.where(masks[0], 1.0, 0.0), log_decay, NN, TOP)
    cumulative_rows = jnp.transpose(cumulative)
    each = range(heads)
    columns = [slice(head * HEAD, (head + 1) * HEAD) for head in each]
    queries = [unit(active[:, cols])[0] * HEAD**-0.5 for cols in columns]
    keys = [unit(active[:, width + head * HEAD : width + (head + 1) * HEAD])[0] for head in each]
    values = [active[:, 2 * width + head * HEAD : 2 * width + (head + 1) * HEAD] for head in each]
    betas = [lane_column(beta_all, heads + head) for head in each]
    spans = [decays(cumulative, cumulative_rows, head, masks) for head in each]
    grams = [
        dot(jnp.concatenate([key, query], axis=0), key, NT, P_FWD)
        for key, query in zip(keys, queries)
    ]
    links = [
        jnp.where(masks[1], beta * span[0] * gram[:CHUNK], 0.0)
        for beta, span, gram in zip(betas, spans, grams)
    ]
    solves = inverses(links, row, col)
    run(2 * step + 1)
    boths = [
        dot(
            solve,
            jnp.concatenate([beta * value, (beta * span[1]) * key], axis=1),
            NN,
            P_FWD,
        )
        for solve, beta, value, key, span in zip(solves, betas, values, keys, spans)
    ]
    entries = [state[head] * keep for head in each]
    carried = [
        dot(jnp.concatenate([both[:, HEAD:], span[1] * query], axis=0), entry, NT, P_FWD)
        for both, span, query, entry in zip(boths, spans, queries, entries)
    ]
    deltas = [both[:, :HEAD] - carry[:CHUNK] for both, carry in zip(boths, carried)]
    states = [
        span[3] * entry + dot(delta * span[2], key, TN, P_FWD)
        for span, entry, delta, key in zip(spans, entries, deltas, keys)
    ]
    raws = [
        carry[CHUNK:] + dot(gram[CHUNK:] * span[0], delta, NN, P_FWD)
        for carry, gram, span, delta in zip(carried, grams, spans, deltas)
    ]
    for head, cols in zip(each, columns):
        solve_ref[head] = solves[head]
        state_ref[0, head] = entries[head]
        state[head] = states[head]
        delta_ref[:, cols] = deltas[head]
        raw = raws[head]
        raw_ref[:, cols] = raw
        scale = lax.rsqrt(jnp.mean(raw * raw, axis=-1, keepdims=True) + EPS)
        gate = main_ref[:, 3 * width + head * HEAD : 3 * width + (head + 1) * HEAD]
        mixed = raw * scale * gain_ref[...] * (gate * jax.nn.sigmoid(gate))
        mixed_ref[:, cols] = mixed.astype(mixed_ref.dtype)
    pl.when(step == chunks - 1)(close)


def spread_ticks(tick, first, ticks, halves):
    def run(half):
        def one(index, _):
            tick(first + index)
            return 0

        lax.fori_loop(half * ticks // halves, (half + 1) * ticks // halves, one, 0)

    return run


def gather_along(step, chunks, count, top_ref, live_ref, full_out, scratch):
    *scratch, out_sems = scratch
    full = scratch[0]
    group = Group(count)
    gather = gather_of(group, GATHER_SHARE, scratch)

    def out(piece):
        rows = gather.rows(piece)
        return pltpu.make_async_copy(
            full.at[:, :, rows], full_out.at[:, :, rows], out_sems.at[piece]
        )

    def prepare(piece):
        rows = gather.rows(piece)
        full[group.z, group.x, rows] = (live_ref[rows] * top_ref[rows].astype(F32)).astype(BF16)

    before, within, behind = gather_ticks(gather, prepare, lambda piece: out(piece).start())

    def tick(time):
        before(time)
        at_each_z(group, functools.partial(within, time))
        behind(time)

    def close():
        gather.drain()

        def finish(piece, _):
            out(piece).wait()
            return 0

        lax.fori_loop(0, gather.pieces, finish, 0)

    pl.when(step == 0)(functools.partial(meet, count))
    return spread_ticks(tick, 0, gather.pieces + gather.last, 2 * chunks), close


def scatter_along(step, chunks, count, hidden_ref, weight_ref, middle_ref, live_ref, out, scratch):
    parts = scratch[0]
    group = Group(count)
    scatter = scatter_of(group, SCATTER_SHARE, scratch)

    def prepare(piece):
        rows = scatter.rows(piece)

        def store(cols, value):
            parts[:, :, rows, cols] = split(value.astype(BF16), group.deep, group.nx)

        wide_dot([(joined(hidden_ref[:, rows]), weight_ref)], NN, 512, store)

    def end(piece, total):
        rows = scatter.rows(piece)
        out[rows] = (middle_ref[rows] + live_ref[rows] * total).astype(BF16)

    before, within, behind = scatter_ticks(scatter, prepare, end)

    def tick(time):
        before(time)
        at_each_z(group, functools.partial(within, time))
        behind(time)

    pl.when(step == 0)(functools.partial(meet, count))
    return spread_ticks(tick, -1, scatter.pieces + scatter.last, 2 * chunks), scatter.drain


def backward_kernel(
    heads, chunks, count, longer_ref, grad_ref, main_ref, conv_out_ref, raw_ref, delta_ref,
    solve_ref, state_ref, conv_ref, params_ref, gain_ref, hidden_ref, down_ref, middle_ref, live_ref,
    dmain_ref, dconv_ref, dparams_ref, dgain_ref, layer_ref, dstate, head_rows, *scratch
):
    step = pl.program_id(0)
    first_row = (chunks - 1 - step) * CHUNK
    run, close = scatter_along(
        step, chunks, count, hidden_ref, down_ref, middle_ref, live_ref, layer_ref, scratch
    )
    run(2 * step)
    longer = longer_ref[0]
    width = heads * HEAD

    @pl.when(step == 0)
    def _():
        dstate[...] = jnp.zeros_like(dstate)
        head_rows[...] = jnp.zeros_like(head_rows)
        dconv_ref[...] = jnp.zeros_like(dconv_ref)
        dparams_ref[...] = jnp.zeros_like(dparams_ref)
        dgain_ref[...] = jnp.zeros_like(dgain_ref)

    keep = keeps(longer, first_row)
    convolved = conv_out_ref[...]
    sigmoid_conv = jax.nn.sigmoid(convolved)
    active = convolved * sigmoid_conv
    slope = sigmoid_conv * (1.0 + convolved * (1.0 - sigmoid_conv))
    gates = main_ref[:, 4 * width :]
    params = params_ref[...]
    rate, shifted_gate, log_decay = gate_values(gates, params, heads)
    beta_all = jax.nn.sigmoid(gates)
    row = grid_index((CHUNK, CHUNK), 0)
    col = grid_index((CHUNK, CHUNK), 1)
    masks = (row >= col, row > col)
    cumulative = dot(jnp.where(masks[0], 1.0, 0.0), log_decay, NN, TOP)
    cumulative_rows = jnp.transpose(cumulative)
    lane = grid_index((CHUNK, 128), 1)
    last_row = grid_index((CHUNK, 1), 0) == CHUNK - 1
    gain = gain_ref[...]
    dgains, dlogs, dbetas, dparts = ([None] * heads for _ in range(4))

    def work(head):
        cols = slice(head * HEAD, (head + 1) * HEAD)
        gate = main_ref[:, 3 * width + head * HEAD : 3 * width + (head + 1) * HEAD]
        raw = raw_ref[:, cols]
        grad = grad_ref[:, cols]
        scale = lax.rsqrt(jnp.mean(raw * raw, axis=-1, keepdims=True) + EPS)
        normed = raw * scale
        sigmoid_gate = jax.nn.sigmoid(gate)
        gated = gate * sigmoid_gate
        product = grad * normed
        dgains[head] = jnp.sum(product * gated, axis=0, keepdims=True)
        dgate = product * gain * (sigmoid_gate * (1.0 + gate * (1.0 - sigmoid_gate)))
        dmain_ref[:, 3 * width + head * HEAD : 3 * width + (head + 1) * HEAD] = dgate.astype(
            dmain_ref.dtype
        )
        dnormed = grad * gain * gated
        draw = scale * (dnormed - normed * jnp.mean(dnormed * normed, axis=-1, keepdims=True))
        query_unit, query_scale = unit(active[:, head * HEAD : (head + 1) * HEAD])
        query = query_unit * HEAD**-0.5
        key, key_scale = unit(active[:, width + head * HEAD : width + (head + 1) * HEAD])
        value = active[:, 2 * width + head * HEAD : 2 * width + (head + 1) * HEAD]
        beta = lane_column(beta_all, heads + head)
        ratio, decay_in, decay_out, decay_all = decays(cumulative, cumulative_rows, head, masks)
        entry = state_ref[0, head]
        delta = delta_ref[:, cols]
        dlater = dstate[head]
        gram = dot(query, key, NT, P_BWD) * ratio
        yield
        key_dlater = dot(key, dlater, NT, P_BWD)
        yield
        ddelta = dot(gram, draw, TN, P_BWD) + decay_out * key_dlater
        yield
        dright = dot(solve_ref[head], ddelta, TN, P_BWD)
        yield
        pairs = dot(jnp.concatenate([dright, draw], axis=0), delta, NT, P_BWD)
        yield
        dlink = jnp.where(masks[1], -pairs[:CHUNK] * ratio, 0.0)
        dgram = pairs[CHUNK:] * ratio
        on_entry = dot(jnp.concatenate([dright, draw], axis=0), entry, NN, P_BWD)
        yield
        key_entry = dot(key, entry, NT, P_BWD)
        yield
        on_key = dot(jnp.concatenate([dlink, dgram], axis=0), key, NN, P_BWD)
        yield
        dquery = decay_in * on_entry[CHUNK:] + on_key[CHUNK:]
        link_key = on_key[:CHUNK]
        key_read = beta * (link_key - decay_in * on_entry[:CHUNK])
        key_tail = decay_out * dot(delta, dlater, NN, P_BWD)
        yield
        key_write = (
            dot(beta * dlink, key, TN, P_BWD) + dot(dgram, query, TN, P_BWD) + key_tail
        )
        yield
        dkey = key_read + key_write
        dvalue = beta * dright
        dbeta = jnp.sum(
            dright * (value - decay_in * key_entry) + key * link_key, axis=-1, keepdims=True
        )
        dlog = jnp.sum(query * dquery + key * (key_read - key_write), axis=-1, keepdims=True)
        ending = decay_all * jnp.sum(
            jnp.sum(entry * dlater, axis=-1, keepdims=True), axis=0, keepdims=True
        ) + jnp.sum(jnp.sum(key * key_tail, axis=-1, keepdims=True), axis=0, keepdims=True)
        dlog = dlog + jnp.where(last_row, ending, 0.0)
        dlogs[head], dbetas[head] = dlog, dbeta
        dstate[head] = keep * (
            decay_all * dlater
            + dot(decay_in * draw, query, TN, P_BWD)
            - dot((beta * decay_in) * dright, key, TN, P_BWD)
        )
        yield
        dquery = (HEAD**-0.5 * query_scale) * (
            dquery - query_unit * jnp.sum(dquery * query_unit, axis=-1, keepdims=True)
        )
        dkey = key_scale * (dkey - key * jnp.sum(dkey * key, axis=-1, keepdims=True))
        dparts[head] = (dquery, dkey, dvalue)

    works = [work(head) for head in range(heads)]
    turns = 0
    while works:
        works = [each for each in works if next(each, "end") != "end"]
        turns += 1
        if turns == 6:
            run(2 * step + 1)
    dcumulative = jnp.zeros((CHUNK, 128), F32)
    dbeta_all = jnp.zeros((CHUNK, 128), F32)
    for head in range(heads):
        dcumulative = jnp.where(lane == head, dlogs[head], dcumulative)
        dbeta_all = jnp.where(lane == heads + head, dbetas[head], dbeta_all)
    dgain = functools.reduce(jnp.add, dgains)
    dconv_parts = [[dparts[head][kind] for head in range(heads)] for kind in range(3)]
    dactive = jnp.concatenate([p for parts in dconv_parts for p in parts], axis=1)
    dconvolved = dactive * slope
    padded = jnp.concatenate([dconvolved, head_rows[...]], axis=0)
    position = positions(longer, first_row, CHUNK + 8)
    taps = conv_ref[...]
    triple = main_ref[:, : 3 * width]
    dtriple = dconvolved * taps[0:1]
    dconv_ref[0:1] += jnp.sum(dconvolved * triple, axis=0, keepdims=True)
    for lag in range(1, 4):
        moved = jnp.where(position >= lag, padded, 0.0)[lag : lag + CHUNK]
        dtriple = dtriple + moved * taps[lag : lag + 1]
        dconv_ref[lag : lag + 1] += jnp.sum(moved * triple, axis=0, keepdims=True)
    head_rows[...] = dconvolved[:8]
    dmain_ref[:, : 3 * width] = dtriple.astype(dmain_ref.dtype)
    dlog_decay = dot(jnp.where(row <= col, 1.0, 0.0), dcumulative, NN, TOP)
    dshifted = -dlog_decay * rate * jax.nn.sigmoid(shifted_gate)
    dshifted = jnp.where(lane < heads, dshifted, 0.0)
    dparams_ref[0:1] += jnp.sum(dlog_decay * log_decay, axis=0, keepdims=True)
    dparams_ref[1:2] += jnp.sum(dshifted, axis=0, keepdims=True)
    dmain_ref[:, 4 * width :] = (dshifted + dbeta_all * beta_all * (1.0 - beta_all)).astype(
        dmain_ref.dtype
    )
    dgain_ref[...] += dgain
    pl.when(step == chunks - 1)(close)


def row_block(width, chunks, backward):
    if backward:
        return pl.BlockSpec((CHUNK, width), lambda i: (chunks - 1 - i, 0))
    return pl.BlockSpec((CHUNK, width), lambda i: (i, 0))


def whole_block(shape):
    return pl.BlockSpec(shape, lambda i: (0,) * len(shape))


def mixer_forward(longer, main, conv, params, gain, top, live, count):
    rows, width = main.shape[0], conv.shape[1] // 3
    heads, chunks = width // HEAD, rows // CHUNK
    own, features = top.shape
    nz, nx = grid_sizes(count)
    rowed = functools.partial(row_block, chunks=chunks, backward=False)
    shape = jax.ShapeDtypeStruct
    return pl.pallas_call(
        functools.partial(forward_kernel, heads, count, chunks),
        grid=(chunks,),
        in_specs=[
            pl.BlockSpec(memory_space=pltpu.SMEM),
            rowed(4 * width + 128),
            whole_block((4, 3 * width)),
            whole_block((2, 128)),
            whole_block((1, HEAD)),
            whole_block((own, features)),
            whole_block((own, 1)),
        ],
        out_specs=[
            rowed(width),
            rowed(3 * width),
            rowed(width),
            rowed(width),
            pl.BlockSpec((heads, CHUNK, CHUNK), lambda i: (0, i, 0)),
            pl.BlockSpec((1, heads, HEAD, HEAD), lambda i: (i, 0, 0, 0)),
            pl.BlockSpec(memory_space=pl.ANY),
        ],
        out_shape=[
            shape((rows, width), BF16),
            shape((rows, 3 * width), F32),
            shape((rows, width), F32),
            shape((rows, width), F32),
            shape((heads, rows, CHUNK), F32),
            shape((chunks, heads, HEAD, HEAD), F32),
            shape((nz, nx, own, features), BF16),
        ],
        scratch_shapes=[
            pltpu.VMEM((heads, HEAD, HEAD), F32),
            pltpu.VMEM((8, 3 * width), F32),
            *gather_scratch(nz, nx, own, features, FEW),
            pltpu.SemaphoreType.DMA((pieces_of(own, FEW),)),
        ],
        compiler_params=linked(4),
        cost_estimate=lasting(95),
        name="mixer_forward",
    )(longer, main, conv, params, gain, top, live)


def mixer_backward(
    longer, grad, main, saved, conv, params, gain, hidden, down_weight, middle, live, count
):
    rows, width = main.shape[0], conv.shape[1] // 3
    heads, chunks = width // HEAD, rows // CHUNK
    own, features = middle.shape
    nz, nx = grid_sizes(count)
    rowed = functools.partial(row_block, chunks=chunks, backward=True)
    shape = jax.ShapeDtypeStruct
    return pl.pallas_call(
        functools.partial(backward_kernel, heads, chunks, count),
        grid=(chunks,),
        in_specs=[
            pl.BlockSpec(memory_space=pltpu.SMEM),
            rowed(width),
            rowed(4 * width + 128),
            rowed(3 * width),
            rowed(width),
            rowed(width),
            pl.BlockSpec((heads, CHUNK, CHUNK), lambda i: (0, chunks - 1 - i, 0)),
            pl.BlockSpec((1, heads, HEAD, HEAD), lambda i: (chunks - 1 - i, 0, 0, 0)),
            whole_block((4, 3 * width)),
            whole_block((2, 128)),
            whole_block((1, HEAD)),
            whole_block(hidden.shape),
            whole_block(down_weight.shape),
            whole_block((own, features)),
            whole_block((own, 1)),
        ],
        out_specs=[
            rowed(4 * width + 128),
            whole_block((4, 3 * width)),
            whole_block((2, 128)),
            whole_block((1, HEAD)),
            whole_block((own, features)),
        ],
        out_shape=[
            shape((rows, 4 * width + 128), BF16),
            shape((4, 3 * width), F32),
            shape((2, 128), F32),
            shape((1, HEAD), F32),
            shape((own, features), BF16),
        ],
        scratch_shapes=[
            pltpu.VMEM((heads, HEAD, HEAD), F32),
            pltpu.VMEM((8, 3 * width), F32),
            *scatter_scratch(nz, nx, own, features, SCATTER_SHARE, FEW),
        ],
        compiler_params=linked(5),
        cost_estimate=lasting(100),
        name="mixer_backward",
    )(
        longer, grad, main, *saved, conv, params, gain, hidden, down_weight, middle, live
    )


MESH = pl.DeviceIdType.MESH
MANY, FEW = 16, 8


def pieces_of(rows, most):
    return min(most, rows // 16)


def grid_sizes(count):
    nz = 4 if count % 4 == 0 else 1
    return nz, count // nz


class Group:
    def __init__(self, count):
        self.deep, self.nx = grid_sizes(count)
        me = lax.axis_index("heads")
        self.z, self.x = me // self.nx, me % self.nx

    def column(self, j):
        return (self.x + j) % self.nx

    def over_x(self, j):
        return {"heads": self.z * self.nx + self.column(j)}

    def along_z(self, z):
        return {"heads": z * self.nx + self.x}


def meet(count, replicas=1):
    barrier = pltpu.get_barrier_semaphore()
    for axis, size in (("heads", count), ("dp", replicas)):
        me = lax.axis_index(axis)

        def greet(k, _, axis=axis, size=size, me=me):
            pl.semaphore_signal(
                barrier, inc=1, device_id={axis: (me + k) % size}, device_id_type=MESH
            )
            return 0

        lax.fori_loop(1, size, greet, 0)
    pl.semaphore_wait(barrier, count + replicas - 2)


def arrived(ref, sem):
    pltpu.make_async_copy(ref, ref, sem).wait()


def during(piece, pieces, work):
    pl.when((piece >= 0) & (piece < pieces))(functools.partial(work, piece))


def push(source, target, send_sem, recv_sem, device):
    pltpu.make_async_remote_copy(
        source, target, send_sem, recv_sem, device_id=device, device_id_type=MESH
    ).start()


class Gather:
    def __init__(self, group, full, cols, sems, x_first):
        self.group, self.full, self.cols, self.x_first = group, full, cols, x_first
        self.line_send, self.line_recv, self.x_send, self.x_recv = sems
        self.pieces = self.x_send.shape[0]
        self.part = full.shape[2] // self.pieces
        self.last = group.deep

    @staticmethod
    def sems(deep, nx, pieces):
        dma = pltpu.SemaphoreType.DMA
        return [dma((pieces, 2)), dma((pieces, deep)), dma((pieces, nx)), dma((pieces, nx))]

    def at(self, piece, z, column):
        rows = pl.ds(pl.multiple_of(piece * self.part, self.part), self.part)
        return self.full.at[z, column, rows, self.cols]

    def columns(self):
        return slice(None) if self.x_first else self.group.x

    def push_line(self, piece, z, way, zz):
        place = self.at(piece, z, self.columns())
        push(
            place,
            place,
            self.line_send.at[piece, way],
            self.line_recv.at[piece, z],
            self.group.along_z(zz + (1 if way == 0 else -1)),
        )

    def push_x(self, piece, z):
        place = self.at(piece, z, self.group.x)
        for j in range(1, self.group.nx):
            push(
                place,
                place,
                self.x_send.at[piece, j],
                self.x_recv.at[piece, self.group.nx - j],
                self.group.over_x(j),
            )

    def own_line(self, piece, zz):
        if zz + 1 < self.group.deep:
            self.push_line(piece, zz, 0, zz)
        if zz > 0:
            self.push_line(piece, zz, 1, zz)

    def begin(self, piece):
        self.push_x(piece, self.group.z)
        if not self.x_first:
            group = self.group
            pl.when(group.z + 1 < group.deep)(lambda: self.push_line(piece, group.z, 0, group.z))
            pl.when(group.z > 0)(lambda: self.push_line(piece, group.z, 1, group.z))

    def phase(self, piece, step, zz):
        deep, nx = self.group.deep, self.group.nx
        if self.x_first:
            if step == 1:
                for j in range(1, nx):
                    arrived(self.at(piece, zz, self.group.column(j)), self.x_recv.at[piece, j])
                self.own_line(piece, zz)
                return
            step -= 1
        elif step == deep:
            for j in range(1, nx):
                place = self.at(piece, slice(None), self.group.column(j))
                arrived(place, self.x_recv.at[piece, j])
            return
        for z, way in ((zz - step, 0), (zz + step, 1)):
            if 0 <= z < deep:
                arrived(self.at(piece, z, self.columns()), self.line_recv.at[piece, z])
                if 0 <= zz + (1 if way == 0 else -1) < deep:
                    self.push_line(piece, z, way, zz)
                if not self.x_first:
                    self.push_x(piece, z)

    def drain(self, piece, zz):
        deep, nx = self.group.deep, self.group.nx
        if zz + 1 < deep:
            place = self.at(piece, pl.ds(0, zz + 1), self.columns())
            arrived(place, self.line_send.at[piece, 0])
        if zz > 0:
            place = self.at(piece, pl.ds(zz, deep - zz), self.columns())
            arrived(place, self.line_send.at[piece, 1])
        z = zz if self.x_first else slice(None)
        for j in range(1, nx):
            arrived(self.at(piece, z, self.group.x), self.x_send.at[piece, j])


class Scatter:
    last = 4

    def __init__(self, group, parts, cols, scratch, z_first):
        self.group, self.parts, self.cols, self.z_first = group, parts, cols, z_first
        self.landed_x, self.line, *sems = scratch
        self.x_send, self.x_recv, self.z_send, self.z_recv = sems
        self.pieces = self.x_send.shape[0]
        self.part = parts.shape[2] // self.pieces

    @staticmethod
    def scratch(deep, nx, rows, cols, z_first, pieces):
        dma = pltpu.SemaphoreType.DMA
        return [
            pltpu.VMEM((max(nx - 1, 1), 1 if z_first else deep, rows, cols), BF16),
            pltpu.VMEM((deep + 1, nx if z_first else 1, rows, cols), BF16),
            *[dma((pieces, nx))] * 2,
            *[dma((pieces, 2))] * 2,
        ]

    def rows(self, piece):
        return pl.ds(pl.multiple_of(piece * self.part, self.part), self.part)

    def columns(self):
        return slice(None) if self.z_first else pl.ds(self.group.x, 1)

    def at(self, piece, z, column):
        return self.parts.at[z, column, self.rows(piece), self.cols]

    def line_at(self, piece, way, zz):
        first, size = (zz + 1, self.group.deep - zz) if way == 0 else (0, zz + 1)
        return self.line.at[pl.ds(first, size), :, self.rows(piece)]

    def push_line(self, piece, way, zz):
        deep = self.group.deep
        first, size = (zz + 1, deep - 1 - zz) if way == 0 else (0, zz)
        if size == 0:
            return
        after = zz + 1 if way == 0 else zz - 1
        push(
            self.at(piece, pl.ds(first, size), self.columns()),
            self.line_at(piece, way, after),
            self.z_send.at[piece, way],
            self.z_recv.at[piece, way],
            self.group.along_z(after),
        )

    def ends(self, piece, zz):
        if zz == 0:
            self.push_line(piece, 0, zz)
        if zz == self.group.deep - 1:
            self.push_line(piece, 1, zz)

    def hand_on(self, piece, near, zz):
        deep = self.group.deep
        if zz == 0 or zz == deep - 1:
            return
        way = 0 if (zz < deep // 2) == near else 1
        arrived(self.line_at(piece, way, zz), self.z_recv.at[piece, way])
        first, size = (zz + 1, deep - 1 - zz) if way == 0 else (0, zz)
        shift = 1 if way == 0 else 0
        ours = self.at(piece, pl.ds(first, size), self.columns())
        landed = self.line.at[pl.ds(first + shift, size), :, self.rows(piece)]
        ours[...] = (ours[...].astype(F32) + landed[...].astype(F32)).astype(BF16)
        self.push_line(piece, way, zz)

    def wait_ends(self, piece, zz):
        deep = self.group.deep
        if deep == 1:
            return
        if zz == 0:
            arrived(self.line_at(piece, 1, zz), self.z_recv.at[piece, 1])
        if zz == deep - 1:
            arrived(self.line_at(piece, 0, zz), self.z_recv.at[piece, 0])

    def total_line(self, piece, column):
        group, rows = self.group, self.rows(piece)
        total = self.parts[group.z, column, rows, self.cols].astype(F32)
        index = column if self.z_first else 0
        for here, place in ((group.z > 0, group.z + 1), (group.z + 1 < group.deep, group.z)):
            landed = self.line[place, index, rows]
            total = total + jnp.where(here, landed.astype(F32), 0.0)
        return total

    def begin(self, piece):
        if not self.z_first:
            for j in range(1, self.group.nx):
                push(
                    self.at(piece, slice(None), self.group.column(j)),
                    self.landed_x.at[self.group.nx - j - 1, :, self.rows(piece)],
                    self.x_send.at[piece, j],
                    self.x_recv.at[piece, self.group.nx - j],
                    self.group.over_x(j),
                )

    def begin_line(self, piece, zz):
        if self.z_first:
            self.ends(piece, zz)

    def wait_x(self, piece, j):
        landed = self.landed_x.at[j - 1, :, self.rows(piece)]
        arrived(landed, self.x_recv.at[piece, j])
        return landed[...].astype(F32)

    def phase(self, piece, step, zz):
        nx = self.group.nx
        if self.z_first:
            if step < 3:
                self.hand_on(piece, step == 1, zz)
            elif step == 3:
                self.wait_ends(piece, zz)
            return
        if step == 1:
            ours = self.at(piece, slice(None), self.group.x)
            total = ours[...].astype(F32)
            for j in range(1, nx):
                total = total + self.wait_x(piece, j)
            ours[...] = total.astype(BF16)
            self.ends(piece, zz)
        elif step < 4:
            self.hand_on(piece, step == 2, zz)
        else:
            self.wait_ends(piece, zz)

    def third(self, piece):
        if not self.z_first:
            return
        group, rows = self.group, self.rows(piece)
        for j in range(1, group.nx):
            column = group.column(j)
            total = self.total_line(piece, column).astype(BF16)
            self.parts[group.z, column, rows, self.cols] = total
            push(
                self.at(piece, pl.ds(group.z, 1), column),
                self.landed_x.at[group.nx - j - 1, :, rows],
                self.x_send.at[piece, j],
                self.x_recv.at[piece, group.nx - j],
                group.over_x(j),
            )

    def total(self, piece):
        total = self.total_line(piece, self.group.x)
        if self.z_first:
            for j in range(1, self.group.nx):
                total = total + self.wait_x(piece, j)[0]
        return total

    def drain(self, piece, zz):
        deep = self.group.deep
        for way, size in ((0, deep - 1 - zz), (1, zz)):
            if size > 0:
                place = self.at(piece, pl.ds(0, size), self.columns())
                arrived(place, self.z_send.at[piece, way])
        z = pl.ds(0, 1 if self.z_first else deep)
        for j in range(1, self.group.nx):
            arrived(self.at(piece, z, self.group.x), self.x_send.at[piece, j])


class Both:
    def __init__(self, first, second):
        self.both = (first, second)
        self.group = first.group
        self.part, self.pieces, self.last = first.part, first.pieces, first.last

    def rows(self, piece):
        return pl.ds(pl.multiple_of(piece * self.part, self.part), self.part)

    def begin(self, piece):
        for each in self.both:
            each.begin(piece)

    def begin_line(self, piece, zz):
        for each in self.both:
            each.begin_line(piece, zz)

    def phase(self, piece, step, zz):
        for each in self.both:
            each.phase(piece, step, zz)

    def third(self, piece):
        for each in self.both:
            each.third(piece)

    def total(self, piece):
        return jnp.concatenate([each.total(piece) for each in self.both], axis=1)

    def drain(self):
        def at(zz):
            def one(piece, _):
                for each in self.both:
                    each.drain(piece, zz)
                return 0

            lax.fori_loop(0, self.pieces, one, 0)

        at_each_z(self.group, at)


def at_each_z(group, work):
    for zz in range(group.deep):
        pl.when(group.z == zz)(functools.partial(work, zz))


def scatter_ticks(scatter, prepare, finish, after=None):
    def before(time):
        def begin(piece):
            prepare(piece)
            scatter.begin(piece)

        during(time + 1, scatter.pieces, begin)

    def within(time, zz):
        during(time + 1, scatter.pieces, functools.partial(scatter.begin_line, zz=zz))
        for step in range(1, scatter.last + 1):
            during(time - step + 1, scatter.pieces, functools.partial(scatter.phase, step=step, zz=zz))

    def behind(time):
        during(time - 2, scatter.pieces, scatter.third)
        during(time - scatter.last + 1, scatter.pieces, lambda piece: finish(piece, scatter.total(piece)))

    return before, within, behind


def gather_ticks(gather, prepare, ready):
    def before(time):
        if prepare is not None:

            def begin(piece):
                prepare(piece)
                gather.begin(piece)

            during(time, gather.pieces, begin)

    def within(time, zz):
        for step in range(1, gather.last + 1):
            during(time - step, gather.pieces, functools.partial(gather.phase, step=step, zz=zz))

    def behind(time):
        during(time - gather.last, gather.pieces, ready)

    return before, within, behind


def cut(cols, share):
    edge = cols - cols * share // 8
    return pl.ds(0, edge), pl.ds(edge, cols - edge)


def gather_of(group, share, scratch):
    full, *sems = scratch
    first, second = cut(full.shape[3], share)
    return Both(
        Gather(group, full, first, sems[:4], False), Gather(group, full, second, sems[4:], True)
    )


def scatter_of(group, share, scratch):
    parts, *rest = scratch
    first, second = cut(parts.shape[3], share)
    return Both(
        Scatter(group, parts, first, rest[:6], False),
        Scatter(group, parts, second, rest[6:], True),
    )


def gather_scratch(nz, nx, rows, cols, most):
    sems = Gather.sems(nz, nx, pieces_of(rows, most))
    return [pltpu.VMEM((nz, nx, rows, cols), BF16), *sems, *sems]


def scatter_scratch(nz, nx, rows, cols, share, most):
    first, second = cut(cols, share)
    pieces = pieces_of(rows, most)
    return [
        pltpu.VMEM((nz, nx, rows, cols), BF16),
        *Scatter.scratch(nz, nx, rows, first.size, False, pieces),
        *Scatter.scratch(nz, nx, rows, second.size, True, pieces),
    ]


SCATTER_COUNT, GATHER_COUNT = 13, 9


def inverse_rms(rows):
    return lax.rsqrt(jnp.mean(rows * rows, axis=-1, keepdims=True) + EPS)


def wide_dot(terms, dims, tile, store):
    total = terms[0][1].shape[0 if dims is NT else 1]
    for first in range(0, total, tile):
        cols = slice(first, min(first + tile, total))
        products = [
            lax.dot_general(
                left,
                right[cols, :] if dims is NT else right[:, cols],
                (dims, ((), ())),
                preferred_element_type=F32,
            )
            for left, right in terms
        ]
        store(cols, functools.reduce(jnp.add, products))


VMEM_SPEC = pl.BlockSpec(memory_space=pltpu.VMEM)
ANY_SPEC = pl.BlockSpec(memory_space=pl.ANY)
PAIR_SHARE, GATHER_SHARE, SCATTER_SHARE = 3, 1, 2


class Late:
    def __init__(self, given, held, sem):
        self.held = held
        self.copy = pltpu.make_async_copy(given, held, sem)
        self.copy.start()

    def wait(self):
        self.copy.wait()


def late_all(given, scratch):
    return [
        Late(ref, held, sem)
        for ref, held, sem in zip(given, scratch[: len(given)], scratch[len(given) :])
    ]


def late_scratch(*values):
    return [
        *[pltpu.VMEM(value.shape, value.dtype) for value in values],
        *[pltpu.SemaphoreType.DMA] * len(values),
    ]


def lasting(microseconds):
    return pl.CostEstimate(
        flops=int(microseconds * 1.1e9), bytes_accessed=2**20, transcendentals=0
    )


def linked(collective):
    return pltpu.CompilerParams(
        collective_id=collective, has_side_effects=True, vmem_limit_bytes=62 * 2**20
    )


def joined(values):
    return values.reshape(-1, values.shape[-1])


def split(values, *parts):
    return values.reshape(*parts, values.shape[0] // math.prod(parts), values.shape[1])


def project_kernel(
    count, rows_ref, gain_ref, weight_ref, gates_ref, full_out, projected_out, weight_out, *scratch
):
    full = scratch[0]
    staged, full_sems, staged_sems, given, weight, given_sem, out_sem = scratch[GATHER_COUNT:]
    late = Late(weight_ref, given, given_sem)
    group = Group(count)
    gather = gather_of(group, GATHER_SHARE, scratch[:GATHER_COUNT])
    meet(count)
    weight_copy = pltpu.make_async_copy(weight, weight_out, out_sem)
    kinds, width = given.shape[1:]
    blocks = given.shape[0] // 256
    shares, share = full_out.shape[0], full_out.shape[4]

    def full_copy(piece, index):
        rows = gather.rows(piece)
        return pltpu.make_async_copy(
            full.at[:, :, rows, pl.ds(index * share, share)],
            full_out.at[index, :, :, rows],
            full_sems.at[piece, index],
        )

    def staged_copy(piece):
        rows = gather.rows(piece)
        return pltpu.make_async_copy(
            staged.at[:, rows], projected_out.at[:, rows], staged_sems.at[piece]
        )

    def prepare(piece):
        rows = rows_ref[gather.rows(piece)].astype(F32)
        full[group.z, group.x, gather.rows(piece)] = (
            rows * inverse_rms(rows) * gain_ref[...]
        ).astype(BF16)

    def ready(piece):
        rows = gather.rows(piece)
        for index in range(shares):
            full_copy(piece, index).start()

        def store(cols, value):
            staged[:, rows, cols] = split(value, count)

        left = joined(full[:, :, rows])
        wide_dot([(left, weight)], NN, 256, store)
        value = lax.dot_general(
            left, gates_ref[...], (NN, ((), ())), preferred_element_type=F32
        )
        staged[:, rows, kinds * width :] = split(value, count)
        staged_copy(piece).start()

    before, within, behind = gather_ticks(gather, prepare, ready)

    def lay_out(block, _):
        rows = pl.ds(pl.multiple_of(block * 256, 256), 256)
        for kind in range(kinds):
            weight[rows, kind * width : (kind + 1) * width] = given[rows, kind, :]
        return 0

    def tick(time, _):
        before(time)
        pl.when(time == 0)(late.wait)
        lax.fori_loop(
            jnp.minimum(time * 2, blocks), jnp.minimum(time * 2 + 2, blocks), lay_out, 0
        )
        pl.when(time == 4)(weight_copy.start)
        at_each_z(group, functools.partial(within, time))
        behind(time)
        return 0

    lax.fori_loop(0, gather.pieces + gather.last, tick, 0)
    gather.drain()
    weight_copy.wait()

    def finish(piece, _):
        for index in range(shares):
            full_copy(piece, index).wait()
        staged_copy(piece).wait()
        return 0

    lax.fori_loop(0, gather.pieces, finish, 0)


def project(rows, gain, weight, gates, count, shares):
    own, features = rows.shape
    kinds, width = weight.shape[1:]
    cols = kinds * width + gates.shape[1]
    nz, nx = grid_sizes(count)
    return pl.pallas_call(
        functools.partial(project_kernel, count),
        out_shape=[
            jax.ShapeDtypeStruct((shares, nz, nx, own, features // shares), BF16),
            jax.ShapeDtypeStruct((count, own, cols), F32),
            jax.ShapeDtypeStruct((features, kinds * width), BF16),
        ],
        in_specs=[VMEM_SPEC, VMEM_SPEC, ANY_SPEC, VMEM_SPEC],
        out_specs=[ANY_SPEC] * 3,
        scratch_shapes=[
            *gather_scratch(nz, nx, own, features, FEW),
            pltpu.VMEM((count, own, cols), F32),
            pltpu.SemaphoreType.DMA((pieces_of(own, FEW), shares)),
            pltpu.SemaphoreType.DMA((pieces_of(own, FEW),)),
            pltpu.VMEM(weight.shape, BF16),
            pltpu.VMEM((features, kinds * width), BF16),
            *[pltpu.SemaphoreType.DMA] * 2,
        ],
        compiler_params=linked(0),
        cost_estimate=lasting(100),
        name="project",
    )(rows, gain, weight, gates)


def sum_and_gather(scatter, gather, prepare, middle, ready, job=None):
    group = gather.group
    full = gather.both[0].full

    def turn(piece, total):
        full[group.z, group.x, gather.rows(piece)] = middle(piece, total).astype(BF16)
        gather.begin(piece)

    late = scatter.last - 1
    before, sum_within, sum_behind = scatter_ticks(scatter, prepare, turn)
    _, gather_within, gather_behind = gather_ticks(gather, None, ready)

    def tick(time, _):
        before(time)

        def within(zz):
            sum_within(time, zz)
            gather_within(time - late, zz)

        at_each_z(group, within)
        sum_behind(time)
        gather_behind(time - late)
        if job is not None:
            job(time + 1)
        return 0

    lax.fori_loop(-1, gather.pieces + late + gather.last, tick, 0)
    scatter.drain()
    gather.drain()


def branch_kernel(
    count, mixed_ref, weight_ref, input_ref, live_ref, gain_ref, feed_weight_ref,
    down_weight_ref, grad_ref, middle_out, full_out, dgate_out, dup_out, hidden_out, *all_scratch
):
    *scratch, grads, grad_sems, dgate, dup, hidden, feed_sems = all_scratch[:-4]
    lates = late_all((feed_weight_ref, down_weight_ref), all_scratch[-4:])
    feed_weight_ref, down_weight_ref = (late.held for late in lates)
    group = Group(count)
    scatter = scatter_of(group, PAIR_SHARE, scratch[:SCATTER_COUNT])
    gather = gather_of(group, PAIR_SHARE, scratch[SCATTER_COUNT:])
    parts, full = scratch[0], scratch[SCATTER_COUNT]

    def fetch(piece):
        slot = piece % 2
        return pltpu.make_async_copy(
            grad_ref.at[:, :, gather.rows(piece)], grads.at[slot], grad_sems.at[slot]
        )

    fetch(0).start()
    meet(count)

    def prepare(piece):
        rows = gather.rows(piece)

        def store(cols, value):
            parts[:, :, rows, cols] = split(value.astype(BF16), group.deep, group.nx)

        wide_dot([(joined(mixed_ref[:, rows]), weight_ref)], NN, 512, store)

    def middle(piece, total):
        rows = gather.rows(piece)
        values = input_ref[rows].astype(F32) + live_ref[rows] * total
        middle_out[rows] = values
        return values * inverse_rms(values) * gain_ref[...]

    def copies(piece):
        rows = gather.rows(piece)
        return [
            pltpu.make_async_copy(ref.at[:, rows], out.at[:, rows], feed_sems.at[piece, index])
            for index, (ref, out) in enumerate(
                ((dgate, dgate_out), (dup, dup_out), (hidden, hidden_out))
            )
        ] + [
            pltpu.make_async_copy(
                full.at[:, :, rows], full_out.at[:, :, rows], feed_sems.at[piece, 3]
            )
        ]

    def ready(piece):
        rows = gather.rows(piece)
        for late in lates:
            pl.when(piece == 0)(late.wait)
        fetch(piece).wait()
        pl.when(piece + 1 < gather.pieces)(lambda: fetch(piece + 1).start())
        left, grad = joined(full[:, :, rows]), joined(grads[piece % 2])
        total = feed_weight_ref.shape[1]
        for first in range(0, total, 256):
            cols = slice(first, min(first + 256, total))

            def product(a, b, dims):
                return lax.dot_general(a, b, (dims, ((), ())), preferred_element_type=F32)

            gate = product(left, feed_weight_ref[0, cols], NT)
            up = product(left, feed_weight_ref[1, cols], NT)
            dhidden = product(grad, down_weight_ref[cols, :], NT)
            sigmoid = jax.nn.sigmoid(gate)
            active = gate * sigmoid
            hidden[:, rows, cols] = split((active * up).astype(BF16), count)
            dup[:, rows, cols] = split((dhidden * active).astype(BF16), count)
            slope = sigmoid * (1.0 + gate * (1.0 - sigmoid))
            dgate[:, rows, cols] = split((dhidden * up * slope).astype(BF16), count)
        for copy in copies(piece):
            copy.start()

    sum_and_gather(scatter, gather, prepare, middle, ready)

    def finish(piece, _):
        for copy in copies(piece):
            copy.wait()
        return 0

    lax.fori_loop(0, gather.pieces, finish, 0)


def branch_and_feed(mixed, weight, rows, live, gain, feed_weight, down_weight, grad, count):
    own, features = rows.shape
    hidden = feed_weight.shape[1]
    nz, nx = grid_sizes(count)
    return pl.pallas_call(
        functools.partial(branch_kernel, count),
        out_shape=[
            jax.ShapeDtypeStruct((own, features), F32),
            jax.ShapeDtypeStruct((nz, nx, own, features), BF16),
            *[jax.ShapeDtypeStruct((count, own, hidden), BF16)] * 3,
        ],
        in_specs=[VMEM_SPEC] * 5 + [ANY_SPEC] * 3,
        out_specs=[VMEM_SPEC] + [ANY_SPEC] * 4,
        scratch_shapes=[
            *scatter_scratch(nz, nx, own, features, PAIR_SHARE, MANY),
            *gather_scratch(nz, nx, own, features, MANY),
            pltpu.VMEM((2, nz, nx, own // pieces_of(own, MANY), features), BF16),
            pltpu.SemaphoreType.DMA((2,)),
            *[pltpu.VMEM((count, own, hidden), BF16)] * 3,
            pltpu.SemaphoreType.DMA((pieces_of(own, MANY), 4)),
            *late_scratch(feed_weight, down_weight),
        ],
        compiler_params=linked(1),
        cost_estimate=lasting(180),
        name="branch_and_feed",
    )(split(mixed, count), weight, rows, live, gain, feed_weight, down_weight, grad)


TILE = 256


class TileJob:
    def __init__(self, rows_ref, tile, factors, staged, outs, fetch_sem, out_sems):
        self.rows_ref, self.tile, self.factors = rows_ref, tile, factors
        self.staged, self.outs = staged, outs
        self.fetch_sem, self.out_sems = fetch_sem, out_sems
        self.count = rows_ref.shape[3] // TILE

    def span(self, index):
        return pl.ds(pl.multiple_of(index * TILE, TILE), TILE)

    def fetch(self, index):
        return pltpu.make_async_copy(
            self.rows_ref.at[:, :, :, self.span(index)], self.tile, self.fetch_sem
        )

    def results(self, index):
        return [
            pltpu.make_async_copy(
                self.staged.at[which], out.at[:, self.span(index)], self.out_sems.at[which]
            )
            for which, out in enumerate(self.outs)
        ]

    def wait_results(self, index):
        for copy in self.results(index):
            copy.wait()

    def run(self, index):
        self.fetch(index).wait()
        left = joined(self.tile[...])
        pl.when(index > 0)(lambda: self.wait_results(index - 1))
        for which, factor in enumerate(self.factors):
            product = lax.dot_general(
                left, joined(factor[...]), (TN, ((), ())), preferred_element_type=F32
            )
            self.staged[which] = jnp.transpose(product).astype(BF16)
        for copy in self.results(index):
            copy.start()
        pl.when(index + 1 < self.count)(lambda: self.fetch(index + 1).start())


def feed_back_kernel(
    count, dgate_ref, dup_ref, feed_weight_ref, top_ref, middle_ref, live_ref,
    gain_ref, out_weight_ref, mixed_ref, hidden_ref, normed_ref, grad_feed_ref,
    dmiddle_out, dgain_out, dmixed_out, dweight_out, dfeed_out, *all_scratch
):
    lates = late_all((out_weight_ref, mixed_ref, hidden_ref), all_scratch[-6:])
    out_weight_ref, mixed_ref, hidden_ref = (late.held for late in lates)
    *scratch, total_out, tile, grad_tile, staged, grad_staged, fetch_sems, out_sems = (
        all_scratch[:-6]
    )
    group = Group(count)
    scatter = scatter_of(group, PAIR_SHARE, scratch[:SCATTER_COUNT])
    gather = gather_of(group, PAIR_SHARE, scratch[SCATTER_COUNT:])
    parts, full = scratch[0], scratch[SCATTER_COUNT]
    jobs = (
        TileJob(
            normed_ref, tile, (dgate_ref, dup_ref), staged, (dfeed_out.at[0], dfeed_out.at[1]),
            fetch_sems.at[0], out_sems.at[0],
        ),
        TileJob(
            grad_feed_ref, grad_tile, (hidden_ref,), grad_staged, (dfeed_out.at[2],),
            fetch_sems.at[1], out_sems.at[1],
        ),
    )
    for each in jobs:
        each.fetch(0).start()
    meet(count)
    dgain_out[...] = jnp.zeros(dgain_out.shape, F32)
    total_out[...] = jnp.zeros(total_out.shape, F32)

    def prepare(piece):
        rows = gather.rows(piece)

        def store(cols, value):
            parts[:, :, rows, cols] = split(value.astype(BF16), group.deep, group.nx)

        wide_dot(
            [
                (joined(dgate_ref[:, rows]), feed_weight_ref.at[0]),
                (joined(dup_ref[:, rows]), feed_weight_ref.at[1]),
            ],
            NN,
            256,
            store,
        )

    def middle(piece, dnormed):
        rows = gather.rows(piece)
        values = middle_ref[rows]
        scale = inverse_rms(values)
        normed = values * scale
        dgain_out[...] += jnp.sum(dnormed * normed, axis=0, keepdims=True)
        scaled = dnormed * gain_ref[...]
        dmiddle = top_ref[rows].astype(F32) + scale * (
            scaled - normed * jnp.mean(scaled * normed, axis=-1, keepdims=True)
        )
        dmiddle_out[rows] = dmiddle
        return live_ref[rows] * dmiddle

    def ready(piece):
        rows = gather.rows(piece)
        for late in lates[:2]:
            pl.when(piece == 0)(late.wait)
        left, mixed = joined(full[:, :, rows]), joined(mixed_ref[:, rows])

        def store(cols, value):
            dmixed_out[:, rows, cols] = split(value, count)

        wide_dot([(left, out_weight_ref)], NT, 256, store)
        for first in range(0, left.shape[1], 256):
            total_out[first : first + 256] += lax.dot_general(
                left[:, first : first + 256], mixed, (TN, ((), ())), preferred_element_type=F32
            )

    def job(time):
        pl.when(time == 1)(lates[2].wait)
        for which, each in enumerate(jobs):
            pl.when((time % 2 == which) & (time < 2 * each.count))(
                functools.partial(each.run, time // 2)
            )

    sum_and_gather(scatter, gather, prepare, middle, ready, job)
    last = gather.pieces + scatter.last + gather.last
    lax.fori_loop(last, max(2 * jobs[0].count, last), lambda time, _: (job(time), 0)[1], 0)
    for each in jobs:
        each.wait_results(each.count - 1)
    dweight_out[...] = total_out[...].astype(BF16)


def feed_back(
    dgate, dup, feed_weight, top, middle, live, gain, out_weight, mixed, hidden, normed, grad_feed,
    count,
):
    own, features = middle.shape
    nz, nx = grid_sizes(count)
    width, units = out_weight.shape[0], feed_weight.shape[1]
    return pl.pallas_call(
        functools.partial(feed_back_kernel, count),
        out_shape=[
            jax.ShapeDtypeStruct((own, features), F32),
            jax.ShapeDtypeStruct((1, features), F32),
            jax.ShapeDtypeStruct((count, own, width), F32),
            jax.ShapeDtypeStruct((features, width), BF16),
            jax.ShapeDtypeStruct((3, units, features), BF16),
        ],
        in_specs=[VMEM_SPEC] * 7 + [ANY_SPEC] * 5,
        out_specs=[VMEM_SPEC] * 4 + [ANY_SPEC],
        scratch_shapes=[
            *scatter_scratch(nz, nx, own, features, PAIR_SHARE, MANY),
            *gather_scratch(nz, nx, own, features, MANY),
            pltpu.VMEM((features, width), F32),
            pltpu.VMEM((nz, nx, own, TILE), BF16),
            pltpu.VMEM((nz, nx, own, TILE), BF16),
            pltpu.VMEM((2, units, TILE), BF16),
            pltpu.VMEM((1, units, TILE), BF16),
            pltpu.SemaphoreType.DMA((2,)),
            pltpu.SemaphoreType.DMA((2, 2)),
            *late_scratch(out_weight, split(mixed, count), hidden),
        ],
        compiler_params=linked(2),
        cost_estimate=lasting(180),
        name="feed_back",
    )(
        dgate, dup, feed_weight, top, middle, live, gain, out_weight,
        split(mixed, count), hidden, normed, grad_feed,
    )


class Replicas:
    def __init__(self, values, from_core, from_y, over_back, over_home, sems):
        self.values, self.from_core, self.from_y = values, from_core, from_y
        self.over_back, self.over_home = over_back, over_home
        self.core_sems, self.y_sems, self.back_sems, self.home_sems = sems
        me = lax.axis_index("dp")
        self.lines = lax.axis_size("dp") // 2
        self.y, self.core = me // 2, me % 2

    @staticmethod
    def scratch(rows, cols, replicas):
        lines, share = replicas // 2, rows // replicas
        return [
            pltpu.VMEM((replicas, share, cols), BF16),
            pltpu.VMEM((lines, share, cols), BF16),
            pltpu.VMEM((max(lines - 1, 1), share, cols), BF16),
            pltpu.VMEM((max(lines - 1, 1), share, cols), BF16),
            pltpu.VMEM((lines, share, cols), BF16),
            *[pltpu.SemaphoreType.DMA((2, lines))] * 4,
        ]

    def share(self, core, y):
        return core * self.lines + y

    def peer(self, y, core):
        return {"dp": y * 2 + core}

    def line(self, k):
        return (self.y + k) % self.lines

    draining = False

    def push(self, source, target, send_sem, recv_sem, device):
        copy = pltpu.make_async_remote_copy(
            source, target, send_sem, recv_sem, device_id=device, device_id_type=MESH
        )
        if self.draining:
            copy.wait_send()
        else:
            copy.start()

    def drain(self):
        self.draining = True
        for k in range(self.lines):
            self.start(k)
            self.cores(k)
        self.over_y()
        self.back()
        self.draining = False

    def add(self, share, others):
        step = 64

        def some(block, _):
            rows = pl.ds(pl.multiple_of(block * step, step), step)
            total = self.values[share, rows].astype(F32)
            for ref, index in others:
                total = total + ref[index, rows].astype(F32)
            self.values[share, rows] = total.astype(BF16)
            return 0

        lax.fori_loop(0, self.values.shape[1] // step, some, 0)

    def start(self, k):
        y = self.line(k)
        self.push(
            self.values.at[self.share(1 - self.core, y)],
            self.from_core.at[y],
            self.core_sems.at[0, k],
            self.core_sems.at[1, k],
            self.peer(self.y, 1 - self.core),
        )

    def cores(self, k):
        y = self.line(k)
        share = self.share(self.core, y)
        if not self.draining:
            arrived(self.from_core.at[y], self.core_sems.at[1, k])
            self.add(share, [(self.from_core, y)])
        if k > 0:
            self.push(
                self.values.at[share],
                self.from_y.at[self.lines - k - 1],
                self.y_sems.at[0, k],
                self.y_sems.at[1, self.lines - k],
                self.peer(y, self.core),
            )

    def over_y(self):
        share = self.share(self.core, self.y)
        if not self.draining:
            for k in range(1, self.lines):
                arrived(self.from_y.at[k - 1], self.y_sems.at[1, k])
            self.add(share, [(self.from_y, k) for k in range(self.lines - 1)])
        for k in range(1, self.lines):
            self.push(
                self.values.at[share],
                self.over_back.at[self.lines - k - 1],
                self.back_sems.at[0, k],
                self.back_sems.at[1, self.lines - k],
                self.peer(self.line(k), self.core),
            )
        self.send_home(0)

    def own(self, k):
        return self.values.at[self.share(self.core, self.y)] if k == 0 else self.over_back.at[k - 1]

    def send_home(self, k):
        self.push(
            self.own(k),
            self.over_home.at[k],
            self.home_sems.at[0, k],
            self.home_sems.at[1, k],
            self.peer(self.y, 1 - self.core),
        )

    def back(self):
        for k in range(1, self.lines):
            if not self.draining:
                arrived(self.over_back.at[k - 1], self.back_sems.at[1, k])
            self.send_home(k)

    def home(self):
        for k in range(self.lines):
            arrived(self.over_home.at[k], self.home_sems.at[1, k])

    def totals(self):
        for k in range(self.lines):
            yield self.own(k), self.share(self.core, self.line(k))
            yield self.over_home.at[k], self.share(1 - self.core, self.line(k))


def sum_small(small, seen, send_sems, recv_sems, axis, rows):
    me, size = lax.axis_index(axis), lax.axis_size(axis)
    copies = []
    seen[me] = small[...]
    for k in range(1, size):
        copy = pltpu.make_async_remote_copy(
            seen.at[me], seen.at[me], send_sems.at[k], recv_sems.at[size - k],
            device_id={axis: (me + k) % size}, device_id_type=MESH,
        )
        copy.start()
        copies.append(copy)
    for k in range(1, size):
        arrived(seen.at[(me + k) % size], recv_sems.at[k])
    total = seen[0]
    for other in range(1, size):
        total = total + seen[other]
    small[...] = jnp.where(grid_index(total.shape, 0) < rows, total, small[...])
    return copies


def input_back_kernel(
    count, grad_ref, weight_ref, gates_ref, later_ref, input_ref, gain_ref, dgain_ref, dnorm_ref,
    dtaps_ref, dparams_ref, wout_ref, normed_ref, grad_out, norm1_out, norm2_out, gain_out,
    taps_out, params_out, dmain_out, drest_out, *scratch
):
    *scratch, small_out, normed, normed_sem = scratch
    late = Late(normed_ref, normed, normed_sem)
    normed_ref = normed
    parts, rest = scratch[0], scratch[SCATTER_COUNT:]
    values = rest[0]
    near, near_send, near_recv, far, far_send, far_recv, staged, out_sems = rest[9:]
    group = Group(count)
    scatter = scatter_of(group, SCATTER_SHARE, scratch[:SCATTER_COUNT])
    replicas = Replicas(*rest[:5], rest[5:9])
    meet(count, lax.axis_size("dp"))
    small_out[...] = jnp.zeros(small_out.shape, F32)
    small_out[1:2] = dnorm_ref[...]
    small_out[2:3, : dgain_ref.shape[1]] = dgain_ref[...]
    small_out[3:7, : dtaps_ref.shape[1]] = dtaps_ref[...]
    for row in range(2):
        small_out[7:8, 128 * row : 128 * (row + 1)] = dparams_ref[row : row + 1]
    width = grad_ref.shape[2]
    values[:, :, width:] = split(wout_ref[...], values.shape[0])

    def prepare(piece):
        rows = scatter.rows(piece)

        def store(cols, value):
            parts[:, :, rows, cols] = split(value.astype(BF16), group.deep, group.nx)

        left, edge = joined(grad_ref[:, rows]), weight_ref.shape[1]
        wide_dot(
            [(left[:, :edge], weight_ref), (left[:, edge:], gates_ref)], NT, 256, store
        )

    def end(piece, dnormed):
        rows = scatter.rows(piece)
        given = input_ref[rows].astype(F32)
        scale = inverse_rms(given)
        normed = given * scale
        small_out[0:1] += jnp.sum(dnormed * normed, axis=0, keepdims=True)
        scaled = dnormed * gain_ref[...]
        grad_out[rows] = later_ref[rows] + scale * (
            scaled - normed * jnp.mean(scaled * normed, axis=-1, keepdims=True)
        )

    def weight_share(core, y, first=False):
        if first:
            late.wait()
        share = replicas.share(core, y)
        left = joined(normed_ref[share])
        grads = joined(grad_ref[...])
        for first in range(0, width, 384):
            cols = slice(first, min(first + 384, width))
            staged[:, cols] = lax.dot_general(
                left, grads[:, cols], (TN, ((), ())), preferred_element_type=F32
            ).astype(BF16)

        def some(block, _):
            rows = pl.ds(pl.multiple_of(block * 64, 64), 64)
            values[share, rows, :width] = staged[rows]
            return 0

        lax.fori_loop(0, staged.shape[0] // 64, some, 0)

    def other_core(k):
        weight_share(1 - replicas.core, replicas.line(k), k == replicas.lines - 1)
        replicas.start(k)

    def this_core(k):
        weight_share(replicas.core, replicas.line(k))
        replicas.cores(k)

    steps = []
    for k in range(replicas.lines - 1, -1, -1):
        steps += [functools.partial(other_core, k), functools.partial(this_core, k)]
    while len(steps) < 5:
        steps.append(lambda: None)
    steps.append(replicas.over_y)

    before, within, behind = scatter_ticks(scatter, prepare, end)

    def tick(time, _):
        before(time)
        at_each_z(group, functools.partial(within, time))
        behind(time)
        for index, step in enumerate(steps):
            pl.when(time == index)(step)
        return 0

    lax.fori_loop(-1, max(scatter.pieces + scatter.last - 1, len(steps)), tick, 0)
    replicas.back()
    copies = sum_small(small_out, near, near_send, near_recv, "heads", 3)
    copies += sum_small(small_out, far, far_send, far_recv, "dp", 8)
    norm1_out[...] = small_out[0:1]
    norm2_out[...] = small_out[1:2]
    gain_out[...] = small_out[2:3, : gain_out.shape[1]]
    kind_width = taps_out.shape[2]
    for kind in range(taps_out.shape[0]):
        taps_out[kind] = small_out[3:7, kind * kind_width : (kind + 1) * kind_width]
    for row in range(2):
        params_out[row : row + 1] = small_out[7:8, 128 * row : 128 * (row + 1)]
    replicas.home()
    part = dmain_out.shape[3]
    outs = []
    for index, (total, share) in enumerate(replicas.totals()):
        for kind in range(4):
            outs.append((total.at[:, pl.ds(kind * part, part)], dmain_out.at[kind, share], index))
        rest_cols = pl.ds(4 * part, drest_out.shape[2])
        outs.append((total.at[:, rest_cols], drest_out.at[share], index))
    outs = [
        pltpu.make_async_copy(source, target, out_sems.at[index, place % 5])
        for place, (source, target, index) in enumerate(outs)
    ]
    for copy in outs:
        copy.start()
    scatter.drain()
    replicas.drain()
    for copy in copies:
        copy.wait_send()
    for copy in outs:
        copy.wait()


def input_back(
    grad, weight, gates, later, rows, gain, dgain, dnorm, dtaps, dparams, grad_wout, normed, count,
    replica_count,
):
    own, features = rows.shape
    nz, nx = grid_sizes(count)
    width, share = grad_wout.shape[1], features // replica_count
    cols = grad.shape[1] + width
    dma = pltpu.SemaphoreType.DMA
    return pl.pallas_call(
        functools.partial(input_back_kernel, count),
        out_shape=[
            jax.ShapeDtypeStruct((own, features), F32),
            *[jax.ShapeDtypeStruct((1, features), F32)] * 2,
            jax.ShapeDtypeStruct(dgain.shape, F32),
            jax.ShapeDtypeStruct((3, 4, width), F32),
            jax.ShapeDtypeStruct(dparams.shape, F32),
            jax.ShapeDtypeStruct((4, replica_count, share, width), BF16),
            jax.ShapeDtypeStruct((replica_count, share, cols - 4 * width), BF16),
        ],
        in_specs=[VMEM_SPEC] * 11 + [ANY_SPEC],
        out_specs=[VMEM_SPEC] * 6 + [ANY_SPEC] * 2,
        scratch_shapes=[
            *scatter_scratch(nz, nx, own, features, SCATTER_SHARE, FEW),
            *Replicas.scratch(features, cols, replica_count),
            pltpu.VMEM((count, 8, features), F32),
            dma((count,)),
            dma((count,)),
            pltpu.VMEM((replica_count, 8, features), F32),
            dma((replica_count,)),
            dma((replica_count,)),
            pltpu.VMEM((share, grad.shape[1]), BF16),
            dma((replica_count, 5)),
            pltpu.VMEM((8, features), F32),
            pltpu.VMEM(normed.shape, BF16),
            dma,
        ],
        compiler_params=linked(3),
        cost_estimate=lasting(120),
        name="input_back",
    )(
        split(grad, count), weight, gates, later, rows, gain, dgain, dnorm, dtaps, dparams,
        grad_wout, normed,
    )


def spread_kernel(given_ref, out_ref):
    for kind in range(given_ref.shape[0]):
        out_ref[:, kind, :] = given_ref[kind].astype(F32)


def by_rows(values):
    kinds, rows, cols = values.shape
    return pl.pallas_call(
        spread_kernel,
        grid=(rows // 256,),
        in_specs=[pl.BlockSpec((kinds, 256, cols), lambda i: (0, i, 0))],
        out_specs=pl.BlockSpec((256, kinds, cols), lambda i: (i, 0, 0)),
        out_shape=jax.ShapeDtypeStruct((rows, kinds, cols), F32),
        name="by_rows",
    )(values)


def on_device(
    block_in,
    seq_counts,
    norm1_gain,
    w_qkvg,
    conv_weight,
    w_gates,
    gate_params,
    out_gain,
    w_out,
    norm2_gain,
    w_gate_up,
    w_down,
    cotangent,
):
    own_rows, features = block_in.shape
    count = lax.axis_size("heads")
    all_rows = own_rows * count
    width = conv_weight.shape[2]
    heads = gate_params.shape[1]
    longer = seq_counts[0, 1:2]
    first_row = lax.axis_index("heads") * own_rows
    row_index = first_row + jnp.arange(own_rows, dtype=jnp.int32)
    live_own = jnp.where(longer[0] > 0, True, row_index < seq_counts[0, 0] * SEQ_SHORT)
    live_own = live_own.astype(F32)[:, None]
    gates_weight = jnp.pad(
        w_gates.reshape(features, 2 * heads), ((0, 0), (0, 128 - 2 * heads))
    )
    full_normed1, projected, weight = project(
        block_in, norm1_gain[None], w_qkvg, gates_weight, count, lax.axis_size("dp")
    )
    projected = projected.reshape(all_rows, -1)
    taps = jnp.transpose(conv_weight, (1, 0, 2)).reshape(4, 3 * width)
    params = jnp.pad(gate_params, ((0, 0), (0, 128 - heads)))
    gain_row = out_gain[None]
    mixed, *saved, grad_feed = mixer_forward(
        longer, projected, taps, params, gain_row, cotangent, live_own, count
    )
    feed_weight = jnp.transpose(w_gate_up, (1, 2, 0))
    middle, full_normed2, grad_gate, grad_up, hidden = branch_and_feed(
        mixed,
        w_out,
        block_in,
        live_own,
        norm2_gain[None],
        feed_weight,
        w_down,
        grad_feed,
        count,
    )
    grad_middle, grad_gain2, grad_mixed, grad_wout, early = feed_back(
        grad_gate,
        grad_up,
        feed_weight,
        cotangent,
        middle,
        live_own,
        norm2_gain[None],
        w_out,
        mixed,
        hidden,
        full_normed2,
        grad_feed,
        count,
    )
    early = lax.psum(early, "dp")
    dprojected, dtaps, dparams, dgain, layer_out = mixer_backward(
        longer,
        grad_mixed.reshape(all_rows, width),
        projected,
        saved,
        taps,
        params,
        gain_row,
        hidden,
        w_down,
        middle,
        live_own,
        count,
    )

    grad_in, grad_gain1, grad_gain2, dgain, grad_conv, dparams, grad_main, grad_rest = input_back(
        dprojected,
        weight,
        gates_weight,
        grad_middle,
        block_in,
        norm1_gain[None],
        dgain,
        grad_gain2,
        dtaps,
        dparams,
        grad_wout,
        full_normed1,
        count,
        lax.axis_size("dp"),
    )
    grad_main = grad_main.reshape(4, features, width)
    grad_rest = grad_rest.reshape(features, -1)
    return (
        layer_out,
        grad_in,
        grad_gain1[0],
        by_rows(grad_main),
        grad_conv,
        grad_rest[:, : 2 * heads].reshape(w_gates.shape).astype(F32),
        dparams[:, :heads],
        dgain[0],
        grad_rest[:, 128:].T.astype(F32),
        grad_gain2[0],
        jnp.transpose(early[:2].astype(F32), (2, 0, 1)),
        early[2].astype(F32),
    )


def solution(mesh):
    return jax.shard_map(
        on_device,
        mesh=mesh,
        in_specs=(
            P(("dp", "heads"), None),
            P("dp", None),
            P(),
            P(None, None, "heads"),
            P(None, None, "heads"),
            P(None, None, "heads"),
            P(None, "heads"),
            P(),
            P("heads", None),
            P(),
            P(None, None, "heads"),
            P("heads", None),
            P(("dp", "heads"), None),
        ),
        out_specs=(
            P(("dp", "heads"), None),
            P(("dp", "heads"), None),
            P(),
            P(None, None, "heads"),
            P(None, None, "heads"),
            P(None, None, "heads"),
            P(None, "heads"),
            P(),
            P("heads", None),
            P(),
            P(None, None, "heads"),
            P("heads", None),
        ),
        check_vma=False,
    )
```

```python
import functools
import math
import jax
import jax.numpy as jnp
from jax import lax
from jax.experimental import pallas as pl
from jax.experimental.pallas import tpu as pltpu
from jax.sharding import PartitionSpec as P

SEQ_SHORT = 512
CHUNK = 256
HEAD = 128
EPS = 1e-06
F32 = jnp.float32
BF16 = jnp.bfloat16
LOW, MID, TOP = lax.Precision.DEFAULT, lax.Precision.HIGH, lax.Precision.HIGHEST
NN, NT, TN = ((1,), (0,)), ((1,), (1,)), ((0,), (0,))
P_FWD, P_BWD = MID, MID


def dot(left, right, dims, precision):
    if precision is LOW:
        left, right = left.astype(BF16), right.astype(BF16)
        return lax.dot_general(left, right, (dims, ((), ())), preferred_element_type=F32)
    return lax.dot_general(
        left, right, (dims, ((), ())), precision=precision, preferred_element_type=F32
    )


def grid_index(shape, axis):
    return lax.broadcasted_iota(jnp.int32, shape, axis)


def positions(longer, first_row, count):
    rows = grid_index((count, 1), 0) + first_row
    return jnp.where(longer > 0, rows, rows % SEQ_SHORT)


def keeps(longer, first_row):
    start = jnp.where(longer > 0, first_row, first_row % SEQ_SHORT)
    return jnp.where(start > 0, 1.0, 0.0).astype(F32)


def softplus(x):
    return jnp.maximum(x, 0.0) + jnp.log1p(jnp.exp(-jnp.abs(x)))


def gate_values(gates, params, heads):
    lane = grid_index(gates.shape, 1)
    rate = jnp.exp(params[0:1])
    shifted = gates + params[1:2]
    log_decay = jnp.where(lane < heads, -rate * softplus(shifted), 0.0)
    return rate, shifted, log_decay


def lane_column(values, index):
    return values[:, index : index + 1]


def decays(cumulative, cumulative_rows, head, masks):
    column = lane_column(cumulative, head)
    row = cumulative_rows[head : head + 1, :]
    inclusive = masks[0]
    ratio = jnp.where(inclusive, jnp.exp(jnp.where(inclusive, column - row, 0.0)), 0.0)
    last = column[CHUNK - 1 : CHUNK, :]
    return ratio, jnp.exp(column), jnp.exp(last - column), jnp.exp(last)


def unit(values):
    scale = lax.rsqrt(jnp.sum(values * values, axis=-1, keepdims=True) + EPS)
    return values * scale, scale


def pair_of(values):
    high = values.astype(BF16)
    return high, (values - high.astype(F32)).astype(BF16)


def pair_dot(left, right):
    def product(a, b):
        return lax.dot_general(a, b, (NN, ((), ())), preferred_element_type=F32)

    return product(left[0], right[0]) + (product(left[0], right[1]) + product(left[1], right[0]))


def inverses(links, row, col):
    apart = row ^ col
    size = links[0].shape[0]
    outs = [jnp.where(row == col, 1.0, 0.0) - jnp.where(apart == 1, link, 0.0) for link in links]
    pairs = [pair_of(link) for link in links]
    step = 2
    while step < size // 2:
        level = (apart >= step) & (apart < 2 * step)
        parts = [tuple(jnp.where(level, half, 0) for half in pair) for pair in pairs]
        out_pairs = [pair_of(out) for out in outs]
        inner = [pair_of(pair_dot(part, out)) for part, out in zip(parts, out_pairs)]
        outs = [out - pair_dot(pair, mid) for out, pair, mid in zip(outs, out_pairs, inner)]
        step *= 2
    half = size // 2
    uppers = [pair_of(out[:half, :half]) for out in outs]
    lowers = [pair_of(out[half:, half:]) for out in outs]
    corners = [tuple(each[half:, :half] for each in pair) for pair in pairs]
    inner = [pair_of(pair_dot(corner, upper)) for corner, upper in zip(corners, uppers)]
    corners = [pair_dot(lower, mid) for lower, mid in zip(lowers, inner)]
    return [
        jnp.concatenate(
            [out[:half], jnp.concatenate([-corner, out[half:, half:]], axis=1)], axis=0
        )
        for out, corner in zip(outs, corners)
    ]


def forward_kernel(
    heads, count, chunks, longer_ref, main_ref, conv_ref, params_ref, gain_ref, top_ref, live_ref,
    mixed_ref, conv_out_ref, raw_ref, delta_ref, solve_ref, state_ref, full_out,
    state, tail_rows, *scratch
):
    step = pl.program_id(0)
    first_row = step * CHUNK
    run, close = gather_along(step, chunks, count, top_ref, live_ref, full_out, scratch)
    run(2 * step)
    longer = longer_ref[0]
    width = heads * HEAD

    @pl.when(step == 0)
    def _():
        state[...] = jnp.zeros_like(state)
        tail_rows[...] = jnp.zeros_like(tail_rows)

    position = positions(longer, first_row, CHUNK)
    keep = keeps(longer, first_row)
    triple = main_ref[:, : 3 * width]
    padded = jnp.concatenate([tail_rows[...], triple], axis=0)
    taps = conv_ref[...]
    convolved = triple * taps[0:1]
    for lag in range(1, 4):
        shifted = padded[8 - lag : 8 - lag + CHUNK]
        convolved = convolved + jnp.where(position >= lag, shifted, 0.0) * taps[lag : lag + 1]
    tail_rows[...] = triple[CHUNK - 8 :]
    conv_out_ref[...] = convolved
    active = convolved * jax.nn.sigmoid(convolved)
    gates = main_ref[:, 4 * width :]
    rate, shifted_gate, log_decay = gate_values(gates, params_ref[...], heads)
    beta_all = jax.nn.sigmoid(gates)
    row = grid_index((CHUNK, CHUNK), 0)
    col = grid_index((CHUNK, CHUNK), 1)
    masks = (row >= col, row > col)
    cumulative = dot(jnp.where(masks[0], 1.0, 0.0), log_decay, NN, TOP)
    cumulative_rows = jnp.transpose(cumulative)
    each = range(heads)
    columns = [slice(head * HEAD, (head + 1) * HEAD) for head in each]
    queries = [unit(active[:, cols])[0] * HEAD**-0.5 for cols in columns]
    keys = [unit(active[:, width + head * HEAD : width + (head + 1) * HEAD])[0] for head in each]
    values = [active[:, 2 * width + head * HEAD : 2 * width + (head + 1) * HEAD] for head in each]
    betas = [lane_column(beta_all, heads + head) for head in each]
    spans = [decays(cumulative, cumulative_rows, head, masks) for head in each]
    grams = [
        dot(jnp.concatenate([key, query], axis=0), key, NT, P_FWD)
        for key, query in zip(keys, queries)
    ]
    links = [
        jnp.where(masks[1], beta * span[0] * gram[:CHUNK], 0.0)
        for beta, span, gram in zip(betas, spans, grams)
    ]
    solves = inverses(links, row, col)
    run(2 * step + 1)
    boths = [
        dot(
            solve,
            jnp.concatenate([beta * value, (beta * span[1]) * key], axis=1),
            NN,
            P_FWD,
        )
        for solve, beta, value, key, span in zip(solves, betas, values, keys, spans)
    ]
    entries = [state[head] * keep for head in each]
    carried = [
        dot(jnp.concatenate([both[:, HEAD:], span[1] * query], axis=0), entry, NT, P_FWD)
        for both, span, query, entry in zip(boths, spans, queries, entries)
    ]
    deltas = [both[:, :HEAD] - carry[:CHUNK] for both, carry in zip(boths, carried)]
    states = [
        span[3] * entry + dot(delta * span[2], key, TN, P_FWD)
        for span, entry, delta, key in zip(spans, entries, deltas, keys)
    ]
    raws = [
        carry[CHUNK:] + dot(gram[CHUNK:] * span[0], delta, NN, P_FWD)
        for carry, gram, span, delta in zip(carried, grams, spans, deltas)
    ]
    for head, cols in zip(each, columns):
        solve_ref[head] = solves[head]
        state_ref[0, head] = entries[head]
        state[head] = states[head]
        delta_ref[:, cols] = deltas[head]
        raw = raws[head]
        raw_ref[:, cols] = raw
        scale = lax.rsqrt(jnp.mean(raw * raw, axis=-1, keepdims=True) + EPS)
        gate = main_ref[:, 3 * width + head * HEAD : 3 * width + (head + 1) * HEAD]
        mixed = raw * scale * gain_ref[...] * (gate * jax.nn.sigmoid(gate))
        mixed_ref[:, cols] = mixed.astype(mixed_ref.dtype)
    pl.when(step == chunks - 1)(close)


def spread_ticks(tick, first, ticks, halves):
    def run(half):
        def one(index, _):
            tick(first + index)
            return 0

        lax.fori_loop(half * ticks // halves, (half + 1) * ticks // halves, one, 0)

    return run


def gather_along(step, chunks, count, top_ref, live_ref, full_out, scratch):
    *scratch, out_sems = scratch
    full = scratch[0]
    group = Group(count)
    gather = gather_of(group, GATHER_SHARE, scratch)

    def out(piece):
        rows = gather.rows(piece)
        return pltpu.make_async_copy(
            full.at[:, :, rows], full_out.at[:, :, rows], out_sems.at[piece]
        )

    def prepare(piece):
        rows = gather.rows(piece)
        full[group.z, group.x, rows] = (live_ref[rows] * top_ref[rows].astype(F32)).astype(BF16)

    before, within, behind = gather_ticks(gather, prepare, lambda piece: out(piece).start())

    def tick(time):
        before(time)
        at_each_z(group, functools.partial(within, time))
        behind(time)

    def close():
        gather.drain()

        def finish(piece, _):
            out(piece).wait()
            return 0

        lax.fori_loop(0, gather.pieces, finish, 0)

    pl.when(step == 0)(functools.partial(meet, count))
    return spread_ticks(tick, 0, gather.pieces + gather.last, 2 * chunks), close


def scatter_along(step, chunks, count, hidden_ref, weight_ref, middle_ref, live_ref, out, scratch):
    parts = scratch[0]
    group = Group(count)
    scatter = scatter_of(group, SCATTER_SHARE, scratch)

    def prepare(piece):
        rows = scatter.rows(piece)

        def store(cols, value):
            parts[:, :, rows, cols] = split(value.astype(BF16), group.deep, group.nx)

        wide_dot([(joined(hidden_ref[:, rows]), weight_ref)], NN, 512, store)

    def end(piece, total):
        rows = scatter.rows(piece)
        out[rows] = (middle_ref[rows] + live_ref[rows] * total).astype(BF16)

    before, within, behind = scatter_ticks(scatter, prepare, end)

    def tick(time):
        before(time)
        at_each_z(group, functools.partial(within, time))
        behind(time)

    pl.when(step == 0)(functools.partial(meet, count))
    return spread_ticks(tick, -1, scatter.pieces + scatter.last, 2 * chunks), scatter.drain


def backward_kernel(
    heads, chunks, count, longer_ref, grad_ref, main_ref, conv_out_ref, raw_ref, delta_ref,
    solve_ref, state_ref, conv_ref, params_ref, gain_ref, hidden_ref, down_ref, middle_ref, live_ref,
    dmain_ref, dconv_ref, dparams_ref, dgain_ref, layer_ref, dstate, head_rows, *scratch
):
    step = pl.program_id(0)
    first_row = (chunks - 1 - step) * CHUNK
    run, close = scatter_along(
        step, chunks, count, hidden_ref, down_ref, middle_ref, live_ref, layer_ref, scratch
    )
    run(2 * step)
    longer = longer_ref[0]
    width = heads * HEAD

    @pl.when(step == 0)
    def _():
        dstate[...] = jnp.zeros_like(dstate)
        head_rows[...] = jnp.zeros_like(head_rows)
        dconv_ref[...] = jnp.zeros_like(dconv_ref)
        dparams_ref[...] = jnp.zeros_like(dparams_ref)
        dgain_ref[...] = jnp.zeros_like(dgain_ref)

    keep = keeps(longer, first_row)
    convolved = conv_out_ref[...]
    sigmoid_conv = jax.nn.sigmoid(convolved)
    active = convolved * sigmoid_conv
    slope = sigmoid_conv * (1.0 + convolved * (1.0 - sigmoid_conv))
    gates = main_ref[:, 4 * width :]
    params = params_ref[...]
    rate, shifted_gate, log_decay = gate_values(gates, params, heads)
    beta_all = jax.nn.sigmoid(gates)
    row = grid_index((CHUNK, CHUNK), 0)
    col = grid_index((CHUNK, CHUNK), 1)
    masks = (row >= col, row > col)
    cumulative = dot(jnp.where(masks[0], 1.0, 0.0), log_decay, NN, TOP)
    cumulative_rows = jnp.transpose(cumulative)
    lane = grid_index((CHUNK, 128), 1)
    last_row = grid_index((CHUNK, 1), 0) == CHUNK - 1
    gain = gain_ref[...]
    dgains, dlogs, dbetas, dparts = ([None] * heads for _ in range(4))

    def work(head):
        cols = slice(head * HEAD, (head + 1) * HEAD)
        gate = main_ref[:, 3 * width + head * HEAD : 3 * width + (head + 1) * HEAD]
        raw = raw_ref[:, cols]
        grad = grad_ref[:, cols]
        scale = lax.rsqrt(jnp.mean(raw * raw, axis=-1, keepdims=True) + EPS)
        normed = raw * scale
        sigmoid_gate = jax.nn.sigmoid(gate)
        gated = gate * sigmoid_gate
        product = grad * normed
        dgains[head] = jnp.sum(product * gated, axis=0, keepdims=True)
        dgate = product * gain * (sigmoid_gate * (1.0 + gate * (1.0 - sigmoid_gate)))
        dmain_ref[:, 3 * width + head * HEAD : 3 * width + (head + 1) * HEAD] = dgate.astype(
            dmain_ref.dtype
        )
        dnormed = grad * gain * gated
        draw = scale * (dnormed - normed * jnp.mean(dnormed * normed, axis=-1, keepdims=True))
        query_unit, query_scale = unit(active[:, head * HEAD : (head + 1) * HEAD])
        query = query_unit * HEAD**-0.5
        key, key_scale = unit(active[:, width + head * HEAD : width + (head + 1) * HEAD])
        value = active[:, 2 * width + head * HEAD : 2 * width + (head + 1) * HEAD]
        beta = lane_column(beta_all, heads + head)
        ratio, decay_in, decay_out, decay_all = decays(cumulative, cumulative_rows, head, masks)
        entry = state_ref[0, head]
        delta = delta_ref[:, cols]
        dlater = dstate[head]
        gram = dot(query, key, NT, P_BWD) * ratio
        yield
        key_dlater = dot(key, dlater, NT, P_BWD)
        yield
        ddelta = dot(gram, draw, TN, P_BWD) + decay_out * key_dlater
        yield
        dright = dot(solve_ref[head], ddelta, TN, P_BWD)
        yield
        pairs = dot(jnp.concatenate([dright, draw], axis=0), delta, NT, P_BWD)
        yield
        dlink = jnp.where(masks[1], -pairs[:CHUNK] * ratio, 0.0)
        dgram = pairs[CHUNK:] * ratio
        on_entry = dot(jnp.concatenate([dright, draw], axis=0), entry, NN, P_BWD)
        yield
        key_entry = dot(key, entry, NT, P_BWD)
        yield
        on_key = dot(jnp.concatenate([dlink, dgram], axis=0), key, NN, P_BWD)
        yield
        dquery = decay_in * on_entry[CHUNK:] + on_key[CHUNK:]
        link_key = on_key[:CHUNK]
        key_read = beta * (link_key - decay_in * on_entry[:CHUNK])
        key_tail = decay_out * dot(delta, dlater, NN, P_BWD)
        yield
        key_write = (
            dot(beta * dlink, key, TN, P_BWD) + dot(dgram, query, TN, P_BWD) + key_tail
        )
        yield
        dkey = key_read + key_write
        dvalue = beta * dright
        dbeta = jnp.sum(
            dright * (value - decay_in * key_entry) + key * link_key, axis=-1, keepdims=True
        )
        dlog = jnp.sum(query * dquery + key * (key_read - key_write), axis=-1, keepdims=True)
        ending = decay_all * jnp.sum(
            jnp.sum(entry * dlater, axis=-1, keepdims=True), axis=0, keepdims=True
        ) + jnp.sum(jnp.sum(key * key_tail, axis=-1, keepdims=True), axis=0, keepdims=True)
        dlog = dlog + jnp.where(last_row, ending, 0.0)
        dlogs[head], dbetas[head] = dlog, dbeta
        dstate[head] = keep * (
            decay_all * dlater
            + dot(decay_in * draw, query, TN, P_BWD)
            - dot((beta * decay_in) * dright, key, TN, P_BWD)
        )
        yield
        dquery = (HEAD**-0.5 * query_scale) * (
            dquery - query_unit * jnp.sum(dquery * query_unit, axis=-1, keepdims=True)
        )
        dkey = key_scale * (dkey - key * jnp.sum(dkey * key, axis=-1, keepdims=True))
        dparts[head] = (dquery, dkey, dvalue)

    works = [work(head) for head in range(heads)]
    turns = 0
    while works:
        works = [each for each in works if next(each, "end") != "end"]
        turns += 1
        if turns == 6:
            run(2 * step + 1)
    dcumulative = jnp.zeros((CHUNK, 128), F32)
    dbeta_all = jnp.zeros((CHUNK, 128), F32)
    for head in range(heads):
        dcumulative = jnp.where(lane == head, dlogs[head], dcumulative)
        dbeta_all = jnp.where(lane == heads + head, dbetas[head], dbeta_all)
    dgain = functools.reduce(jnp.add, dgains)
    dconv_parts = [[dparts[head][kind] for head in range(heads)] for kind in range(3)]
    dactive = jnp.concatenate([p for parts in dconv_parts for p in parts], axis=1)
    dconvolved = dactive * slope
    padded = jnp.concatenate([dconvolved, head_rows[...]], axis=0)
    position = positions(longer, first_row, CHUNK + 8)
    taps = conv_ref[...]
    triple = main_ref[:, : 3 * width]
    dtriple = dconvolved * taps[0:1]
    dconv_ref[0:1] += jnp.sum(dconvolved * triple, axis=0, keepdims=True)
    for lag in range(1, 4):
        moved = jnp.where(position >= lag, padded, 0.0)[lag : lag + CHUNK]
        dtriple = dtriple + moved * taps[lag : lag + 1]
        dconv_ref[lag : lag + 1] += jnp.sum(moved * triple, axis=0, keepdims=True)
    head_rows[...] = dconvolved[:8]
    dmain_ref[:, : 3 * width] = dtriple.astype(dmain_ref.dtype)
    dlog_decay = dot(jnp.where(row <= col, 1.0, 0.0), dcumulative, NN, TOP)
    dshifted = -dlog_decay * rate * jax.nn.sigmoid(shifted_gate)
    dshifted = jnp.where(lane < heads, dshifted, 0.0)
    dparams_ref[0:1] += jnp.sum(dlog_decay * log_decay, axis=0, keepdims=True)
    dparams_ref[1:2] += jnp.sum(dshifted, axis=0, keepdims=True)
    dmain_ref[:, 4 * width :] = (dshifted + dbeta_all * beta_all * (1.0 - beta_all)).astype(
        dmain_ref.dtype
    )
    dgain_ref[...] += dgain
    pl.when(step == chunks - 1)(close)


def row_block(width, chunks, backward):
    if backward:
        return pl.BlockSpec((CHUNK, width), lambda i: (chunks - 1 - i, 0))
    return pl.BlockSpec((CHUNK, width), lambda i: (i, 0))


def whole_block(shape):
    return pl.BlockSpec(shape, lambda i: (0,) * len(shape))


def mixer_forward(longer, main, conv, params, gain, top, live, count):
    rows, width = main.shape[0], conv.shape[1] // 3
    heads, chunks = width // HEAD, rows // CHUNK
    own, features = top.shape
    nz, nx = grid_sizes(count)
    rowed = functools.partial(row_block, chunks=chunks, backward=False)
    shape = jax.ShapeDtypeStruct
    return pl.pallas_call(
        functools.partial(forward_kernel, heads, count, chunks),
        grid=(chunks,),
        in_specs=[
            pl.BlockSpec(memory_space=pltpu.SMEM),
            rowed(4 * width + 128),
            whole_block((4, 3 * width)),
            whole_block((2, 128)),
            whole_block((1, HEAD)),
            whole_block((own, features)),
            whole_block((own, 1)),
        ],
        out_specs=[
            rowed(width),
            rowed(3 * width),
            rowed(width),
            rowed(width),
            pl.BlockSpec((heads, CHUNK, CHUNK), lambda i: (0, i, 0)),
            pl.BlockSpec((1, heads, HEAD, HEAD), lambda i: (i, 0, 0, 0)),
            pl.BlockSpec(memory_space=pl.ANY),
        ],
        out_shape=[
            shape((rows, width), BF16),
            shape((rows, 3 * width), F32),
            shape((rows, width), F32),
            shape((rows, width), F32),
            shape((heads, rows, CHUNK), F32),
            shape((chunks, heads, HEAD, HEAD), F32),
            shape((nz, nx, own, features), BF16),
        ],
        scratch_shapes=[
            pltpu.VMEM((heads, HEAD, HEAD), F32),
            pltpu.VMEM((8, 3 * width), F32),
            *gather_scratch(nz, nx, own, features, FEW),
            pltpu.SemaphoreType.DMA((pieces_of(own, FEW),)),
        ],
        compiler_params=linked(4),
        cost_estimate=lasting(95),
        name="mixer_forward",
    )(longer, main, conv, params, gain, top, live)


def mixer_backward(
    longer, grad, main, saved, conv, params, gain, hidden, down_weight, middle, live, count
):
    rows, width = main.shape[0], conv.shape[1] // 3
    heads, chunks = width // HEAD, rows // CHUNK
    own, features = middle.shape
    nz, nx = grid_sizes(count)
    rowed = functools.partial(row_block, chunks=chunks, backward=True)
    shape = jax.ShapeDtypeStruct
    return pl.pallas_call(
        functools.partial(backward_kernel, heads, chunks, count),
        grid=(chunks,),
        in_specs=[
            pl.BlockSpec(memory_space=pltpu.SMEM),
            rowed(width),
            rowed(4 * width + 128),
            rowed(3 * width),
            rowed(width),
            rowed(width),
            pl.BlockSpec((heads, CHUNK, CHUNK), lambda i: (0, chunks - 1 - i, 0)),
            pl.BlockSpec((1, heads, HEAD, HEAD), lambda i: (chunks - 1 - i, 0, 0, 0)),
            whole_block((4, 3 * width)),
            whole_block((2, 128)),
            whole_block((1, HEAD)),
            whole_block(hidden.shape),
            whole_block(down_weight.shape),
            whole_block((own, features)),
            whole_block((own, 1)),
        ],
        out_specs=[
            rowed(4 * width + 128),
            whole_block((4, 3 * width)),
            whole_block((2, 128)),
            whole_block((1, HEAD)),
            whole_block((own, features)),
        ],
        out_shape=[
            shape((rows, 4 * width + 128), BF16),
            shape((4, 3 * width), F32),
            shape((2, 128), F32),
            shape((1, HEAD), F32),
            shape((own, features), BF16),
        ],
        scratch_shapes=[
            pltpu.VMEM((heads, HEAD, HEAD), F32),
            pltpu.VMEM((8, 3 * width), F32),
            *scatter_scratch(nz, nx, own, features, SCATTER_SHARE, FEW),
        ],
        compiler_params=linked(5),
        cost_estimate=lasting(100),
        name="mixer_backward",
    )(
        longer, grad, main, *saved, conv, params, gain, hidden, down_weight, middle, live
    )


MESH = pl.DeviceIdType.MESH
MANY, FEW = 16, 8


def pieces_of(rows, most):
    return min(most, rows // 16)


def grid_sizes(count):
    nz = 4 if count % 4 == 0 else 1
    return nz, count // nz


class Group:
    def __init__(self, count):
        self.deep, self.nx = grid_sizes(count)
        me = lax.axis_index("heads")
        self.z, self.x = me // self.nx, me % self.nx

    def column(self, j):
        return (self.x + j) % self.nx

    def over_x(self, j):
        return {"heads": self.z * self.nx + self.column(j)}

    def along_z(self, z):
        return {"heads": z * self.nx + self.x}


def meet(count, replicas=1):
    barrier = pltpu.get_barrier_semaphore()
    for axis, size in (("heads", count), ("dp", replicas)):
        me = lax.axis_index(axis)

        def greet(k, _, axis=axis, size=size, me=me):
            pl.semaphore_signal(
                barrier, inc=1, device_id={axis: (me + k) % size}, device_id_type=MESH
            )
            return 0

        lax.fori_loop(1, size, greet, 0)
    pl.semaphore_wait(barrier, count + replicas - 2)


def arrived(ref, sem):
    pltpu.make_async_copy(ref, ref, sem).wait()


def during(piece, pieces, work):
    pl.when((piece >= 0) & (piece < pieces))(functools.partial(work, piece))


def push(source, target, send_sem, recv_sem, device):
    pltpu.make_async_remote_copy(
        source, target, send_sem, recv_sem, device_id=device, device_id_type=MESH
    ).start()


class Gather:
    def __init__(self, group, full, cols, sems, x_first):
        self.group, self.full, self.cols, self.x_first = group, full, cols, x_first
        self.line_send, self.line_recv, self.x_send, self.x_recv = sems
        self.pieces = self.x_send.shape[0]
        self.part = full.shape[2] // self.pieces
        self.last = group.deep

    @staticmethod
    def sems(deep, nx, pieces):
        dma = pltpu.SemaphoreType.DMA
        return [dma((pieces, 2)), dma((pieces, deep)), dma((pieces, nx)), dma((pieces, nx))]

    def at(self, piece, z, column):
        rows = pl.ds(pl.multiple_of(piece * self.part, self.part), self.part)
        return self.full.at[z, column, rows, self.cols]

    def columns(self):
        return slice(None) if self.x_first else self.group.x

    def push_line(self, piece, z, way, zz):
        place = self.at(piece, z, self.columns())
        push(
            place,
            place,
            self.line_send.at[piece, way],
            self.line_recv.at[piece, z],
            self.group.along_z(zz + (1 if way == 0 else -1)),
        )

    def push_x(self, piece, z):
        place = self.at(piece, z, self.group.x)
        for j in range(1, self.group.nx):
            push(
                place,
                place,
                self.x_send.at[piece, j],
                self.x_recv.at[piece, self.group.nx - j],
                self.group.over_x(j),
            )

    def own_line(self, piece, zz):
        if zz + 1 < self.group.deep:
            self.push_line(piece, zz, 0, zz)
        if zz > 0:
            self.push_line(piece, zz, 1, zz)

    def begin(self, piece):
        self.push_x(piece, self.group.z)
        if not self.x_first:
            group = self.group
            pl.when(group.z + 1 < group.deep)(lambda: self.push_line(piece, group.z, 0, group.z))
            pl.when(group.z > 0)(lambda: self.push_line(piece, group.z, 1, group.z))

    def phase(self, piece, step, zz):
        deep, nx = self.group.deep, self.group.nx
        if self.x_first:
            if step == 1:
                for j in range(1, nx):
                    arrived(self.at(piece, zz, self.group.column(j)), self.x_recv.at[piece, j])
                self.own_line(piece, zz)
                return
            step -= 1
        elif step == deep:
            for j in range(1, nx):
                place = self.at(piece, slice(None), self.group.column(j))
                arrived(place, self.x_recv.at[piece, j])
            return
        for z, way in ((zz - step, 0), (zz + step, 1)):
            if 0 <= z < deep:
                arrived(self.at(piece, z, self.columns()), self.line_recv.at[piece, z])
                if 0 <= zz + (1 if way == 0 else -1) < deep:
                    self.push_line(piece, z, way, zz)
                if not self.x_first:
                    self.push_x(piece, z)

    def drain(self, piece, zz):
        deep, nx = self.group.deep, self.group.nx
        if zz + 1 < deep:
            place = self.at(piece, pl.ds(0, zz + 1), self.columns())
            arrived(place, self.line_send.at[piece, 0])
        if zz > 0:
            place = self.at(piece, pl.ds(zz, deep - zz), self.columns())
            arrived(place, self.line_send.at[piece, 1])
        z = zz if self.x_first else slice(None)
        for j in range(1, nx):
            arrived(self.at(piece, z, self.group.x), self.x_send.at[piece, j])


class Scatter:
    last = 4

    def __init__(self, group, parts, cols, scratch, z_first):
        self.group, self.parts, self.cols, self.z_first = group, parts, cols, z_first
        self.landed_x, self.line, *sems = scratch
        self.x_send, self.x_recv, self.z_send, self.z_recv = sems
        self.pieces = self.x_send.shape[0]
        self.part = parts.shape[2] // self.pieces

    @staticmethod
    def scratch(deep, nx, rows, cols, z_first, pieces):
        dma = pltpu.SemaphoreType.DMA
        return [
            pltpu.VMEM((max(nx - 1, 1), 1 if z_first else deep, rows, cols), BF16),
            pltpu.VMEM((deep + 1, nx if z_first else 1, rows, cols), BF16),
            *[dma((pieces, nx))] * 2,
            *[dma((pieces, 2))] * 2,
        ]

    def rows(self, piece):
        return pl.ds(pl.multiple_of(piece * self.part, self.part), self.part)

    def columns(self):
        return slice(None) if self.z_first else pl.ds(self.group.x, 1)

    def at(self, piece, z, column):
        return self.parts.at[z, column, self.rows(piece), self.cols]

    def line_at(self, piece, way, zz):
        first, size = (zz + 1, self.group.deep - zz) if way == 0 else (0, zz + 1)
        return self.line.at[pl.ds(first, size), :, self.rows(piece)]

    def push_line(self, piece, way, zz):
        deep = self.group.deep
        first, size = (zz + 1, deep - 1 - zz) if way == 0 else (0, zz)
        if size == 0:
            return
        after = zz + 1 if way == 0 else zz - 1
        push(
            self.at(piece, pl.ds(first, size), self.columns()),
            self.line_at(piece, way, after),
            self.z_send.at[piece, way],
            self.z_recv.at[piece, way],
            self.group.along_z(after),
        )

    def ends(self, piece, zz):
        if zz == 0:
            self.push_line(piece, 0, zz)
        if zz == self.group.deep - 1:
            self.push_line(piece, 1, zz)

    def hand_on(self, piece, near, zz):
        deep = self.group.deep
        if zz == 0 or zz == deep - 1:
            return
        way = 0 if (zz < deep // 2) == near else 1
        arrived(self.line_at(piece, way, zz), self.z_recv.at[piece, way])
        first, size = (zz + 1, deep - 1 - zz) if way == 0 else (0, zz)
        shift = 1 if way == 0 else 0
        ours = self.at(piece, pl.ds(first, size), self.columns())
        landed = self.line.at[pl.ds(first + shift, size), :, self.rows(piece)]
        ours[...] = (ours[...].astype(F32) + landed[...].astype(F32)).astype(BF16)
        self.push_line(piece, way, zz)

    def wait_ends(self, piece, zz):
        deep = self.group.deep
        if deep == 1:
            return
        if zz == 0:
            arrived(self.line_at(piece, 1, zz), self.z_recv.at[piece, 1])
        if zz == deep - 1:
            arrived(self.line_at(piece, 0, zz), self.z_recv.at[piece, 0])

    def total_line(self, piece, column):
        group, rows = self.group, self.rows(piece)
        total = self.parts[group.z, column, rows, self.cols].astype(F32)
        index = column if self.z_first else 0
        for here, place in ((group.z > 0, group.z + 1), (group.z + 1 < group.deep, group.z)):
            landed = self.line[place, index, rows]
            total = total + jnp.where(here, landed.astype(F32), 0.0)
        return total

    def begin(self, piece):
        if not self.z_first:
            for j in range(1, self.group.nx):
                push(
                    self.at(piece, slice(None), self.group.column(j)),
                    self.landed_x.at[self.group.nx - j - 1, :, self.rows(piece)],
                    self.x_send.at[piece, j],
                    self.x_recv.at[piece, self.group.nx - j],
                    self.group.over_x(j),
                )

    def begin_line(self, piece, zz):
        if self.z_first:
            self.ends(piece, zz)

    def wait_x(self, piece, j):
        landed = self.landed_x.at[j - 1, :, self.rows(piece)]
        arrived(landed, self.x_recv.at[piece, j])
        return landed[...].astype(F32)

    def phase(self, piece, step, zz):
        nx = self.group.nx
        if self.z_first:
            if step < 3:
                self.hand_on(piece, step == 1, zz)
            elif step == 3:
                self.wait_ends(piece, zz)
            return
        if step == 1:
            ours = self.at(piece, slice(None), self.group.x)
            total = ours[...].astype(F32)
            for j in range(1, nx):
                total = total + self.wait_x(piece, j)
            ours[...] = total.astype(BF16)
            self.ends(piece, zz)
        elif step < 4:
            self.hand_on(piece, step == 2, zz)
        else:
            self.wait_ends(piece, zz)

    def third(self, piece):
        if not self.z_first:
            return
        group, rows = self.group, self.rows(piece)
        for j in range(1, group.nx):
            column = group.column(j)
            total = self.total_line(piece, column).astype(BF16)
            self.parts[group.z, column, rows, self.cols] = total
            push(
                self.at(piece, pl.ds(group.z, 1), column),
                self.landed_x.at[group.nx - j - 1, :, rows],
                self.x_send.at[piece, j],
                self.x_recv.at[piece, group.nx - j],
                group.over_x(j),
            )

    def total(self, piece):
        total = self.total_line(piece, self.group.x)
        if self.z_first:
            for j in range(1, self.group.nx):
                total = total + self.wait_x(piece, j)[0]
        return total

    def drain(self, piece, zz):
        deep = self.group.deep
        for way, size in ((0, deep - 1 - zz), (1, zz)):
            if size > 0:
                place = self.at(piece, pl.ds(0, size), self.columns())
                arrived(place, self.z_send.at[piece, way])
        z = pl.ds(0, 1 if self.z_first else deep)
        for j in range(1, self.group.nx):
            arrived(self.at(piece, z, self.group.x), self.x_send.at[piece, j])


class Both:
    def __init__(self, first, second):
        self.both = (first, second)
        self.group = first.group
        self.part, self.pieces, self.last = first.part, first.pieces, first.last

    def rows(self, piece):
        return pl.ds(pl.multiple_of(piece * self.part, self.part), self.part)

    def begin(self, piece):
        for each in self.both:
            each.begin(piece)

    def begin_line(self, piece, zz):
        for each in self.both:
            each.begin_line(piece, zz)

    def phase(self, piece, step, zz):
        for each in self.both:
            each.phase(piece, step, zz)

    def third(self, piece):
        for each in self.both:
            each.third(piece)

    def total(self, piece):
        return jnp.concatenate([each.total(piece) for each in self.both], axis=1)

    def drain(self):
        def at(zz):
            def one(piece, _):
                for each in self.both:
                    each.drain(piece, zz)
                return 0

            lax.fori_loop(0, self.pieces, one, 0)

        at_each_z(self.group, at)


def at_each_z(group, work):
    for zz in range(group.deep):
        pl.when(group.z == zz)(functools.partial(work, zz))


def scatter_ticks(scatter, prepare, finish, after=None):
    def before(time):
        def begin(piece):
            prepare(piece)
            scatter.begin(piece)

        during(time + 1, scatter.pieces, begin)

    def within(time, zz):
        during(time + 1, scatter.pieces, functools.partial(scatter.begin_line, zz=zz))
        for step in range(1, scatter.last + 1):
            during(time - step + 1, scatter.pieces, functools.partial(scatter.phase, step=step, zz=zz))

    def behind(time):
        during(time - 2, scatter.pieces, scatter.third)
        during(time - scatter.last + 1, scatter.pieces, lambda piece: finish(piece, scatter.total(piece)))

    return before, within, behind


def gather_ticks(gather, prepare, ready):
    def before(time):
        if prepare is not None:

            def begin(piece):
                prepare(piece)
                gather.begin(piece)

            during(time, gather.pieces, begin)

    def within(time, zz):
        for step in range(1, gather.last + 1):
            during(time - step, gather.pieces, functools.partial(gather.phase, step=step, zz=zz))

    def behind(time):
        during(time - gather.last, gather.pieces, ready)

    return before, within, behind


def cut(cols, share):
    edge = cols - cols * share // 8
    return pl.ds(0, edge), pl.ds(edge, cols - edge)


def gather_of(group, share, scratch):
    full, *sems = scratch
    first, second = cut(full.shape[3], share)
    return Both(
        Gather(group, full, first, sems[:4], False), Gather(group, full, second, sems[4:], True)
    )


def scatter_of(group, share, scratch):
    parts, *rest = scratch
    first, second = cut(parts.shape[3], share)
    return Both(
        Scatter(group, parts, first, rest[:6], False),
        Scatter(group, parts, second, rest[6:], True),
    )


def gather_scratch(nz, nx, rows, cols, most):
    sems = Gather.sems(nz, nx, pieces_of(rows, most))
    return [pltpu.VMEM((nz, nx, rows, cols), BF16), *sems, *sems]


def scatter_scratch(nz, nx, rows, cols, share, most):
    first, second = cut(cols, share)
    pieces = pieces_of(rows, most)
    return [
        pltpu.VMEM((nz, nx, rows, cols), BF16),
        *Scatter.scratch(nz, nx, rows, first.size, False, pieces),
        *Scatter.scratch(nz, nx, rows, second.size, True, pieces),
    ]


SCATTER_COUNT, GATHER_COUNT = 13, 9


def inverse_rms(rows):
    return lax.rsqrt(jnp.mean(rows * rows, axis=-1, keepdims=True) + EPS)


def wide_dot(terms, dims, tile, store):
    total = terms[0][1].shape[0 if dims is NT else 1]
    for first in range(0, total, tile):
        cols = slice(first, min(first + tile, total))
        products = [
            lax.dot_general(
                left,
                right[cols, :] if dims is NT else right[:, cols],
                (dims, ((), ())),
                preferred_element_type=F32,
            )
            for left, right in terms
        ]
        store(cols, functools.reduce(jnp.add, products))


VMEM_SPEC = pl.BlockSpec(memory_space=pltpu.VMEM)
ANY_SPEC = pl.BlockSpec(memory_space=pl.ANY)
PAIR_SHARE, GATHER_SHARE, SCATTER_SHARE = 3, 1, 2


class Late:
    def __init__(self, given, held, sem):
        self.held = held
        self.copy = pltpu.make_async_copy(given, held, sem)
        self.copy.start()

    def wait(self):
        self.copy.wait()


def late_all(given, scratch):
    return [
        Late(ref, held, sem)
        for ref, held, sem in zip(given, scratch[: len(given)], scratch[len(given) :])
    ]


def late_scratch(*values):
    return [
        *[pltpu.VMEM(value.shape, value.dtype) for value in values],
        *[pltpu.SemaphoreType.DMA] * len(values),
    ]


def lasting(microseconds):
    return pl.CostEstimate(
        flops=int(microseconds * 1.1e9), bytes_accessed=2**20, transcendentals=0
    )


def linked(collective):
    return pltpu.CompilerParams(
        collective_id=collective, has_side_effects=True, vmem_limit_bytes=62 * 2**20
    )


def joined(values):
    return values.reshape(-1, values.shape[-1])


def split(values, *parts):
    return values.reshape(*parts, values.shape[0] // math.prod(parts), values.shape[1])


def project_kernel(
    count, rows_ref, gain_ref, weight_ref, gates_ref, full_out, projected_out, weight_out, *scratch
):
    full = scratch[0]
    staged, full_sems, staged_sems, given, weight, given_sem, out_sem = scratch[GATHER_COUNT:]
    late = Late(weight_ref, given, given_sem)
    group = Group(count)
    gather = gather_of(group, GATHER_SHARE, scratch[:GATHER_COUNT])
    meet(count)
    weight_copy = pltpu.make_async_copy(weight, weight_out, out_sem)
    kinds, width = given.shape[1:]
    blocks = given.shape[0] // 256
    shares, share = full_out.shape[0], full_out.shape[4]

    def full_copy(piece, index):
        rows = gather.rows(piece)
        return pltpu.make_async_copy(
            full.at[:, :, rows, pl.ds(index * share, share)],
            full_out.at[index, :, :, rows],
            full_sems.at[piece, index],
        )

    def staged_copy(piece):
        rows = gather.rows(piece)
        return pltpu.make_async_copy(
            staged.at[:, rows], projected_out.at[:, rows], staged_sems.at[piece]
        )

    def prepare(piece):
        rows = rows_ref[gather.rows(piece)].astype(F32)
        full[group.z, group.x, gather.rows(piece)] = (
            rows * inverse_rms(rows) * gain_ref[...]
        ).astype(BF16)

    def ready(piece):
        rows = gather.rows(piece)
        for index in range(shares):
            full_copy(piece, index).start()

        def store(cols, value):
            staged[:, rows, cols] = split(value, count)

        left = joined(full[:, :, rows])
        wide_dot([(left, weight)], NN, 256, store)
        value = lax.dot_general(
            left, gates_ref[...], (NN, ((), ())), preferred_element_type=F32
        )
        staged[:, rows, kinds * width :] = split(value, count)
        staged_copy(piece).start()

    before, within, behind = gather_ticks(gather, prepare, ready)

    def lay_out(block, _):
        rows = pl.ds(pl.multiple_of(block * 256, 256), 256)
        for kind in range(kinds):
            weight[rows, kind * width : (kind + 1) * width] = given[rows, kind, :]
        return 0

    def tick(time, _):
        before(time)
        pl.when(time == 0)(late.wait)
        lax.fori_loop(
            jnp.minimum(time * 2, blocks), jnp.minimum(time * 2 + 2, blocks), lay_out, 0
        )
        pl.when(time == 4)(weight_copy.start)
        at_each_z(group, functools.partial(within, time))
        behind(time)
        return 0

    lax.fori_loop(0, gather.pieces + gather.last, tick, 0)
    gather.drain()
    weight_copy.wait()

    def finish(piece, _):
        for index in range(shares):
            full_copy(piece, index).wait()
        staged_copy(piece).wait()
        return 0

    lax.fori_loop(0, gather.pieces, finish, 0)


def project(rows, gain, weight, gates, count, shares):
    own, features = rows.shape
    kinds, width = weight.shape[1:]
    cols = kinds * width + gates.shape[1]
    nz, nx = grid_sizes(count)
    return pl.pallas_call(
        functools.partial(project_kernel, count),
        out_shape=[
            jax.ShapeDtypeStruct((shares, nz, nx, own, features // shares), BF16),
            jax.ShapeDtypeStruct((count, own, cols), F32),
            jax.ShapeDtypeStruct((features, kinds * width), BF16),
        ],
        in_specs=[VMEM_SPEC, VMEM_SPEC, ANY_SPEC, VMEM_SPEC],
        out_specs=[ANY_SPEC] * 3,
        scratch_shapes=[
            *gather_scratch(nz, nx, own, features, FEW),
            pltpu.VMEM((count, own, cols), F32),
            pltpu.SemaphoreType.DMA((pieces_of(own, FEW), shares)),
            pltpu.SemaphoreType.DMA((pieces_of(own, FEW),)),
            pltpu.VMEM(weight.shape, BF16),
            pltpu.VMEM((features, kinds * width), BF16),
            *[pltpu.SemaphoreType.DMA] * 2,
        ],
        compiler_params=linked(0),
        cost_estimate=lasting(100),
        name="project",
    )(rows, gain, weight, gates)


def sum_and_gather(scatter, gather, prepare, middle, ready, job=None):
    group = gather.group
    full = gather.both[0].full

    def turn(piece, total):
        full[group.z, group.x, gather.rows(piece)] = middle(piece, total).astype(BF16)
        gather.begin(piece)

    late = scatter.last - 1
    before, sum_within, sum_behind = scatter_ticks(scatter, prepare, turn)
    _, gather_within, gather_behind = gather_ticks(gather, None, ready)

    def tick(time, _):
        before(time)

        def within(zz):
            sum_within(time, zz)
            gather_within(time - late, zz)

        at_each_z(group, within)
        sum_behind(time)
        gather_behind(time - late)
        if job is not None:
            job(time + 1)
        return 0

    lax.fori_loop(-1, gather.pieces + late + gather.last, tick, 0)
    scatter.drain()
    gather.drain()


def branch_kernel(
    count, mixed_ref, weight_ref, input_ref, live_ref, gain_ref, feed_weight_ref,
    down_weight_ref, grad_ref, middle_out, full_out, dgate_out, dup_out, hidden_out, *all_scratch
):
    *scratch, grads, grad_sems, dgate, dup, hidden, feed_sems = all_scratch[:-4]
    lates = late_all((feed_weight_ref, down_weight_ref), all_scratch[-4:])
    feed_weight_ref, down_weight_ref = (late.held for late in lates)
    group = Group(count)
    scatter = scatter_of(group, PAIR_SHARE, scratch[:SCATTER_COUNT])
    gather = gather_of(group, PAIR_SHARE, scratch[SCATTER_COUNT:])
    parts, full = scratch[0], scratch[SCATTER_COUNT]

    def fetch(piece):
        slot = piece % 2
        return pltpu.make_async_copy(
            grad_ref.at[:, :, gather.rows(piece)], grads.at[slot], grad_sems.at[slot]
        )

    fetch(0).start()
    meet(count)

    def prepare(piece):
        rows = gather.rows(piece)

        def store(cols, value):
            parts[:, :, rows, cols] = split(value.astype(BF16), group.deep, group.nx)

        wide_dot([(joined(mixed_ref[:, rows]), weight_ref)], NN, 512, store)

    def middle(piece, total):
        rows = gather.rows(piece)
        values = input_ref[rows].astype(F32) + live_ref[rows] * total
        middle_out[rows] = values
        return values * inverse_rms(values) * gain_ref[...]

    def copies(piece):
        rows = gather.rows(piece)
        return [
            pltpu.make_async_copy(ref.at[:, rows], out.at[:, rows], feed_sems.at[piece, index])
            for index, (ref, out) in enumerate(
                ((dgate, dgate_out), (dup, dup_out), (hidden, hidden_out))
            )
        ] + [
            pltpu.make_async_copy(
                full.at[:, :, rows], full_out.at[:, :, rows], feed_sems.at[piece, 3]
            )
        ]

    def ready(piece):
        rows = gather.rows(piece)
        for late in lates:
            pl.when(piece == 0)(late.wait)
        fetch(piece).wait()
        pl.when(piece + 1 < gather.pieces)(lambda: fetch(piece + 1).start())
        left, grad = joined(full[:, :, rows]), joined(grads[piece % 2])
        total = feed_weight_ref.shape[1]
        for first in range(0, total, 256):
            cols = slice(first, min(first + 256, total))

            def product(a, b, dims):
                return lax.dot_general(a, b, (dims, ((), ())), preferred_element_type=F32)

            gate = product(left, feed_weight_ref[0, cols], NT)
            up = product(left, feed_weight_ref[1, cols], NT)
            dhidden = product(grad, down_weight_ref[cols, :], NT)
            sigmoid = jax.nn.sigmoid(gate)
            active = gate * sigmoid
            hidden[:, rows, cols] = split((active * up).astype(BF16), count)
            dup[:, rows, cols] = split((dhidden * active).astype(BF16), count)
            slope = sigmoid * (1.0 + gate * (1.0 - sigmoid))
            dgate[:, rows, cols] = split((dhidden * up * slope).astype(BF16), count)
        for copy in copies(piece):
            copy.start()

    sum_and_gather(scatter, gather, prepare, middle, ready)

    def finish(piece, _):
        for copy in copies(piece):
            copy.wait()
        return 0

    lax.fori_loop(0, gather.pieces, finish, 0)


def branch_and_feed(mixed, weight, rows, live, gain, feed_weight, down_weight, grad, count):
    own, features = rows.shape
    hidden = feed_weight.shape[1]
    nz, nx = grid_sizes(count)
    return pl.pallas_call(
        functools.partial(branch_kernel, count),
        out_shape=[
            jax.ShapeDtypeStruct((own, features), F32),
            jax.ShapeDtypeStruct((nz, nx, own, features), BF16),
            *[jax.ShapeDtypeStruct((count, own, hidden), BF16)] * 3,
        ],
        in_specs=[VMEM_SPEC] * 5 + [ANY_SPEC] * 3,
        out_specs=[VMEM_SPEC] + [ANY_SPEC] * 4,
        scratch_shapes=[
            *scatter_scratch(nz, nx, own, features, PAIR_SHARE, MANY),
            *gather_scratch(nz, nx, own, features, MANY),
            pltpu.VMEM((2, nz, nx, own // pieces_of(own, MANY), features), BF16),
            pltpu.SemaphoreType.DMA((2,)),
            *[pltpu.VMEM((count, own, hidden), BF16)] * 3,
            pltpu.SemaphoreType.DMA((pieces_of(own, MANY), 4)),
            *late_scratch(feed_weight, down_weight),
        ],
        compiler_params=linked(1),
        cost_estimate=lasting(180),
        name="branch_and_feed",
    )(split(mixed, count), weight, rows, live, gain, feed_weight, down_weight, grad)


TILE = 256


class TileJob:
    def __init__(self, rows_ref, tile, factors, staged, outs, fetch_sem, out_sems):
        self.rows_ref, self.tile, self.factors = rows_ref, tile, factors
        self.staged, self.outs = staged, outs
        self.fetch_sem, self.out_sems = fetch_sem, out_sems
        self.count = rows_ref.shape[3] // TILE

    def span(self, index):
        return pl.ds(pl.multiple_of(index * TILE, TILE), TILE)

    def fetch(self, index):
        return pltpu.make_async_copy(
            self.rows_ref.at[:, :, :, self.span(index)], self.tile, self.fetch_sem
        )

    def results(self, index):
        return [
            pltpu.make_async_copy(
                self.staged.at[which], out.at[:, self.span(index)], self.out_sems.at[which]
            )
            for which, out in enumerate(self.outs)
        ]

    def wait_results(self, index):
        for copy in self.results(index):
            copy.wait()

    def run(self, index):
        self.fetch(index).wait()
        left = joined(self.tile[...])
        pl.when(index > 0)(lambda: self.wait_results(index - 1))
        for which, factor in enumerate(self.factors):
            product = lax.dot_general(
                left, joined(factor[...]), (TN, ((), ())), preferred_element_type=F32
            )
            self.staged[which] = jnp.transpose(product).astype(BF16)
        for copy in self.results(index):
            copy.start()
        pl.when(index + 1 < self.count)(lambda: self.fetch(index + 1).start())


def feed_back_kernel(
    count, dgate_ref, dup_ref, feed_weight_ref, top_ref, middle_ref, live_ref,
    gain_ref, out_weight_ref, mixed_ref, hidden_ref, normed_ref, grad_feed_ref,
    dmiddle_out, dgain_out, dmixed_out, dweight_out, dfeed_out, *all_scratch
):
    lates = late_all((out_weight_ref, mixed_ref, hidden_ref), all_scratch[-6:])
    out_weight_ref, mixed_ref, hidden_ref = (late.held for late in lates)
    *scratch, total_out, tile, grad_tile, staged, grad_staged, fetch_sems, out_sems = (
        all_scratch[:-6]
    )
    group = Group(count)
    scatter = scatter_of(group, PAIR_SHARE, scratch[:SCATTER_COUNT])
    gather = gather_of(group, PAIR_SHARE, scratch[SCATTER_COUNT:])
    parts, full = scratch[0], scratch[SCATTER_COUNT]
    jobs = (
        TileJob(
            normed_ref, tile, (dgate_ref, dup_ref), staged, (dfeed_out.at[0], dfeed_out.at[1]),
            fetch_sems.at[0], out_sems.at[0],
        ),
        TileJob(
            grad_feed_ref, grad_tile, (hidden_ref,), grad_staged, (dfeed_out.at[2],),
            fetch_sems.at[1], out_sems.at[1],
        ),
    )
    for each in jobs:
        each.fetch(0).start()
    meet(count)
    dgain_out[...] = jnp.zeros(dgain_out.shape, F32)
    total_out[...] = jnp.zeros(total_out.shape, F32)

    def prepare(piece):
        rows = gather.rows(piece)

        def store(cols, value):
            parts[:, :, rows, cols] = split(value.astype(BF16), group.deep, group.nx)

        wide_dot(
            [
                (joined(dgate_ref[:, rows]), feed_weight_ref.at[0]),
                (joined(dup_ref[:, rows]), feed_weight_ref.at[1]),
            ],
            NN,
            256,
            store,
        )

    def middle(piece, dnormed):
        rows = gather.rows(piece)
        values = middle_ref[rows]
        scale = inverse_rms(values)
        normed = values * scale
        dgain_out[...] += jnp.sum(dnormed * normed, axis=0, keepdims=True)
        scaled = dnormed * gain_ref[...]
        dmiddle = top_ref[rows].astype(F32) + scale * (
            scaled - normed * jnp.mean(scaled * normed, axis=-1, keepdims=True)
        )
        dmiddle_out[rows] = dmiddle
        return live_ref[rows] * dmiddle

    def ready(piece):
        rows = gather.rows(piece)
        for late in lates[:2]:
            pl.when(piece == 0)(late.wait)
        left, mixed = joined(full[:, :, rows]), joined(mixed_ref[:, rows])

        def store(cols, value):
            dmixed_out[:, rows, cols] = split(value, count)

        wide_dot([(left, out_weight_ref)], NT, 256, store)
        for first in range(0, left.shape[1], 256):
            total_out[first : first + 256] += lax.dot_general(
                left[:, first : first + 256], mixed, (TN, ((), ())), preferred_element_type=F32
            )

    def job(time):
        pl.when(time == 1)(lates[2].wait)
        for which, each in enumerate(jobs):
            pl.when((time % 2 == which) & (time < 2 * each.count))(
                functools.partial(each.run, time // 2)
            )

    sum_and_gather(scatter, gather, prepare, middle, ready, job)
    last = gather.pieces + scatter.last + gather.last
    lax.fori_loop(last, max(2 * jobs[0].count, last), lambda time, _: (job(time), 0)[1], 0)
    for each in jobs:
        each.wait_results(each.count - 1)
    dweight_out[...] = total_out[...].astype(BF16)


def feed_back(
    dgate, dup, feed_weight, top, middle, live, gain, out_weight, mixed, hidden, normed, grad_feed,
    count,
):
    own, features = middle.shape
    nz, nx = grid_sizes(count)
    width, units = out_weight.shape[0], feed_weight.shape[1]
    return pl.pallas_call(
        functools.partial(feed_back_kernel, count),
        out_shape=[
            jax.ShapeDtypeStruct((own, features), F32),
            jax.ShapeDtypeStruct((1, features), F32),
            jax.ShapeDtypeStruct((count, own, width), F32),
            jax.ShapeDtypeStruct((features, width), BF16),
            jax.ShapeDtypeStruct((3, units, features), BF16),
        ],
        in_specs=[VMEM_SPEC] * 7 + [ANY_SPEC] * 5,
        out_specs=[VMEM_SPEC] * 4 + [ANY_SPEC],
        scratch_shapes=[
            *scatter_scratch(nz, nx, own, features, PAIR_SHARE, MANY),
            *gather_scratch(nz, nx, own, features, MANY),
            pltpu.VMEM((features, width), F32),
            pltpu.VMEM((nz, nx, own, TILE), BF16),
            pltpu.VMEM((nz, nx, own, TILE), BF16),
            pltpu.VMEM((2, units, TILE), BF16),
            pltpu.VMEM((1, units, TILE), BF16),
            pltpu.SemaphoreType.DMA((2,)),
            pltpu.SemaphoreType.DMA((2, 2)),
            *late_scratch(out_weight, split(mixed, count), hidden),
        ],
        compiler_params=linked(2),
        cost_estimate=lasting(180),
        name="feed_back",
    )(
        dgate, dup, feed_weight, top, middle, live, gain, out_weight,
        split(mixed, count), hidden, normed, grad_feed,
    )


class Replicas:
    def __init__(self, values, from_core, from_y, over_back, over_home, sems):
        self.values, self.from_core, self.from_y = values, from_core, from_y
        self.over_back, self.over_home = over_back, over_home
        self.core_sems, self.y_sems, self.back_sems, self.home_sems = sems
        me = lax.axis_index("dp")
        self.lines = lax.axis_size("dp") // 2
        self.y, self.core = me // 2, me % 2

    @staticmethod
    def scratch(rows, cols, replicas):
        lines, share = replicas // 2, rows // replicas
        return [
            pltpu.VMEM((replicas, share, cols), BF16),
            pltpu.VMEM((lines, share, cols), BF16),
            pltpu.VMEM((max(lines - 1, 1), share, cols), BF16),
            pltpu.VMEM((max(lines - 1, 1), share, cols), BF16),
            pltpu.VMEM((lines, share, cols), BF16),
            *[pltpu.SemaphoreType.DMA((2, lines))] * 4,
        ]

    def share(self, core, y):
        return core * self.lines + y

    def peer(self, y, core):
        return {"dp": y * 2 + core}

    def line(self, k):
        return (self.y + k) % self.lines

    draining = False

    def push(self, source, target, send_sem, recv_sem, device):
        copy = pltpu.make_async_remote_copy(
            source, target, send_sem, recv_sem, device_id=device, device_id_type=MESH
        )
        if self.draining:
            copy.wait_send()
        else:
            copy.start()

    def drain(self):
        self.draining = True
        for k in range(self.lines):
            self.start(k)
            self.cores(k)
        self.over_y()
        self.back()
        self.draining = False

    def add(self, share, others):
        step = 64

        def some(block, _):
            rows = pl.ds(pl.multiple_of(block * step, step), step)
            total = self.values[share, rows].astype(F32)
            for ref, index in others:
                total = total + ref[index, rows].astype(F32)
            self.values[share, rows] = total.astype(BF16)
            return 0

        lax.fori_loop(0, self.values.shape[1] // step, some, 0)

    def start(self, k):
        y = self.line(k)
        self.push(
            self.values.at[self.share(1 - self.core, y)],
            self.from_core.at[y],
            self.core_sems.at[0, k],
            self.core_sems.at[1, k],
            self.peer(self.y, 1 - self.core),
        )

    def cores(self, k):
        y = self.line(k)
        share = self.share(self.core, y)
        if not self.draining:
            arrived(self.from_core.at[y], self.core_sems.at[1, k])
            self.add(share, [(self.from_core, y)])
        if k > 0:
            self.push(
                self.values.at[share],
                self.from_y.at[self.lines - k - 1],
                self.y_sems.at[0, k],
                self.y_sems.at[1, self.lines - k],
                self.peer(y, self.core),
            )

    def over_y(self):
        share = self.share(self.core, self.y)
        if not self.draining:
            for k in range(1, self.lines):
                arrived(self.from_y.at[k - 1], self.y_sems.at[1, k])
            self.add(share, [(self.from_y, k) for k in range(self.lines - 1)])
        for k in range(1, self.lines):
            self.push(
                self.values.at[share],
                self.over_back.at[self.lines - k - 1],
                self.back_sems.at[0, k],
                self.back_sems.at[1, self.lines - k],
                self.peer(self.line(k), self.core),
            )
        self.send_home(0)

    def own(self, k):
        return self.values.at[self.share(self.core, self.y)] if k == 0 else self.over_back.at[k - 1]

    def send_home(self, k):
        self.push(
            self.own(k),
            self.over_home.at[k],
            self.home_sems.at[0, k],
            self.home_sems.at[1, k],
            self.peer(self.y, 1 - self.core),
        )

    def back(self):
        for k in range(1, self.lines):
            if not self.draining:
                arrived(self.over_back.at[k - 1], self.back_sems.at[1, k])
            self.send_home(k)

    def home(self):
        for k in range(self.lines):
            arrived(self.over_home.at[k], self.home_sems.at[1, k])

    def totals(self):
        for k in range(self.lines):
            yield self.own(k), self.share(self.core, self.line(k))
            yield self.over_home.at[k], self.share(1 - self.core, self.line(k))


def sum_small(small, seen, send_sems, recv_sems, axis, rows):
    me, size = lax.axis_index(axis), lax.axis_size(axis)
    copies = []
    seen[me] = small[...]
    for k in range(1, size):
        copy = pltpu.make_async_remote_copy(
            seen.at[me], seen.at[me], send_sems.at[k], recv_sems.at[size - k],
            device_id={axis: (me + k) % size}, device_id_type=MESH,
        )
        copy.start()
        copies.append(copy)
    for k in range(1, size):
        arrived(seen.at[(me + k) % size], recv_sems.at[k])
    total = seen[0]
    for other in range(1, size):
        total = total + seen[other]
    small[...] = jnp.where(grid_index(total.shape, 0) < rows, total, small[...])
    return copies


def input_back_kernel(
    count, grad_ref, weight_ref, gates_ref, later_ref, input_ref, gain_ref, dgain_ref, dnorm_ref,
    dtaps_ref, dparams_ref, wout_ref, normed_ref, grad_out, norm1_out, norm2_out, gain_out,
    taps_out, params_out, dmain_out, drest_out, *scratch
):
    *scratch, small_out, normed, normed_sem = scratch
    late = Late(normed_ref, normed, normed_sem)
    normed_ref = normed
    parts, rest = scratch[0], scratch[SCATTER_COUNT:]
    values = rest[0]
    near, near_send, near_recv, far, far_send, far_recv, staged, out_sems = rest[9:]
    group = Group(count)
    scatter = scatter_of(group, SCATTER_SHARE, scratch[:SCATTER_COUNT])
    replicas = Replicas(*rest[:5], rest[5:9])
    meet(count, lax.axis_size("dp"))
    small_out[...] = jnp.zeros(small_out.shape, F32)
    small_out[1:2] = dnorm_ref[...]
    small_out[2:3, : dgain_ref.shape[1]] = dgain_ref[...]
    small_out[3:7, : dtaps_ref.shape[1]] = dtaps_ref[...]
    for row in range(2):
        small_out[7:8, 128 * row : 128 * (row + 1)] = dparams_ref[row : row + 1]
    width = grad_ref.shape[2]
    values[:, :, width:] = split(wout_ref[...], values.shape[0])

    def prepare(piece):
        rows = scatter.rows(piece)

        def store(cols, value):
            parts[:, :, rows, cols] = split(value.astype(BF16), group.deep, group.nx)

        left, edge = joined(grad_ref[:, rows]), weight_ref.shape[1]
        wide_dot(
            [(left[:, :edge], weight_ref), (left[:, edge:], gates_ref)], NT, 256, store
        )

    def end(piece, dnormed):
        rows = scatter.rows(piece)
        given = input_ref[rows].astype(F32)
        scale = inverse_rms(given)
        normed = given * scale
        small_out[0:1] += jnp.sum(dnormed * normed, axis=0, keepdims=True)
        scaled = dnormed * gain_ref[...]
        grad_out[rows] = later_ref[rows] + scale * (
            scaled - normed * jnp.mean(scaled * normed, axis=-1, keepdims=True)
        )

    def weight_share(core, y, first=False):
        if first:
            late.wait()
        share = replicas.share(core, y)
        left = joined(normed_ref[share])
        grads = joined(grad_ref[...])
        for first in range(0, width, 384):
            cols = slice(first, min(first + 384, width))
            staged[:, cols] = lax.dot_general(
                left, grads[:, cols], (TN, ((), ())), preferred_element_type=F32
            ).astype(BF16)

        def some(block, _):
            rows = pl.ds(pl.multiple_of(block * 64, 64), 64)
            values[share, rows, :width] = staged[rows]
            return 0

        lax.fori_loop(0, staged.shape[0] // 64, some, 0)

    def other_core(k):
        weight_share(1 - replicas.core, replicas.line(k), k == replicas.lines - 1)
        replicas.start(k)

    def this_core(k):
        weight_share(replicas.core, replicas.line(k))
        replicas.cores(k)

    steps = []
    for k in range(replicas.lines - 1, -1, -1):
        steps += [functools.partial(other_core, k), functools.partial(this_core, k)]
    while len(steps) < 7:
        steps.append(lambda: None)
    steps.append(replicas.over_y)

    before, within, behind = scatter_ticks(scatter, prepare, end)

    def tick(time, _):
        before(time)
        at_each_z(group, functools.partial(within, time))
        behind(time)
        for index, step in enumerate(steps):
            pl.when(time == index)(step)
        return 0

    lax.fori_loop(-1, max(scatter.pieces + scatter.last - 1, len(steps)), tick, 0)
    replicas.back()
    copies = sum_small(small_out, near, near_send, near_recv, "heads", 3)
    copies += sum_small(small_out, far, far_send, far_recv, "dp", 8)
    norm1_out[...] = small_out[0:1]
    norm2_out[...] = small_out[1:2]
    gain_out[...] = small_out[2:3, : gain_out.shape[1]]
    kind_width = taps_out.shape[2]
    for kind in range(taps_out.shape[0]):
        taps_out[kind] = small_out[3:7, kind * kind_width : (kind + 1) * kind_width]
    for row in range(2):
        params_out[row : row + 1] = small_out[7:8, 128 * row : 128 * (row + 1)]
    replicas.home()
    part = dmain_out.shape[3]
    outs = []
    for index, (total, share) in enumerate(replicas.totals()):
        for kind in range(4):
            outs.append((total.at[:, pl.ds(kind * part, part)], dmain_out.at[kind, share], index))
        rest_cols = pl.ds(4 * part, drest_out.shape[2])
        outs.append((total.at[:, rest_cols], drest_out.at[share], index))
    outs = [
        pltpu.make_async_copy(source, target, out_sems.at[index, place % 5])
        for place, (source, target, index) in enumerate(outs)
    ]
    for copy in outs:
        copy.start()
    scatter.drain()
    replicas.drain()
    for copy in copies:
        copy.wait_send()
    for copy in outs:
        copy.wait()


def input_back(
    grad, weight, gates, later, rows, gain, dgain, dnorm, dtaps, dparams, grad_wout, normed, count,
    replica_count,
):
    own, features = rows.shape
    nz, nx = grid_sizes(count)
    width, share = grad_wout.shape[1], features // replica_count
    cols = grad.shape[1] + width
    dma = pltpu.SemaphoreType.DMA
    return pl.pallas_call(
        functools.partial(input_back_kernel, count),
        out_shape=[
            jax.ShapeDtypeStruct((own, features), F32),
            *[jax.ShapeDtypeStruct((1, features), F32)] * 2,
            jax.ShapeDtypeStruct(dgain.shape, F32),
            jax.ShapeDtypeStruct((3, 4, width), F32),
            jax.ShapeDtypeStruct(dparams.shape, F32),
            jax.ShapeDtypeStruct((4, replica_count, share, width), BF16),
            jax.ShapeDtypeStruct((replica_count, share, cols - 4 * width), BF16),
        ],
        in_specs=[VMEM_SPEC] * 11 + [ANY_SPEC],
        out_specs=[VMEM_SPEC] * 6 + [ANY_SPEC] * 2,
        scratch_shapes=[
            *scatter_scratch(nz, nx, own, features, SCATTER_SHARE, FEW),
            *Replicas.scratch(features, cols, replica_count),
            pltpu.VMEM((count, 8, features), F32),
            dma((count,)),
            dma((count,)),
            pltpu.VMEM((replica_count, 8, features), F32),
            dma((replica_count,)),
            dma((replica_count,)),
            pltpu.VMEM((share, grad.shape[1]), BF16),
            dma((replica_count, 5)),
            pltpu.VMEM((8, features), F32),
            pltpu.VMEM(normed.shape, BF16),
            dma,
        ],
        compiler_params=linked(3),
        cost_estimate=lasting(120),
        name="input_back",
    )(
        split(grad, count), weight, gates, later, rows, gain, dgain, dnorm, dtaps, dparams,
        grad_wout, normed,
    )


def results_kernel(main_ref, rest_ref, feed_ref, main_out, wout_out, gate_up_out, down_out):
    for kind in range(main_ref.shape[0]):
        main_out[:, kind, :] = main_ref[kind].astype(F32)
    wout_out[...] = jnp.transpose(rest_ref[:, 128:].astype(F32))
    gate_up_out[...] = feed_ref[:2].astype(F32)
    down_out[...] = feed_ref[2].astype(F32)


def results(main, rest, feed):
    kinds, features, width = main.shape
    units = feed.shape[1]
    step = 256
    return pl.pallas_call(
        results_kernel,
        grid=(features // step,),
        in_specs=[
            pl.BlockSpec((kinds, step, width), lambda i: (0, i, 0)),
            pl.BlockSpec((step, rest.shape[1]), lambda i: (i, 0)),
            pl.BlockSpec((3, units, step), lambda i: (0, 0, i)),
        ],
        out_specs=[
            pl.BlockSpec((step, kinds, width), lambda i: (i, 0, 0)),
            pl.BlockSpec((width, step), lambda i: (0, i)),
            pl.BlockSpec((2, units, step), lambda i: (0, 0, i)),
            pl.BlockSpec((units, step), lambda i: (0, i)),
        ],
        out_shape=[
            jax.ShapeDtypeStruct((features, kinds, width), F32),
            jax.ShapeDtypeStruct((width, features), F32),
            jax.ShapeDtypeStruct((2, units, features), F32),
            jax.ShapeDtypeStruct((units, features), F32),
        ],
        compiler_params=pltpu.CompilerParams(vmem_limit_bytes=48 * 2**20),
        name="results",
    )(main, rest, feed)


def on_device(
    block_in,
    seq_counts,
    norm1_gain,
    w_qkvg,
    conv_weight,
    w_gates,
    gate_params,
    out_gain,
    w_out,
    norm2_gain,
    w_gate_up,
    w_down,
    cotangent,
):
    own_rows, features = block_in.shape
    count = lax.axis_size("heads")
    all_rows = own_rows * count
    width = conv_weight.shape[2]
    heads = gate_params.shape[1]
    longer = seq_counts[0, 1:2]
    first_row = lax.axis_index("heads") * own_rows
    row_index = first_row + jnp.arange(own_rows, dtype=jnp.int32)
    live_own = jnp.where(longer[0] > 0, True, row_index < seq_counts[0, 0] * SEQ_SHORT)
    live_own = live_own.astype(F32)[:, None]
    gates_weight = jnp.pad(
        w_gates.reshape(features, 2 * heads), ((0, 0), (0, 128 - 2 * heads))
    )
    full_normed1, projected, weight = project(
        block_in, norm1_gain[None], w_qkvg, gates_weight, count, lax.axis_size("dp")
    )
    projected = projected.reshape(all_rows, -1)
    taps = jnp.transpose(conv_weight, (1, 0, 2)).reshape(4, 3 * width)
    params = jnp.pad(gate_params, ((0, 0), (0, 128 - heads)))
    gain_row = out_gain[None]
    mixed, *saved, grad_feed = mixer_forward(
        longer, projected, taps, params, gain_row, cotangent, live_own, count
    )
    feed_weight = jnp.transpose(w_gate_up, (1, 2, 0))
    middle, full_normed2, grad_gate, grad_up, hidden = branch_and_feed(
        mixed,
        w_out,
        block_in,
        live_own,
        norm2_gain[None],
        feed_weight,
        w_down,
        grad_feed,
        count,
    )
    grad_middle, grad_gain2, grad_mixed, grad_wout, early = feed_back(
        grad_gate,
        grad_up,
        feed_weight,
        cotangent,
        middle,
        live_own,
        norm2_gain[None],
        w_out,
        mixed,
        hidden,
        full_normed2,
        grad_feed,
        count,
    )
    early = lax.psum(early, "dp")
    dprojected, dtaps, dparams, dgain, layer_out = mixer_backward(
        longer,
        grad_mixed.reshape(all_rows, width),
        projected,
        saved,
        taps,
        params,
        gain_row,
        hidden,
        w_down,
        middle,
        live_own,
        count,
    )

    grad_in, grad_gain1, grad_gain2, dgain, grad_conv, dparams, grad_main, grad_rest = input_back(
        dprojected,
        weight,
        gates_weight,
        grad_middle,
        block_in,
        norm1_gain[None],
        dgain,
        grad_gain2,
        dtaps,
        dparams,
        grad_wout,
        full_normed1,
        count,
        lax.axis_size("dp"),
    )
    grad_main = grad_main.reshape(4, features, width)
    grad_rest = grad_rest.reshape(features, -1)
    grad_qkvg, grad_out_weight, grad_gate_up, grad_down = results(grad_main, grad_rest, early)
    return (
        layer_out,
        grad_in,
        grad_gain1[0],
        grad_qkvg,
        grad_conv,
        grad_rest[:, : 2 * heads].reshape(w_gates.shape).astype(F32),
        dparams[:, :heads],
        dgain[0],
        grad_out_weight,
        grad_gain2[0],
        jnp.transpose(grad_gate_up, (2, 0, 1)),
        grad_down,
    )


def solution(mesh):
    return jax.shard_map(
        on_device,
        mesh=mesh,
        in_specs=(
            P(("dp", "heads"), None),
            P("dp", None),
            P(),
            P(None, None, "heads"),
            P(None, None, "heads"),
            P(None, None, "heads"),
            P(None, "heads"),
            P(),
            P("heads", None),
            P(),
            P(None, None, "heads"),
            P("heads", None),
            P(("dp", "heads"), None),
        ),
        out_specs=(
            P(("dp", "heads"), None),
            P(("dp", "heads"), None),
            P(),
            P(None, None, "heads"),
            P(None, None, "heads"),
            P(None, None, "heads"),
            P(None, "heads"),
            P(),
            P("heads", None),
            P(),
            P(None, None, "heads"),
            P("heads", None),
        ),
        check_vma=False,
    )
```

```python
import functools
import math
import jax
import jax.numpy as jnp
from jax import lax
from jax.experimental import pallas as pl
from jax.experimental.pallas import tpu as pltpu
from jax.sharding import PartitionSpec as P

SEQ_SHORT = 512
CHUNK = 256
HEAD = 128
EPS = 1e-06
F32 = jnp.float32
BF16 = jnp.bfloat16
LOW, MID, TOP = lax.Precision.DEFAULT, lax.Precision.HIGH, lax.Precision.HIGHEST
NN, NT, TN = ((1,), (0,)), ((1,), (1,)), ((0,), (0,))
P_FWD, P_BWD = MID, MID


def dot(left, right, dims, precision):
    if precision is LOW:
        left, right = left.astype(BF16), right.astype(BF16)
        return lax.dot_general(left, right, (dims, ((), ())), preferred_element_type=F32)
    return lax.dot_general(
        left, right, (dims, ((), ())), precision=precision, preferred_element_type=F32
    )


def grid_index(shape, axis):
    return lax.broadcasted_iota(jnp.int32, shape, axis)


def positions(longer, first_row, count):
    rows = grid_index((count, 1), 0) + first_row
    return jnp.where(longer > 0, rows, rows % SEQ_SHORT)


def keeps(longer, first_row):
    start = jnp.where(longer > 0, first_row, first_row % SEQ_SHORT)
    return jnp.where(start > 0, 1.0, 0.0).astype(F32)


def softplus(x):
    return jnp.maximum(x, 0.0) + jnp.log1p(jnp.exp(-jnp.abs(x)))


def gate_values(gates, params, heads):
    lane = grid_index(gates.shape, 1)
    rate = jnp.exp(params[0:1])
    shifted = gates + params[1:2]
    log_decay = jnp.where(lane < heads, -rate * softplus(shifted), 0.0)
    return rate, shifted, log_decay


def lane_column(values, index):
    return values[:, index : index + 1]


def decays(cumulative, cumulative_rows, head, masks):
    column = lane_column(cumulative, head)
    row = cumulative_rows[head : head + 1, :]
    inclusive = masks[0]
    ratio = jnp.where(inclusive, jnp.exp(jnp.where(inclusive, column - row, 0.0)), 0.0)
    last = column[CHUNK - 1 : CHUNK, :]
    return ratio, jnp.exp(column), jnp.exp(last - column), jnp.exp(last)


def unit(values):
    scale = lax.rsqrt(jnp.sum(values * values, axis=-1, keepdims=True) + EPS)
    return values * scale, scale


def pair_of(values):
    high = values.astype(BF16)
    return high, (values - high.astype(F32)).astype(BF16)


def pair_dot(left, right):
    def product(a, b):
        return lax.dot_general(a, b, (NN, ((), ())), preferred_element_type=F32)

    return product(left[0], right[0]) + (product(left[0], right[1]) + product(left[1], right[0]))


def inverses(links, row, col):
    apart = row ^ col
    size = links[0].shape[0]
    outs = [jnp.where(row == col, 1.0, 0.0) - jnp.where(apart == 1, link, 0.0) for link in links]
    pairs = [pair_of(link) for link in links]
    step = 2
    while step < size // 2:
        level = (apart >= step) & (apart < 2 * step)
        parts = [tuple(jnp.where(level, half, 0) for half in pair) for pair in pairs]
        out_pairs = [pair_of(out) for out in outs]
        inner = [pair_of(pair_dot(part, out)) for part, out in zip(parts, out_pairs)]
        outs = [out - pair_dot(pair, mid) for out, pair, mid in zip(outs, out_pairs, inner)]
        step *= 2
    half = size // 2
    uppers = [pair_of(out[:half, :half]) for out in outs]
    lowers = [pair_of(out[half:, half:]) for out in outs]
    corners = [tuple(each[half:, :half] for each in pair) for pair in pairs]
    inner = [pair_of(pair_dot(corner, upper)) for corner, upper in zip(corners, uppers)]
    corners = [pair_dot(lower, mid) for lower, mid in zip(lowers, inner)]
    return [
        jnp.concatenate(
            [out[:half], jnp.concatenate([-corner, out[half:, half:]], axis=1)], axis=0
        )
        for out, corner in zip(outs, corners)
    ]


def forward_kernel(
    heads, count, chunks, longer_ref, main_ref, conv_ref, params_ref, gain_ref, top_ref, live_ref,
    mixed_ref, conv_out_ref, raw_ref, delta_ref, solve_ref, state_ref, full_out,
    state, tail_rows, *scratch
):
    step = pl.program_id(0)
    first_row = step * CHUNK
    run, close = gather_along(step, chunks, count, top_ref, live_ref, full_out, scratch)
    run(2 * step)
    longer = longer_ref[0]
    width = heads * HEAD

    @pl.when(step == 0)
    def _():
        state[...] = jnp.zeros_like(state)
        tail_rows[...] = jnp.zeros_like(tail_rows)

    position = positions(longer, first_row, CHUNK)
    keep = keeps(longer, first_row)
    triple = main_ref[:, : 3 * width]
    padded = jnp.concatenate([tail_rows[...], triple], axis=0)
    taps = conv_ref[...]
    convolved = triple * taps[0:1]
    for lag in range(1, 4):
        shifted = padded[8 - lag : 8 - lag + CHUNK]
        convolved = convolved + jnp.where(position >= lag, shifted, 0.0) * taps[lag : lag + 1]
    tail_rows[...] = triple[CHUNK - 8 :]
    conv_out_ref[...] = convolved
    active = convolved * jax.nn.sigmoid(convolved)
    gates = main_ref[:, 4 * width :]
    rate, shifted_gate, log_decay = gate_values(gates, params_ref[...], heads)
    beta_all = jax.nn.sigmoid(gates)
    row = grid_index((CHUNK, CHUNK), 0)
    col = grid_index((CHUNK, CHUNK), 1)
    masks = (row >= col, row > col)
    cumulative = dot(jnp.where(masks[0], 1.0, 0.0), log_decay, NN, TOP)
    cumulative_rows = jnp.transpose(cumulative)
    each = range(heads)
    columns = [slice(head * HEAD, (head + 1) * HEAD) for head in each]
    queries = [unit(active[:, cols])[0] * HEAD**-0.5 for cols in columns]
    keys = [unit(active[:, width + head * HEAD : width + (head + 1) * HEAD])[0] for head in each]
    values = [active[:, 2 * width + head * HEAD : 2 * width + (head + 1) * HEAD] for head in each]
    betas = [lane_column(beta_all, heads + head) for head in each]
    spans = [decays(cumulative, cumulative_rows, head, masks) for head in each]
    grams = [
        dot(jnp.concatenate([key, query], axis=0), key, NT, P_FWD)
        for key, query in zip(keys, queries)
    ]
    links = [
        jnp.where(masks[1], beta * span[0] * gram[:CHUNK], 0.0)
        for beta, span, gram in zip(betas, spans, grams)
    ]
    solves = inverses(links, row, col)
    run(2 * step + 1)
    boths = [
        dot(
            solve,
            jnp.concatenate([beta * value, (beta * span[1]) * key], axis=1),
            NN,
            P_FWD,
        )
        for solve, beta, value, key, span in zip(solves, betas, values, keys, spans)
    ]
    entries = [state[head] * keep for head in each]
    carried = [
        dot(jnp.concatenate([both[:, HEAD:], span[1] * query], axis=0), entry, NT, P_FWD)
        for both, span, query, entry in zip(boths, spans, queries, entries)
    ]
    deltas = [both[:, :HEAD] - carry[:CHUNK] for both, carry in zip(boths, carried)]
    states = [
        span[3] * entry + dot(delta * span[2], key, TN, P_FWD)
        for span, entry, delta, key in zip(spans, entries, deltas, keys)
    ]
    raws = [
        carry[CHUNK:] + dot(gram[CHUNK:] * span[0], delta, NN, P_FWD)
        for carry, gram, span, delta in zip(carried, grams, spans, deltas)
    ]
    for head, cols in zip(each, columns):
        solve_ref[head] = solves[head]
        state_ref[0, head] = entries[head]
        state[head] = states[head]
        delta_ref[:, cols] = deltas[head]
        raw = raws[head]
        raw_ref[:, cols] = raw
        scale = lax.rsqrt(jnp.mean(raw * raw, axis=-1, keepdims=True) + EPS)
        gate = main_ref[:, 3 * width + head * HEAD : 3 * width + (head + 1) * HEAD]
        mixed = raw * scale * gain_ref[...] * (gate * jax.nn.sigmoid(gate))
        mixed_ref[:, cols] = mixed.astype(mixed_ref.dtype)
    pl.when(step == chunks - 1)(close)


def spread_ticks(tick, first, ticks, halves):
    def run(half):
        def one(index, _):
            tick(first + index)
            return 0

        lax.fori_loop(half * ticks // halves, (half + 1) * ticks // halves, one, 0)

    return run


def gather_along(step, chunks, count, top_ref, live_ref, full_out, scratch):
    *scratch, out_sems = scratch
    full = scratch[0]
    group = Group(count)
    gather = gather_of(group, GATHER_SHARE, scratch)

    def out(piece):
        rows = gather.rows(piece)
        return pltpu.make_async_copy(
            full.at[:, :, rows], full_out.at[:, :, rows], out_sems.at[piece]
        )

    def prepare(piece):
        rows = gather.rows(piece)
        full[group.z, group.x, rows] = (live_ref[rows] * top_ref[rows].astype(F32)).astype(BF16)

    before, within, behind = gather_ticks(gather, prepare, lambda piece: out(piece).start())

    def tick(time):
        before(time)
        at_each_z(group, functools.partial(within, time))
        behind(time)

    def close():
        gather.drain()

        def finish(piece, _):
            out(piece).wait()
            return 0

        lax.fori_loop(0, gather.pieces, finish, 0)

    pl.when(step == 0)(functools.partial(meet, count))
    return spread_ticks(tick, 0, gather.pieces + gather.last, 2 * chunks), close


def scatter_along(step, chunks, count, hidden_ref, weight_ref, middle_ref, live_ref, out, scratch):
    parts = scratch[0]
    group = Group(count)
    scatter = scatter_of(group, SCATTER_SHARE, scratch)

    def prepare(piece):
        rows = scatter.rows(piece)

        def store(cols, value):
            parts[:, :, rows, cols] = split(value.astype(BF16), group.deep, group.nx)

        wide_dot([(joined(hidden_ref[:, rows]), weight_ref)], NN, 512, store)

    def end(piece, total):
        rows = scatter.rows(piece)
        out[rows] = (middle_ref[rows] + live_ref[rows] * total).astype(BF16)

    before, within, behind = scatter_ticks(scatter, prepare, end)

    def tick(time):
        before(time)
        at_each_z(group, functools.partial(within, time))
        behind(time)

    pl.when(step == 0)(functools.partial(meet, count))
    return spread_ticks(tick, -1, scatter.pieces + scatter.last, 2 * chunks), scatter.drain


def backward_kernel(
    heads, chunks, count, longer_ref, grad_ref, main_ref, conv_out_ref, raw_ref, delta_ref,
    solve_ref, state_ref, conv_ref, params_ref, gain_ref, hidden_ref, down_ref, middle_ref, live_ref,
    dmain_ref, dconv_ref, dparams_ref, dgain_ref, layer_ref, dstate, head_rows, *scratch
):
    step = pl.program_id(0)
    first_row = (chunks - 1 - step) * CHUNK
    run, close = scatter_along(
        step, chunks, count, hidden_ref, down_ref, middle_ref, live_ref, layer_ref, scratch
    )
    run(2 * step)
    longer = longer_ref[0]
    width = heads * HEAD

    @pl.when(step == 0)
    def _():
        dstate[...] = jnp.zeros_like(dstate)
        head_rows[...] = jnp.zeros_like(head_rows)
        dconv_ref[...] = jnp.zeros_like(dconv_ref)
        dparams_ref[...] = jnp.zeros_like(dparams_ref)
        dgain_ref[...] = jnp.zeros_like(dgain_ref)

    keep = keeps(longer, first_row)
    convolved = conv_out_ref[...]
    sigmoid_conv = jax.nn.sigmoid(convolved)
    active = convolved * sigmoid_conv
    slope = sigmoid_conv * (1.0 + convolved * (1.0 - sigmoid_conv))
    gates = main_ref[:, 4 * width :]
    params = params_ref[...]
    rate, shifted_gate, log_decay = gate_values(gates, params, heads)
    beta_all = jax.nn.sigmoid(gates)
    row = grid_index((CHUNK, CHUNK), 0)
    col = grid_index((CHUNK, CHUNK), 1)
    masks = (row >= col, row > col)
    cumulative = dot(jnp.where(masks[0], 1.0, 0.0), log_decay, NN, TOP)
    cumulative_rows = jnp.transpose(cumulative)
    lane = grid_index((CHUNK, 128), 1)
    last_row = grid_index((CHUNK, 1), 0) == CHUNK - 1
    gain = gain_ref[...]
    dgains, dlogs, dbetas, dparts = ([None] * heads for _ in range(4))

    def work(head):
        cols = slice(head * HEAD, (head + 1) * HEAD)
        gate = main_ref[:, 3 * width + head * HEAD : 3 * width + (head + 1) * HEAD]
        raw = raw_ref[:, cols]
        grad = grad_ref[:, cols]
        scale = lax.rsqrt(jnp.mean(raw * raw, axis=-1, keepdims=True) + EPS)
        normed = raw * scale
        sigmoid_gate = jax.nn.sigmoid(gate)
        gated = gate * sigmoid_gate
        product = grad * normed
        dgains[head] = jnp.sum(product * gated, axis=0, keepdims=True)
        dgate = product * gain * (sigmoid_gate * (1.0 + gate * (1.0 - sigmoid_gate)))
        dmain_ref[:, 3 * width + head * HEAD : 3 * width + (head + 1) * HEAD] = dgate.astype(
            dmain_ref.dtype
        )
        dnormed = grad * gain * gated
        draw = scale * (dnormed - normed * jnp.mean(dnormed * normed, axis=-1, keepdims=True))
        query_unit, query_scale = unit(active[:, head * HEAD : (head + 1) * HEAD])
        query = query_unit * HEAD**-0.5
        key, key_scale = unit(active[:, width + head * HEAD : width + (head + 1) * HEAD])
        value = active[:, 2 * width + head * HEAD : 2 * width + (head + 1) * HEAD]
        beta = lane_column(beta_all, heads + head)
        ratio, decay_in, decay_out, decay_all = decays(cumulative, cumulative_rows, head, masks)
        entry = state_ref[0, head]
        delta = delta_ref[:, cols]
        dlater = dstate[head]
        gram = dot(query, key, NT, P_BWD) * ratio
        yield
        key_dlater = dot(key, dlater, NT, P_BWD)
        yield
        ddelta = dot(gram, draw, TN, P_BWD) + decay_out * key_dlater
        yield
        dright = dot(solve_ref[head], ddelta, TN, P_BWD)
        yield
        pairs = dot(jnp.concatenate([dright, draw], axis=0), delta, NT, P_BWD)
        yield
        dlink = jnp.where(masks[1], -pairs[:CHUNK] * ratio, 0.0)
        dgram = pairs[CHUNK:] * ratio
        on_entry = dot(jnp.concatenate([dright, draw], axis=0), entry, NN, P_BWD)
        yield
        key_entry = dot(key, entry, NT, P_BWD)
        yield
        on_key = dot(jnp.concatenate([dlink, dgram], axis=0), key, NN, P_BWD)
        yield
        dquery = decay_in * on_entry[CHUNK:] + on_key[CHUNK:]
        link_key = on_key[:CHUNK]
        key_read = beta * (link_key - decay_in * on_entry[:CHUNK])
        key_tail = decay_out * dot(delta, dlater, NN, P_BWD)
        yield
        key_write = (
            dot(beta * dlink, key, TN, P_BWD) + dot(dgram, query, TN, P_BWD) + key_tail
        )
        yield
        dkey = key_read + key_write
        dvalue = beta * dright
        dbeta = jnp.sum(
            dright * (value - decay_in * key_entry) + key * link_key, axis=-1, keepdims=True
        )
        dlog = jnp.sum(query * dquery + key * (key_read - key_write), axis=-1, keepdims=True)
        ending = decay_all * jnp.sum(
            jnp.sum(entry * dlater, axis=-1, keepdims=True), axis=0, keepdims=True
        ) + jnp.sum(jnp.sum(key * key_tail, axis=-1, keepdims=True), axis=0, keepdims=True)
        dlog = dlog + jnp.where(last_row, ending, 0.0)
        dlogs[head], dbetas[head] = dlog, dbeta
        dstate[head] = keep * (
            decay_all * dlater
            + dot(decay_in * draw, query, TN, P_BWD)
            - dot((beta * decay_in) * dright, key, TN, P_BWD)
        )
        yield
        dquery = (HEAD**-0.5 * query_scale) * (
            dquery - query_unit * jnp.sum(dquery * query_unit, axis=-1, keepdims=True)
        )
        dkey = key_scale * (dkey - key * jnp.sum(dkey * key, axis=-1, keepdims=True))
        dparts[head] = (dquery, dkey, dvalue)

    works = [work(head) for head in range(heads)]
    turns = 0
    while works:
        works = [each for each in works if next(each, "end") != "end"]
        turns += 1
        if turns == 6:
            run(2 * step + 1)
    dcumulative = jnp.zeros((CHUNK, 128), F32)
    dbeta_all = jnp.zeros((CHUNK, 128), F32)
    for head in range(heads):
        dcumulative = jnp.where(lane == head, dlogs[head], dcumulative)
        dbeta_all = jnp.where(lane == heads + head, dbetas[head], dbeta_all)
    dgain = functools.reduce(jnp.add, dgains)
    dconv_parts = [[dparts[head][kind] for head in range(heads)] for kind in range(3)]
    dactive = jnp.concatenate([p for parts in dconv_parts for p in parts], axis=1)
    dconvolved = dactive * slope
    padded = jnp.concatenate([dconvolved, head_rows[...]], axis=0)
    position = positions(longer, first_row, CHUNK + 8)
    taps = conv_ref[...]
    triple = main_ref[:, : 3 * width]
    dtriple = dconvolved * taps[0:1]
    dconv_ref[0:1] += jnp.sum(dconvolved * triple, axis=0, keepdims=True)
    for lag in range(1, 4):
        moved = jnp.where(position >= lag, padded, 0.0)[lag : lag + CHUNK]
        dtriple = dtriple + moved * taps[lag : lag + 1]
        dconv_ref[lag : lag + 1] += jnp.sum(moved * triple, axis=0, keepdims=True)
    head_rows[...] = dconvolved[:8]
    dmain_ref[:, : 3 * width] = dtriple.astype(dmain_ref.dtype)
    dlog_decay = dot(jnp.where(row <= col, 1.0, 0.0), dcumulative, NN, TOP)
    dshifted = -dlog_decay * rate * jax.nn.sigmoid(shifted_gate)
    dshifted = jnp.where(lane < heads, dshifted, 0.0)
    dparams_ref[0:1] += jnp.sum(dlog_decay * log_decay, axis=0, keepdims=True)
    dparams_ref[1:2] += jnp.sum(dshifted, axis=0, keepdims=True)
    dmain_ref[:, 4 * width :] = (dshifted + dbeta_all * beta_all * (1.0 - beta_all)).astype(
        dmain_ref.dtype
    )
    dgain_ref[...] += dgain
    pl.when(step == chunks - 1)(close)


def row_block(width, chunks, backward):
    if backward:
        return pl.BlockSpec((CHUNK, width), lambda i: (chunks - 1 - i, 0))
    return pl.BlockSpec((CHUNK, width), lambda i: (i, 0))


def whole_block(shape):
    return pl.BlockSpec(shape, lambda i: (0,) * len(shape))


def mixer_forward(longer, main, conv, params, gain, top, live, count):
    rows, width = main.shape[0], conv.shape[1] // 3
    heads, chunks = width // HEAD, rows // CHUNK
    own, features = top.shape
    nz, nx = grid_sizes(count)
    rowed = functools.partial(row_block, chunks=chunks, backward=False)
    shape = jax.ShapeDtypeStruct
    return pl.pallas_call(
        functools.partial(forward_kernel, heads, count, chunks),
        grid=(chunks,),
        in_specs=[
            pl.BlockSpec(memory_space=pltpu.SMEM),
            rowed(4 * width + 128),
            whole_block((4, 3 * width)),
            whole_block((2, 128)),
            whole_block((1, HEAD)),
            whole_block((own, features)),
            whole_block((own, 1)),
        ],
        out_specs=[
            rowed(width),
            rowed(3 * width),
            rowed(width),
            rowed(width),
            pl.BlockSpec((heads, CHUNK, CHUNK), lambda i: (0, i, 0)),
            pl.BlockSpec((1, heads, HEAD, HEAD), lambda i: (i, 0, 0, 0)),
            pl.BlockSpec(memory_space=pl.ANY),
        ],
        out_shape=[
            shape((rows, width), BF16),
            shape((rows, 3 * width), F32),
            shape((rows, width), F32),
            shape((rows, width), F32),
            shape((heads, rows, CHUNK), F32),
            shape((chunks, heads, HEAD, HEAD), F32),
            shape((nz, nx, own, features), BF16),
        ],
        scratch_shapes=[
            pltpu.VMEM((heads, HEAD, HEAD), F32),
            pltpu.VMEM((8, 3 * width), F32),
            *gather_scratch(nz, nx, own, features, FEW),
            pltpu.SemaphoreType.DMA((pieces_of(own, FEW),)),
        ],
        compiler_params=linked(4),
        cost_estimate=lasting(95),
        name="mixer_forward",
    )(longer, main, conv, params, gain, top, live)


def mixer_backward(
    longer, grad, main, saved, conv, params, gain, hidden, down_weight, middle, live, count
):
    rows, width = main.shape[0], conv.shape[1] // 3
    heads, chunks = width // HEAD, rows // CHUNK
    own, features = middle.shape
    nz, nx = grid_sizes(count)
    rowed = functools.partial(row_block, chunks=chunks, backward=True)
    shape = jax.ShapeDtypeStruct
    return pl.pallas_call(
        functools.partial(backward_kernel, heads, chunks, count),
        grid=(chunks,),
        in_specs=[
            pl.BlockSpec(memory_space=pltpu.SMEM),
            rowed(width),
            rowed(4 * width + 128),
            rowed(3 * width),
            rowed(width),
            rowed(width),
            pl.BlockSpec((heads, CHUNK, CHUNK), lambda i: (0, chunks - 1 - i, 0)),
            pl.BlockSpec((1, heads, HEAD, HEAD), lambda i: (chunks - 1 - i, 0, 0, 0)),
            whole_block((4, 3 * width)),
            whole_block((2, 128)),
            whole_block((1, HEAD)),
            whole_block(hidden.shape),
            whole_block(down_weight.shape),
            whole_block((own, features)),
            whole_block((own, 1)),
        ],
        out_specs=[
            rowed(4 * width + 128),
            whole_block((4, 3 * width)),
            whole_block((2, 128)),
            whole_block((1, HEAD)),
            whole_block((own, features)),
        ],
        out_shape=[
            shape((rows, 4 * width + 128), BF16),
            shape((4, 3 * width), F32),
            shape((2, 128), F32),
            shape((1, HEAD), F32),
            shape((own, features), BF16),
        ],
        scratch_shapes=[
            pltpu.VMEM((heads, HEAD, HEAD), F32),
            pltpu.VMEM((8, 3 * width), F32),
            *scatter_scratch(nz, nx, own, features, SCATTER_SHARE, FEW),
        ],
        compiler_params=linked(5),
        cost_estimate=lasting(100),
        name="mixer_backward",
    )(
        longer, grad, main, *saved, conv, params, gain, hidden, down_weight, middle, live
    )


MESH = pl.DeviceIdType.MESH
MANY, FEW = 16, 8


def pieces_of(rows, most):
    return min(most, rows // 16)


def grid_sizes(count):
    nz = 4 if count % 4 == 0 else 1
    return nz, count // nz


class Group:
    def __init__(self, count):
        self.deep, self.nx = grid_sizes(count)
        me = lax.axis_index("heads")
        self.z, self.x = me // self.nx, me % self.nx

    def column(self, j):
        return (self.x + j) % self.nx

    def over_x(self, j):
        return {"heads": self.z * self.nx + self.column(j)}

    def along_z(self, z):
        return {"heads": z * self.nx + self.x}


def meet(count, replicas=1):
    barrier = pltpu.get_barrier_semaphore()
    for axis, size in (("heads", count), ("dp", replicas)):
        me = lax.axis_index(axis)

        def greet(k, _, axis=axis, size=size, me=me):
            pl.semaphore_signal(
                barrier, inc=1, device_id={axis: (me + k) % size}, device_id_type=MESH
            )
            return 0

        lax.fori_loop(1, size, greet, 0)
    pl.semaphore_wait(barrier, count + replicas - 2)


def arrived(ref, sem):
    pltpu.make_async_copy(ref, ref, sem).wait()


def during(piece, pieces, work):
    pl.when((piece >= 0) & (piece < pieces))(functools.partial(work, piece))


def push(source, target, send_sem, recv_sem, device):
    pltpu.make_async_remote_copy(
        source, target, send_sem, recv_sem, device_id=device, device_id_type=MESH
    ).start()


class Gather:
    def __init__(self, group, full, cols, sems, x_first):
        self.group, self.full, self.cols, self.x_first = group, full, cols, x_first
        self.line_send, self.line_recv, self.x_send, self.x_recv = sems
        self.pieces = self.x_send.shape[0]
        self.part = full.shape[2] // self.pieces
        self.last = group.deep

    @staticmethod
    def sems(deep, nx, pieces):
        dma = pltpu.SemaphoreType.DMA
        return [dma((pieces, 2)), dma((pieces, deep)), dma((pieces, nx)), dma((pieces, nx))]

    def at(self, piece, z, column):
        rows = pl.ds(pl.multiple_of(piece * self.part, self.part), self.part)
        return self.full.at[z, column, rows, self.cols]

    def columns(self):
        return slice(None) if self.x_first else self.group.x

    def push_line(self, piece, z, way, zz):
        place = self.at(piece, z, self.columns())
        push(
            place,
            place,
            self.line_send.at[piece, way],
            self.line_recv.at[piece, z],
            self.group.along_z(zz + (1 if way == 0 else -1)),
        )

    def push_x(self, piece, z):
        place = self.at(piece, z, self.group.x)
        for j in range(1, self.group.nx):
            push(
                place,
                place,
                self.x_send.at[piece, j],
                self.x_recv.at[piece, self.group.nx - j],
                self.group.over_x(j),
            )

    def own_line(self, piece, zz):
        if zz + 1 < self.group.deep:
            self.push_line(piece, zz, 0, zz)
        if zz > 0:
            self.push_line(piece, zz, 1, zz)

    def begin(self, piece):
        self.push_x(piece, self.group.z)
        if not self.x_first:
            group = self.group
            pl.when(group.z + 1 < group.deep)(lambda: self.push_line(piece, group.z, 0, group.z))
            pl.when(group.z > 0)(lambda: self.push_line(piece, group.z, 1, group.z))

    def phase(self, piece, step, zz):
        deep, nx = self.group.deep, self.group.nx
        if self.x_first:
            if step == 1:
                for j in range(1, nx):
                    arrived(self.at(piece, zz, self.group.column(j)), self.x_recv.at[piece, j])
                self.own_line(piece, zz)
                return
            step -= 1
        elif step == deep:
            for j in range(1, nx):
                place = self.at(piece, slice(None), self.group.column(j))
                arrived(place, self.x_recv.at[piece, j])
            return
        for z, way in ((zz - step, 0), (zz + step, 1)):
            if 0 <= z < deep:
                arrived(self.at(piece, z, self.columns()), self.line_recv.at[piece, z])
                if 0 <= zz + (1 if way == 0 else -1) < deep:
                    self.push_line(piece, z, way, zz)
                if not self.x_first:
                    self.push_x(piece, z)

    def drain(self, piece, zz):
        deep, nx = self.group.deep, self.group.nx
        if zz + 1 < deep:
            place = self.at(piece, pl.ds(0, zz + 1), self.columns())
            arrived(place, self.line_send.at[piece, 0])
        if zz > 0:
            place = self.at(piece, pl.ds(zz, deep - zz), self.columns())
            arrived(place, self.line_send.at[piece, 1])
        z = zz if self.x_first else slice(None)
        for j in range(1, nx):
            arrived(self.at(piece, z, self.group.x), self.x_send.at[piece, j])


class Scatter:
    last = 4

    def __init__(self, group, parts, cols, scratch, z_first):
        self.group, self.parts, self.cols, self.z_first = group, parts, cols, z_first
        self.landed_x, self.line, *sems = scratch
        self.x_send, self.x_recv, self.z_send, self.z_recv = sems
        self.pieces = self.x_send.shape[0]
        self.part = parts.shape[2] // self.pieces

    @staticmethod
    def scratch(deep, nx, rows, cols, z_first, pieces):
        dma = pltpu.SemaphoreType.DMA
        return [
            pltpu.VMEM((max(nx - 1, 1), 1 if z_first else deep, rows, cols), BF16),
            pltpu.VMEM((deep + 1, nx if z_first else 1, rows, cols), BF16),
            *[dma((pieces, nx))] * 2,
            *[dma((pieces, 2))] * 2,
        ]

    def rows(self, piece):
        return pl.ds(pl.multiple_of(piece * self.part, self.part), self.part)

    def columns(self):
        return slice(None) if self.z_first else pl.ds(self.group.x, 1)

    def at(self, piece, z, column):
        return self.parts.at[z, column, self.rows(piece), self.cols]

    def line_at(self, piece, way, zz):
        first, size = (zz + 1, self.group.deep - zz) if way == 0 else (0, zz + 1)
        return self.line.at[pl.ds(first, size), :, self.rows(piece)]

    def push_line(self, piece, way, zz):
        deep = self.group.deep
        first, size = (zz + 1, deep - 1 - zz) if way == 0 else (0, zz)
        if size == 0:
            return
        after = zz + 1 if way == 0 else zz - 1
        push(
            self.at(piece, pl.ds(first, size), self.columns()),
            self.line_at(piece, way, after),
            self.z_send.at[piece, way],
            self.z_recv.at[piece, way],
            self.group.along_z(after),
        )

    def ends(self, piece, zz):
        if zz == 0:
            self.push_line(piece, 0, zz)
        if zz == self.group.deep - 1:
            self.push_line(piece, 1, zz)

    def hand_on(self, piece, near, zz):
        deep = self.group.deep
        if zz == 0 or zz == deep - 1:
            return
        way = 0 if (zz < deep // 2) == near else 1
        arrived(self.line_at(piece, way, zz), self.z_recv.at[piece, way])
        first, size = (zz + 1, deep - 1 - zz) if way == 0 else (0, zz)
        shift = 1 if way == 0 else 0
        ours = self.at(piece, pl.ds(first, size), self.columns())
        landed = self.line.at[pl.ds(first + shift, size), :, self.rows(piece)]
        ours[...] = (ours[...].astype(F32) + landed[...].astype(F32)).astype(BF16)
        self.push_line(piece, way, zz)

    def wait_ends(self, piece, zz):
        deep = self.group.deep
        if deep == 1:
            return
        if zz == 0:
            arrived(self.line_at(piece, 1, zz), self.z_recv.at[piece, 1])
        if zz == deep - 1:
            arrived(self.line_at(piece, 0, zz), self.z_recv.at[piece, 0])

    def total_line(self, piece, column):
        group, rows = self.group, self.rows(piece)
        total = self.parts[group.z, column, rows, self.cols].astype(F32)
        index = column if self.z_first else 0
        for here, place in ((group.z > 0, group.z + 1), (group.z + 1 < group.deep, group.z)):
            landed = self.line[place, index, rows]
            total = total + jnp.where(here, landed.astype(F32), 0.0)
        return total

    def begin(self, piece):
        if not self.z_first:
            for j in range(1, self.group.nx):
                push(
                    self.at(piece, slice(None), self.group.column(j)),
                    self.landed_x.at[self.group.nx - j - 1, :, self.rows(piece)],
                    self.x_send.at[piece, j],
                    self.x_recv.at[piece, self.group.nx - j],
                    self.group.over_x(j),
                )

    def begin_line(self, piece, zz):
        if self.z_first:
            self.ends(piece, zz)

    def wait_x(self, piece, j):
        landed = self.landed_x.at[j - 1, :, self.rows(piece)]
        arrived(landed, self.x_recv.at[piece, j])
        return landed[...].astype(F32)

    def phase(self, piece, step, zz):
        nx = self.group.nx
        if self.z_first:
            if step < 3:
                self.hand_on(piece, step == 1, zz)
            elif step == 3:
                self.wait_ends(piece, zz)
            return
        if step == 1:
            ours = self.at(piece, slice(None), self.group.x)
            total = ours[...].astype(F32)
            for j in range(1, nx):
                total = total + self.wait_x(piece, j)
            ours[...] = total.astype(BF16)
            self.ends(piece, zz)
        elif step < 4:
            self.hand_on(piece, step == 2, zz)
        else:
            self.wait_ends(piece, zz)

    def third(self, piece):
        if not self.z_first:
            return
        group, rows = self.group, self.rows(piece)
        for j in range(1, group.nx):
            column = group.column(j)
            total = self.total_line(piece, column).astype(BF16)
            self.parts[group.z, column, rows, self.cols] = total
            push(
                self.at(piece, pl.ds(group.z, 1), column),
                self.landed_x.at[group.nx - j - 1, :, rows],
                self.x_send.at[piece, j],
                self.x_recv.at[piece, group.nx - j],
                group.over_x(j),
            )

    def total(self, piece):
        total = self.total_line(piece, self.group.x)
        if self.z_first:
            for j in range(1, self.group.nx):
                total = total + self.wait_x(piece, j)[0]
        return total

    def drain(self, piece, zz):
        deep = self.group.deep
        for way, size in ((0, deep - 1 - zz), (1, zz)):
            if size > 0:
                place = self.at(piece, pl.ds(0, size), self.columns())
                arrived(place, self.z_send.at[piece, way])
        z = pl.ds(0, 1 if self.z_first else deep)
        for j in range(1, self.group.nx):
            arrived(self.at(piece, z, self.group.x), self.x_send.at[piece, j])


class Both:
    def __init__(self, first, second):
        self.both = (first, second)
        self.group = first.group
        self.part, self.pieces, self.last = first.part, first.pieces, first.last

    def rows(self, piece):
        return pl.ds(pl.multiple_of(piece * self.part, self.part), self.part)

    def begin(self, piece):
        for each in self.both:
            each.begin(piece)

    def begin_line(self, piece, zz):
        for each in self.both:
            each.begin_line(piece, zz)

    def phase(self, piece, step, zz):
        for each in self.both:
            each.phase(piece, step, zz)

    def third(self, piece):
        for each in self.both:
            each.third(piece)

    def total(self, piece):
        return jnp.concatenate([each.total(piece) for each in self.both], axis=1)

    def drain(self):
        def at(zz):
            def one(piece, _):
                for each in self.both:
                    each.drain(piece, zz)
                return 0

            lax.fori_loop(0, self.pieces, one, 0)

        at_each_z(self.group, at)


def at_each_z(group, work):
    for zz in range(group.deep):
        pl.when(group.z == zz)(functools.partial(work, zz))


def scatter_ticks(scatter, prepare, finish, after=None):
    def before(time):
        def begin(piece):
            prepare(piece)
            scatter.begin(piece)

        during(time + 1, scatter.pieces, begin)

    def within(time, zz):
        during(time + 1, scatter.pieces, functools.partial(scatter.begin_line, zz=zz))
        for step in range(1, scatter.last + 1):
            during(time - step + 1, scatter.pieces, functools.partial(scatter.phase, step=step, zz=zz))

    def behind(time):
        during(time - 2, scatter.pieces, scatter.third)
        during(time - scatter.last + 1, scatter.pieces, lambda piece: finish(piece, scatter.total(piece)))

    return before, within, behind


def gather_ticks(gather, prepare, ready):
    def before(time):
        if prepare is not None:

            def begin(piece):
                prepare(piece)
                gather.begin(piece)

            during(time, gather.pieces, begin)

    def within(time, zz):
        for step in range(1, gather.last + 1):
            during(time - step, gather.pieces, functools.partial(gather.phase, step=step, zz=zz))

    def behind(time):
        during(time - gather.last, gather.pieces, ready)

    return before, within, behind


def cut(cols, share):
    edge = cols - cols * share // 8
    return pl.ds(0, edge), pl.ds(edge, cols - edge)


def gather_of(group, share, scratch):
    full, *sems = scratch
    first, second = cut(full.shape[3], share)
    return Both(
        Gather(group, full, first, sems[:4], False), Gather(group, full, second, sems[4:], True)
    )


def scatter_of(group, share, scratch):
    parts, *rest = scratch
    first, second = cut(parts.shape[3], share)
    return Both(
        Scatter(group, parts, first, rest[:6], False),
        Scatter(group, parts, second, rest[6:], True),
    )


def gather_scratch(nz, nx, rows, cols, most):
    sems = Gather.sems(nz, nx, pieces_of(rows, most))
    return [pltpu.VMEM((nz, nx, rows, cols), BF16), *sems, *sems]


def scatter_scratch(nz, nx, rows, cols, share, most):
    first, second = cut(cols, share)
    pieces = pieces_of(rows, most)
    return [
        pltpu.VMEM((nz, nx, rows, cols), BF16),
        *Scatter.scratch(nz, nx, rows, first.size, False, pieces),
        *Scatter.scratch(nz, nx, rows, second.size, True, pieces),
    ]


SCATTER_COUNT, GATHER_COUNT = 13, 9


def inverse_rms(rows):
    return lax.rsqrt(jnp.mean(rows * rows, axis=-1, keepdims=True) + EPS)


def wide_dot(terms, dims, tile, store):
    total = terms[0][1].shape[0 if dims is NT else 1]
    for first in range(0, total, tile):
        cols = slice(first, min(first + tile, total))
        products = [
            lax.dot_general(
                left,
                right[cols, :] if dims is NT else right[:, cols],
                (dims, ((), ())),
                preferred_element_type=F32,
            )
            for left, right in terms
        ]
        store(cols, functools.reduce(jnp.add, products))


VMEM_SPEC = pl.BlockSpec(memory_space=pltpu.VMEM)
ANY_SPEC = pl.BlockSpec(memory_space=pl.ANY)
PAIR_SHARE, GATHER_SHARE, SCATTER_SHARE = 3, 1, 2


class Late:
    def __init__(self, given, held, sem):
        self.held = held
        self.copy = pltpu.make_async_copy(given, held, sem)
        self.copy.start()

    def wait(self):
        self.copy.wait()


def late_all(given, scratch):
    return [
        Late(ref, held, sem)
        for ref, held, sem in zip(given, scratch[: len(given)], scratch[len(given) :])
    ]


def late_scratch(*values):
    return [
        *[pltpu.VMEM(value.shape, value.dtype) for value in values],
        *[pltpu.SemaphoreType.DMA] * len(values),
    ]


def lasting(microseconds):
    return pl.CostEstimate(
        flops=int(microseconds * 1.1e9), bytes_accessed=2**20, transcendentals=0
    )


def linked(collective):
    return pltpu.CompilerParams(
        collective_id=collective, has_side_effects=True, vmem_limit_bytes=62 * 2**20
    )


def joined(values):
    return values.reshape(-1, values.shape[-1])


def split(values, *parts):
    return values.reshape(*parts, values.shape[0] // math.prod(parts), values.shape[1])


def project_kernel(
    count, rows_ref, gain_ref, weight_ref, gates_ref, full_out, projected_out, weight_out, *scratch
):
    full = scratch[0]
    staged, full_sems, staged_sems, given, weight, given_sem, out_sem = scratch[GATHER_COUNT:]
    late = Late(weight_ref, given, given_sem)
    group = Group(count)
    gather = gather_of(group, GATHER_SHARE, scratch[:GATHER_COUNT])
    meet(count)
    weight_copy = pltpu.make_async_copy(weight, weight_out, out_sem)
    kinds, width = given.shape[1:]
    blocks = given.shape[0] // 256
    shares, share = full_out.shape[0], full_out.shape[4]

    def full_copy(piece, index):
        rows = gather.rows(piece)
        return pltpu.make_async_copy(
            full.at[:, :, rows, pl.ds(index * share, share)],
            full_out.at[index, :, :, rows],
            full_sems.at[piece, index],
        )

    def staged_copy(piece):
        rows = gather.rows(piece)
        return pltpu.make_async_copy(
            staged.at[:, rows], projected_out.at[:, rows], staged_sems.at[piece]
        )

    def prepare(piece):
        rows = rows_ref[gather.rows(piece)].astype(F32)
        full[group.z, group.x, gather.rows(piece)] = (
            rows * inverse_rms(rows) * gain_ref[...]
        ).astype(BF16)

    def ready(piece):
        rows = gather.rows(piece)
        for index in range(shares):
            full_copy(piece, index).start()

        def store(cols, value):
            staged[:, rows, cols] = split(value, count)

        left = joined(full[:, :, rows])
        wide_dot([(left, weight)], NN, 256, store)
        value = lax.dot_general(
            left, gates_ref[...], (NN, ((), ())), preferred_element_type=F32
        )
        staged[:, rows, kinds * width :] = split(value, count)
        staged_copy(piece).start()

    before, within, behind = gather_ticks(gather, prepare, ready)

    def lay_out(block, _):
        rows = pl.ds(pl.multiple_of(block * 256, 256), 256)
        for kind in range(kinds):
            weight[rows, kind * width : (kind + 1) * width] = given[rows, kind, :]
        return 0

    def tick(time, _):
        before(time)
        pl.when(time == 0)(late.wait)
        lax.fori_loop(
            jnp.minimum(time * 2, blocks), jnp.minimum(time * 2 + 2, blocks), lay_out, 0
        )
        pl.when(time == 4)(weight_copy.start)
        at_each_z(group, functools.partial(within, time))
        behind(time)
        return 0

    lax.fori_loop(0, gather.pieces + gather.last, tick, 0)
    gather.drain()
    weight_copy.wait()

    def finish(piece, _):
        for index in range(shares):
            full_copy(piece, index).wait()
        staged_copy(piece).wait()
        return 0

    lax.fori_loop(0, gather.pieces, finish, 0)


def project(rows, gain, weight, gates, count, shares):
    own, features = rows.shape
    kinds, width = weight.shape[1:]
    cols = kinds * width + gates.shape[1]
    nz, nx = grid_sizes(count)
    return pl.pallas_call(
        functools.partial(project_kernel, count),
        out_shape=[
            jax.ShapeDtypeStruct((shares, nz, nx, own, features // shares), BF16),
            jax.ShapeDtypeStruct((count, own, cols), F32),
            jax.ShapeDtypeStruct((features, kinds * width), BF16),
        ],
        in_specs=[VMEM_SPEC, VMEM_SPEC, ANY_SPEC, VMEM_SPEC],
        out_specs=[ANY_SPEC] * 3,
        scratch_shapes=[
            *gather_scratch(nz, nx, own, features, FEW),
            pltpu.VMEM((count, own, cols), F32),
            pltpu.SemaphoreType.DMA((pieces_of(own, FEW), shares)),
            pltpu.SemaphoreType.DMA((pieces_of(own, FEW),)),
            pltpu.VMEM(weight.shape, BF16),
            pltpu.VMEM((features, kinds * width), BF16),
            *[pltpu.SemaphoreType.DMA] * 2,
        ],
        compiler_params=linked(0),
        cost_estimate=lasting(100),
        name="project",
    )(rows, gain, weight, gates)


def sum_and_gather(scatter, gather, prepare, middle, ready, job=None):
    group = gather.group
    full = gather.both[0].full

    def turn(piece, total):
        full[group.z, group.x, gather.rows(piece)] = middle(piece, total).astype(BF16)
        gather.begin(piece)

    late = scatter.last - 1
    before, sum_within, sum_behind = scatter_ticks(scatter, prepare, turn)
    _, gather_within, gather_behind = gather_ticks(gather, None, ready)

    def tick(time, _):
        before(time)

        def within(zz):
            sum_within(time, zz)
            gather_within(time - late, zz)

        at_each_z(group, within)
        sum_behind(time)
        gather_behind(time - late)
        if job is not None:
            job(time + 1)
        return 0

    lax.fori_loop(-1, gather.pieces + late + gather.last, tick, 0)
    scatter.drain()
    gather.drain()


def branch_kernel(
    count, mixed_ref, weight_ref, input_ref, live_ref, gain_ref, feed_weight_ref,
    down_weight_ref, grad_ref, middle_out, full_out, dgate_out, dup_out, hidden_out, *all_scratch
):
    *scratch, grads, grad_sems, dgate, dup, hidden, feed_sems = all_scratch[:-4]
    lates = late_all((feed_weight_ref, down_weight_ref), all_scratch[-4:])
    feed_weight_ref, down_weight_ref = (late.held for late in lates)
    group = Group(count)
    scatter = scatter_of(group, PAIR_SHARE, scratch[:SCATTER_COUNT])
    gather = gather_of(group, PAIR_SHARE, scratch[SCATTER_COUNT:])
    parts, full = scratch[0], scratch[SCATTER_COUNT]

    def fetch(piece):
        slot = piece % 2
        return pltpu.make_async_copy(
            grad_ref.at[:, :, gather.rows(piece)], grads.at[slot], grad_sems.at[slot]
        )

    fetch(0).start()
    meet(count)

    def prepare(piece):
        rows = gather.rows(piece)

        def store(cols, value):
            parts[:, :, rows, cols] = split(value.astype(BF16), group.deep, group.nx)

        wide_dot([(joined(mixed_ref[:, rows]), weight_ref)], NN, 512, store)

    def middle(piece, total):
        rows = gather.rows(piece)
        values = input_ref[rows].astype(F32) + live_ref[rows] * total
        middle_out[rows] = values
        return values * inverse_rms(values) * gain_ref[...]

    def copies(piece):
        rows = gather.rows(piece)
        return [
            pltpu.make_async_copy(ref.at[:, rows], out.at[:, rows], feed_sems.at[piece, index])
            for index, (ref, out) in enumerate(
                ((dgate, dgate_out), (dup, dup_out), (hidden, hidden_out))
            )
        ] + [
            pltpu.make_async_copy(
                full.at[:, :, rows], full_out.at[:, :, rows], feed_sems.at[piece, 3]
            )
        ]

    def ready(piece):
        rows = gather.rows(piece)
        for late in lates:
            pl.when(piece == 0)(late.wait)
        fetch(piece).wait()
        pl.when(piece + 1 < gather.pieces)(lambda: fetch(piece + 1).start())
        left, grad = joined(full[:, :, rows]), joined(grads[piece % 2])
        total = feed_weight_ref.shape[1]
        for first in range(0, total, 256):
            cols = slice(first, min(first + 256, total))

            def product(a, b, dims):
                return lax.dot_general(a, b, (dims, ((), ())), preferred_element_type=F32)

            gate = product(left, feed_weight_ref[0, cols], NT)
            up = product(left, feed_weight_ref[1, cols], NT)
            dhidden = product(grad, down_weight_ref[cols, :], NT)
            sigmoid = jax.nn.sigmoid(gate)
            active = gate * sigmoid
            hidden[:, rows, cols] = split((active * up).astype(BF16), count)
            dup[:, rows, cols] = split((dhidden * active).astype(BF16), count)
            slope = sigmoid * (1.0 + gate * (1.0 - sigmoid))
            dgate[:, rows, cols] = split((dhidden * up * slope).astype(BF16), count)
        for copy in copies(piece):
            copy.start()

    sum_and_gather(scatter, gather, prepare, middle, ready)

    def finish(piece, _):
        for copy in copies(piece):
            copy.wait()
        return 0

    lax.fori_loop(0, gather.pieces, finish, 0)


def branch_and_feed(mixed, weight, rows, live, gain, feed_weight, down_weight, grad, count):
    own, features = rows.shape
    hidden = feed_weight.shape[1]
    nz, nx = grid_sizes(count)
    return pl.pallas_call(
        functools.partial(branch_kernel, count),
        out_shape=[
            jax.ShapeDtypeStruct((own, features), F32),
            jax.ShapeDtypeStruct((nz, nx, own, features), BF16),
            *[jax.ShapeDtypeStruct((count, own, hidden), BF16)] * 3,
        ],
        in_specs=[VMEM_SPEC] * 5 + [ANY_SPEC] * 3,
        out_specs=[VMEM_SPEC] + [ANY_SPEC] * 4,
        scratch_shapes=[
            *scatter_scratch(nz, nx, own, features, PAIR_SHARE, MANY),
            *gather_scratch(nz, nx, own, features, MANY),
            pltpu.VMEM((2, nz, nx, own // pieces_of(own, MANY), features), BF16),
            pltpu.SemaphoreType.DMA((2,)),
            *[pltpu.VMEM((count, own, hidden), BF16)] * 3,
            pltpu.SemaphoreType.DMA((pieces_of(own, MANY), 4)),
            *late_scratch(feed_weight, down_weight),
        ],
        compiler_params=linked(1),
        cost_estimate=lasting(180),
        name="branch_and_feed",
    )(split(mixed, count), weight, rows, live, gain, feed_weight, down_weight, grad)


TILE = 256


class TileJob:
    def __init__(self, rows_ref, tile, factors, staged, outs, fetch_sem, out_sems):
        self.rows_ref, self.tile, self.factors = rows_ref, tile, factors
        self.staged, self.outs = staged, outs
        self.fetch_sem, self.out_sems = fetch_sem, out_sems
        self.count = rows_ref.shape[3] // TILE

    def span(self, index):
        return pl.ds(pl.multiple_of(index * TILE, TILE), TILE)

    def fetch(self, index):
        return pltpu.make_async_copy(
            self.rows_ref.at[:, :, :, self.span(index)], self.tile, self.fetch_sem
        )

    def results(self, index):
        return [
            pltpu.make_async_copy(
                self.staged.at[which], out.at[:, self.span(index)], self.out_sems.at[which]
            )
            for which, out in enumerate(self.outs)
        ]

    def wait_results(self, index):
        for copy in self.results(index):
            copy.wait()

    def run(self, index):
        self.fetch(index).wait()
        left = joined(self.tile[...])
        pl.when(index > 0)(lambda: self.wait_results(index - 1))
        for which, factor in enumerate(self.factors):
            product = lax.dot_general(
                left, joined(factor[...]), (TN, ((), ())), preferred_element_type=F32
            )
            self.staged[which] = jnp.transpose(product).astype(BF16)
        for copy in self.results(index):
            copy.start()
        pl.when(index + 1 < self.count)(lambda: self.fetch(index + 1).start())


def feed_back_kernel(
    count, dgate_ref, dup_ref, feed_weight_ref, top_ref, middle_ref, live_ref,
    gain_ref, out_weight_ref, mixed_ref, hidden_ref, normed_ref, grad_feed_ref,
    dmiddle_out, dgain_out, dmixed_out, dweight_out, dfeed_out, *all_scratch
):
    lates = late_all((out_weight_ref, mixed_ref, hidden_ref), all_scratch[-6:])
    out_weight_ref, mixed_ref, hidden_ref = (late.held for late in lates)
    *scratch, total_out, tile, grad_tile, staged, grad_staged, fetch_sems, out_sems = (
        all_scratch[:-6]
    )
    group = Group(count)
    scatter = scatter_of(group, PAIR_SHARE, scratch[:SCATTER_COUNT])
    gather = gather_of(group, PAIR_SHARE, scratch[SCATTER_COUNT:])
    parts, full = scratch[0], scratch[SCATTER_COUNT]
    jobs = (
        TileJob(
            normed_ref, tile, (dgate_ref, dup_ref), staged, (dfeed_out.at[0], dfeed_out.at[1]),
            fetch_sems.at[0], out_sems.at[0],
        ),
        TileJob(
            grad_feed_ref, grad_tile, (hidden_ref,), grad_staged, (dfeed_out.at[2],),
            fetch_sems.at[1], out_sems.at[1],
        ),
    )
    for each in jobs:
        each.fetch(0).start()
    meet(count)
    dgain_out[...] = jnp.zeros(dgain_out.shape, F32)
    total_out[...] = jnp.zeros(total_out.shape, F32)

    def prepare(piece):
        rows = gather.rows(piece)

        def store(cols, value):
            parts[:, :, rows, cols] = split(value.astype(BF16), group.deep, group.nx)

        wide_dot(
            [
                (joined(dgate_ref[:, rows]), feed_weight_ref.at[0]),
                (joined(dup_ref[:, rows]), feed_weight_ref.at[1]),
            ],
            NN,
            256,
            store,
        )

    def middle(piece, dnormed):
        rows = gather.rows(piece)
        values = middle_ref[rows]
        scale = inverse_rms(values)
        normed = values * scale
        dgain_out[...] += jnp.sum(dnormed * normed, axis=0, keepdims=True)
        scaled = dnormed * gain_ref[...]
        dmiddle = top_ref[rows].astype(F32) + scale * (
            scaled - normed * jnp.mean(scaled * normed, axis=-1, keepdims=True)
        )
        dmiddle_out[rows] = dmiddle
        return live_ref[rows] * dmiddle

    def ready(piece):
        rows = gather.rows(piece)
        for late in lates[:2]:
            pl.when(piece == 0)(late.wait)
        left, mixed = joined(full[:, :, rows]), joined(mixed_ref[:, rows])

        def store(cols, value):
            dmixed_out[:, rows, cols] = split(value, count)

        wide_dot([(left, out_weight_ref)], NT, 256, store)
        for first in range(0, left.shape[1], 256):
            total_out[first : first + 256] += lax.dot_general(
                left[:, first : first + 256], mixed, (TN, ((), ())), preferred_element_type=F32
            )

    def job(time):
        pl.when(time == 1)(lates[2].wait)
        for which, each in enumerate(jobs):
            pl.when((time % 2 == which) & (time < 2 * each.count))(
                functools.partial(each.run, time // 2)
            )

    sum_and_gather(scatter, gather, prepare, middle, ready, job)
    last = gather.pieces + scatter.last + gather.last
    lax.fori_loop(last, max(2 * jobs[0].count, last), lambda time, _: (job(time), 0)[1], 0)
    for each in jobs:
        each.wait_results(each.count - 1)
    dweight_out[...] = total_out[...].astype(BF16)


def feed_back(
    dgate, dup, feed_weight, top, middle, live, gain, out_weight, mixed, hidden, normed, grad_feed,
    count,
):
    own, features = middle.shape
    nz, nx = grid_sizes(count)
    width, units = out_weight.shape[0], feed_weight.shape[1]
    return pl.pallas_call(
        functools.partial(feed_back_kernel, count),
        out_shape=[
            jax.ShapeDtypeStruct((own, features), F32),
            jax.ShapeDtypeStruct((1, features), F32),
            jax.ShapeDtypeStruct((count, own, width), F32),
            jax.ShapeDtypeStruct((features, width), BF16),
            jax.ShapeDtypeStruct((3, units, features), BF16),
        ],
        in_specs=[VMEM_SPEC] * 7 + [ANY_SPEC] * 5,
        out_specs=[VMEM_SPEC] * 4 + [ANY_SPEC],
        scratch_shapes=[
            *scatter_scratch(nz, nx, own, features, PAIR_SHARE, MANY),
            *gather_scratch(nz, nx, own, features, MANY),
            pltpu.VMEM((features, width), F32),
            pltpu.VMEM((nz, nx, own, TILE), BF16),
            pltpu.VMEM((nz, nx, own, TILE), BF16),
            pltpu.VMEM((2, units, TILE), BF16),
            pltpu.VMEM((1, units, TILE), BF16),
            pltpu.SemaphoreType.DMA((2,)),
            pltpu.SemaphoreType.DMA((2, 2)),
            *late_scratch(out_weight, split(mixed, count), hidden),
        ],
        compiler_params=linked(2),
        cost_estimate=lasting(180),
        name="feed_back",
    )(
        dgate, dup, feed_weight, top, middle, live, gain, out_weight,
        split(mixed, count), hidden, normed, grad_feed,
    )


class Replicas:
    def __init__(self, values, from_core, from_y, over_back, over_home, sems):
        self.values, self.from_core, self.from_y = values, from_core, from_y
        self.over_back, self.over_home = over_back, over_home
        self.core_sems, self.y_sems, self.back_sems, self.home_sems = sems
        me = lax.axis_index("dp")
        self.lines = lax.axis_size("dp") // 2
        self.y, self.core = me // 2, me % 2

    @staticmethod
    def scratch(rows, cols, replicas):
        lines, share = replicas // 2, rows // replicas
        return [
            pltpu.VMEM((replicas, share, cols), BF16),
            pltpu.VMEM((lines, share, cols), BF16),
            pltpu.VMEM((max(lines - 1, 1), share, cols), BF16),
            pltpu.VMEM((max(lines - 1, 1), share, cols), BF16),
            pltpu.VMEM((lines, share, cols), BF16),
            *[pltpu.SemaphoreType.DMA((2, lines))] * 4,
        ]

    def share(self, core, y):
        return core * self.lines + y

    def peer(self, y, core):
        return {"dp": y * 2 + core}

    def line(self, k):
        return (self.y + k) % self.lines

    draining = False

    def push(self, source, target, send_sem, recv_sem, device):
        copy = pltpu.make_async_remote_copy(
            source, target, send_sem, recv_sem, device_id=device, device_id_type=MESH
        )
        if self.draining:
            copy.wait_send()
        else:
            copy.start()

    def drain(self):
        self.draining = True
        for k in range(self.lines):
            self.start(k)
            self.cores(k)
        self.over_y()
        self.back()
        self.draining = False

    def add(self, share, others):
        step = 64

        def some(block, _):
            rows = pl.ds(pl.multiple_of(block * step, step), step)
            total = self.values[share, rows].astype(F32)
            for ref, index in others:
                total = total + ref[index, rows].astype(F32)
            self.values[share, rows] = total.astype(BF16)
            return 0

        lax.fori_loop(0, self.values.shape[1] // step, some, 0)

    def start(self, k):
        y = self.line(k)
        self.push(
            self.values.at[self.share(1 - self.core, y)],
            self.from_core.at[y],
            self.core_sems.at[0, k],
            self.core_sems.at[1, k],
            self.peer(self.y, 1 - self.core),
        )

    def cores(self, k):
        y = self.line(k)
        share = self.share(self.core, y)
        if not self.draining:
            arrived(self.from_core.at[y], self.core_sems.at[1, k])
            self.add(share, [(self.from_core, y)])
        if k > 0:
            self.push(
                self.values.at[share],
                self.from_y.at[self.lines - k - 1],
                self.y_sems.at[0, k],
                self.y_sems.at[1, self.lines - k],
                self.peer(y, self.core),
            )

    def over_y(self):
        share = self.share(self.core, self.y)
        if not self.draining:
            for k in range(1, self.lines):
                arrived(self.from_y.at[k - 1], self.y_sems.at[1, k])
            self.add(share, [(self.from_y, k) for k in range(self.lines - 1)])
        for k in range(1, self.lines):
            self.push(
                self.values.at[share],
                self.over_back.at[self.lines - k - 1],
                self.back_sems.at[0, k],
                self.back_sems.at[1, self.lines - k],
                self.peer(self.line(k), self.core),
            )
        self.send_home(0)

    def own(self, k):
        return self.values.at[self.share(self.core, self.y)] if k == 0 else self.over_back.at[k - 1]

    def send_home(self, k):
        self.push(
            self.own(k),
            self.over_home.at[k],
            self.home_sems.at[0, k],
            self.home_sems.at[1, k],
            self.peer(self.y, 1 - self.core),
        )

    def back(self):
        for k in range(1, self.lines):
            if not self.draining:
                arrived(self.over_back.at[k - 1], self.back_sems.at[1, k])
            self.send_home(k)

    def home(self):
        for k in range(self.lines):
            arrived(self.over_home.at[k], self.home_sems.at[1, k])

    def totals(self):
        for k in range(self.lines):
            yield self.own(k), self.share(self.core, self.line(k))
            yield self.over_home.at[k], self.share(1 - self.core, self.line(k))


class SmallSum:
    def __init__(self, small, seen, send_sems, recv_sems, axis, cols):
        self.small, self.seen, self.cols = small, seen, pl.ds(0, cols)
        self.send_sems, self.recv_sems, self.axis = send_sems, recv_sems, axis
        self.me, self.size = lax.axis_index(axis), lax.axis_size(axis)

    def copy(self, k):
        place = self.seen.at[self.me, :, self.cols]
        return pltpu.make_async_remote_copy(
            place, place, self.send_sems.at[k], self.recv_sems.at[self.size - k],
            device_id={self.axis: (self.me + k) % self.size}, device_id_type=MESH,
        )

    def start(self):
        self.seen[self.me, :, self.cols] = self.small[:, self.cols]
        for k in range(1, self.size):
            self.copy(k).start()

    def finish(self):
        for k in range(1, self.size):
            landed = self.seen.at[(self.me + k) % self.size, :, self.cols]
            arrived(landed, self.recv_sems.at[k])
        total = self.seen[0, :, self.cols]
        for other in range(1, self.size):
            total = total + self.seen[other, :, self.cols]
        self.small[:, self.cols] = total

    def drain(self):
        for k in range(1, self.size):
            self.copy(k).wait_send()


def input_back_kernel(
    count, grad_ref, weight_ref, gates_ref, later_ref, input_ref, gain_ref, dgain_ref, dnorm_ref,
    dtaps_ref, dparams_ref, wout_ref, normed_ref, grad_out, norm1_out, norm2_out, gain_out,
    taps_out, params_out, dmain_out, drest_out, *scratch
):
    *scratch, small, normed, normed_sem = scratch
    late = Late(normed_ref, normed, normed_sem)
    normed_ref = normed
    parts, rest = scratch[0], scratch[SCATTER_COUNT:]
    values = rest[0]
    small_scratch, staged, out_sems = rest[9:15], *rest[15:]
    group = Group(count)
    scatter = scatter_of(group, SCATTER_SHARE, scratch[:SCATTER_COUNT])
    replicas = Replicas(*rest[:5], rest[5:9])
    meet(count, lax.axis_size("dp"))
    tall = norm1_out.shape[1] // 8
    edges = [tall, 2 * tall, 2 * tall + 128]
    small[...] = jnp.zeros(small.shape, F32)
    norm1_out[...] = jnp.zeros(norm1_out.shape, F32)
    for row in range(8):
        small[row : row + 1, edges[0] : edges[1]] = dnorm_ref[:, row * tall : (row + 1) * tall]
    small[0:1, edges[1] : edges[2]] = dgain_ref[...]
    small[0:4, edges[2] :] = dtaps_ref[...]
    small[4:6, edges[2] : edges[2] + 128] = dparams_ref[...]
    near = SmallSum(small, *small_scratch[:3], "heads", edges[2])
    far = SmallSum(small, *small_scratch[3:6], "dp", small.shape[1])
    width = grad_ref.shape[2]
    values[:, :, width:] = split(wout_ref[...], values.shape[0])

    def prepare(piece):
        rows = scatter.rows(piece)

        def store(cols, value):
            parts[:, :, rows, cols] = split(value.astype(BF16), group.deep, group.nx)

        left, edge = joined(grad_ref[:, rows]), weight_ref.shape[1]
        wide_dot(
            [(left[:, :edge], weight_ref), (left[:, edge:], gates_ref)], NT, 256, store
        )

    def end(piece, dnormed):
        rows = scatter.rows(piece)
        given = input_ref[rows].astype(F32)
        scale = inverse_rms(given)
        normed = given * scale
        norm1_out[...] += jnp.sum(dnormed * normed, axis=0, keepdims=True)
        scaled = dnormed * gain_ref[...]
        grad_out[rows] = later_ref[rows] + scale * (
            scaled - normed * jnp.mean(scaled * normed, axis=-1, keepdims=True)
        )

    def weight_share(core, y, first=False):
        if first:
            late.wait()
        share = replicas.share(core, y)
        left = joined(normed_ref[share])
        grads = joined(grad_ref[...])
        for first in range(0, width, 384):
            cols = slice(first, min(first + 384, width))
            staged[:, cols] = lax.dot_general(
                left, grads[:, cols], (TN, ((), ())), preferred_element_type=F32
            ).astype(BF16)

        def some(block, _):
            rows = pl.ds(pl.multiple_of(block * 64, 64), 64)
            values[share, rows, :width] = staged[rows]
            return 0

        lax.fori_loop(0, staged.shape[0] // 64, some, 0)

    def other_core(k):
        weight_share(1 - replicas.core, replicas.line(k), k == replicas.lines - 1)
        replicas.start(k)

    def this_core(k):
        weight_share(replicas.core, replicas.line(k))
        replicas.cores(k)

    steps = []
    for k in range(replicas.lines - 1, -1, -1):
        steps += [functools.partial(other_core, k), functools.partial(this_core, k)]
    while len(steps) < 7:
        steps.append(lambda: None)
    steps.append(replicas.over_y)

    before, within, behind = scatter_ticks(scatter, prepare, end)

    def tick(time, _):
        before(time)
        at_each_z(group, functools.partial(within, time))
        behind(time)
        for index, step in enumerate(steps):
            pl.when(time == index)(step)
        return 0

    lax.fori_loop(-1, max(scatter.pieces + scatter.last - 1, len(steps)), tick, 0)
    for row in range(8):
        small[row : row + 1, : edges[0]] = norm1_out[:, row * tall : (row + 1) * tall]
    near.start()
    replicas.back()
    near.finish()
    far.start()
    far.finish()
    for row in range(8):
        cols = slice(row * tall, (row + 1) * tall)
        norm1_out[:, cols] = small[row : row + 1, : edges[0]]
        norm2_out[:, cols] = small[row : row + 1, edges[0] : edges[1]]
    gain_out[...] = small[0:1, edges[1] : edges[2]]
    kind_width = taps_out.shape[2]
    for kind in range(taps_out.shape[0]):
        first = edges[2] + kind * kind_width
        taps_out[kind] = small[0:4, first : first + kind_width]
    params_out[...] = small[4:6, edges[2] : edges[2] + 128]
    replicas.home()
    part = dmain_out.shape[3]
    outs = []
    for index, (total, share) in enumerate(replicas.totals()):
        for kind in range(4):
            outs.append((total.at[:, pl.ds(kind * part, part)], dmain_out.at[kind, share], index))
        rest_cols = pl.ds(4 * part, drest_out.shape[2])
        outs.append((total.at[:, rest_cols], drest_out.at[share], index))
    outs = [
        pltpu.make_async_copy(source, target, out_sems.at[index, place % 5])
        for place, (source, target, index) in enumerate(outs)
    ]
    for copy in outs:
        copy.start()
    scatter.drain()
    replicas.drain()
    near.drain()
    far.drain()
    for copy in outs:
        copy.wait()


def input_back(
    grad, weight, gates, later, rows, gain, dgain, dnorm, dtaps, dparams, grad_wout, normed, count,
    replica_count,
):
    own, features = rows.shape
    nz, nx = grid_sizes(count)
    width, share = grad_wout.shape[1], features // replica_count
    cols = grad.shape[1] + width
    small_cols = features // 4 + 128 + dtaps.shape[1]
    dma = pltpu.SemaphoreType.DMA
    return pl.pallas_call(
        functools.partial(input_back_kernel, count),
        out_shape=[
            jax.ShapeDtypeStruct((own, features), F32),
            *[jax.ShapeDtypeStruct((1, features), F32)] * 2,
            jax.ShapeDtypeStruct(dgain.shape, F32),
            jax.ShapeDtypeStruct((3, 4, width), F32),
            jax.ShapeDtypeStruct(dparams.shape, F32),
            jax.ShapeDtypeStruct((4, replica_count, share, width), BF16),
            jax.ShapeDtypeStruct((replica_count, share, cols - 4 * width), BF16),
        ],
        in_specs=[VMEM_SPEC] * 11 + [ANY_SPEC],
        out_specs=[VMEM_SPEC] * 6 + [ANY_SPEC] * 2,
        scratch_shapes=[
            *scatter_scratch(nz, nx, own, features, SCATTER_SHARE, FEW),
            *Replicas.scratch(features, cols, replica_count),
            pltpu.VMEM((count, 8, small_cols), F32),
            dma((count,)),
            dma((count,)),
            pltpu.VMEM((replica_count, 8, small_cols), F32),
            dma((replica_count,)),
            dma((replica_count,)),
            pltpu.VMEM((share, grad.shape[1]), BF16),
            dma((replica_count, 5)),
            pltpu.VMEM((8, small_cols), F32),
            pltpu.VMEM(normed.shape, BF16),
            dma,
        ],
        compiler_params=linked(3),
        cost_estimate=lasting(120),
        name="input_back",
    )(
        split(grad, count), weight, gates, later, rows, gain, dgain, dnorm, dtaps, dparams,
        grad_wout, normed,
    )


def results_kernel(main_ref, rest_ref, feed_ref, main_out, wout_out, gate_up_out, down_out):
    for kind in range(main_ref.shape[0]):
        main_out[:, kind, :] = main_ref[kind].astype(F32)
    wout_out[...] = jnp.transpose(rest_ref[:, 128:].astype(F32))
    gate_up_out[...] = feed_ref[:2].astype(F32)
    down_out[...] = feed_ref[2].astype(F32)


def results(main, rest, feed):
    kinds, features, width = main.shape
    units = feed.shape[1]
    step = 256
    return pl.pallas_call(
        results_kernel,
        grid=(features // step,),
        in_specs=[
            pl.BlockSpec((kinds, step, width), lambda i: (0, i, 0)),
            pl.BlockSpec((step, rest.shape[1]), lambda i: (i, 0)),
            pl.BlockSpec((3, units, step), lambda i: (0, 0, i)),
        ],
        out_specs=[
            pl.BlockSpec((step, kinds, width), lambda i: (i, 0, 0)),
            pl.BlockSpec((width, step), lambda i: (0, i)),
            pl.BlockSpec((2, units, step), lambda i: (0, 0, i)),
            pl.BlockSpec((units, step), lambda i: (0, i)),
        ],
        out_shape=[
            jax.ShapeDtypeStruct((features, kinds, width), F32),
            jax.ShapeDtypeStruct((width, features), F32),
            jax.ShapeDtypeStruct((2, units, features), F32),
            jax.ShapeDtypeStruct((units, features), F32),
        ],
        compiler_params=pltpu.CompilerParams(vmem_limit_bytes=48 * 2**20),
        name="results",
    )(main, rest, feed)


def on_device(
    block_in,
    seq_counts,
    norm1_gain,
    w_qkvg,
    conv_weight,
    w_gates,
    gate_params,
    out_gain,
    w_out,
    norm2_gain,
    w_gate_up,
    w_down,
    cotangent,
):
    own_rows, features = block_in.shape
    count = lax.axis_size("heads")
    all_rows = own_rows * count
    width = conv_weight.shape[2]
    heads = gate_params.shape[1]
    longer = seq_counts[0, 1:2]
    first_row = lax.axis_index("heads") * own_rows
    row_index = first_row + jnp.arange(own_rows, dtype=jnp.int32)
    live_own = jnp.where(longer[0] > 0, True, row_index < seq_counts[0, 0] * SEQ_SHORT)
    live_own = live_own.astype(F32)[:, None]
    gates_weight = jnp.pad(
        w_gates.reshape(features, 2 * heads), ((0, 0), (0, 128 - 2 * heads))
    )
    full_normed1, projected, weight = project(
        block_in, norm1_gain[None], w_qkvg, gates_weight, count, lax.axis_size("dp")
    )
    projected = projected.reshape(all_rows, -1)
    taps = jnp.transpose(conv_weight, (1, 0, 2)).reshape(4, 3 * width)
    params = jnp.pad(gate_params, ((0, 0), (0, 128 - heads)))
    gain_row = out_gain[None]
    mixed, *saved, grad_feed = mixer_forward(
        longer, projected, taps, params, gain_row, cotangent, live_own, count
    )
    feed_weight = jnp.transpose(w_gate_up, (1, 2, 0))
    middle, full_normed2, grad_gate, grad_up, hidden = branch_and_feed(
        mixed,
        w_out,
        block_in,
        live_own,
        norm2_gain[None],
        feed_weight,
        w_down,
        grad_feed,
        count,
    )
    grad_middle, grad_gain2, grad_mixed, grad_wout, early = feed_back(
        grad_gate,
        grad_up,
        feed_weight,
        cotangent,
        middle,
        live_own,
        norm2_gain[None],
        w_out,
        mixed,
        hidden,
        full_normed2,
        grad_feed,
        count,
    )
    early = lax.psum(early, "dp")
    dprojected, dtaps, dparams, dgain, layer_out = mixer_backward(
        longer,
        grad_mixed.reshape(all_rows, width),
        projected,
        saved,
        taps,
        params,
        gain_row,
        hidden,
        w_down,
        middle,
        live_own,
        count,
    )

    grad_in, grad_gain1, grad_gain2, dgain, grad_conv, dparams, grad_main, grad_rest = input_back(
        dprojected,
        weight,
        gates_weight,
        grad_middle,
        block_in,
        norm1_gain[None],
        dgain,
        grad_gain2,
        dtaps,
        dparams,
        grad_wout,
        full_normed1,
        count,
        lax.axis_size("dp"),
    )
    grad_main = grad_main.reshape(4, features, width)
    grad_rest = grad_rest.reshape(features, -1)
    grad_qkvg, grad_out_weight, grad_gate_up, grad_down = results(grad_main, grad_rest, early)
    return (
        layer_out,
        grad_in,
        grad_gain1[0],
        grad_qkvg,
        grad_conv,
        grad_rest[:, : 2 * heads].reshape(w_gates.shape).astype(F32),
        dparams[:, :heads],
        dgain[0],
        grad_out_weight,
        grad_gain2[0],
        jnp.transpose(grad_gate_up, (2, 0, 1)),
        grad_down,
    )


def solution(mesh):
    return jax.shard_map(
        on_device,
        mesh=mesh,
        in_specs=(
            P(("dp", "heads"), None),
            P("dp", None),
            P(),
            P(None, None, "heads"),
            P(None, None, "heads"),
            P(None, None, "heads"),
            P(None, "heads"),
            P(),
            P("heads", None),
            P(),
            P(None, None, "heads"),
            P("heads", None),
            P(("dp", "heads"), None),
        ),
        out_specs=(
            P(("dp", "heads"), None),
            P(("dp", "heads"), None),
            P(),
            P(None, None, "heads"),
            P(None, None, "heads"),
            P(None, None, "heads"),
            P(None, "heads"),
            P(),
            P("heads", None),
            P(),
            P(None, None, "heads"),
            P("heads", None),
        ),
        check_vma=False,
    )
```

```python
import functools
import math
import jax
import jax.numpy as jnp
from jax import lax
from jax.experimental import pallas as pl
from jax.experimental.pallas import tpu as pltpu
from jax.sharding import PartitionSpec as P

SEQ_SHORT = 512
CHUNK = 256
HEAD = 128
EPS = 1e-06
F32 = jnp.float32
BF16 = jnp.bfloat16
LOW, MID, TOP = lax.Precision.DEFAULT, lax.Precision.HIGH, lax.Precision.HIGHEST
NN, NT, TN = ((1,), (0,)), ((1,), (1,)), ((0,), (0,))
P_FWD, P_BWD = MID, MID


def dot(left, right, dims, precision):
    if precision is LOW:
        left, right = left.astype(BF16), right.astype(BF16)
        return lax.dot_general(left, right, (dims, ((), ())), preferred_element_type=F32)
    return lax.dot_general(
        left, right, (dims, ((), ())), precision=precision, preferred_element_type=F32
    )


def grid_index(shape, axis):
    return lax.broadcasted_iota(jnp.int32, shape, axis)


def positions(longer, first_row, count):
    rows = grid_index((count, 1), 0) + first_row
    return jnp.where(longer > 0, rows, rows % SEQ_SHORT)


def keeps(longer, first_row):
    start = jnp.where(longer > 0, first_row, first_row % SEQ_SHORT)
    return jnp.where(start > 0, 1.0, 0.0).astype(F32)


def softplus(x):
    return jnp.maximum(x, 0.0) + jnp.log1p(jnp.exp(-jnp.abs(x)))


def gate_values(gates, params, heads):
    lane = grid_index(gates.shape, 1)
    rate = jnp.exp(params[0:1])
    shifted = gates + params[1:2]
    log_decay = jnp.where(lane < heads, -rate * softplus(shifted), 0.0)
    return rate, shifted, log_decay


def lane_column(values, index):
    return values[:, index : index + 1]


def decays(cumulative, cumulative_rows, head, masks):
    column = lane_column(cumulative, head)
    row = cumulative_rows[head : head + 1, :]
    inclusive = masks[0]
    ratio = jnp.where(inclusive, jnp.exp(jnp.where(inclusive, column - row, 0.0)), 0.0)
    last = column[CHUNK - 1 : CHUNK, :]
    return ratio, jnp.exp(column), jnp.exp(last - column), jnp.exp(last)


def unit(values):
    scale = lax.rsqrt(jnp.sum(values * values, axis=-1, keepdims=True) + EPS)
    return values * scale, scale


def pair_of(values):
    high = values.astype(BF16)
    return high, (values - high.astype(F32)).astype(BF16)


def pair_dot(left, right):
    def product(a, b):
        return lax.dot_general(a, b, (NN, ((), ())), preferred_element_type=F32)

    return product(left[0], right[0]) + (product(left[0], right[1]) + product(left[1], right[0]))


def inverses(links, row, col):
    apart = row ^ col
    size = links[0].shape[0]
    outs = [jnp.where(row == col, 1.0, 0.0) - jnp.where(apart == 1, link, 0.0) for link in links]
    pairs = [pair_of(link) for link in links]
    step = 2
    while step < size // 2:
        level = (apart >= step) & (apart < 2 * step)
        parts = [tuple(jnp.where(level, half, 0) for half in pair) for pair in pairs]
        out_pairs = [pair_of(out) for out in outs]
        inner = [pair_of(pair_dot(part, out)) for part, out in zip(parts, out_pairs)]
        outs = [out - pair_dot(pair, mid) for out, pair, mid in zip(outs, out_pairs, inner)]
        step *= 2
    half = size // 2
    uppers = [pair_of(out[:half, :half]) for out in outs]
    lowers = [pair_of(out[half:, half:]) for out in outs]
    corners = [tuple(each[half:, :half] for each in pair) for pair in pairs]
    inner = [pair_of(pair_dot(corner, upper)) for corner, upper in zip(corners, uppers)]
    corners = [pair_dot(lower, mid) for lower, mid in zip(lowers, inner)]
    return [
        jnp.concatenate(
            [out[:half], jnp.concatenate([-corner, out[half:, half:]], axis=1)], axis=0
        )
        for out, corner in zip(outs, corners)
    ]


def forward_kernel(
    heads, count, chunks, longer_ref, main_ref, conv_ref, params_ref, gain_ref, top_ref, live_ref,
    mixed_ref, conv_out_ref, raw_ref, delta_ref, solve_ref, state_ref, full_out,
    state, tail_rows, *scratch
):
    step = pl.program_id(0)
    first_row = step * CHUNK
    run, close = gather_along(step, chunks, count, top_ref, live_ref, full_out, scratch)
    run(2 * step)
    longer = longer_ref[0]
    width = heads * HEAD

    @pl.when(step == 0)
    def _():
        state[...] = jnp.zeros_like(state)
        tail_rows[...] = jnp.zeros_like(tail_rows)

    position = positions(longer, first_row, CHUNK)
    keep = keeps(longer, first_row)
    triple = main_ref[:, : 3 * width]
    padded = jnp.concatenate([tail_rows[...], triple], axis=0)
    taps = conv_ref[...]
    convolved = triple * taps[0:1]
    for lag in range(1, 4):
        shifted = padded[8 - lag : 8 - lag + CHUNK]
        convolved = convolved + jnp.where(position >= lag, shifted, 0.0) * taps[lag : lag + 1]
    tail_rows[...] = triple[CHUNK - 8 :]
    conv_out_ref[...] = convolved
    active = convolved * jax.nn.sigmoid(convolved)
    gates = main_ref[:, 4 * width :]
    rate, shifted_gate, log_decay = gate_values(gates, params_ref[...], heads)
    beta_all = jax.nn.sigmoid(gates)
    row = grid_index((CHUNK, CHUNK), 0)
    col = grid_index((CHUNK, CHUNK), 1)
    masks = (row >= col, row > col)
    cumulative = dot(jnp.where(masks[0], 1.0, 0.0), log_decay, NN, TOP)
    cumulative_rows = jnp.transpose(cumulative)
    each = range(heads)
    columns = [slice(head * HEAD, (head + 1) * HEAD) for head in each]
    queries = [unit(active[:, cols])[0] * HEAD**-0.5 for cols in columns]
    keys = [unit(active[:, width + head * HEAD : width + (head + 1) * HEAD])[0] for head in each]
    values = [active[:, 2 * width + head * HEAD : 2 * width + (head + 1) * HEAD] for head in each]
    betas = [lane_column(beta_all, heads + head) for head in each]
    spans = [decays(cumulative, cumulative_rows, head, masks) for head in each]
    grams = [
        dot(jnp.concatenate([key, query], axis=0), key, NT, P_FWD)
        for key, query in zip(keys, queries)
    ]
    links = [
        jnp.where(masks[1], beta * span[0] * gram[:CHUNK], 0.0)
        for beta, span, gram in zip(betas, spans, grams)
    ]
    solves = inverses(links, row, col)
    run(2 * step + 1)
    boths = [
        dot(
            solve,
            jnp.concatenate([beta * value, (beta * span[1]) * key], axis=1),
            NN,
            P_FWD,
        )
        for solve, beta, value, key, span in zip(solves, betas, values, keys, spans)
    ]
    entries = [state[head] * keep for head in each]
    carried = [
        dot(jnp.concatenate([both[:, HEAD:], span[1] * query], axis=0), entry, NT, P_FWD)
        for both, span, query, entry in zip(boths, spans, queries, entries)
    ]
    deltas = [both[:, :HEAD] - carry[:CHUNK] for both, carry in zip(boths, carried)]
    states = [
        span[3] * entry + dot(delta * span[2], key, TN, P_FWD)
        for span, entry, delta, key in zip(spans, entries, deltas, keys)
    ]
    raws = [
        carry[CHUNK:] + dot(gram[CHUNK:] * span[0], delta, NN, P_FWD)
        for carry, gram, span, delta in zip(carried, grams, spans, deltas)
    ]
    for head, cols in zip(each, columns):
        solve_ref[head] = solves[head]
        state_ref[0, head] = entries[head]
        state[head] = states[head]
        delta_ref[:, cols] = deltas[head]
        raw = raws[head]
        raw_ref[:, cols] = raw
        scale = lax.rsqrt(jnp.mean(raw * raw, axis=-1, keepdims=True) + EPS)
        gate = main_ref[:, 3 * width + head * HEAD : 3 * width + (head + 1) * HEAD]
        mixed = raw * scale * gain_ref[...] * (gate * jax.nn.sigmoid(gate))
        mixed_ref[:, cols] = mixed.astype(mixed_ref.dtype)
    pl.when(step == chunks - 1)(close)


def spread_ticks(tick, first, ticks, halves):
    def run(half):
        def one(index, _):
            tick(first + index)
            return 0

        lax.fori_loop(half * ticks // halves, (half + 1) * ticks // halves, one, 0)

    return run


def gather_along(step, chunks, count, top_ref, live_ref, full_out, scratch):
    *scratch, out_sems = scratch
    full = scratch[0]
    group = Group(count)
    gather = gather_of(group, GATHER_SHARE, scratch)

    def out(piece):
        rows = gather.rows(piece)
        return pltpu.make_async_copy(
            full.at[:, :, rows], full_out.at[:, :, rows], out_sems.at[piece]
        )

    def prepare(piece):
        rows = gather.rows(piece)
        full[group.z, group.x, rows] = (live_ref[rows] * top_ref[rows].astype(F32)).astype(BF16)

    before, within, behind = gather_ticks(gather, prepare, lambda piece: out(piece).start())

    def tick(time):
        before(time)
        at_each_z(group, functools.partial(within, time))
        behind(time)

    def close():
        gather.drain()

        def finish(piece, _):
            out(piece).wait()
            return 0

        lax.fori_loop(0, gather.pieces, finish, 0)

    pl.when(step == 0)(functools.partial(meet, count))
    return spread_ticks(tick, 0, gather.pieces + gather.last, 2 * chunks), close


def scatter_along(step, chunks, count, hidden_ref, weight_ref, middle_ref, live_ref, out, scratch):
    parts = scratch[0]
    group = Group(count)
    scatter = scatter_of(group, SCATTER_SHARE, scratch)

    def prepare(piece):
        rows = scatter.rows(piece)

        def store(cols, value):
            parts[:, :, rows, cols] = split(value.astype(BF16), group.deep, group.nx)

        wide_dot([(joined(hidden_ref[:, rows]), weight_ref)], NN, 512, store)

    def end(piece, total):
        rows = scatter.rows(piece)
        out[rows] = (middle_ref[rows] + live_ref[rows] * total).astype(BF16)

    before, within, behind = scatter_ticks(scatter, prepare, end)

    def tick(time):
        before(time)
        at_each_z(group, functools.partial(within, time))
        behind(time)

    pl.when(step == 0)(functools.partial(meet, count))
    return spread_ticks(tick, -1, scatter.pieces + scatter.last, 2 * chunks), scatter.drain


def backward_kernel(
    heads, chunks, count, longer_ref, grad_ref, main_ref, conv_out_ref, raw_ref, delta_ref,
    solve_ref, state_ref, conv_ref, params_ref, gain_ref, hidden_ref, down_ref, middle_ref, live_ref,
    dmain_ref, dconv_ref, dparams_ref, dgain_ref, layer_ref, dstate, head_rows, *scratch
):
    step = pl.program_id(0)
    first_row = (chunks - 1 - step) * CHUNK
    run, close = scatter_along(
        step, chunks, count, hidden_ref, down_ref, middle_ref, live_ref, layer_ref, scratch
    )
    run(2 * step)
    longer = longer_ref[0]
    width = heads * HEAD

    @pl.when(step == 0)
    def _():
        dstate[...] = jnp.zeros_like(dstate)
        head_rows[...] = jnp.zeros_like(head_rows)
        dconv_ref[...] = jnp.zeros_like(dconv_ref)
        dparams_ref[...] = jnp.zeros_like(dparams_ref)
        dgain_ref[...] = jnp.zeros_like(dgain_ref)

    keep = keeps(longer, first_row)
    convolved = conv_out_ref[...]
    sigmoid_conv = jax.nn.sigmoid(convolved)
    active = convolved * sigmoid_conv
    slope = sigmoid_conv * (1.0 + convolved * (1.0 - sigmoid_conv))
    gates = main_ref[:, 4 * width :]
    params = params_ref[...]
    rate, shifted_gate, log_decay = gate_values(gates, params, heads)
    beta_all = jax.nn.sigmoid(gates)
    row = grid_index((CHUNK, CHUNK), 0)
    col = grid_index((CHUNK, CHUNK), 1)
    masks = (row >= col, row > col)
    cumulative = dot(jnp.where(masks[0], 1.0, 0.0), log_decay, NN, TOP)
    cumulative_rows = jnp.transpose(cumulative)
    lane = grid_index((CHUNK, 128), 1)
    last_row = grid_index((CHUNK, 1), 0) == CHUNK - 1
    gain = gain_ref[...]
    dgains, dlogs, dbetas, dparts = ([None] * heads for _ in range(4))

    def work(head):
        cols = slice(head * HEAD, (head + 1) * HEAD)
        gate = main_ref[:, 3 * width + head * HEAD : 3 * width + (head + 1) * HEAD]
        raw = raw_ref[:, cols]
        grad = grad_ref[:, cols]
        scale = lax.rsqrt(jnp.mean(raw * raw, axis=-1, keepdims=True) + EPS)
        normed = raw * scale
        sigmoid_gate = jax.nn.sigmoid(gate)
        gated = gate * sigmoid_gate
        product = grad * normed
        dgains[head] = jnp.sum(product * gated, axis=0, keepdims=True)
        dgate = product * gain * (sigmoid_gate * (1.0 + gate * (1.0 - sigmoid_gate)))
        dmain_ref[:, 3 * width + head * HEAD : 3 * width + (head + 1) * HEAD] = dgate.astype(
            dmain_ref.dtype
        )
        dnormed = grad * gain * gated
        draw = scale * (dnormed - normed * jnp.mean(dnormed * normed, axis=-1, keepdims=True))
        query_unit, query_scale = unit(active[:, head * HEAD : (head + 1) * HEAD])
        query = query_unit * HEAD**-0.5
        key, key_scale = unit(active[:, width + head * HEAD : width + (head + 1) * HEAD])
        value = active[:, 2 * width + head * HEAD : 2 * width + (head + 1) * HEAD]
        beta = lane_column(beta_all, heads + head)
        ratio, decay_in, decay_out, decay_all = decays(cumulative, cumulative_rows, head, masks)
        entry = state_ref[0, head]
        delta = delta_ref[:, cols]
        dlater = dstate[head]
        gram = dot(query, key, NT, P_BWD) * ratio
        yield
        key_dlater = dot(key, dlater, NT, P_BWD)
        yield
        ddelta = dot(gram, draw, TN, P_BWD) + decay_out * key_dlater
        yield
        dright = dot(solve_ref[head], ddelta, TN, P_BWD)
        yield
        pairs = dot(jnp.concatenate([dright, draw], axis=0), delta, NT, P_BWD)
        yield
        dlink = jnp.where(masks[1], -pairs[:CHUNK] * ratio, 0.0)
        dgram = pairs[CHUNK:] * ratio
        on_entry = dot(jnp.concatenate([dright, draw], axis=0), entry, NN, P_BWD)
        yield
        key_entry = dot(key, entry, NT, P_BWD)
        yield
        on_key = dot(jnp.concatenate([dlink, dgram], axis=0), key, NN, TOP)
        yield
        dquery = decay_in * on_entry[CHUNK:] + on_key[CHUNK:]
        link_key = on_key[:CHUNK]
        key_read = beta * (link_key - decay_in * on_entry[:CHUNK])
        key_tail = decay_out * dot(delta, dlater, NN, P_BWD)
        yield
        key_write = (
            dot(beta * dlink, key, TN, TOP) + dot(dgram, query, TN, TOP) + key_tail
        )
        yield
        dkey = key_read + key_write
        dvalue = beta * dright
        dbeta = jnp.sum(
            dright * (value - decay_in * key_entry) + key * link_key, axis=-1, keepdims=True
        )
        dlog = jnp.sum(query * dquery + key * (key_read - key_write), axis=-1, keepdims=True)
        ending = decay_all * jnp.sum(
            jnp.sum(entry * dlater, axis=-1, keepdims=True), axis=0, keepdims=True
        ) + jnp.sum(jnp.sum(key * key_tail, axis=-1, keepdims=True), axis=0, keepdims=True)
        dlog = dlog + jnp.where(last_row, ending, 0.0)
        dlogs[head], dbetas[head] = dlog, dbeta
        dstate[head] = keep * (
            decay_all * dlater
            + dot(decay_in * draw, query, TN, P_BWD)
            - dot((beta * decay_in) * dright, key, TN, P_BWD)
        )
        yield
        dquery = (HEAD**-0.5 * query_scale) * (
            dquery - query_unit * jnp.sum(dquery * query_unit, axis=-1, keepdims=True)
        )
        dkey = key_scale * (dkey - key * jnp.sum(dkey * key, axis=-1, keepdims=True))
        dparts[head] = (dquery, dkey, dvalue)

    works = [work(head) for head in range(heads)]
    turns = 0
    while works:
        works = [each for each in works if next(each, "end") != "end"]
        turns += 1
        if turns == 6:
            run(2 * step + 1)
    dcumulative = jnp.zeros((CHUNK, 128), F32)
    dbeta_all = jnp.zeros((CHUNK, 128), F32)
    for head in range(heads):
        dcumulative = jnp.where(lane == head, dlogs[head], dcumulative)
        dbeta_all = jnp.where(lane == heads + head, dbetas[head], dbeta_all)
    dgain = functools.reduce(jnp.add, dgains)
    dconv_parts = [[dparts[head][kind] for head in range(heads)] for kind in range(3)]
    dactive = jnp.concatenate([p for parts in dconv_parts for p in parts], axis=1)
    dconvolved = dactive * slope
    padded = jnp.concatenate([dconvolved, head_rows[...]], axis=0)
    position = positions(longer, first_row, CHUNK + 8)
    taps = conv_ref[...]
    triple = main_ref[:, : 3 * width]
    dtriple = dconvolved * taps[0:1]
    dconv_ref[0:1] += jnp.sum(dconvolved * triple, axis=0, keepdims=True)
    for lag in range(1, 4):
        moved = jnp.where(position >= lag, padded, 0.0)[lag : lag + CHUNK]
        dtriple = dtriple + moved * taps[lag : lag + 1]
        dconv_ref[lag : lag + 1] += jnp.sum(moved * triple, axis=0, keepdims=True)
    head_rows[...] = dconvolved[:8]
    dmain_ref[:, : 3 * width] = dtriple.astype(dmain_ref.dtype)
    dlog_decay = dot(jnp.where(row <= col, 1.0, 0.0), dcumulative, NN, TOP)
    dshifted = -dlog_decay * rate * jax.nn.sigmoid(shifted_gate)
    dshifted = jnp.where(lane < heads, dshifted, 0.0)
    dparams_ref[0:1] += jnp.sum(dlog_decay * log_decay, axis=0, keepdims=True)
    dparams_ref[1:2] += jnp.sum(dshifted, axis=0, keepdims=True)
    dmain_ref[:, 4 * width :] = (dshifted + dbeta_all * beta_all * (1.0 - beta_all)).astype(
        dmain_ref.dtype
    )
    dgain_ref[...] += dgain
    pl.when(step == chunks - 1)(close)


def row_block(width, chunks, backward):
    if backward:
        return pl.BlockSpec((CHUNK, width), lambda i: (chunks - 1 - i, 0))
    return pl.BlockSpec((CHUNK, width), lambda i: (i, 0))


def whole_block(shape):
    return pl.BlockSpec(shape, lambda i: (0,) * len(shape))


def mixer_forward(longer, main, conv, params, gain, top, live, count):
    rows, width = main.shape[0], conv.shape[1] // 3
    heads, chunks = width // HEAD, rows // CHUNK
    own, features = top.shape
    nz, nx = grid_sizes(count)
    rowed = functools.partial(row_block, chunks=chunks, backward=False)
    shape = jax.ShapeDtypeStruct
    return pl.pallas_call(
        functools.partial(forward_kernel, heads, count, chunks),
        grid=(chunks,),
        in_specs=[
            pl.BlockSpec(memory_space=pltpu.SMEM),
            rowed(4 * width + 128),
            whole_block((4, 3 * width)),
            whole_block((2, 128)),
            whole_block((1, HEAD)),
            whole_block((own, features)),
            whole_block((own, 1)),
        ],
        out_specs=[
            rowed(width),
            rowed(3 * width),
            rowed(width),
            rowed(width),
            pl.BlockSpec((heads, CHUNK, CHUNK), lambda i: (0, i, 0)),
            pl.BlockSpec((1, heads, HEAD, HEAD), lambda i: (i, 0, 0, 0)),
            pl.BlockSpec(memory_space=pl.ANY),
        ],
        out_shape=[
            shape((rows, width), BF16),
            shape((rows, 3 * width), F32),
            shape((rows, width), F32),
            shape((rows, width), F32),
            shape((heads, rows, CHUNK), F32),
            shape((chunks, heads, HEAD, HEAD), F32),
            shape((nz, nx, own, features), BF16),
        ],
        scratch_shapes=[
            pltpu.VMEM((heads, HEAD, HEAD), F32),
            pltpu.VMEM((8, 3 * width), F32),
            *gather_scratch(nz, nx, own, features, FEW),
            pltpu.SemaphoreType.DMA((pieces_of(own, FEW),)),
        ],
        compiler_params=linked(4),
        cost_estimate=lasting(95),
        name="mixer_forward",
    )(longer, main, conv, params, gain, top, live)


def mixer_backward(
    longer, grad, main, saved, conv, params, gain, hidden, down_weight, middle, live, count
):
    rows, width = main.shape[0], conv.shape[1] // 3
    heads, chunks = width // HEAD, rows // CHUNK
    own, features = middle.shape
    nz, nx = grid_sizes(count)
    rowed = functools.partial(row_block, chunks=chunks, backward=True)
    shape = jax.ShapeDtypeStruct
    return pl.pallas_call(
        functools.partial(backward_kernel, heads, chunks, count),
        grid=(chunks,),
        in_specs=[
            pl.BlockSpec(memory_space=pltpu.SMEM),
            rowed(width),
            rowed(4 * width + 128),
            rowed(3 * width),
            rowed(width),
            rowed(width),
            pl.BlockSpec((heads, CHUNK, CHUNK), lambda i: (0, chunks - 1 - i, 0)),
            pl.BlockSpec((1, heads, HEAD, HEAD), lambda i: (chunks - 1 - i, 0, 0, 0)),
            whole_block((4, 3 * width)),
            whole_block((2, 128)),
            whole_block((1, HEAD)),
            whole_block(hidden.shape),
            whole_block(down_weight.shape),
            whole_block((own, features)),
            whole_block((own, 1)),
        ],
        out_specs=[
            rowed(4 * width + 128),
            whole_block((4, 3 * width)),
            whole_block((2, 128)),
            whole_block((1, HEAD)),
            whole_block((own, features)),
        ],
        out_shape=[
            shape((rows, 4 * width + 128), BF16),
            shape((4, 3 * width), F32),
            shape((2, 128), F32),
            shape((1, HEAD), F32),
            shape((own, features), BF16),
        ],
        scratch_shapes=[
            pltpu.VMEM((heads, HEAD, HEAD), F32),
            pltpu.VMEM((8, 3 * width), F32),
            *scatter_scratch(nz, nx, own, features, SCATTER_SHARE, FEW),
        ],
        compiler_params=linked(5),
        cost_estimate=lasting(100),
        name="mixer_backward",
    )(
        longer, grad, main, *saved, conv, params, gain, hidden, down_weight, middle, live
    )


MESH = pl.DeviceIdType.MESH
MANY, FEW = 16, 8


def pieces_of(rows, most):
    return min(most, rows // 16)


def grid_sizes(count):
    nz = 4 if count % 4 == 0 else 1
    return nz, count // nz


class Group:
    def __init__(self, count):
        self.deep, self.nx = grid_sizes(count)
        me = lax.axis_index("heads")
        self.z, self.x = me // self.nx, me % self.nx

    def column(self, j):
        return (self.x + j) % self.nx

    def over_x(self, j):
        return {"heads": self.z * self.nx + self.column(j)}

    def along_z(self, z):
        return {"heads": z * self.nx + self.x}


def meet(count, replicas=1):
    barrier = pltpu.get_barrier_semaphore()
    for axis, size in (("heads", count), ("dp", replicas)):
        me = lax.axis_index(axis)

        def greet(k, _, axis=axis, size=size, me=me):
            pl.semaphore_signal(
                barrier, inc=1, device_id={axis: (me + k) % size}, device_id_type=MESH
            )
            return 0

        lax.fori_loop(1, size, greet, 0)
    pl.semaphore_wait(barrier, count + replicas - 2)


def arrived(ref, sem):
    pltpu.make_async_copy(ref, ref, sem).wait()


def during(piece, pieces, work):
    pl.when((piece >= 0) & (piece < pieces))(functools.partial(work, piece))


def push(source, target, send_sem, recv_sem, device):
    pltpu.make_async_remote_copy(
        source, target, send_sem, recv_sem, device_id=device, device_id_type=MESH
    ).start()


class Gather:
    def __init__(self, group, full, cols, sems, x_first):
        self.group, self.full, self.cols, self.x_first = group, full, cols, x_first
        self.line_send, self.line_recv, self.x_send, self.x_recv = sems
        self.pieces = self.x_send.shape[0]
        self.part = full.shape[2] // self.pieces
        self.last = group.deep

    @staticmethod
    def sems(deep, nx, pieces):
        dma = pltpu.SemaphoreType.DMA
        return [dma((pieces, 2)), dma((pieces, deep)), dma((pieces, nx)), dma((pieces, nx))]

    def at(self, piece, z, column):
        rows = pl.ds(pl.multiple_of(piece * self.part, self.part), self.part)
        return self.full.at[z, column, rows, self.cols]

    def columns(self):
        return slice(None) if self.x_first else self.group.x

    def push_line(self, piece, z, way, zz):
        place = self.at(piece, z, self.columns())
        push(
            place,
            place,
            self.line_send.at[piece, way],
            self.line_recv.at[piece, z],
            self.group.along_z(zz + (1 if way == 0 else -1)),
        )

    def push_x(self, piece, z):
        place = self.at(piece, z, self.group.x)
        for j in range(1, self.group.nx):
            push(
                place,
                place,
                self.x_send.at[piece, j],
                self.x_recv.at[piece, self.group.nx - j],
                self.group.over_x(j),
            )

    def own_line(self, piece, zz):
        if zz + 1 < self.group.deep:
            self.push_line(piece, zz, 0, zz)
        if zz > 0:
            self.push_line(piece, zz, 1, zz)

    def begin(self, piece):
        self.push_x(piece, self.group.z)
        if not self.x_first:
            group = self.group
            pl.when(group.z + 1 < group.deep)(lambda: self.push_line(piece, group.z, 0, group.z))
            pl.when(group.z > 0)(lambda: self.push_line(piece, group.z, 1, group.z))

    def phase(self, piece, step, zz):
        deep, nx = self.group.deep, self.group.nx
        if self.x_first:
            if step == 1:
                for j in range(1, nx):
                    arrived(self.at(piece, zz, self.group.column(j)), self.x_recv.at[piece, j])
                self.own_line(piece, zz)
                return
            step -= 1
        elif step == deep:
            for j in range(1, nx):
                place = self.at(piece, slice(None), self.group.column(j))
                arrived(place, self.x_recv.at[piece, j])
            return
        for z, way in ((zz - step, 0), (zz + step, 1)):
            if 0 <= z < deep:
                arrived(self.at(piece, z, self.columns()), self.line_recv.at[piece, z])
                if 0 <= zz + (1 if way == 0 else -1) < deep:
                    self.push_line(piece, z, way, zz)
                if not self.x_first:
                    self.push_x(piece, z)

    def drain(self, piece, zz):
        deep, nx = self.group.deep, self.group.nx
        if zz + 1 < deep:
            place = self.at(piece, pl.ds(0, zz + 1), self.columns())
            arrived(place, self.line_send.at[piece, 0])
        if zz > 0:
            place = self.at(piece, pl.ds(zz, deep - zz), self.columns())
            arrived(place, self.line_send.at[piece, 1])
        z = zz if self.x_first else slice(None)
        for j in range(1, nx):
            arrived(self.at(piece, z, self.group.x), self.x_send.at[piece, j])


class Scatter:
    last = 4

    def __init__(self, group, parts, cols, scratch, z_first):
        self.group, self.parts, self.cols, self.z_first = group, parts, cols, z_first
        self.landed_x, self.line, *sems = scratch
        self.x_send, self.x_recv, self.z_send, self.z_recv = sems
        self.pieces = self.x_send.shape[0]
        self.part = parts.shape[2] // self.pieces

    @staticmethod
    def scratch(deep, nx, rows, cols, z_first, pieces):
        dma = pltpu.SemaphoreType.DMA
        return [
            pltpu.VMEM((max(nx - 1, 1), 1 if z_first else deep, rows, cols), BF16),
            pltpu.VMEM((deep + 1, nx if z_first else 1, rows, cols), BF16),
            *[dma((pieces, nx))] * 2,
            *[dma((pieces, 2))] * 2,
        ]

    def rows(self, piece):
        return pl.ds(pl.multiple_of(piece * self.part, self.part), self.part)

    def columns(self):
        return slice(None) if self.z_first else pl.ds(self.group.x, 1)

    def at(self, piece, z, column):
        return self.parts.at[z, column, self.rows(piece), self.cols]

    def line_at(self, piece, way, zz):
        first, size = (zz + 1, self.group.deep - zz) if way == 0 else (0, zz + 1)
        return self.line.at[pl.ds(first, size), :, self.rows(piece)]

    def push_line(self, piece, way, zz):
        deep = self.group.deep
        first, size = (zz + 1, deep - 1 - zz) if way == 0 else (0, zz)
        if size == 0:
            return
        after = zz + 1 if way == 0 else zz - 1
        push(
            self.at(piece, pl.ds(first, size), self.columns()),
            self.line_at(piece, way, after),
            self.z_send.at[piece, way],
            self.z_recv.at[piece, way],
            self.group.along_z(after),
        )

    def ends(self, piece, zz):
        if zz == 0:
            self.push_line(piece, 0, zz)
        if zz == self.group.deep - 1:
            self.push_line(piece, 1, zz)

    def hand_on(self, piece, near, zz):
        deep = self.group.deep
        if zz == 0 or zz == deep - 1:
            return
        way = 0 if (zz < deep // 2) == near else 1
        arrived(self.line_at(piece, way, zz), self.z_recv.at[piece, way])
        first, size = (zz + 1, deep - 1 - zz) if way == 0 else (0, zz)
        shift = 1 if way == 0 else 0
        ours = self.at(piece, pl.ds(first, size), self.columns())
        landed = self.line.at[pl.ds(first + shift, size), :, self.rows(piece)]
        ours[...] = (ours[...].astype(F32) + landed[...].astype(F32)).astype(BF16)
        self.push_line(piece, way, zz)

    def wait_ends(self, piece, zz):
        deep = self.group.deep
        if deep == 1:
            return
        if zz == 0:
            arrived(self.line_at(piece, 1, zz), self.z_recv.at[piece, 1])
        if zz == deep - 1:
            arrived(self.line_at(piece, 0, zz), self.z_recv.at[piece, 0])

    def total_line(self, piece, column):
        group, rows = self.group, self.rows(piece)
        total = self.parts[group.z, column, rows, self.cols].astype(F32)
        index = column if self.z_first else 0
        for here, place in ((group.z > 0, group.z + 1), (group.z + 1 < group.deep, group.z)):
            landed = self.line[place, index, rows]
            total = total + jnp.where(here, landed.astype(F32), 0.0)
        return total

    def begin(self, piece):
        if not self.z_first:
            for j in range(1, self.group.nx):
                push(
                    self.at(piece, slice(None), self.group.column(j)),
                    self.landed_x.at[self.group.nx - j - 1, :, self.rows(piece)],
                    self.x_send.at[piece, j],
                    self.x_recv.at[piece, self.group.nx - j],
                    self.group.over_x(j),
                )

    def begin_line(self, piece, zz):
        if self.z_first:
            self.ends(piece, zz)

    def wait_x(self, piece, j):
        landed = self.landed_x.at[j - 1, :, self.rows(piece)]
        arrived(landed, self.x_recv.at[piece, j])
        return landed[...].astype(F32)

    def phase(self, piece, step, zz):
        nx = self.group.nx
        if self.z_first:
            if step < 3:
                self.hand_on(piece, step == 1, zz)
            elif step == 3:
                self.wait_ends(piece, zz)
            return
        if step == 1:
            ours = self.at(piece, slice(None), self.group.x)
            total = ours[...].astype(F32)
            for j in range(1, nx):
                total = total + self.wait_x(piece, j)
            ours[...] = total.astype(BF16)
            self.ends(piece, zz)
        elif step < 4:
            self.hand_on(piece, step == 2, zz)
        else:
            self.wait_ends(piece, zz)

    def third(self, piece):
        if not self.z_first:
            return
        group, rows = self.group, self.rows(piece)
        for j in range(1, group.nx):
            column = group.column(j)
            total = self.total_line(piece, column).astype(BF16)
            self.parts[group.z, column, rows, self.cols] = total
            push(
                self.at(piece, pl.ds(group.z, 1), column),
                self.landed_x.at[group.nx - j - 1, :, rows],
                self.x_send.at[piece, j],
                self.x_recv.at[piece, group.nx - j],
                group.over_x(j),
            )

    def total(self, piece):
        total = self.total_line(piece, self.group.x)
        if self.z_first:
            for j in range(1, self.group.nx):
                total = total + self.wait_x(piece, j)[0]
        return total

    def drain(self, piece, zz):
        deep = self.group.deep
        for way, size in ((0, deep - 1 - zz), (1, zz)):
            if size > 0:
                place = self.at(piece, pl.ds(0, size), self.columns())
                arrived(place, self.z_send.at[piece, way])
        z = pl.ds(0, 1 if self.z_first else deep)
        for j in range(1, self.group.nx):
            arrived(self.at(piece, z, self.group.x), self.x_send.at[piece, j])


class Both:
    def __init__(self, first, second):
        self.both = (first, second)
        self.group = first.group
        self.part, self.pieces, self.last = first.part, first.pieces, first.last

    def rows(self, piece):
        return pl.ds(pl.multiple_of(piece * self.part, self.part), self.part)

    def begin(self, piece):
        for each in self.both:
            each.begin(piece)

    def begin_line(self, piece, zz):
        for each in self.both:
            each.begin_line(piece, zz)

    def phase(self, piece, step, zz):
        for each in self.both:
            each.phase(piece, step, zz)

    def third(self, piece):
        for each in self.both:
            each.third(piece)

    def total(self, piece):
        return jnp.concatenate([each.total(piece) for each in self.both], axis=1)

    def drain(self):
        def at(zz):
            def one(piece, _):
                for each in self.both:
                    each.drain(piece, zz)
                return 0

            lax.fori_loop(0, self.pieces, one, 0)

        at_each_z(self.group, at)


def at_each_z(group, work):
    for zz in range(group.deep):
        pl.when(group.z == zz)(functools.partial(work, zz))


def scatter_ticks(scatter, prepare, finish, after=None):
    def before(time):
        def begin(piece):
            prepare(piece)
            scatter.begin(piece)

        during(time + 1, scatter.pieces, begin)

    def within(time, zz):
        during(time + 1, scatter.pieces, functools.partial(scatter.begin_line, zz=zz))
        for step in range(1, scatter.last + 1):
            during(time - step + 1, scatter.pieces, functools.partial(scatter.phase, step=step, zz=zz))

    def behind(time):
        during(time - 2, scatter.pieces, scatter.third)
        during(time - scatter.last + 1, scatter.pieces, lambda piece: finish(piece, scatter.total(piece)))

    return before, within, behind


def gather_ticks(gather, prepare, ready):
    def before(time):
        if prepare is not None:

            def begin(piece):
                prepare(piece)
                gather.begin(piece)

            during(time, gather.pieces, begin)

    def within(time, zz):
        for step in range(1, gather.last + 1):
            during(time - step, gather.pieces, functools.partial(gather.phase, step=step, zz=zz))

    def behind(time):
        during(time - gather.last, gather.pieces, ready)

    return before, within, behind


def cut(cols, share):
    edge = cols - cols * share // 8
    return pl.ds(0, edge), pl.ds(edge, cols - edge)


def gather_of(group, share, scratch):
    full, *sems = scratch
    first, second = cut(full.shape[3], share)
    return Both(
        Gather(group, full, first, sems[:4], False), Gather(group, full, second, sems[4:], True)
    )


def scatter_of(group, share, scratch):
    parts, *rest = scratch
    first, second = cut(parts.shape[3], share)
    return Both(
        Scatter(group, parts, first, rest[:6], False),
        Scatter(group, parts, second, rest[6:], True),
    )


def gather_scratch(nz, nx, rows, cols, most):
    sems = Gather.sems(nz, nx, pieces_of(rows, most))
    return [pltpu.VMEM((nz, nx, rows, cols), BF16), *sems, *sems]


def scatter_scratch(nz, nx, rows, cols, share, most):
    first, second = cut(cols, share)
    pieces = pieces_of(rows, most)
    return [
        pltpu.VMEM((nz, nx, rows, cols), BF16),
        *Scatter.scratch(nz, nx, rows, first.size, False, pieces),
        *Scatter.scratch(nz, nx, rows, second.size, True, pieces),
    ]


SCATTER_COUNT, GATHER_COUNT = 13, 9


def inverse_rms(rows):
    return lax.rsqrt(jnp.mean(rows * rows, axis=-1, keepdims=True) + EPS)


def wide_dot(terms, dims, tile, store):
    total = terms[0][1].shape[0 if dims is NT else 1]
    for first in range(0, total, tile):
        cols = slice(first, min(first + tile, total))
        products = [
            lax.dot_general(
                left,
                right[cols, :] if dims is NT else right[:, cols],
                (dims, ((), ())),
                preferred_element_type=F32,
            )
            for left, right in terms
        ]
        store(cols, functools.reduce(jnp.add, products))


VMEM_SPEC = pl.BlockSpec(memory_space=pltpu.VMEM)
ANY_SPEC = pl.BlockSpec(memory_space=pl.ANY)
PAIR_SHARE, GATHER_SHARE, SCATTER_SHARE = 3, 1, 2


class Late:
    def __init__(self, given, held, sem):
        self.held = held
        self.copy = pltpu.make_async_copy(given, held, sem)
        self.copy.start()

    def wait(self):
        self.copy.wait()


def late_all(given, scratch):
    return [
        Late(ref, held, sem)
        for ref, held, sem in zip(given, scratch[: len(given)], scratch[len(given) :])
    ]


def late_scratch(*values):
    return [
        *[pltpu.VMEM(value.shape, value.dtype) for value in values],
        *[pltpu.SemaphoreType.DMA] * len(values),
    ]


def lasting(microseconds):
    return pl.CostEstimate(
        flops=int(microseconds * 1.1e9), bytes_accessed=2**20, transcendentals=0
    )


def linked(collective):
    return pltpu.CompilerParams(
        collective_id=collective, has_side_effects=True, vmem_limit_bytes=62 * 2**20
    )


def joined(values):
    return values.reshape(-1, values.shape[-1])


def split(values, *parts):
    return values.reshape(*parts, values.shape[0] // math.prod(parts), values.shape[1])


def project_kernel(
    count, rows_ref, gain_ref, weight_ref, gates_ref, full_out, projected_out, weight_out, *scratch
):
    full = scratch[0]
    staged, full_sems, staged_sems, given, weight, given_sem, out_sem = scratch[GATHER_COUNT:]
    late = Late(weight_ref, given, given_sem)
    group = Group(count)
    gather = gather_of(group, GATHER_SHARE, scratch[:GATHER_COUNT])
    meet(count)
    weight_copy = pltpu.make_async_copy(weight, weight_out, out_sem)
    kinds, width = given.shape[1:]
    blocks = given.shape[0] // 256
    shares, share = full_out.shape[0], full_out.shape[4]

    def full_copy(piece, index):
        rows = gather.rows(piece)
        return pltpu.make_async_copy(
            full.at[:, :, rows, pl.ds(index * share, share)],
            full_out.at[index, :, :, rows],
            full_sems.at[piece, index],
        )

    def staged_copy(piece):
        rows = gather.rows(piece)
        return pltpu.make_async_copy(
            staged.at[:, rows], projected_out.at[:, rows], staged_sems.at[piece]
        )

    def prepare(piece):
        rows = rows_ref[gather.rows(piece)].astype(F32)
        full[group.z, group.x, gather.rows(piece)] = (
            rows * inverse_rms(rows) * gain_ref[...]
        ).astype(BF16)

    def ready(piece):
        rows = gather.rows(piece)
        for index in range(shares):
            full_copy(piece, index).start()

        def store(cols, value):
            staged[:, rows, cols] = split(value, count)

        left = joined(full[:, :, rows])
        wide_dot([(left, weight)], NN, 256, store)
        value = lax.dot_general(
            left, gates_ref[...], (NN, ((), ())), preferred_element_type=F32
        )
        staged[:, rows, kinds * width :] = split(value, count)
        staged_copy(piece).start()

    before, within, behind = gather_ticks(gather, prepare, ready)

    def lay_out(block, _):
        rows = pl.ds(pl.multiple_of(block * 256, 256), 256)
        for kind in range(kinds):
            weight[rows, kind * width : (kind + 1) * width] = given[rows, kind, :]
        return 0

    def tick(time, _):
        before(time)
        pl.when(time == 0)(late.wait)
        lax.fori_loop(
            jnp.minimum(time * 2, blocks), jnp.minimum(time * 2 + 2, blocks), lay_out, 0
        )
        pl.when(time == 4)(weight_copy.start)
        at_each_z(group, functools.partial(within, time))
        behind(time)
        return 0

    lax.fori_loop(0, gather.pieces + gather.last, tick, 0)
    gather.drain()
    weight_copy.wait()

    def finish(piece, _):
        for index in range(shares):
            full_copy(piece, index).wait()
        staged_copy(piece).wait()
        return 0

    lax.fori_loop(0, gather.pieces, finish, 0)


def project(rows, gain, weight, gates, count, shares):
    own, features = rows.shape
    kinds, width = weight.shape[1:]
    cols = kinds * width + gates.shape[1]
    nz, nx = grid_sizes(count)
    return pl.pallas_call(
        functools.partial(project_kernel, count),
        out_shape=[
            jax.ShapeDtypeStruct((shares, nz, nx, own, features // shares), BF16),
            jax.ShapeDtypeStruct((count, own, cols), F32),
            jax.ShapeDtypeStruct((features, kinds * width), BF16),
        ],
        in_specs=[VMEM_SPEC, VMEM_SPEC, ANY_SPEC, VMEM_SPEC],
        out_specs=[ANY_SPEC] * 3,
        scratch_shapes=[
            *gather_scratch(nz, nx, own, features, FEW),
            pltpu.VMEM((count, own, cols), F32),
            pltpu.SemaphoreType.DMA((pieces_of(own, FEW), shares)),
            pltpu.SemaphoreType.DMA((pieces_of(own, FEW),)),
            pltpu.VMEM(weight.shape, BF16),
            pltpu.VMEM((features, kinds * width), BF16),
            *[pltpu.SemaphoreType.DMA] * 2,
        ],
        compiler_params=linked(0),
        cost_estimate=lasting(100),
        name="project",
    )(rows, gain, weight, gates)


def sum_and_gather(scatter, gather, prepare, middle, ready, job=None):
    group = gather.group
    full = gather.both[0].full

    def turn(piece, total):
        full[group.z, group.x, gather.rows(piece)] = middle(piece, total).astype(BF16)
        gather.begin(piece)

    late = scatter.last - 1
    before, sum_within, sum_behind = scatter_ticks(scatter, prepare, turn)
    _, gather_within, gather_behind = gather_ticks(gather, None, ready)

    def tick(time, _):
        before(time)

        def within(zz):
            sum_within(time, zz)
            gather_within(time - late, zz)

        at_each_z(group, within)
        sum_behind(time)
        gather_behind(time - late)
        if job is not None:
            job(time + 1)
        return 0

    lax.fori_loop(-1, gather.pieces + late + gather.last, tick, 0)
    scatter.drain()
    gather.drain()


def branch_kernel(
    count, mixed_ref, weight_ref, input_ref, live_ref, gain_ref, feed_weight_ref,
    down_weight_ref, grad_ref, middle_out, full_out, dgate_out, dup_out, hidden_out, *all_scratch
):
    *scratch, grads, grad_sems, dgate, dup, hidden, feed_sems = all_scratch[:-4]
    lates = late_all((feed_weight_ref, down_weight_ref), all_scratch[-4:])
    feed_weight_ref, down_weight_ref = (late.held for late in lates)
    group = Group(count)
    scatter = scatter_of(group, PAIR_SHARE, scratch[:SCATTER_COUNT])
    gather = gather_of(group, PAIR_SHARE, scratch[SCATTER_COUNT:])
    parts, full = scratch[0], scratch[SCATTER_COUNT]

    def fetch(piece):
        slot = piece % 2
        return pltpu.make_async_copy(
            grad_ref.at[:, :, gather.rows(piece)], grads.at[slot], grad_sems.at[slot]
        )

    fetch(0).start()
    meet(count)

    def prepare(piece):
        rows = gather.rows(piece)

        def store(cols, value):
            parts[:, :, rows, cols] = split(value.astype(BF16), group.deep, group.nx)

        wide_dot([(joined(mixed_ref[:, rows]), weight_ref)], NN, 512, store)

    def middle(piece, total):
        rows = gather.rows(piece)
        values = input_ref[rows].astype(F32) + live_ref[rows] * total
        middle_out[rows] = values
        return values * inverse_rms(values) * gain_ref[...]

    def copies(piece):
        rows = gather.rows(piece)
        return [
            pltpu.make_async_copy(ref.at[:, rows], out.at[:, rows], feed_sems.at[piece, index])
            for index, (ref, out) in enumerate(
                ((dgate, dgate_out), (dup, dup_out), (hidden, hidden_out))
            )
        ] + [
            pltpu.make_async_copy(
                full.at[:, :, rows], full_out.at[:, :, rows], feed_sems.at[piece, 3]
            )
        ]

    def ready(piece):
        rows = gather.rows(piece)
        for late in lates:
            pl.when(piece == 0)(late.wait)
        fetch(piece).wait()
        pl.when(piece + 1 < gather.pieces)(lambda: fetch(piece + 1).start())
        left, grad = joined(full[:, :, rows]), joined(grads[piece % 2])
        total = feed_weight_ref.shape[1]
        for first in range(0, total, 256):
            cols = slice(first, min(first + 256, total))

            def product(a, b, dims):
                return lax.dot_general(a, b, (dims, ((), ())), preferred_element_type=F32)

            gate = product(left, feed_weight_ref[0, cols], NT)
            up = product(left, feed_weight_ref[1, cols], NT)
            dhidden = product(grad, down_weight_ref[cols, :], NT)
            sigmoid = jax.nn.sigmoid(gate)
            active = gate * sigmoid
            hidden[:, rows, cols] = split((active * up).astype(BF16), count)
            dup[:, rows, cols] = split((dhidden * active).astype(BF16), count)
            slope = sigmoid * (1.0 + gate * (1.0 - sigmoid))
            dgate[:, rows, cols] = split((dhidden * up * slope).astype(BF16), count)
        for copy in copies(piece):
            copy.start()

    sum_and_gather(scatter, gather, prepare, middle, ready)

    def finish(piece, _):
        for copy in copies(piece):
            copy.wait()
        return 0

    lax.fori_loop(0, gather.pieces, finish, 0)


def branch_and_feed(mixed, weight, rows, live, gain, feed_weight, down_weight, grad, count):
    own, features = rows.shape
    hidden = feed_weight.shape[1]
    nz, nx = grid_sizes(count)
    return pl.pallas_call(
        functools.partial(branch_kernel, count),
        out_shape=[
            jax.ShapeDtypeStruct((own, features), F32),
            jax.ShapeDtypeStruct((nz, nx, own, features), BF16),
            *[jax.ShapeDtypeStruct((count, own, hidden), BF16)] * 3,
        ],
        in_specs=[VMEM_SPEC] * 5 + [ANY_SPEC] * 3,
        out_specs=[VMEM_SPEC] + [ANY_SPEC] * 4,
        scratch_shapes=[
            *scatter_scratch(nz, nx, own, features, PAIR_SHARE, MANY),
            *gather_scratch(nz, nx, own, features, MANY),
            pltpu.VMEM((2, nz, nx, own // pieces_of(own, MANY), features), BF16),
            pltpu.SemaphoreType.DMA((2,)),
            *[pltpu.VMEM((count, own, hidden), BF16)] * 3,
            pltpu.SemaphoreType.DMA((pieces_of(own, MANY), 4)),
            *late_scratch(feed_weight, down_weight),
        ],
        compiler_params=linked(1),
        cost_estimate=lasting(180),
        name="branch_and_feed",
    )(split(mixed, count), weight, rows, live, gain, feed_weight, down_weight, grad)


TILE = 256


class TileJob:
    def __init__(self, rows_ref, tile, factors, staged, outs, fetch_sem, out_sems):
        self.rows_ref, self.tile, self.factors = rows_ref, tile, factors
        self.staged, self.outs = staged, outs
        self.fetch_sem, self.out_sems = fetch_sem, out_sems
        self.count = rows_ref.shape[3] // TILE

    def span(self, index):
        return pl.ds(pl.multiple_of(index * TILE, TILE), TILE)

    def fetch(self, index):
        return pltpu.make_async_copy(
            self.rows_ref.at[:, :, :, self.span(index)], self.tile, self.fetch_sem
        )

    def results(self, index):
        return [
            pltpu.make_async_copy(
                self.staged.at[which], out.at[:, self.span(index)], self.out_sems.at[which]
            )
            for which, out in enumerate(self.outs)
        ]

    def wait_results(self, index):
        for copy in self.results(index):
            copy.wait()

    def run(self, index):
        self.fetch(index).wait()
        left = joined(self.tile[...])
        pl.when(index > 0)(lambda: self.wait_results(index - 1))
        for which, factor in enumerate(self.factors):
            product = lax.dot_general(
                left, joined(factor[...]), (TN, ((), ())), preferred_element_type=F32
            )
            self.staged[which] = jnp.transpose(product).astype(BF16)
        for copy in self.results(index):
            copy.start()
        pl.when(index + 1 < self.count)(lambda: self.fetch(index + 1).start())


def feed_back_kernel(
    count, dgate_ref, dup_ref, feed_weight_ref, top_ref, middle_ref, live_ref,
    gain_ref, out_weight_ref, mixed_ref, hidden_ref, normed_ref, grad_feed_ref,
    dmiddle_out, dgain_out, dmixed_out, dweight_out, dfeed_out, *all_scratch
):
    lates = late_all((out_weight_ref, mixed_ref, hidden_ref), all_scratch[-6:])
    out_weight_ref, mixed_ref, hidden_ref = (late.held for late in lates)
    *scratch, total_out, tile, grad_tile, staged, grad_staged, fetch_sems, out_sems = (
        all_scratch[:-6]
    )
    group = Group(count)
    scatter = scatter_of(group, PAIR_SHARE, scratch[:SCATTER_COUNT])
    gather = gather_of(group, PAIR_SHARE, scratch[SCATTER_COUNT:])
    parts, full = scratch[0], scratch[SCATTER_COUNT]
    jobs = (
        TileJob(
            normed_ref, tile, (dgate_ref, dup_ref), staged, (dfeed_out.at[0], dfeed_out.at[1]),
            fetch_sems.at[0], out_sems.at[0],
        ),
        TileJob(
            grad_feed_ref, grad_tile, (hidden_ref,), grad_staged, (dfeed_out.at[2],),
            fetch_sems.at[1], out_sems.at[1],
        ),
    )
    for each in jobs:
        each.fetch(0).start()
    meet(count)
    dgain_out[...] = jnp.zeros(dgain_out.shape, F32)
    total_out[...] = jnp.zeros(total_out.shape, F32)

    def prepare(piece):
        rows = gather.rows(piece)

        def store(cols, value):
            parts[:, :, rows, cols] = split(value.astype(BF16), group.deep, group.nx)

        wide_dot(
            [
                (joined(dgate_ref[:, rows]), feed_weight_ref.at[0]),
                (joined(dup_ref[:, rows]), feed_weight_ref.at[1]),
            ],
            NN,
            256,
            store,
        )

    def middle(piece, dnormed):
        rows = gather.rows(piece)
        values = middle_ref[rows]
        scale = inverse_rms(values)
        normed = values * scale
        dgain_out[...] += jnp.sum(dnormed * normed, axis=0, keepdims=True)
        scaled = dnormed * gain_ref[...]
        dmiddle = top_ref[rows].astype(F32) + scale * (
            scaled - normed * jnp.mean(scaled * normed, axis=-1, keepdims=True)
        )
        dmiddle_out[rows] = dmiddle
        return live_ref[rows] * dmiddle

    def ready(piece):
        rows = gather.rows(piece)
        for late in lates[:2]:
            pl.when(piece == 0)(late.wait)
        left, mixed = joined(full[:, :, rows]), joined(mixed_ref[:, rows])

        def store(cols, value):
            dmixed_out[:, rows, cols] = split(value, count)

        wide_dot([(left, out_weight_ref)], NT, 256, store)
        for first in range(0, left.shape[1], 256):
            total_out[first : first + 256] += lax.dot_general(
                left[:, first : first + 256], mixed, (TN, ((), ())), preferred_element_type=F32
            )

    def job(time):
        pl.when(time == 1)(lates[2].wait)
        for which, each in enumerate(jobs):
            pl.when((time % 2 == which) & (time < 2 * each.count))(
                functools.partial(each.run, time // 2)
            )

    sum_and_gather(scatter, gather, prepare, middle, ready, job)
    last = gather.pieces + scatter.last + gather.last
    lax.fori_loop(last, max(2 * jobs[0].count, last), lambda time, _: (job(time), 0)[1], 0)
    for each in jobs:
        each.wait_results(each.count - 1)
    dweight_out[...] = total_out[...].astype(BF16)


def feed_back(
    dgate, dup, feed_weight, top, middle, live, gain, out_weight, mixed, hidden, normed, grad_feed,
    count,
):
    own, features = middle.shape
    nz, nx = grid_sizes(count)
    width, units = out_weight.shape[0], feed_weight.shape[1]
    return pl.pallas_call(
        functools.partial(feed_back_kernel, count),
        out_shape=[
            jax.ShapeDtypeStruct((own, features), F32),
            jax.ShapeDtypeStruct((1, features), F32),
            jax.ShapeDtypeStruct((count, own, width), F32),
            jax.ShapeDtypeStruct((features, width), BF16),
            jax.ShapeDtypeStruct((3, units, features), BF16),
        ],
        in_specs=[VMEM_SPEC] * 7 + [ANY_SPEC] * 5,
        out_specs=[VMEM_SPEC] * 4 + [ANY_SPEC],
        scratch_shapes=[
            *scatter_scratch(nz, nx, own, features, PAIR_SHARE, MANY),
            *gather_scratch(nz, nx, own, features, MANY),
            pltpu.VMEM((features, width), F32),
            pltpu.VMEM((nz, nx, own, TILE), BF16),
            pltpu.VMEM((nz, nx, own, TILE), BF16),
            pltpu.VMEM((2, units, TILE), BF16),
            pltpu.VMEM((1, units, TILE), BF16),
            pltpu.SemaphoreType.DMA((2,)),
            pltpu.SemaphoreType.DMA((2, 2)),
            *late_scratch(out_weight, split(mixed, count), hidden),
        ],
        compiler_params=linked(2),
        cost_estimate=lasting(180),
        name="feed_back",
    )(
        dgate, dup, feed_weight, top, middle, live, gain, out_weight,
        split(mixed, count), hidden, normed, grad_feed,
    )


class Replicas:
    def __init__(self, values, from_core, from_y, over_back, over_home, sems):
        self.values, self.from_core, self.from_y = values, from_core, from_y
        self.over_back, self.over_home = over_back, over_home
        self.core_sems, self.y_sems, self.back_sems, self.home_sems = sems
        me = lax.axis_index("dp")
        self.lines = lax.axis_size("dp") // 2
        self.y, self.core = me // 2, me % 2

    @staticmethod
    def scratch(rows, cols, replicas):
        lines, share = replicas // 2, rows // replicas
        return [
            pltpu.VMEM((replicas, share, cols), BF16),
            pltpu.VMEM((lines, share, cols), BF16),
            pltpu.VMEM((max(lines - 1, 1), share, cols), BF16),
            pltpu.VMEM((max(lines - 1, 1), share, cols), BF16),
            pltpu.VMEM((lines, share, cols), BF16),
            *[pltpu.SemaphoreType.DMA((2, lines))] * 4,
        ]

    def share(self, core, y):
        return core * self.lines + y

    def peer(self, y, core):
        return {"dp": y * 2 + core}

    def line(self, k):
        return (self.y + k) % self.lines

    draining = False

    def push(self, source, target, send_sem, recv_sem, device):
        copy = pltpu.make_async_remote_copy(
            source, target, send_sem, recv_sem, device_id=device, device_id_type=MESH
        )
        if self.draining:
            copy.wait_send()
        else:
            copy.start()

    def drain(self):
        self.draining = True
        for k in range(self.lines):
            self.start(k)
            self.cores(k)
        self.over_y()
        self.back()
        self.draining = False

    def add(self, share, others):
        step = 64

        def some(block, _):
            rows = pl.ds(pl.multiple_of(block * step, step), step)
            total = self.values[share, rows].astype(F32)
            for ref, index in others:
                total = total + ref[index, rows].astype(F32)
            self.values[share, rows] = total.astype(BF16)
            return 0

        lax.fori_loop(0, self.values.shape[1] // step, some, 0)

    def start(self, k):
        y = self.line(k)
        self.push(
            self.values.at[self.share(1 - self.core, y)],
            self.from_core.at[y],
            self.core_sems.at[0, k],
            self.core_sems.at[1, k],
            self.peer(self.y, 1 - self.core),
        )

    def cores(self, k):
        y = self.line(k)
        share = self.share(self.core, y)
        if not self.draining:
            arrived(self.from_core.at[y], self.core_sems.at[1, k])
            self.add(share, [(self.from_core, y)])
        if k > 0:
            self.push(
                self.values.at[share],
                self.from_y.at[self.lines - k - 1],
                self.y_sems.at[0, k],
                self.y_sems.at[1, self.lines - k],
                self.peer(y, self.core),
            )

    def over_y(self):
        share = self.share(self.core, self.y)
        if not self.draining:
            for k in range(1, self.lines):
                arrived(self.from_y.at[k - 1], self.y_sems.at[1, k])
            self.add(share, [(self.from_y, k) for k in range(self.lines - 1)])
        for k in range(1, self.lines):
            self.push(
                self.values.at[share],
                self.over_back.at[self.lines - k - 1],
                self.back_sems.at[0, k],
                self.back_sems.at[1, self.lines - k],
                self.peer(self.line(k), self.core),
            )
        self.send_home(0)

    def own(self, k):
        return self.values.at[self.share(self.core, self.y)] if k == 0 else self.over_back.at[k - 1]

    def send_home(self, k):
        self.push(
            self.own(k),
            self.over_home.at[k],
            self.home_sems.at[0, k],
            self.home_sems.at[1, k],
            self.peer(self.y, 1 - self.core),
        )

    def back(self):
        for k in range(1, self.lines):
            if not self.draining:
                arrived(self.over_back.at[k - 1], self.back_sems.at[1, k])
            self.send_home(k)

    def home(self):
        for k in range(self.lines):
            arrived(self.over_home.at[k], self.home_sems.at[1, k])

    def totals(self):
        for k in range(self.lines):
            yield self.own(k), self.share(self.core, self.line(k))
            yield self.over_home.at[k], self.share(1 - self.core, self.line(k))


class SmallSum:
    def __init__(self, small, seen, send_sems, recv_sems, axis, cols):
        self.small, self.seen, self.cols = small, seen, pl.ds(0, cols)
        self.send_sems, self.recv_sems, self.axis = send_sems, recv_sems, axis
        self.me, self.size = lax.axis_index(axis), lax.axis_size(axis)

    def copy(self, k):
        place = self.seen.at[self.me, :, self.cols]
        return pltpu.make_async_remote_copy(
            place, place, self.send_sems.at[k], self.recv_sems.at[self.size - k],
            device_id={self.axis: (self.me + k) % self.size}, device_id_type=MESH,
        )

    def start(self):
        self.seen[self.me, :, self.cols] = self.small[:, self.cols]
        for k in range(1, self.size):
            self.copy(k).start()

    def finish(self):
        for k in range(1, self.size):
            landed = self.seen.at[(self.me + k) % self.size, :, self.cols]
            arrived(landed, self.recv_sems.at[k])
        total = self.seen[0, :, self.cols]
        for other in range(1, self.size):
            total = total + self.seen[other, :, self.cols]
        self.small[:, self.cols] = total

    def drain(self):
        for k in range(1, self.size):
            self.copy(k).wait_send()


def input_back_kernel(
    count, grad_ref, weight_ref, gates_ref, later_ref, input_ref, gain_ref, dgain_ref, dnorm_ref,
    dtaps_ref, dparams_ref, wout_ref, normed_ref, grad_out, norm1_out, norm2_out, gain_out,
    taps_out, params_out, dmain_out, drest_out, *scratch
):
    *scratch, small, normed, normed_sem = scratch
    late = Late(normed_ref, normed, normed_sem)
    normed_ref = normed
    parts, rest = scratch[0], scratch[SCATTER_COUNT:]
    values = rest[0]
    small_scratch, staged, out_sems = rest[9:15], *rest[15:]
    group = Group(count)
    scatter = scatter_of(group, SCATTER_SHARE, scratch[:SCATTER_COUNT])
    replicas = Replicas(*rest[:5], rest[5:9])
    meet(count, lax.axis_size("dp"))
    tall = norm1_out.shape[1] // 8
    edges = [tall, 2 * tall, 2 * tall + 128]
    small[...] = jnp.zeros(small.shape, F32)
    norm1_out[...] = jnp.zeros(norm1_out.shape, F32)
    for row in range(8):
        small[row : row + 1, edges[0] : edges[1]] = dnorm_ref[:, row * tall : (row + 1) * tall]
    small[0:1, edges[1] : edges[2]] = dgain_ref[...]
    small[0:4, edges[2] :] = dtaps_ref[...]
    small[4:6, edges[2] : edges[2] + 128] = dparams_ref[...]
    near = SmallSum(small, *small_scratch[:3], "heads", edges[2])
    far = SmallSum(small, *small_scratch[3:6], "dp", small.shape[1])
    width = grad_ref.shape[2]
    values[:, :, width:] = split(wout_ref[...], values.shape[0])

    def prepare(piece):
        rows = scatter.rows(piece)

        def store(cols, value):
            parts[:, :, rows, cols] = split(value.astype(BF16), group.deep, group.nx)

        left, edge = joined(grad_ref[:, rows]), weight_ref.shape[1]
        wide_dot(
            [(left[:, :edge], weight_ref), (left[:, edge:], gates_ref)], NT, 256, store
        )

    def end(piece, dnormed):
        rows = scatter.rows(piece)
        given = input_ref[rows].astype(F32)
        scale = inverse_rms(given)
        normed = given * scale
        norm1_out[...] += jnp.sum(dnormed * normed, axis=0, keepdims=True)
        scaled = dnormed * gain_ref[...]
        grad_out[rows] = later_ref[rows] + scale * (
            scaled - normed * jnp.mean(scaled * normed, axis=-1, keepdims=True)
        )

    def weight_share(core, y, first=False):
        if first:
            late.wait()
        share = replicas.share(core, y)
        left = joined(normed_ref[share])
        grads = joined(grad_ref[...])
        for first in range(0, width, 384):
            cols = slice(first, min(first + 384, width))
            staged[:, cols] = lax.dot_general(
                left, grads[:, cols], (TN, ((), ())), preferred_element_type=F32
            ).astype(BF16)

        def some(block, _):
            rows = pl.ds(pl.multiple_of(block * 64, 64), 64)
            values[share, rows, :width] = staged[rows]
            return 0

        lax.fori_loop(0, staged.shape[0] // 64, some, 0)

    def other_core(k):
        weight_share(1 - replicas.core, replicas.line(k), k == replicas.lines - 1)
        replicas.start(k)

    def this_core(k):
        weight_share(replicas.core, replicas.line(k))
        replicas.cores(k)

    steps = []
    for k in range(replicas.lines - 1, -1, -1):
        steps += [functools.partial(other_core, k), functools.partial(this_core, k)]
    while len(steps) < 7:
        steps.append(lambda: None)
    steps.append(replicas.over_y)

    before, within, behind = scatter_ticks(scatter, prepare, end)

    def tick(time, _):
        before(time)
        at_each_z(group, functools.partial(within, time))
        behind(time)
        for index, step in enumerate(steps):
            pl.when(time == index)(step)
        return 0

    lax.fori_loop(-1, max(scatter.pieces + scatter.last - 1, len(steps)), tick, 0)
    for row in range(8):
        small[row : row + 1, : edges[0]] = norm1_out[:, row * tall : (row + 1) * tall]
    near.start()
    replicas.back()
    near.finish()
    far.start()
    far.finish()
    for row in range(8):
        cols = slice(row * tall, (row + 1) * tall)
        norm1_out[:, cols] = small[row : row + 1, : edges[0]]
        norm2_out[:, cols] = small[row : row + 1, edges[0] : edges[1]]
    gain_out[...] = small[0:1, edges[1] : edges[2]]
    kind_width = taps_out.shape[2]
    for kind in range(taps_out.shape[0]):
        first = edges[2] + kind * kind_width
        taps_out[kind] = small[0:4, first : first + kind_width]
    params_out[...] = small[4:6, edges[2] : edges[2] + 128]
    replicas.home()
    part = dmain_out.shape[3]
    outs = []
    for index, (total, share) in enumerate(replicas.totals()):
        for kind in range(4):
            outs.append((total.at[:, pl.ds(kind * part, part)], dmain_out.at[kind, share], index))
        rest_cols = pl.ds(4 * part, drest_out.shape[2])
        outs.append((total.at[:, rest_cols], drest_out.at[share], index))
    outs = [
        pltpu.make_async_copy(source, target, out_sems.at[index, place % 5])
        for place, (source, target, index) in enumerate(outs)
    ]
    for copy in outs:
        copy.start()
    scatter.drain()
    replicas.drain()
    near.drain()
    far.drain()
    for copy in outs:
        copy.wait()


def input_back(
    grad, weight, gates, later, rows, gain, dgain, dnorm, dtaps, dparams, grad_wout, normed, count,
    replica_count,
):
    own, features = rows.shape
    nz, nx = grid_sizes(count)
    width, share = grad_wout.shape[1], features // replica_count
    cols = grad.shape[1] + width
    small_cols = features // 4 + 128 + dtaps.shape[1]
    dma = pltpu.SemaphoreType.DMA
    return pl.pallas_call(
        functools.partial(input_back_kernel, count),
        out_shape=[
            jax.ShapeDtypeStruct((own, features), F32),
            *[jax.ShapeDtypeStruct((1, features), F32)] * 2,
            jax.ShapeDtypeStruct(dgain.shape, F32),
            jax.ShapeDtypeStruct((3, 4, width), F32),
            jax.ShapeDtypeStruct(dparams.shape, F32),
            jax.ShapeDtypeStruct((4, replica_count, share, width), BF16),
            jax.ShapeDtypeStruct((replica_count, share, cols - 4 * width), BF16),
        ],
        in_specs=[VMEM_SPEC] * 11 + [ANY_SPEC],
        out_specs=[VMEM_SPEC] * 6 + [ANY_SPEC] * 2,
        scratch_shapes=[
            *scatter_scratch(nz, nx, own, features, SCATTER_SHARE, FEW),
            *Replicas.scratch(features, cols, replica_count),
            pltpu.VMEM((count, 8, small_cols), F32),
            dma((count,)),
            dma((count,)),
            pltpu.VMEM((replica_count, 8, small_cols), F32),
            dma((replica_count,)),
            dma((replica_count,)),
            pltpu.VMEM((share, grad.shape[1]), BF16),
            dma((replica_count, 5)),
            pltpu.VMEM((8, small_cols), F32),
            pltpu.VMEM(normed.shape, BF16),
            dma,
        ],
        compiler_params=linked(3),
        cost_estimate=lasting(120),
        name="input_back",
    )(
        split(grad, count), weight, gates, later, rows, gain, dgain, dnorm, dtaps, dparams,
        grad_wout, normed,
    )


def results_kernel(main_ref, rest_ref, feed_ref, main_out, wout_out, gate_up_out, down_out):
    for kind in range(main_ref.shape[0]):
        main_out[:, kind, :] = main_ref[kind].astype(F32)
    wout_out[...] = jnp.transpose(rest_ref[:, 128:].astype(F32))
    gate_up_out[...] = feed_ref[:2].astype(F32)
    down_out[...] = feed_ref[2].astype(F32)


def results(main, rest, feed):
    kinds, features, width = main.shape
    units = feed.shape[1]
    step = 256
    return pl.pallas_call(
        results_kernel,
        grid=(features // step,),
        in_specs=[
            pl.BlockSpec((kinds, step, width), lambda i: (0, i, 0)),
            pl.BlockSpec((step, rest.shape[1]), lambda i: (i, 0)),
            pl.BlockSpec((3, units, step), lambda i: (0, 0, i)),
        ],
        out_specs=[
            pl.BlockSpec((step, kinds, width), lambda i: (i, 0, 0)),
            pl.BlockSpec((width, step), lambda i: (0, i)),
            pl.BlockSpec((2, units, step), lambda i: (0, 0, i)),
            pl.BlockSpec((units, step), lambda i: (0, i)),
        ],
        out_shape=[
            jax.ShapeDtypeStruct((features, kinds, width), F32),
            jax.ShapeDtypeStruct((width, features), F32),
            jax.ShapeDtypeStruct((2, units, features), F32),
            jax.ShapeDtypeStruct((units, features), F32),
        ],
        compiler_params=pltpu.CompilerParams(vmem_limit_bytes=48 * 2**20),
        name="results",
    )(main, rest, feed)


def on_device(
    block_in,
    seq_counts,
    norm1_gain,
    w_qkvg,
    conv_weight,
    w_gates,
    gate_params,
    out_gain,
    w_out,
    norm2_gain,
    w_gate_up,
    w_down,
    cotangent,
):
    own_rows, features = block_in.shape
    count = lax.axis_size("heads")
    all_rows = own_rows * count
    width = conv_weight.shape[2]
    heads = gate_params.shape[1]
    longer = seq_counts[0, 1:2]
    first_row = lax.axis_index("heads") * own_rows
    row_index = first_row + jnp.arange(own_rows, dtype=jnp.int32)
    live_own = jnp.where(longer[0] > 0, True, row_index < seq_counts[0, 0] * SEQ_SHORT)
    live_own = live_own.astype(F32)[:, None]
    gates_weight = jnp.pad(
        w_gates.reshape(features, 2 * heads), ((0, 0), (0, 128 - 2 * heads))
    )
    full_normed1, projected, weight = project(
        block_in, norm1_gain[None], w_qkvg, gates_weight, count, lax.axis_size("dp")
    )
    projected = projected.reshape(all_rows, -1)
    taps = jnp.transpose(conv_weight, (1, 0, 2)).reshape(4, 3 * width)
    params = jnp.pad(gate_params, ((0, 0), (0, 128 - heads)))
    gain_row = out_gain[None]
    mixed, *saved, grad_feed = mixer_forward(
        longer, projected, taps, params, gain_row, cotangent, live_own, count
    )
    feed_weight = jnp.transpose(w_gate_up, (1, 2, 0))
    middle, full_normed2, grad_gate, grad_up, hidden = branch_and_feed(
        mixed,
        w_out,
        block_in,
        live_own,
        norm2_gain[None],
        feed_weight,
        w_down,
        grad_feed,
        count,
    )
    grad_middle, grad_gain2, grad_mixed, grad_wout, early = feed_back(
        grad_gate,
        grad_up,
        feed_weight,
        cotangent,
        middle,
        live_own,
        norm2_gain[None],
        w_out,
        mixed,
        hidden,
        full_normed2,
        grad_feed,
        count,
    )
    early = lax.psum(early, "dp")
    dprojected, dtaps, dparams, dgain, layer_out = mixer_backward(
        longer,
        grad_mixed.reshape(all_rows, width),
        projected,
        saved,
        taps,
        params,
        gain_row,
        hidden,
        w_down,
        middle,
        live_own,
        count,
    )

    grad_in, grad_gain1, grad_gain2, dgain, grad_conv, dparams, grad_main, grad_rest = input_back(
        dprojected,
        weight,
        gates_weight,
        grad_middle,
        block_in,
        norm1_gain[None],
        dgain,
        grad_gain2,
        dtaps,
        dparams,
        grad_wout,
        full_normed1,
        count,
        lax.axis_size("dp"),
    )
    grad_main = grad_main.reshape(4, features, width)
    grad_rest = grad_rest.reshape(features, -1)
    grad_qkvg, grad_out_weight, grad_gate_up, grad_down = results(grad_main, grad_rest, early)
    return (
        layer_out,
        grad_in,
        grad_gain1[0],
        grad_qkvg,
        grad_conv,
        grad_rest[:, : 2 * heads].reshape(w_gates.shape).astype(F32),
        dparams[:, :heads],
        dgain[0],
        grad_out_weight,
        grad_gain2[0],
        jnp.transpose(grad_gate_up, (2, 0, 1)),
        grad_down,
    )


def solution(mesh):
    return jax.shard_map(
        on_device,
        mesh=mesh,
        in_specs=(
            P(("dp", "heads"), None),
            P("dp", None),
            P(),
            P(None, None, "heads"),
            P(None, None, "heads"),
            P(None, None, "heads"),
            P(None, "heads"),
            P(),
            P("heads", None),
            P(),
            P(None, None, "heads"),
            P("heads", None),
            P(("dp", "heads"), None),
        ),
        out_specs=(
            P(("dp", "heads"), None),
            P(("dp", "heads"), None),
            P(),
            P(None, None, "heads"),
            P(None, None, "heads"),
            P(None, None, "heads"),
            P(None, "heads"),
            P(),
            P("heads", None),
            P(),
            P(None, None, "heads"),
            P("heads", None),
        ),
        check_vma=False,
    )
```
